32 devices in a mesh: groups: 2 (over x), inst: 4 (over z), tp: 4 (over y, core).
Axes of the slice: x: 2, y: 2, z: 4, core: 2. Of those that a mesh axis runs over, the one named last changes fastest.
Arguments:
- res_pool: bfloat16 [8, 8, 64, 16, 256], P(('groups', 'inst'), 'tp'), parts along dimension 0, may hold values from -6 to 6
- res_table: int32 [8, 125, 8], P(('groups', 'inst')), parts along dimension 0, may hold values from 0 to 63
- res_len: int32 [8, 125], P(('groups', 'inst')), parts along dimension 0, may hold values from 1 to 128
- out_pool: bfloat16 [8, 8, 64, 16, 256], P(('groups', 'inst'), 'tp'), parts along dimension 0, may hold values from -6 to 6, as said below
- src_table: int32 [8, 2, 32], P(('groups', 'inst')), parts along dimension 0, may hold values from 0 to 63, as said below
- mig_len: int32 [16], P('groups'), parts along dimension 0, may hold values from 1 to 512
- mig_dest: int32 [16], P('groups'), parts along dimension 0, may hold values from 0 to 3, as said below
- queries: bfloat16 [1024, 4, 64, 128], P(('groups', 'inst'), None, 'tp'), parts along dimension 0, may hold values from -480 to 480
- new_kv: bfloat16 [1024, 4, 8, 256], P(('groups', 'inst'), None, 'tp'), parts along dimension 0, may hold values from -6 to 6
- out_weight: bfloat16 [8192, 8192], P('tp'), may hold values from -0.75 to 0.75
Outputs:
- arrived: bfloat16 [8, 3, 8, 512, 256], P(('groups', 'inst'), None, 'tp'), parts along dimension 0
- hidden: bfloat16 [8192, 4096], P('tp', ('groups', 'inst')), parts along dimension 1
The draws below stay inside these ranges and needn't reach their ends.
There are 2 independent parts, one for each index of `groups`. The reference program is written for one: setup_inputs(seed, part) draws one part's arguments, and reference() takes and returns one part's arrays. A program takes and returns all parts, laid end to end along the dimension named above; an argument that names none is the same for every part. Nothing has to cross between parts.
Inputs may be any that keep to these rules, and one draw needn't show every extreme that they name: `mig_dest`: no request stays on its source instance; the 2 requests of one instance go to different instances; half of the instances receive exactly 3 requests and the other half one. `src_table`: the entries of one instance are all different. `out_pool`: head slots s and s2 hold equal entries where s * 1 equals s2 * 1.
All inputs are finite; a program needn't handle non-finite values.
Results may differ from the reference program's by a relative error of at most 0.0053.
Values may be sent and summed in bfloat16 or wider, within the bound.
No kernel may reach another device: no remote copies, remote signals or barrier semaphores. Data moves between devices by JAX's collectives and lax.ppermute only.
A program may use at most 192 MiB of HBM per device.

```python
import math
import jax
import jax.numpy as jnp
from jax import lax

D = 8192
QH = 64
KVH = 8
HD = 128
BLOCK = 16
STEPS = 4
MAXB = 32
RES_BLK = 8
POOL = 64
BATCH = 128
MIG_DEV = 2
CAP = 3
KV_SLOTS = 8
RES_DEV = 125
ROWS = 512
TOKENS = 2048
MIGR = 8
OUTB = 64
N_INST = 4


def draw_out_pool(key, part):
    key = jax.random.fold_in(key, 11)
    shape = (N_INST, KVH, OUTB, BLOCK, 2 * HD)
    base = jnp.clip(jax.random.normal(key, shape, jnp.float32), -6.0, 6.0)
    return jnp.repeat(base, KV_SLOTS // KVH, axis=1).astype(jnp.bfloat16)


def draw_queries(key, part):
    key = jax.random.fold_in(key, 12)
    shape = (ROWS, STEPS, QH, HD)
    base = jnp.clip(jax.random.normal(key, shape, jnp.float32), -6.0, 6.0)
    return base.astype(jnp.bfloat16)


def draw_mig_dest(key, part):
    key = jax.random.fold_in(key, 13)
    order_perm = jax.random.permutation(key, N_INST).astype(jnp.int32)
    position = jnp.zeros((N_INST,), jnp.int32).at[order_perm].set(jnp.arange(N_INST, dtype=jnp.int32))
    odd_slot = (position % 2)[:, None]
    offsets = jnp.arange(MIG_DEV, dtype=jnp.int32)[None, :]
    odd_step = jnp.where(offsets == 0, 1, 2 * offsets)
    even_step = 1 + 2 * offsets
    step = jnp.where(odd_slot == 1, odd_step, even_step)
    targets = order_perm[(position[:, None] + step) % N_INST]
    return targets.reshape(MIGR).astype(jnp.int32)


def draw_src_table(key, part):
    key = jax.random.fold_in(key, 14)
    sub_keys = jax.random.split(key, N_INST)
    tables = jax.vmap(lambda one_key: jax.random.permutation(one_key, OUTB))(sub_keys)
    return tables.reshape(N_INST, MIG_DEV, MAXB).astype(jnp.int32)


def place_ends(values, rng, least, high):
    dims = values.shape
    index_at = [jax.random.randint(jax.random.fold_in(rng, axis), (), 0, dims[axis]) for axis in range(len(dims))]
    values = values.at[tuple(index_at)].set(least)
    longest = dims.index(max(dims))
    index_at[longest] = (index_at[longest] + 1) % dims[longest]
    return values.at[tuple(index_at)].set(high)


def raised(values, rng, source, target, blocks, factor):
    def block_of(dim):
        return (jnp.arange(values.shape[dim]) // (values.shape[dim] // blocks)).reshape((-1,) + (1,) * (values.ndim - 1 - dim))

    near = jax.random.permutation(rng, blocks)[block_of(target)]
    far = (block_of(target) + blocks // 2) % blocks
    return jnp.where((block_of(source) == near) | (block_of(source) == far), factor * values, values)


def block_scale(own_key, dims, cuts, smallest, top_value):
    def one(axis_at, shards_of):
        heights = jax.random.uniform(jax.random.fold_in(jax.random.fold_in(own_key, 6), axis_at), (shards_of,), jnp.float32, smallest / len(cuts), top_value / len(cuts))
        return jnp.repeat(jnp.exp(heights), dims[axis_at] // shards_of).reshape((-1,) + (1,) * (len(dims) - axis_at - 1))

    gain = one(*cuts[0])
    for cut in cuts[1:]:
        gain = gain * one(*cut)
    return gain


def centred(stream_key, shape, width, bound, cuts=(), kind=jnp.bfloat16):
    gain = block_scale(stream_key, shape, cuts, -0.22, 0.18) if cuts else 1.0
    array = jax.random.normal(stream_key, shape, jnp.float32) * width * gain
    return jnp.minimum(jnp.maximum(array, -bound), bound).astype(kind)


def gaussian_with(stream_key, shape, scale, most, shards, heavy, held_as=jnp.bfloat16):
    result = scale * jax.random.normal(stream_key, shape, jnp.float32)
    if shards:
        result = result * block_scale(stream_key, shape, shards, -0.22, 0.18)
    return jnp.clip(raised(result, jax.random.fold_in(stream_key, 3), *heavy), -most, most).astype(held_as)


def setup_inputs(seed: int = 0, part: int = 0) -> dict:
    keys = jax.random.split(jax.random.key(seed), 11)
    own_keys = jax.random.split(jax.random.fold_in(keys[10], part), 11)
    return {
        "res_pool": centred(own_keys[0], (N_INST, KV_SLOTS, POOL, BLOCK, 2 * HD), 1.0, 6.0, ((0, 4), (1, 4))),
        "res_table": place_ends(jax.random.randint(own_keys[1], (N_INST, RES_DEV, RES_BLK), 0, POOL), jax.random.fold_in(own_keys[1], 1), 0, POOL - 1).astype(jnp.int32),
        "res_len": place_ends(jax.random.randint(own_keys[2], (N_INST, RES_DEV), 1, RES_BLK * BLOCK + 1), jax.random.fold_in(own_keys[2], 1), 1, RES_BLK * BLOCK).astype(jnp.int32),
        "out_pool": draw_out_pool(jax.random.fold_in(jax.random.fold_in(keys[10], part), 71), part),
        "src_table": draw_src_table(jax.random.fold_in(jax.random.fold_in(keys[10], part), 71), part),
        "mig_len": place_ends(jax.random.randint(own_keys[5], (MIGR,), 1, MAXB * BLOCK + 1), jax.random.fold_in(own_keys[5], 1), 1, MAXB * BLOCK).astype(jnp.int32),
        "mig_dest": draw_mig_dest(jax.random.fold_in(jax.random.fold_in(keys[10], part), 71), part),
        "queries": draw_queries(jax.random.fold_in(jax.random.fold_in(keys[10], part), 71), part),
        "new_kv": centred(own_keys[8], (ROWS, STEPS, KV_SLOTS, 2 * HD), 1.0, 6.0, ((0, 4), (2, 4))),
        "out_weight": gaussian_with(keys[9], (QH * HD, D), HD ** -0.5, 0.75, ((0, 4),), (0, 1, 4, 2.0)),
    }


def attend(query_in, context, lengths, newest, layout):
    head_width = query_in.shape[-1]
    step_count = query_in.shape[1]
    inv_root = 1.0 / math.sqrt(head_width)
    query_f = query_in.astype(jnp.float32)
    key_part = context[..., :head_width].astype(jnp.float32)
    value_part = context[..., head_width:].astype(jnp.float32)
    fresh_keys = newest[..., :head_width].astype(jnp.float32)
    fresh_values = newest[..., head_width:].astype(jnp.float32)
    cached_scores = jnp.einsum('rsngd,' + layout + '->rsngc', query_f, key_part) * inv_root
    fresh_scores = jnp.einsum('rsngd,rtnd->rsngt', query_f, fresh_keys) * inv_root
    extent = context.shape[2]
    in_range = (jnp.arange(extent, dtype=jnp.int32)[None, :] < lengths[:, None])[:, None, None, None, :]
    causal = (jnp.arange(step_count, dtype=jnp.int32)[None, :] <= jnp.arange(step_count, dtype=jnp.int32)[:, None])[None, :, None, None, :]
    largest = jnp.maximum(lax.optimization_barrier(jnp.max(jnp.where(in_range, cached_scores, -jnp.inf), axis=-1)), lax.optimization_barrier(jnp.max(jnp.where(causal, fresh_scores, -jnp.inf), axis=-1)))
    cached_weights = jnp.where(in_range, jnp.exp(cached_scores - largest[..., None]), 0.0)
    fresh_weights = jnp.where(causal, jnp.exp(fresh_scores - largest[..., None]), 0.0)
    totals = lax.optimization_barrier(jnp.sum(cached_weights, axis=-1)) + lax.optimization_barrier(jnp.sum(fresh_weights, axis=-1))
    cached_round = lax.optimization_barrier(cached_weights.astype(jnp.bfloat16)).astype(jnp.float32)
    fresh_round = lax.optimization_barrier(fresh_weights.astype(jnp.bfloat16)).astype(jnp.float32)
    blended = jnp.einsum('rsngc,' + layout + '->rsngd', cached_round, value_part)
    blended = blended + jnp.einsum('rsngt,rtnd->rsngd', fresh_round, fresh_values)
    return (blended / totals[..., None]).astype(jnp.bfloat16)

def reference(res_pool, res_table, res_len, out_pool, src_table, mig_len, mig_dest, queries, new_kv, out_weight):
    per_slot = QH // KV_SLOTS
    request_ids = jnp.arange(MIGR, dtype=jnp.int32)
    same_dest = mig_dest[:, None] == mig_dest[None, :]
    standing = lax.optimization_barrier(jnp.sum(same_dest & (request_ids[None, :] < request_ids[:, None]), axis=1)).astype(jnp.int32)

    def arrivals(instance):
        matches = (mig_dest[None, :] == instance) & (standing[None, :] == jnp.arange(CAP, dtype=jnp.int32)[:, None])
        request = lax.optimization_barrier(jnp.sum(jnp.where(matches, request_ids[None, :], 0), axis=1)).astype(jnp.int32)
        lengths = lax.optimization_barrier(jnp.sum(jnp.where(matches, mig_len[None, :], 0), axis=1)).astype(jnp.int32)
        sources = request // MIG_DEV
        tables = src_table[sources, request % MIG_DEV]
        blocks = jax.vmap(lambda src_inst, src_ids: out_pool[src_inst][:, src_ids])(sources, tables)
        flattened = blocks.reshape(CAP, KV_SLOTS, MAXB * BLOCK, 2 * HD)
        inside = (jnp.arange(MAXB * BLOCK, dtype=jnp.int32)[None, :] < lengths[:, None])[:, None, :, None]
        return (jnp.where(inside, flattened, jnp.zeros_like(flattened)), lengths)

    def per_instance(instance):
        arrived, lengths = arrivals(instance)
        row_queries = lax.dynamic_slice_in_dim(queries, instance * BATCH, BATCH, 0)
        row_queries = row_queries.reshape(BATCH, STEPS, KV_SLOTS, per_slot, HD)
        newest = lax.dynamic_slice_in_dim(new_kv, instance * BATCH, BATCH, 0)
        block_ids = res_table[instance]
        context = res_pool[instance][:, block_ids].reshape(KV_SLOTS, RES_DEV, RES_BLK * BLOCK, 2 * HD)
        resident_out = attend(row_queries[:RES_DEV], context, res_len[instance], newest[:RES_DEV], 'nrcd')
        arrival_out = attend(row_queries[RES_DEV:], arrived, lengths, newest[RES_DEV:], 'rncd')
        blended = jnp.concatenate([resident_out, arrival_out], axis=0).reshape(BATCH * STEPS, QH * HD)
        return (arrived, blended)
    arrived, blended = lax.map(per_instance, jnp.arange(N_INST, dtype=jnp.int32))
    blended = blended.reshape(TOKENS, QH * HD)
    hidden = lax.dot_general(out_weight, blended, (((0,), (1,)), ((), ())), preferred_element_type=jnp.float32)
    return (arrived, hidden.astype(jnp.bfloat16))
```

```python
import functools
import math

import jax
import jax.numpy as jnp
from jax import lax
from jax.experimental import pallas as pl
from jax.experimental.pallas import tpu as pltpu
from jax.sharding import PartitionSpec as P

CORES = 2
LOW = -1e30
MIB = 1 << 20
LANES = 128


def params(limit):
    return pltpu.CompilerParams(vmem_limit_bytes=limit * MIB)


def dot_t(left, right):
    return lax.dot_general(
        left, right, (((1,), (1,)), ((), ())), preferred_element_type=jnp.float32
    )


def row_plan(dest_ref, inst, cap):
    requests = [jnp.int32(-1)] * cap
    seen = jnp.int32(0)
    for g in range(dest_ref.shape[0]):
        here = dest_ref[g] == inst
        requests = [jnp.where(here & (seen == a), g, requests[a]) for a in range(cap)]
        seen = seen + here.astype(jnp.int32)
    return requests


def standing_of(dest_ref, request):
    dest = dest_ref[request]
    count = jnp.int32(0)
    for g in range(dest_ref.shape[0]):
        count = count + ((dest_ref[g] == dest) & (g < request)).astype(jnp.int32)
    return dest, count


def pick(choices, index):
    chosen = choices[0]
    for k in range(1, len(choices)):
        chosen = jnp.where(index == k, choices[k], chosen)
    return chosen


def pack_kernel(table_ref, dest_ref, pool_ref, *send_refs, insts, mig_per):
    inst = lax.axis_index("inst")
    slots, blocks = send_refs[0].shape[0], send_refs[0].shape[1]
    shifts = [lax.rem(dest_ref[inst * mig_per + m] - inst + insts, insts) for m in range(mig_per)]
    for k in range(1, insts):
        m = jnp.int32(0)
        for other in range(1, mig_per):
            m = jnp.where(shifts[other] == k, other, m)

        def copy_block(b, carry, m=m, k=k):
            block = table_ref[0, m, b]
            for s in range(slots):
                send_refs[k - 1][s, b] = pool_ref[0, s, block]
            return carry

        lax.fori_loop(0, blocks, copy_block, 0, unroll=8)


def pack(src_table, mig_dest, out_pool, insts):
    _, slots, _, block, width = out_pool.shape
    mig_per, blocks = src_table.shape[1:]
    shape = jax.ShapeDtypeStruct((slots, blocks, block, width), out_pool.dtype)
    smem = pl.BlockSpec(memory_space=pltpu.SMEM)
    vmem = pl.BlockSpec(memory_space=pltpu.VMEM)
    return pl.pallas_call(
        functools.partial(pack_kernel, insts=insts, mig_per=mig_per),
        out_shape=[shape] * (insts - 1),
        in_specs=[smem, smem, vmem],
        out_specs=[vmem] * (insts - 1),
        compiler_params=params(24),
        name="pack",
    )(src_table, mig_dest, out_pool)


def arrived_kernel(dest_ref, len_ref, *refs, insts, mig_per, cap):
    got, out_ref = refs[:-1], refs[-1]
    inst = lax.axis_index("inst")
    slots, blocks, block, width = got[0].shape
    requests = row_plan(dest_ref, inst, cap)
    place = lax.broadcasted_iota(jnp.int32, (block, width), 0)
    for a in range(cap):
        request = requests[a]
        known = jnp.maximum(request, 0)
        length = jnp.where(request >= 0, len_ref[known], 0)
        shift = lax.rem(known // mig_per - inst + insts, insts)

        for k in range(1, insts):

            @pl.when((shift == k) | ((request < 0) & (k == 1)))
            def _(a=a, k=k, length=length):
                def one(b, carry):
                    inside = place + b * block < length
                    for s in range(slots):
                        value = got[k - 1][s, b].astype(jnp.float32)
                        value = jnp.where(inside, value, 0.0).astype(jnp.bfloat16)
                        out_ref[0, a, s, pl.ds(pl.multiple_of(b * block, block), block), :] = value
                    return carry

                lax.fori_loop(0, blocks, one, 0, unroll=4)


def assemble(mig_dest, mig_len, got, insts, mig_per):
    slots, blocks, block, width = got[0].shape
    cap = insts - 1
    smem = pl.BlockSpec(memory_space=pltpu.SMEM)
    vmem = pl.BlockSpec(memory_space=pltpu.VMEM)
    return pl.pallas_call(
        functools.partial(arrived_kernel, insts=insts, mig_per=mig_per, cap=cap),
        out_shape=jax.ShapeDtypeStruct((1, cap, slots, blocks * block, width), jnp.bfloat16),
        in_specs=[smem, smem] + [vmem] * len(got),
        out_specs=vmem,
        compiler_params=params(32),
        name="assemble",
    )(mig_dest, mig_len, *got)


def fresh_code(rows, keys, steps, heads, slots):
    index = lax.broadcasted_iota(jnp.int32, (rows, keys), 0)
    key = lax.broadcasted_iota(jnp.int32, (rows, keys), 1)
    step = index // heads
    slot = lax.rem(index, heads) // (heads // slots)
    per_row = steps * slots
    in_row = lax.rem(key, per_row)
    seen = (in_row // slots <= step) & (lax.rem(in_row, slots) == slot)
    return jnp.where(seen, key // per_row, -1)


def blend(query, keys, values, length, fresh, fresh_seen, slot_of, slots):
    extent = keys.shape[0] // slots
    scale = math.log2(math.e) / math.sqrt(query.shape[1])
    scores = dot_t(query, keys)
    own = scores[:, :extent]
    for s in range(1, slots):
        own = jnp.where(slot_of == s, scores[:, s * extent : (s + 1) * extent], own)
    place = lax.broadcasted_iota(jnp.int32, own.shape, 1)
    own = jnp.where(place < length, own, LOW)
    fresh = jnp.where(fresh_seen, fresh, LOW)
    if own.shape == fresh.shape:
        largest = jnp.max(jnp.maximum(own, fresh), axis=1, keepdims=True)
    else:
        largest = jnp.maximum(
            jnp.max(own, axis=1, keepdims=True), jnp.max(fresh, axis=1, keepdims=True)
        )
    own = jnp.exp2((own - largest) * scale)
    fresh = jnp.exp2((fresh - largest) * scale)
    if own.shape == fresh.shape:
        total = jnp.sum(own + fresh, axis=1, keepdims=True)
    else:
        total = jnp.sum(own, axis=1, keepdims=True) + jnp.sum(fresh, axis=1, keepdims=True)
    spread = own
    if slots > 1:
        spread = jnp.concatenate([jnp.where(slot_of == s, own, 0.0) for s in range(slots)], axis=1)
    context = jnp.dot(spread.astype(jnp.bfloat16), values, preferred_element_type=jnp.float32)
    return context, fresh.astype(jnp.bfloat16), total


def gather_blocks(pool_ref, slots, ids):
    tiles = [pool_ref[0, s, block] for s in range(slots) for block in ids]
    return jnp.concatenate(tiles, axis=0)


def slot_index(rows, extent, heads, slots):
    index = lax.broadcasted_iota(jnp.int32, (rows, extent), 0)
    return lax.rem(index, heads) // (heads // slots)


def attend_kernel(
    table_ref, len_ref, dest_ref, query_ref, kv_ref, pool_ref, *refs,
    first_row, batch, steps, heads, slots, insts, mig_per, back_count,
):
    back = refs[:back_count]
    out_ref, fresh_ref, pf_ref, blend_ref, inv_ref = refs[back_count:]
    width = query_ref.shape[1]
    per = steps * heads
    rows = query_ref.shape[0] // per
    resident = len_ref.shape[1]
    blocks = table_ref.shape[0]
    extent = blocks * pool_ref.shape[3]
    start = first_row + pl.program_id(0) * rows

    fresh_ref[...] = dot_t(query_ref[...], kv_ref[:, :width])
    code = fresh_code(per, kv_ref.shape[0], steps, heads, slots)
    slot_of = slot_index(per, extent, heads, slots)
    for r in range(rows):
        row = start + r
        known = jnp.minimum(row, resident - 1)
        length = jnp.where(row < resident, len_ref[0, known], 0)
        ids = [table_ref[j, known] for j in range(blocks)]
        both = gather_blocks(pool_ref, slots, ids)
        at = slice(r * per, (r + 1) * per)
        context, weights, total = blend(
            query_ref[at, :], both[:, :width], both[:, width:], length,
            fresh_ref[at, :], code == r, slot_of, slots,
        )
        blend_ref[at, :] = context
        pf_ref[at, :] = weights
        inv_ref[at, :] = jnp.broadcast_to(1.0 / total, (per, width))

    done = blend_ref[...] + jnp.dot(
        pf_ref[...], kv_ref[:, width:], preferred_element_type=jnp.float32
    )
    blend_ref[...] = done * inv_ref[...]

    if back_count:
        cap = insts - 1
        inst = lax.axis_index("inst")
        requests = row_plan(dest_ref, inst, cap)

        @pl.when(pl.program_id(0) == pl.num_programs(0) - 1)
        def _():
            for a in range(cap):
                request = requests[a]
                known = jnp.maximum(request, 0)
                shift = lax.rem(known // mig_per - inst + insts, insts)
                begin = pl.multiple_of(lax.rem(known, mig_per) * per, per)
                choices = [ref[pl.ds(begin, per), :].astype(jnp.float32) for ref in back]
                at = slice((rows - cap + a) * per, (rows - cap + a + 1) * per)
                blend_ref[at, :] = jnp.where(
                    request >= 0, pick(choices, shift - 1), blend_ref[at, :]
                )

    for h in range(heads):
        column = blend_ref[pl.ds(h, rows * steps, stride=heads), :]
        out_ref[:, h * width : (h + 1) * width] = column.astype(jnp.bfloat16)


def attend(table, lengths, dest, queries, new_kv, pool, back, first_row, rows, dims):
    steps, heads, slots, insts, mig_per = dims
    width = queries.shape[1]
    per = steps * heads
    per_kv = steps * slots
    group = min(rows, LANES // per_kv)
    first = first_row // group
    smem = pl.BlockSpec(memory_space=pltpu.SMEM)
    vmem = pl.BlockSpec(memory_space=pltpu.VMEM)
    kernel = functools.partial(
        attend_kernel, first_row=first_row, batch=None, steps=steps, heads=heads, slots=slots,
        insts=insts, mig_per=mig_per, back_count=len(back),
    )
    tokens = rows * steps
    return pl.pallas_call(
        kernel,
        grid=(rows // group,),
        out_shape=jax.ShapeDtypeStruct((tokens, heads * width), jnp.bfloat16),
        in_specs=[
            smem, smem, smem,
            pl.BlockSpec((group * per, width), lambda i: (first + i, 0)),
            pl.BlockSpec((group * per_kv, 2 * width), lambda i: (first + i, 0)),
            vmem,
        ] + [vmem] * len(back),
        out_specs=pl.BlockSpec((group * steps, heads * width), lambda i: (i, 0)),
        scratch_shapes=[
            pltpu.VMEM((group * per, group * per_kv), jnp.float32),
            pltpu.VMEM((group * per, group * per_kv), jnp.bfloat16),
            pltpu.VMEM((group * per, width), jnp.float32),
            pltpu.VMEM((group * per, width), jnp.float32),
        ],
        compiler_params=params(24),
        cost_estimate=pl.CostEstimate(
            flops=rows * per * 1100 * width, bytes_accessed=4 * MIB, transcendentals=rows * per * 256
        ),
        name="attend",
    )(table, lengths, dest, queries, new_kv, pool, *back)


def serve_kernel(
    table_ref, len_ref, dest_ref, pool_ref, *refs, steps, heads, slots, insts, mig_per, query_rows
):
    tails, out_ref = refs[:-1], refs[-1]
    inst = lax.axis_index("inst")
    per = steps * heads
    width = out_ref.shape[1]
    blocks = table_ref.shape[2]
    extent = blocks * pool_ref.shape[3]
    fresh_keys = (tails[0].shape[0] - query_rows) // 2
    code = fresh_code(per, fresh_keys, steps, heads, slots)
    slot_of = slot_index(per, extent, heads, slots)
    for m in range(mig_per):
        request = inst * mig_per + m
        dest, place = standing_of(dest_ref, request)
        shift = lax.rem(dest - inst + insts, insts)
        begin = pl.multiple_of((place + 1) * per, per)
        query = pick([ref[pl.ds(begin, per), :] for ref in tails], shift - 1)
        keys = pick([ref[query_rows : query_rows + fresh_keys, :] for ref in tails], shift - 1)
        values = pick([ref[query_rows + fresh_keys :, :] for ref in tails], shift - 1)
        both = gather_blocks(pool_ref, slots, [table_ref[0, m, b] for b in range(blocks)])
        context, weights, total = blend(
            query, both[:, :width], both[:, width:], len_ref[request],
            dot_t(query, keys), code == place + 1, slot_of, slots,
        )
        context = context + jnp.dot(weights, values, preferred_element_type=jnp.float32)
        out_ref[m * per : (m + 1) * per, :] = (context / total).astype(jnp.bfloat16)


def serve(src_table, mig_len, mig_dest, out_pool, tails, query_rows, dims):
    steps, heads, slots, insts, mig_per = dims
    width = tails[0].shape[1]
    smem = pl.BlockSpec(memory_space=pltpu.SMEM)
    vmem = pl.BlockSpec(memory_space=pltpu.VMEM)
    return pl.pallas_call(
        functools.partial(
            serve_kernel, steps=steps, heads=heads, slots=slots, insts=insts, mig_per=mig_per,
            query_rows=query_rows,
        ),
        out_shape=jax.ShapeDtypeStruct((mig_per * steps * heads, width), jnp.bfloat16),
        in_specs=[smem, smem, smem] + [vmem] * (1 + len(tails)),
        out_specs=vmem,
        compiler_params=params(24),
        cost_estimate=pl.CostEstimate(flops=200_000_000, bytes_accessed=MIB, transcendentals=0),
        name="serve",
    )(src_table, mig_len, mig_dest, out_pool, *tails)


def project_kernel(pos_ref, weight_ref, *refs, parts, added, turned):
    attention = refs[:parts]
    extra = refs[parts : parts + added]
    out_ref = refs[-1]
    begin = 0
    for part in attention:
        tokens = part.shape[0]
        result = jnp.dot(part[...], weight_ref[...], preferred_element_type=jnp.float32)
        if extra:
            result = result + extra[0][begin : begin + tokens, :].astype(jnp.float32)
        if turned:
            out_ref[:, begin : begin + tokens] = result.T.astype(out_ref.dtype)
        else:
            out_ref[begin : begin + tokens, :] = result.astype(out_ref.dtype)
        begin += tokens


def project(pos, which, out_weight, attention, extra, turned, columns, tile, dtype, name):
    depth = out_weight.shape[0]
    tokens = sum(part.shape[0] for part in attention)
    tiles = columns // tile
    out_spec = (
        pl.BlockSpec((tile, tokens), lambda j, pos: (j, 0))
        if turned
        else pl.BlockSpec((tokens, tile), lambda j, pos: (0, j))
    )
    out_shape = (columns, tokens) if turned else (tokens, columns)
    return pl.pallas_call(
        functools.partial(project_kernel, parts=len(attention), added=len(extra), turned=turned),
        grid_spec=pltpu.PrefetchScalarGridSpec(
            num_scalar_prefetch=1,
            grid=(tiles,),
            in_specs=[pl.BlockSpec((depth, tile), lambda j, pos: (0, pos[which] * tiles + j))]
            + [pl.BlockSpec(part.shape, lambda j, pos: (0, 0)) for part in attention]
            + [pl.BlockSpec((tokens, tile), lambda j, pos: (0, j)) for _ in extra],
            out_specs=out_spec,
        ),
        out_shape=jax.ShapeDtypeStruct(out_shape, dtype),
        compiler_params=params(32),
        cost_estimate=pl.CostEstimate(
            flops=2 * tokens * depth * columns, bytes_accessed=2 * depth * columns, transcendentals=0
        ),
        name=name,
    )(pos, out_weight, *attention, *extra)


def finish_kernel(part_ref, *refs):
    got, out_ref = refs[:-1], refs[-1]
    begin = 0
    sums = part_ref[...]
    count = len(got)
    for ref in got:
        sums = sums + ref[...].astype(jnp.float32)
    out_ref[...] = sums.astype(jnp.bfloat16)


def shards(
    res_pool,
    res_table,
    res_len,
    out_pool,
    src_table,
    mig_len,
    mig_dest,
    queries,
    new_kv,
    out_weight,
):
    batch, steps, heads, width = queries.shape
    slots = res_pool.shape[1]
    insts = lax.axis_size("inst")
    tps = lax.axis_size("tp")
    chips = tps // CORES
    mig_per = src_table.shape[1]
    dims = (steps, heads, slots, insts, mig_per)
    features = out_weight.shape[1] // tps

    tp = lax.axis_index("tp")
    chip, core = tp // CORES, lax.rem(tp, CORES)
    order = [lax.rem(chip + k, chips) * CORES for k in list(range(1, chips)) + [0]]
    pos = jnp.stack([base + core for base in order] + [base + 1 - core for base in order])

    query_rows = queries.reshape(batch * steps * heads, width)
    kv_rows = new_kv.reshape(batch * steps * slots, 2 * width)
    table = res_table[0].T

    from_inst = [
        [((i + k) % insts, i) for i in range(insts)] for k in range(1, insts)
    ]
    to_inst = [[(i, (i + k) % insts) for i in range(insts)] for k in range(1, insts)]
    to_mate = [(i, i + 1 - 2 * (i % CORES)) for i in range(tps)]

    tail_q = query_rows[-insts * steps * heads :]
    tail_kv = kv_rows[-insts * steps * slots :]
    tail = jnp.concatenate([tail_q, tail_kv[:, :width], tail_kv[:, width:]], axis=0)
    tails = [lax.ppermute(tail, "inst", perm) for perm in from_inst]

    counts = (batch // 4, batch // 4, batch // 2)
    starts = (0, batch // 4, batch // 2)

    def remote(attention):
        got = []
        for k in range(chips - 1):
            give = project(
                pos, chips + k, out_weight, [attention], [], False, features, min(features, 256),
                jnp.bfloat16, "give",
            )
            mate = lax.ppermute(give, "tp", to_mate)
            keep = project(
                pos, k, out_weight, [attention], [mate], True, features, min(features, 256),
                jnp.bfloat16, "keep",
            )
            shift = (k + 1) * CORES
            got.append(lax.ppermute(keep, "tp", [(i, (i + shift) % tps) for i in range(tps)]))
        return got

    attention = []
    received = []
    sends = None
    for index, (start, rows) in enumerate(zip(starts, counts)):
        last = index == len(counts) - 1
        back = []
        if last:
            served = serve(
                src_table, mig_len, mig_dest, out_pool, tails, insts * steps * heads, dims
            )
            back = [lax.ppermute(served, "inst", perm) for perm in from_inst]
        piece = attend(
            table, res_len, mig_dest, query_rows, kv_rows, res_pool, back, start, rows, dims
        )
        attention.append(piece)
        received.append(remote(piece))
        if index == 0:
            sends = pack(src_table, mig_dest, out_pool, insts)
            arriving = [
                lax.ppermute(sends[insts - 1 - k], "inst", from_inst[k - 1])
                for k in range(1, insts)
            ]

    give = project(
        pos, 2 * chips - 1, out_weight, attention, [], False, features, min(features, 512),
        jnp.bfloat16, "give_own",
    )
    mate = lax.ppermute(give, "tp", to_mate)
    own = project(
        pos, chips - 1, out_weight, attention, [mate], True, features, min(features, 512),
        jnp.float32, "keep_own",
    )
    arrived = assemble(mig_dest, mig_len, arriving, insts, mig_per)

    hidden = finish(own, received, [rows * steps for rows in counts])
    return (arrived, hidden)


def finish(own, received, counts):
    features, tokens = own.shape
    tile = min(features, 512)
    hidden = None
    begin = 0
    for got, count in zip(received, counts):
        block = begin // count
        spec = pl.BlockSpec((tile, count), lambda j, block=block: (j, block))
        pieces = pl.BlockSpec((tile, count), lambda j: (j, 0))
        operands = [own] + list(got)
        in_specs = [spec] + [pieces] * len(got)
        aliases = {}
        kernel = finish_kernel
        if hidden is not None:
            operands = [hidden] + operands
            in_specs = [pl.BlockSpec(memory_space=pl.ANY)] + in_specs
            aliases = {0: 0}
            kernel = lambda _, *refs: finish_kernel(*refs)
        hidden = pl.pallas_call(
            kernel,
            grid=(features // tile,),
            out_shape=jax.ShapeDtypeStruct((features, tokens), jnp.bfloat16),
            in_specs=in_specs,
            out_specs=spec,
            input_output_aliases=aliases,
            compiler_params=params(24),
            name="finish",
        )(*operands)
        begin += count
    return hidden


def solution(mesh):
    placed = (
        P(("groups", "inst"), "tp", None, None, None),
        P(("groups", "inst"), None, None),
        P(("groups", "inst"), None),
        P(("groups", "inst"), "tp", None, None, None),
        P(("groups", "inst"), None, None),
        P("groups"),
        P("groups"),
        P(("groups", "inst"), None, "tp", None),
        P(("groups", "inst"), None, "tp", None),
        P("tp", None),
    )
    return jax.shard_map(
        shards,
        mesh=mesh,
        in_specs=placed,
        out_specs=(P(("groups", "inst"), None, "tp", None, None), P("tp", ("groups", "inst"))),
        check_vma=False,
    )
```

```python
import functools
import math

import jax
import jax.numpy as jnp
from jax import lax
from jax.experimental import pallas as pl
from jax.experimental.pallas import tpu as pltpu
from jax.sharding import PartitionSpec as P

CORES = 2
LOW = -1e30
MIB = 1 << 20
LANES = 128


def dot_t(left, right):
    return lax.dot_general(
        left, right, (((1,), (1,)), ((), ())), preferred_element_type=jnp.float32
    )


def row_plan(dest_ref, inst, cap):
    requests = [jnp.int32(-1)] * cap
    seen = jnp.int32(0)
    for g in range(dest_ref.shape[0]):
        here = dest_ref[g] == inst
        requests = [jnp.where(here & (seen == a), g, requests[a]) for a in range(cap)]
        seen = seen + here.astype(jnp.int32)
    return requests


def standing_of(dest_ref, request):
    dest = dest_ref[request]
    count = jnp.int32(0)
    for g in range(dest_ref.shape[0]):
        count = count + ((dest_ref[g] == dest) & (g < request)).astype(jnp.int32)
    return dest, count


SMEM = pl.BlockSpec(memory_space=pltpu.SMEM)
VMEM = pl.BlockSpec(memory_space=pltpu.VMEM)
ANY = pl.BlockSpec(memory_space=pl.ANY)


def run(kernel, operands, in_specs, deps, out_shape, out_specs, name, limit=56, grid=(),
        scratch=(), prefetch=0, aliases=None, flops=0):
    inputs = len(operands)
    count = len(deps)

    def call(*refs):
        return kernel(*refs[:inputs], *refs[inputs + count :])

    return pl.pallas_call(
        call,
        grid_spec=pltpu.PrefetchScalarGridSpec(
            num_scalar_prefetch=prefetch,
            grid=grid,
            in_specs=list(in_specs) + [ANY] * count,
            out_specs=out_specs,
            scratch_shapes=list(scratch),
        ),
        out_shape=out_shape,
        input_output_aliases=aliases or {},
        compiler_params=pltpu.CompilerParams(vmem_limit_bytes=limit * MIB),
        cost_estimate=pl.CostEstimate(flops=flops, bytes_accessed=1024, transcendentals=0),
        name=name,
    )(*operands, *deps)


def pack_kernel(
    table_ref, dest_ref, pool_ref, query_ref, kv_ref, send_ref, tail_ref, *, mig_per, rows, steps
):
    inst = lax.axis_index("inst")
    insts, slots, blocks = send_ref.shape[:3]
    width = query_ref.shape[1]
    tail_q = query_ref[...]
    tail_kv = kv_ref[...]
    queries, keys = tail_q.shape[0], tail_kv.shape[0]
    for i in range(insts):
        tail_ref[i, :queries, :] = tail_q
        tail_ref[i, queries : queries + keys, :] = tail_kv[:, :width]
        tail_ref[i, queries + keys :, :] = tail_kv[:, width:]
    for m in range(mig_per):
        dest = dest_ref[inst * mig_per + m]

        def copy_block(b, carry, m=m, dest=dest):
            block = table_ref[0, m, b]
            for s in range(slots):
                send_ref[dest, s, b] = pool_ref[0, s, block]
            return carry

        lax.fori_loop(0, blocks, copy_block, 0, unroll=8)


def pack(src_table, mig_dest, out_pool, query_rows, kv_rows, dims, deps):
    steps, heads, slots, insts, mig_per = dims
    _, _, _, block, width = out_pool.shape
    blocks = src_table.shape[2]
    tail_q, tail_kv = insts * steps * heads, insts * steps * slots
    shapes = (
        jax.ShapeDtypeStruct((insts, slots, blocks, block, width), out_pool.dtype),
        jax.ShapeDtypeStruct((insts, tail_q + 2 * tail_kv, width // 2), out_pool.dtype),
    )
    last_q = query_rows.shape[0] // tail_q - 1
    last_kv = kv_rows.shape[0] // tail_kv - 1
    return run(
        functools.partial(pack_kernel, mig_per=mig_per, rows=insts, steps=steps),
        [src_table, mig_dest, out_pool, query_rows, kv_rows],
        [
            SMEM, SMEM, pl.BlockSpec(out_pool.shape, lambda i: (0, 0, 0, 0, 0)),
            pl.BlockSpec((tail_q, width // 2), lambda i: (last_q, 0)),
            pl.BlockSpec((tail_kv, width), lambda i: (last_kv, 0)),
        ],
        deps,
        shapes,
        [
            pl.BlockSpec(shapes[0].shape, lambda i: (0, 0, 0, 0, 0)),
            pl.BlockSpec(shapes[1].shape, lambda i: (0, 0, 0)),
        ],
        "pack",
        grid=(1,),
    )


def arrived_kernel(dest_ref, len_ref, got_ref, out_ref, *, mig_per, cap):
    inst = lax.axis_index("inst")
    insts, slots, blocks, block, width = got_ref.shape
    requests = row_plan(dest_ref, inst, cap)
    place = lax.broadcasted_iota(jnp.int32, (block, width), 0)
    for a in range(cap):
        request = requests[a]
        known = jnp.maximum(request, 0)
        length = jnp.where(request >= 0, len_ref[known], 0)
        source = known // mig_per

        def one(b, carry, a=a, source=source, length=length):
            inside = place + b * block < length
            at = pl.ds(pl.multiple_of(b * block, block), block)
            for s in range(slots):
                value = got_ref[source, s, b].astype(jnp.float32)
                out_ref[0, a, s, at, :] = jnp.where(inside, value, 0.0).astype(jnp.bfloat16)
            return carry

        lax.fori_loop(0, blocks, one, 0, unroll=4)


def assemble(mig_dest, mig_len, got, mig_per, deps):
    insts, slots, blocks, block, width = got.shape
    cap = insts - 1
    return run(
        functools.partial(arrived_kernel, mig_per=mig_per, cap=cap),
        [mig_dest, mig_len, got],
        [SMEM, SMEM, VMEM],
        deps,
        jax.ShapeDtypeStruct((1, cap, slots, blocks * block, width), jnp.bfloat16),
        VMEM,
        "assemble",
    )


def fresh_code(rows, keys, steps, heads, slots):
    index = lax.broadcasted_iota(jnp.int32, (rows, keys), 0)
    key = lax.broadcasted_iota(jnp.int32, (rows, keys), 1)
    step = index // heads
    slot = lax.rem(index, heads) // (heads // slots)
    per_row = steps * slots
    in_row = lax.rem(key, per_row)
    seen = (in_row // slots <= step) & (lax.rem(in_row, slots) == slot)
    return jnp.where(seen, key // per_row, -1)


def own_scores(scores, slot_of, slots):
    extent = scores.shape[1] // slots
    own = scores[:, :extent]
    for s in range(1, slots):
        own = jnp.where(slot_of == s, scores[:, s * extent : (s + 1) * extent], own)
    return own


def weigh(own, length, fresh, fresh_seen, scale):
    place = lax.broadcasted_iota(jnp.int32, own.shape, 1)
    own = jnp.where(place < length, own, LOW)
    fresh = jnp.where(fresh_seen, fresh, LOW)
    same = own.shape == fresh.shape
    if same:
        largest = jnp.max(jnp.maximum(own, fresh), axis=1, keepdims=True)
    else:
        largest = jnp.maximum(
            jnp.max(own, axis=1, keepdims=True), jnp.max(fresh, axis=1, keepdims=True)
        )
    own = jnp.exp2((own - largest) * scale)
    fresh = jnp.exp2((fresh - largest) * scale)
    if same:
        total = jnp.sum(own + fresh, axis=1, keepdims=True)
    else:
        total = jnp.sum(own, axis=1, keepdims=True) + jnp.sum(fresh, axis=1, keepdims=True)
    return own, fresh, total


def spread(own, slot_of, slots):
    if slots == 1:
        return own.astype(jnp.bfloat16)
    parts = [jnp.where(slot_of == s, own, 0.0) for s in range(slots)]
    return jnp.concatenate(parts, axis=1).astype(jnp.bfloat16)


def gather_blocks(pool_ref, slots, ids):
    tiles = [pool_ref[0, s, block] for s in range(slots) for block in ids]
    return jnp.concatenate(tiles, axis=0)


def slot_index(rows, extent, heads, slots):
    index = lax.broadcasted_iota(jnp.int32, (rows, extent), 0)
    return lax.rem(index, heads) // (heads // slots)


def attend_kernel(
    table_ref, len_ref, dest_ref, query_ref, kv_ref, pool_ref, *refs,
    first_row, steps, heads, slots, insts, mig_per, with_back,
):
    back_ref = refs[0] if with_back else None
    out_ref, fresh_ref, pf_ref, blend_ref, inv_ref = refs[with_back:]
    width = query_ref.shape[1]
    per = steps * heads
    rows = query_ref.shape[0] // per
    resident = len_ref.shape[1]
    blocks = table_ref.shape[0]
    extent = blocks * pool_ref.shape[3]
    start = first_row + pl.program_id(0) * rows
    scale = math.log2(math.e) / math.sqrt(width)

    fresh_ref[...] = dot_t(query_ref[...], kv_ref[:, :width])
    code = fresh_code(per, kv_ref.shape[0], steps, heads, slots)
    slot_of = slot_index(per, extent, heads, slots)
    together = min(4, rows)
    for begin in range(0, rows, together):
        group = range(begin, begin + together)
        at = [slice(r * per, (r + 1) * per) for r in group]
        known = [jnp.minimum(start + r, resident - 1) for r in group]
        length = [
            jnp.where(start + r < resident, len_ref[0, k], 0) for r, k in zip(group, known)
        ]
        both = [
            gather_blocks(pool_ref, slots, [table_ref[j, k] for j in range(blocks)]) for k in known
        ]
        fresh = [fresh_ref[a, :] for a in at]
        scores = [dot_t(query_ref[a, :], b[:, :width]) for a, b in zip(at, both)]
        weights = [
            weigh(own_scores(s, slot_of, slots), n, f, code == r, scale)
            for s, n, f, r in zip(scores, length, fresh, group)
        ]
        context = [
            jnp.dot(spread(w[0], slot_of, slots), b[:, width:], preferred_element_type=jnp.float32)
            for w, b in zip(weights, both)
        ]
        for a, c, w in zip(at, context, weights):
            blend_ref[a, :] = c
            pf_ref[a, :] = w[1].astype(jnp.bfloat16)
            inv_ref[a, :] = jnp.broadcast_to(1.0 / w[2], (per, width))

    done = blend_ref[...] + jnp.dot(
        pf_ref[...], kv_ref[:, width:], preferred_element_type=jnp.float32
    )
    blend_ref[...] = done * inv_ref[...]

    if with_back:
        cap = insts - 1
        inst = lax.axis_index("inst")
        requests = row_plan(dest_ref, inst, cap)

        @pl.when(pl.program_id(0) == pl.num_programs(0) - 1)
        def _():
            for a in range(cap):
                request = requests[a]
                known = jnp.maximum(request, 0)
                begin = pl.multiple_of(lax.rem(known, mig_per) * per, per)
                served = back_ref[known // mig_per, pl.ds(begin, per), :].astype(jnp.float32)
                at = slice((rows - cap + a) * per, (rows - cap + a + 1) * per)
                blend_ref[at, :] = jnp.where(request >= 0, served, blend_ref[at, :])

    for h in range(heads):
        column = blend_ref[pl.ds(h, rows * steps, stride=heads), :]
        out_ref[:, h * width : (h + 1) * width] = column.astype(jnp.bfloat16)


def attend(table, lengths, dest, queries, new_kv, pool, back, first_row, rows, dims, deps):
    steps, heads, slots, insts, mig_per = dims
    width = queries.shape[1]
    per = steps * heads
    per_kv = steps * slots
    group = min(rows, LANES // per_kv)
    first = first_row // group
    kernel = functools.partial(
        attend_kernel, first_row=first_row, steps=steps, heads=heads, slots=slots,
        insts=insts, mig_per=mig_per, with_back=len(back),
    )
    return run(
        kernel,
        [table, lengths, dest, queries, new_kv, pool] + back,
        [
            SMEM, SMEM, SMEM,
            pl.BlockSpec((group * per, width), lambda i: (first + i, 0)),
            pl.BlockSpec((group * per_kv, 2 * width), lambda i: (first + i, 0)),
            VMEM,
        ] + [VMEM] * len(back),
        deps,
        jax.ShapeDtypeStruct((rows * steps, heads * width), jnp.bfloat16),
        pl.BlockSpec((group * steps, heads * width), lambda i: (i, 0)),
        "attend",
        grid=(rows // group,),
        scratch=[
            pltpu.VMEM((group * per, group * per_kv), jnp.float32),
            pltpu.VMEM((group * per, group * per_kv), jnp.bfloat16),
            pltpu.VMEM((group * per, width), jnp.float32),
            pltpu.VMEM((group * per, width), jnp.float32),
        ],
    )


def serve_kernel(
    table_ref, len_ref, dest_ref, pool_ref, tail_ref, out_ref, *, steps, heads, slots, insts, mig_per
):
    inst = lax.axis_index("inst")
    per = steps * heads
    width = out_ref.shape[2]
    blocks = table_ref.shape[2]
    extent = blocks * pool_ref.shape[3]
    queries = insts * per
    keys = insts * steps * slots
    code = fresh_code(per, keys, steps, heads, slots)
    slot_of = slot_index(per, extent, heads, slots)
    scale = math.log2(math.e) / math.sqrt(width)
    for m in range(mig_per):
        request = inst * mig_per + m
        dest, place = standing_of(dest_ref, request)
        begin = pl.multiple_of((place + 1) * per, per)
        query = tail_ref[dest, pl.ds(begin, per), :]
        new_keys = tail_ref[dest, queries : queries + keys, :]
        new_values = tail_ref[dest, queries + keys :, :]
        both = gather_blocks(pool_ref, slots, [table_ref[0, m, b] for b in range(blocks)])
        scores = dot_t(query, both[:, :width])
        own, fresh, total = weigh(
            own_scores(scores, slot_of, slots), len_ref[request],
            dot_t(query, new_keys), code == place + 1, scale,
        )
        context = jnp.dot(
            spread(own, slot_of, slots), both[:, width:], preferred_element_type=jnp.float32
        )
        context = context + jnp.dot(
            fresh.astype(jnp.bfloat16), new_values, preferred_element_type=jnp.float32
        )
        result = (context / total).astype(jnp.bfloat16)
        for i in range(insts):
            out_ref[i, m * per : (m + 1) * per, :] = result


def serve(src_table, mig_len, mig_dest, out_pool, tails, dims, deps):
    steps, heads, slots, insts, mig_per = dims
    return run(
        functools.partial(
            serve_kernel, steps=steps, heads=heads, slots=slots, insts=insts, mig_per=mig_per
        ),
        [src_table, mig_len, mig_dest, out_pool, tails],
        [SMEM, SMEM, SMEM, VMEM, VMEM],
        deps,
        jax.ShapeDtypeStruct((insts, mig_per * steps * heads, tails.shape[2]), jnp.bfloat16),
        VMEM,
        "serve",
    )


def project_kernel(pos_ref, *refs, cuts, parts, added, turned):
    weights = refs[:cuts]
    attention = refs[cuts : cuts + parts]
    extra = refs[cuts + parts : cuts + parts + added]
    out_ref = refs[-1]
    depth = weights[0].shape[0]
    begin = 0
    for part in attention:
        tokens = part.shape[0]
        result = None
        for c in range(cuts):
            term = jnp.dot(
                part[:, c * depth : (c + 1) * depth], weights[c][...],
                preferred_element_type=jnp.float32,
            )
            result = term if result is None else result + term
        if extra:
            result = result + extra[0][begin : begin + tokens, :].astype(jnp.float32)
        if turned:
            out_ref[:, begin : begin + tokens] = result.T.astype(out_ref.dtype)
        else:
            out_ref[begin : begin + tokens, :] = result.astype(out_ref.dtype)
        begin += tokens


def project(pos, which, begin, columns, out_weight, attention, extra, turned, features, tile, dtype,
            name, deps):
    cuts = 4
    depth = out_weight.shape[0] // cuts
    tokens = sum(part.shape[0] for part in attention)
    per_device = features // tile
    first = begin // tile
    out_spec = (
        pl.BlockSpec((tile, tokens), lambda j, pos: (j, 0))
        if turned
        else pl.BlockSpec((tokens, tile), lambda j, pos: (0, j))
    )
    return run(
        functools.partial(
            project_kernel, cuts=cuts, parts=len(attention), added=len(extra), turned=turned
        ),
        [pos] + [out_weight] * cuts + attention + extra,
        [
            pl.BlockSpec((depth, tile), lambda j, pos, c=c: (c, pos[which] * per_device + first + j))
            for c in range(cuts)
        ]
        + [pl.BlockSpec(part.shape, lambda j, pos: (0, 0)) for part in attention]
        + [pl.BlockSpec((tokens, tile), lambda j, pos: (0, j)) for _ in extra],
        deps,
        jax.ShapeDtypeStruct((columns, tokens) if turned else (tokens, columns), dtype),
        out_spec,
        name,
        grid=(columns // tile,),
        prefetch=1,
    )


def finish_kernel(part_ref, *refs):
    got, out_ref = refs[:-1], refs[-1]
    sums = part_ref[...]
    for ref in got:
        sums = sums + ref[...].astype(jnp.float32)
    out_ref[...] = sums.astype(jnp.bfloat16)


def finish(hidden, own, got, row, column, deps):
    height, count = got[0].shape
    tile = min(height, 512)
    first = row // tile
    block = column // count
    spec = pl.BlockSpec((tile, count), lambda j: (first + j, block))
    operands = [own] + got
    in_specs = [spec] + [pl.BlockSpec((tile, count), lambda j: (j, 0))] * len(got)
    kernel = finish_kernel
    aliases = None
    if hidden is not None:
        aliases = {len(operands): 0}
        deps = [hidden] + deps
    return run(
        kernel, operands, in_specs, deps,
        jax.ShapeDtypeStruct(own.shape, jnp.bfloat16), spec, "finish",
        grid=(height // tile,), aliases=aliases,
    )


def shards(
    res_pool,
    res_table,
    res_len,
    out_pool,
    src_table,
    mig_len,
    mig_dest,
    queries,
    new_kv,
    out_weight,
):
    batch, steps, heads, width = queries.shape
    slots = res_pool.shape[1]
    insts = lax.axis_size("inst")
    tps = lax.axis_size("tp")
    chips = tps // CORES
    mig_per = src_table.shape[1]
    dims = (steps, heads, slots, insts, mig_per)
    features = out_weight.shape[1] // tps

    tp = lax.axis_index("tp")
    chip, core = tp // CORES, lax.rem(tp, CORES)
    order = [lax.rem(chip + k, chips) * CORES for k in list(range(1, chips)) + [0]]
    pos = jnp.stack([base + core for base in order] + [base + 1 - core for base in order])

    query_rows = queries.reshape(batch * steps * heads, width)
    kv_rows = new_kv.reshape(batch * steps * slots, 2 * width)
    table = res_table[0].T

    to_mate = [(i, i + 1 - 2 * (i % CORES)) for i in range(tps)]
    half = features // 2
    tile = min(half, 512)
    rows = batch // 2

    def exchange(x):
        return lax.all_to_all(x, "inst", split_axis=0, concat_axis=0, tiled=True)

    def give(attention, k, part, deps):
        result = project(
            pos, chips + k, part * half, half, out_weight, [attention], [], False, features, tile,
            jnp.bfloat16, "give", deps,
        )
        return result, lax.ppermute(result, "tp", to_mate)

    def keep(attention, k, part, mate, deps):
        result = project(
            pos, k, part * half, half, out_weight, [attention], [mate], True, features, tile,
            jnp.bfloat16, "keep", deps,
        )
        shift = (k + 1) * CORES
        return result, lax.ppermute(result, "tp", [(i, (i + shift) % tps) for i in range(tps)])

    def remote(attention, between):
        got = [[], []]
        last = []
        extra = None
        for k in range(chips - 1):
            mates = []
            for part in range(2):
                result, mate = give(attention, k, part, last)
                mates.append(mate)
                last = [result]
            if between is not None and k == 0:
                extra, last = between(last)
            for part in range(2):
                result, sent = keep(attention, k, part, mates[part], last)
                last = [result]
                got[part].append(sent)
        return got, last, extra

    def ship(deps):
        sends, tail = pack(src_table, mig_dest, out_pool, query_rows, kv_rows, dims, deps)
        return (exchange(tail), exchange(sends)), [sends]

    first = attend(
        table, res_len, mig_dest, query_rows, kv_rows, res_pool, [], 0, rows, dims, []
    )
    got_first, last, (tails, arriving) = remote(first, ship)
    served = serve(src_table, mig_len, mig_dest, out_pool, tails, dims, last)
    second = attend(
        table, res_len, mig_dest, query_rows, kv_rows, res_pool, [exchange(served)], rows, rows,
        dims, [],
    )
    got_second, last, _ = remote(second, None)

    attention = [first, second]
    tile = min(features, 512)
    given = project(
        pos, 2 * chips - 1, 0, features, out_weight, attention, [], False, features, tile,
        jnp.bfloat16, "give_own", last,
    )
    mate = lax.ppermute(given, "tp", to_mate)
    own = project(
        pos, chips - 1, 0, features, out_weight, attention, [mate], True, features, tile,
        jnp.float32, "keep_own", [],
    )
    arrived = assemble(mig_dest, mig_len, arriving, mig_per, [own])
    hidden = None
    for column, got in ((0, got_first), (rows * steps, got_second)):
        for part in range(2):
            hidden = finish(hidden, own, got[part], part * half, column, [])
    return (arrived, hidden)


def solution(mesh):
    placed = (
        P(("groups", "inst"), "tp", None, None, None),
        P(("groups", "inst"), None, None),
        P(("groups", "inst"), None),
        P(("groups", "inst"), "tp", None, None, None),
        P(("groups", "inst"), None, None),
        P("groups"),
        P("groups"),
        P(("groups", "inst"), None, "tp", None),
        P(("groups", "inst"), None, "tp", None),
        P("tp", None),
    )
    return jax.shard_map(
        shards,
        mesh=mesh,
        in_specs=placed,
        out_specs=(P(("groups", "inst"), None, "tp", None, None), P("tp", ("groups", "inst"))),
        check_vma=False,
    )
```

```python
import functools
import math

import jax
import jax.numpy as jnp
from jax import lax
from jax.experimental import pallas as pl
from jax.experimental.pallas import tpu as pltpu
from jax.sharding import PartitionSpec as P

CORES = 2
LOW = -1e30
MIB = 1 << 20
LANES = 128
GROUP = 16
TOGETHER = 8


def dot_t(left, right):
    return lax.dot_general(
        left, right, (((1,), (1,)), ((), ())), preferred_element_type=jnp.float32
    )


def row_plan(dest_ref, inst, cap):
    requests = [jnp.int32(-1)] * cap
    seen = jnp.int32(0)
    for g in range(dest_ref.shape[0]):
        here = dest_ref[g] == inst
        requests = [jnp.where(here & (seen == a), g, requests[a]) for a in range(cap)]
        seen = seen + here.astype(jnp.int32)
    return requests


def standing_of(dest_ref, request):
    dest = dest_ref[request]
    standing = jnp.int32(0)
    for g in range(dest_ref.shape[0]):
        standing = standing + ((dest_ref[g] == dest) & (g < request)).astype(jnp.int32)
    return dest, standing


VMEM = pl.BlockSpec(memory_space=pltpu.VMEM)
ANY = pl.BlockSpec(memory_space=pl.ANY)
HBM = pl.BlockSpec(memory_space=pltpu.HBM)


class Sizes:
    def __init__(self, queries, res_pool, res_table, src_table, mig_dest, out_weight):
        self.batch, self.steps, self.heads, self.width = queries.shape
        self.slots = res_pool.shape[1]
        self.block = res_pool.shape[3]
        self.resident, self.blocks = res_table.shape[1:]
        self.mig_per, self.mig_blocks = src_table.shape[1:]
        self.requests = mig_dest.shape[0]
        self.insts = lax.axis_size("inst")
        self.tps = lax.axis_size("tp")
        self.chips = self.tps // CORES
        self.cap = self.insts - 1
        self.per = self.steps * self.heads
        self.per_kv = self.steps * self.slots
        self.depth = out_weight.shape[0]
        self.features = out_weight.shape[1] // self.tps
        self.quarter = self.features // 4
        self.tail_q = self.insts * self.per
        self.tail_kv = self.insts * self.per_kv


def piece_columns(piece, sizes):
    ahead, mine, part = piece
    tp = lax.axis_index("tp")
    core = lax.rem(tp, CORES)
    chip = lax.rem(tp // CORES + ahead, sizes.chips)
    owner = chip * CORES + (core if mine else 1 - core)
    return owner * sizes.features + part * sizes.quarter


def run(kernel, tables, operands, in_specs, deps, out_shapes, out_specs, name, sizes,
        pieces=(), weight=None, limit=16, grid=(), scratch=(), aliases=None):
    inputs, outputs, many = len(operands), len(out_shapes), len(tables)
    count = len(deps)
    fetches = len(pieces)
    extra_in = [weight] if fetches else []
    limit = max(limit, 36) if fetches else limit

    def call(*refs):
        table_in, refs = refs[:many], refs[many:]
        own_in = refs[:inputs]
        position = inputs + len(extra_in) + count
        own_out = refs[position : position + outputs]
        fetched = refs[position + outputs : position + outputs + fetches]
        rest = list(refs[position + outputs + fetches :])
        copies, reads = [], []
        if fetches:
            source, sems = refs[inputs], rest.pop()
            for n, piece in enumerate(pieces):
                first = pl.multiple_of(piece_columns(piece, sizes), LANES)
                copies.append(
                    pltpu.make_async_copy(
                        source.at[:, pl.ds(first, sizes.quarter)], fetched[n], sems.at[n]
                    )
                )
        table_refs = []
        if many:
            sems = rest.pop()
            table_refs = rest[len(rest) - many :]
            rest = rest[: len(rest) - many]
            reads = [
                pltpu.make_async_copy(source, target, sems.at[n])
                for n, (source, target) in enumerate(zip(table_in, table_refs))
            ]

        def ready():
            for read in reads:
                read.wait()

        def launch():
            for copy in copies:
                copy.start()

        def each(step, action):
            if not grid:
                action()
            else:
                pl.when(pl.program_id(0) == step)(action)

        def begin():
            for read in reads:
                read.start()

        def end():
            for copy in copies:
                copy.wait()

        if reads:
            each(0, begin)
        kernel(ready, launch, *table_refs, *own_in, *own_out, *rest)
        if copies:
            each(grid[0] - 1 if grid else 0, end)

    result = pl.pallas_call(
        call,
        grid_spec=pltpu.PrefetchScalarGridSpec(
            num_scalar_prefetch=0,
            grid=grid,
            in_specs=[HBM] * many + list(in_specs) + [HBM] * len(extra_in) + [ANY] * count,
            out_specs=list(out_specs) + [ANY] * fetches,
            scratch_shapes=list(scratch)
            + [pltpu.SMEM(t.shape, t.dtype) for t in tables]
            + ([pltpu.SemaphoreType.DMA((many,))] if many else [])
            + ([pltpu.SemaphoreType.DMA((fetches,))] if fetches else []),
        ),
        out_shape=list(out_shapes)
        + [jax.ShapeDtypeStruct((sizes.depth, sizes.quarter), jnp.bfloat16)] * fetches,
        input_output_aliases=aliases or {},
        compiler_params=pltpu.CompilerParams(vmem_limit_bytes=limit * MIB),
        cost_estimate=pl.CostEstimate(flops=0, bytes_accessed=1024, transcendentals=0),
        name=name,
    )(*tables, *operands, *extra_in, *deps)
    return result[:outputs], result[outputs:]


def pack_kernel(
    ready, launch, table_ref, dest_ref, pool_ref, query_ref, kv_ref, send_ref, tail_ref, *, sizes
):
    inst = lax.axis_index("inst")
    queries, keys, width = sizes.tail_q, sizes.tail_kv, sizes.width
    launch()
    tail_kv = kv_ref[...].reshape(keys, 2 * width)
    tail_ref[:queries, :] = query_ref[...]
    tail_ref[queries : queries + keys, :] = tail_kv[:, :width]
    tail_ref[queries + keys :, :] = tail_kv[:, width:]
    ready()
    for m in range(sizes.mig_per):
        dest = dest_ref[inst * sizes.mig_per + m]

        def copy_block(b, carry, m=m, dest=dest):
            block = table_ref[0, m, b]
            for s in range(sizes.slots):
                send_ref[dest, s, b] = pool_ref[0, s, block]
            return carry

        lax.fori_loop(0, sizes.mig_blocks, copy_block, 0, unroll=8)


def pack(src_table, mig_dest, out_pool, query_rows, new_kv, sizes, deps, **fetch):
    z = sizes
    shapes = (
        jax.ShapeDtypeStruct(
            (z.insts, z.slots, z.mig_blocks, z.block, 2 * z.width), out_pool.dtype
        ),
        jax.ShapeDtypeStruct((z.tail_q + 2 * z.tail_kv, z.width), out_pool.dtype),
    )
    last_q = query_rows.shape[0] // z.tail_q - 1
    last_kv = z.batch // z.insts - 1
    return run(
        functools.partial(pack_kernel, sizes=z),
        [src_table, mig_dest],
        [out_pool, query_rows, new_kv],
        [
            pl.BlockSpec(out_pool.shape, lambda i: (0, 0, 0, 0, 0)),
            pl.BlockSpec((z.tail_q, z.width), lambda i: (last_q, 0)),
            pl.BlockSpec((z.insts,) + new_kv.shape[1:], lambda i: (last_kv, 0, 0, 0)),
        ],
        deps,
        shapes,
        [VMEM, VMEM],
        "pack", z, grid=(1,), **fetch,
    )


def arrived_kernel(ready, launch, dest_ref, len_ref, got_ref, out_ref, *, sizes):
    ready()
    inst = lax.axis_index("inst")
    block = sizes.block
    requests = row_plan(dest_ref, inst, sizes.cap)
    place = lax.broadcasted_iota(jnp.int32, (block, 2 * sizes.width), 0)
    for a in range(sizes.cap):
        request = requests[a]
        known = jnp.maximum(request, 0)
        length = jnp.where(request >= 0, len_ref[known], 0)
        source = known // sizes.mig_per

        def one(b, carry, a=a, source=source, length=length):
            inside = place + b * block < length
            at = pl.ds(pl.multiple_of(b * block, block), block)
            for s in range(sizes.slots):
                value = got_ref[source, s, b].astype(jnp.float32)
                out_ref[0, a, s, at, :] = jnp.where(inside, value, 0.0).astype(jnp.bfloat16)
            return carry

        lax.fori_loop(0, sizes.mig_blocks, one, 0, unroll=4)


def assemble(mig_dest, mig_len, got, sizes, deps):
    z = sizes
    shape = (1, z.cap, z.slots, z.mig_blocks * z.block, 2 * z.width)
    result, _ = run(
        functools.partial(arrived_kernel, sizes=z),
        [mig_dest, mig_len], [got], [VMEM], deps,
        [jax.ShapeDtypeStruct(shape, jnp.bfloat16)], [VMEM], "assemble", z,
    )
    return result[0]


def fresh_code(rows, keys, sizes):
    index = lax.broadcasted_iota(jnp.int32, (rows, keys), 0)
    key = lax.broadcasted_iota(jnp.int32, (rows, keys), 1)
    step = index // sizes.heads
    slot = lax.rem(index, sizes.heads) // (sizes.heads // sizes.slots)
    in_row = lax.rem(key, sizes.per_kv)
    seen = (in_row // sizes.slots <= step) & (lax.rem(in_row, sizes.slots) == slot)
    return jnp.where(seen, key // sizes.per_kv, -1)


def slot_index(extent, sizes):
    index = lax.broadcasted_iota(jnp.int32, (sizes.per, extent), 0)
    return lax.rem(index, sizes.heads) // (sizes.heads // sizes.slots)


def own_scores(scores, slot_of, slots):
    extent = scores.shape[1] // slots
    own = scores[:, :extent]
    for s in range(1, slots):
        own = jnp.where(slot_of == s, scores[:, s * extent : (s + 1) * extent], own)
    return own


def weigh(own, length, fresh, fresh_seen, scale):
    place = lax.broadcasted_iota(jnp.int32, own.shape, 1)
    own = jnp.where(place < length, own, LOW)
    fresh = jnp.where(fresh_seen, fresh, LOW)
    if own.shape == fresh.shape:
        largest = jnp.max(jnp.maximum(own, fresh), axis=1, keepdims=True)
    else:
        largest = jnp.maximum(
            jnp.max(own, axis=1, keepdims=True), jnp.max(fresh, axis=1, keepdims=True)
        )
    return jnp.exp2((own - largest) * scale), jnp.exp2((fresh - largest) * scale)


def spread(own, slot_of, slots):
    if slots == 1:
        return own.astype(jnp.bfloat16)
    parts = [jnp.where(slot_of == s, own, 0.0) for s in range(slots)]
    return jnp.concatenate(parts, axis=1).astype(jnp.bfloat16)


def gather_blocks(pool_ref, slots, ids):
    tiles = [pool_ref[0, s, block] for s in range(slots) for block in ids]
    return jnp.concatenate(tiles, axis=0)


def with_ones(values):
    return jnp.concatenate([values, jnp.ones_like(values)], axis=1)


def dot(left, right):
    return jnp.dot(left, right, preferred_element_type=jnp.float32)


def attend_kernel(
    ready, launch, table_ref, len_ref, query_hbm, kv_hbm, pool_in, out_ref, *refs,
    first_row, steps_in_all, brings, sizes,
):
    z = sizes
    pool_ref, refs = (refs[0], refs[1:]) if brings else (pool_in, refs)
    query_all, kv_all, fresh_ref, pf_ref, blend_ref, done_ref, sems = refs
    width, per = z.width, z.per
    rows = GROUP
    step = pl.program_id(0)
    extent = z.blocks * z.block
    start = first_row + step * rows
    scale = math.log2(math.e) / math.sqrt(width)

    def copies(n):
        begin = first_row + n * rows
        return (
            pltpu.make_async_copy(
                query_hbm.at[pl.ds(pl.multiple_of(begin * per, rows * per), rows * per)],
                query_all.at[n], sems.at[0, n],
            ),
            pltpu.make_async_copy(kv_hbm.at[pl.ds(begin, rows)], kv_all.at[n], sems.at[1, n]),
        )

    @pl.when(step == 0)
    def _():
        if brings:
            pool_copy = pltpu.make_async_copy(pool_in, pool_ref, sems.at[2, 0])
            pool_copy.start()
        for n in range(steps_in_all):
            for copy in copies(n):
                copy.start()
        launch()
        ready()
        if brings:
            pool_copy.wait()

    for copy in copies(step):
        copy.wait()

    query_ref = query_all.at[step]
    new_kv = kv_all[step].reshape(rows * z.per_kv, 2 * width)
    fresh_ref[...] = dot_t(query_ref[...], new_kv[:, :width])
    code = fresh_code(per, rows * z.per_kv, z)
    slot_of = slot_index(extent, z)
    together = min(TOGETHER, rows)
    for begin in range(0, rows, together):
        group = range(begin, begin + together)
        at = [slice(r * per, (r + 1) * per) for r in group]
        known = [jnp.minimum(start + r, z.resident - 1) for r in group]
        length = [
            jnp.where(start + r < z.resident, len_ref[0, k], 0) for r, k in zip(group, known)
        ]
        both = [
            gather_blocks(pool_ref, z.slots, [table_ref[j, k] for j in range(z.blocks)])
            for k in known
        ]
        fresh = [fresh_ref[a, :] for a in at]
        scores = [dot_t(query_ref[a, :], b[:, :width]) for a, b in zip(at, both)]
        weights = [
            weigh(own_scores(s, slot_of, z.slots), n, f, code == r, scale)
            for s, n, f, r in zip(scores, length, fresh, group)
        ]
        context = [
            dot(spread(w[0], slot_of, z.slots), with_ones(b[:, width:]))
            for w, b in zip(weights, both)
        ]
        for a, c, w in zip(at, context, weights):
            blend_ref[a, :] = c
            pf_ref[a, :] = w[1].astype(jnp.bfloat16)

    done = blend_ref[...] + dot(pf_ref[...], with_ones(new_kv[:, width:]))
    done_ref[...] = done[:, :width] / done[:, width:]
    for h in range(z.heads):
        column = done_ref[pl.ds(h, rows * z.steps, stride=z.heads), :]
        out_ref[:, h * width : (h + 1) * width] = column.astype(jnp.bfloat16)


def attend(table, lengths, queries, new_kv, pool, brings, first_row, rows, sizes, deps, **fetch):
    z = sizes
    groups = rows // GROUP
    tokens = rows * z.steps
    shapes = [jax.ShapeDtypeStruct((tokens, z.heads * z.width), jnp.bfloat16)]
    specs = [pl.BlockSpec((GROUP * z.steps, z.heads * z.width), lambda i: (i, 0))]
    if brings:
        shapes.append(jax.ShapeDtypeStruct(pool.shape, pool.dtype))
        specs.append(VMEM)
    return run(
        functools.partial(
            attend_kernel, first_row=first_row, steps_in_all=groups, brings=brings, sizes=z
        ),
        [table, lengths],
        [queries, new_kv, pool],
        [HBM, HBM, HBM if brings else VMEM],
        deps, shapes, specs, "attend", z, limit=46 if brings else 36,
        grid=(groups,),
        scratch=[
            pltpu.VMEM((groups, GROUP * z.per, z.width), jnp.bfloat16),
            pltpu.VMEM((groups, GROUP) + new_kv.shape[1:], jnp.bfloat16),
            pltpu.VMEM((GROUP * z.per, GROUP * z.per_kv), jnp.float32),
            pltpu.VMEM((GROUP * z.per, GROUP * z.per_kv), jnp.bfloat16),
            pltpu.VMEM((GROUP * z.per, 2 * z.width), jnp.float32),
            pltpu.VMEM((GROUP * z.per, z.width), jnp.float32),
            pltpu.SemaphoreType.DMA((3, groups)),
        ],
        **fetch,
    )


def serve_kernel(ready, launch, table_ref, len_ref, dest_ref, pool_ref, *refs, sizes):
    z = sizes
    launch()
    ready()
    tails, out_ref = refs[:-1], refs[-1]
    inst = lax.axis_index("inst")
    queries, keys = z.tail_q, z.tail_kv
    extent = z.mig_blocks * z.block
    code = fresh_code(z.per, keys, z)
    slot_of = slot_index(extent, z)
    scale = math.log2(math.e) / math.sqrt(z.width)
    for m in range(z.mig_per):
        request = inst * z.mig_per + m
        dest, place = standing_of(dest_ref, request)
        ahead = lax.rem(dest - inst + z.insts, z.insts)
        begin = pl.multiple_of((place + 1) * z.per, z.per)
        query = pick([ref[pl.ds(begin, z.per), :] for ref in tails], ahead - 1)
        new_keys = pick([ref[queries : queries + keys, :] for ref in tails], ahead - 1)
        new_values = pick([ref[queries + keys :, :] for ref in tails], ahead - 1)
        ids = [table_ref[0, m, b] for b in range(z.mig_blocks)]
        both = gather_blocks(pool_ref, z.slots, ids)
        scores = dot_t(query, both[:, : z.width])
        own, fresh = weigh(
            own_scores(scores, slot_of, z.slots), len_ref[request],
            dot_t(query, new_keys), code == place + 1, scale,
        )
        done = dot(spread(own, slot_of, z.slots), with_ones(both[:, z.width :]))
        done = done + dot(fresh.astype(jnp.bfloat16), with_ones(new_values))
        result = done[:, : z.width] / done[:, z.width :]
        out_ref[m * z.per : (m + 1) * z.per, :] = result.astype(jnp.bfloat16)


def pick(choices, index):
    chosen = choices[0]
    for k in range(1, len(choices)):
        chosen = jnp.where(index == k, choices[k], chosen)
    return chosen


def serve(src_table, mig_len, mig_dest, out_pool, tails, sizes, deps, **fetch):
    z = sizes
    result, pieces = run(
        functools.partial(serve_kernel, sizes=z),
        [src_table, mig_len, mig_dest],
        [out_pool] + tails,
        [VMEM] * (1 + len(tails)),
        deps,
        [jax.ShapeDtypeStruct((z.mig_per * z.per, z.width), jnp.bfloat16)],
        [VMEM], "serve", z, **fetch,
    )
    return result[0], pieces


def merge_kernel(ready, launch, dest_ref, *refs, sizes):
    z = sizes
    launch()
    ready()
    back, old_ref, out_ref, rows_ref = refs[:-3], refs[-3], refs[-2], refs[-1]
    inst = lax.axis_index("inst")
    requests = row_plan(dest_ref, inst, z.cap)
    for a in range(z.cap):
        known = jnp.maximum(requests[a], 0)
        ahead = lax.rem(known // z.mig_per - inst + z.insts, z.insts)
        begin = pl.multiple_of(lax.rem(known, z.mig_per) * z.per, z.per)
        served = pick([ref[pl.ds(begin, z.per), :].astype(jnp.float32) for ref in back], ahead - 1)
        rows_ref[(a + 1) * z.per : (a + 2) * z.per, :] = served
    rows_ref[: z.per, :] = jnp.zeros((z.per, z.width), jnp.float32)
    tokens = z.insts * z.steps
    row = lax.broadcasted_iota(jnp.int32, (tokens, z.width), 0) // z.steps
    filled = row < 0
    for a in range(z.cap):
        filled = filled | ((row == a + 1) & (requests[a] >= 0))
    for h in range(z.heads):
        at = slice(h * z.width, (h + 1) * z.width)
        column = rows_ref[pl.ds(h, tokens, stride=z.heads), :]
        old = old_ref[:, at].astype(jnp.float32)
        out_ref[:, at] = jnp.where(filled, column, old).astype(jnp.bfloat16)


def merge(mig_dest, attention, back, sizes, deps, **fetch):
    z = sizes
    tokens = z.insts * z.steps
    last = attention.shape[0] // tokens - 1
    spec = pl.BlockSpec((tokens, attention.shape[1]), lambda i: (last, 0))
    result, pieces = run(
        functools.partial(merge_kernel, sizes=z),
        [mig_dest],
        back + [attention],
        [pl.BlockSpec(b.shape, lambda i: (0, 0)) for b in back] + [spec],
        deps,
        [jax.ShapeDtypeStruct(attention.shape, jnp.bfloat16)],
        [spec], "merge", z, grid=(1,),
        scratch=[pltpu.VMEM((z.insts * z.per, z.width), jnp.float32)],
        aliases={1 + len(back): 0}, **fetch,
    )
    return result[0], pieces


def project_kernel(
    ready, launch, *refs, parts, count, streamed, added, turned, sizes
):
    launch()
    attention, weights = refs[:parts], list(refs[parts : parts + count])
    extra = refs[parts + count : parts + count + added]
    position = parts + count + added
    copies = [None] * count
    if streamed:
        source = refs[position]
        buffers, sems = refs[position + 2], refs[position + 3]
        for n, piece in enumerate(streamed):
            first = pl.multiple_of(piece_columns(piece, sizes), LANES)
            copy = pltpu.make_async_copy(
                source.at[:, pl.ds(first, sizes.quarter)], buffers.at[n], sems.at[n]
            )
            copy.start()
            copies.append(copy)
            weights.append(buffers.at[n])
        position += 1
    out_ref = refs[position]
    width = sizes.quarter
    tile = min(width, 256)
    for n, (weight, copy) in enumerate(zip(weights, copies)):
        if copy is not None:
            copy.wait()

        def one(j, carry, n=n, weight=weight):
            at = pl.ds(pl.multiple_of(j * tile, tile), tile)
            to = pl.ds(pl.multiple_of(n * width + j * tile, tile), tile)
            begin = 0
            for part in attention:
                tokens = part.shape[0]
                result = dot(part[...], weight[:, at])
                if extra:
                    mate = extra[0][begin : begin + tokens, to]
                    result = result + mate.astype(jnp.float32)
                if turned:
                    out_ref[to, begin : begin + tokens] = result.T.astype(out_ref.dtype)
                else:
                    out_ref[begin : begin + tokens, to] = result.astype(out_ref.dtype)
                begin += tokens
            return carry

        lax.fori_loop(0, width // tile, one, 0)


def project(attention, weights, streamed, out_weight, mate, sizes, name, deps, pieces=()):
    tokens = sum(a.shape[0] for a in attention)
    columns = (len(weights) + len(streamed)) * sizes.quarter
    turned = mate is not None
    extra = [mate] if turned else []
    shape = (columns, tokens) if turned else (tokens, columns)
    operands = attention + weights + extra
    specs = [VMEM] * len(operands)
    scratch = []
    if streamed:
        operands = operands + [out_weight]
        specs = specs + [HBM]
        scratch = [
            pltpu.VMEM((len(streamed), sizes.depth, sizes.quarter), jnp.bfloat16),
            pltpu.SemaphoreType.DMA((len(streamed),)),
        ]
    result, new = run(
        functools.partial(
            project_kernel, parts=len(attention), count=len(weights), streamed=streamed,
            added=len(extra), turned=turned, sizes=sizes,
        ),
        [], operands, specs, deps,
        [jax.ShapeDtypeStruct(shape, jnp.bfloat16)], [VMEM], name, sizes,
        limit=36 if streamed or pieces else 16, scratch=scratch,
        pieces=pieces, weight=out_weight,
    )
    return result[0], new


def finish_kernel(ready, launch, part_ref, *refs):
    got, out_ref = refs[:-1], refs[-1]
    sums = part_ref[...].astype(jnp.float32)
    for ref in got:
        sums = sums + ref[...].astype(jnp.float32)
    out_ref[...] = sums.astype(jnp.bfloat16)


def finish(hidden, own, got, row, column, sizes, deps):
    height, count = got[0].shape
    tile = min(height, 512)
    first = row // tile
    block = column // count
    spec = pl.BlockSpec((tile, count), lambda j: (first + j, block))
    operands = [own] + got
    in_specs = [spec] + [pl.BlockSpec((tile, count), lambda j: (j, 0))] * len(got)
    aliases = None
    if hidden is not None:
        aliases = {len(operands): 0}
        deps = [hidden] + deps
    result, _ = run(
        finish_kernel, [], operands, in_specs, deps,
        [jax.ShapeDtypeStruct(own.shape, jnp.bfloat16)], [spec], "finish", sizes,
        grid=(height // tile,), aliases=aliases,
    )
    return result[0]


def shards(
    res_pool,
    res_table,
    res_len,
    out_pool,
    src_table,
    mig_len,
    mig_dest,
    queries,
    new_kv,
    out_weight,
):
    z = Sizes(queries, res_pool, res_table, src_table, mig_dest, out_weight)
    tps, insts, chips = z.tps, z.insts, z.chips
    table = res_table[0].T
    query_rows = queries.reshape(z.batch * z.per, z.width)

    from_inst = [[((i + k) % insts, i) for i in range(insts)] for k in range(1, insts)]
    to_mate = [(i, i + 1 - 2 * (i % CORES)) for i in range(tps)]
    far = range(1, chips)
    held = {}

    def mate_of(x):
        return lax.ppermute(x, "tp", to_mate)

    def across(x, ahead):
        shift = ahead * CORES
        return lax.ppermute(x, "tp", [(i, (i + shift) % tps) for i in range(tps)])

    def bringing(pieces):
        return dict(pieces=pieces, weight=out_weight)

    def gives(ks, parts):
        return [(k, False, part) for k in ks for part in parts]

    def keeps(ks, parts):
        return [(k, True, part) for k in ks for part in parts]

    def at_hand(pieces):
        here = [held[piece] for piece in pieces if piece in held]
        return here, [piece for piece in pieces if piece not in held]

    def hold(pieces, arrays):
        held.update(zip(pieces, arrays))

    def give(attention, ks, parts, name, deps, pieces=()):
        weights, streamed = at_hand(gives(ks, parts))
        result, new = project(
            attention, weights, streamed, out_weight, None, z, name, deps, pieces
        )
        hold(pieces, new)
        return result, mate_of(result)

    def keep(attention, ks, parts, mate, name, deps, pieces=()):
        results = []
        width = mate.shape[1] // len(ks)
        for n, k in enumerate(ks):
            weights, streamed = at_hand(keeps([k], parts))
            given = mate if len(ks) == 1 else mate[:, n * width : (n + 1) * width]
            now = pieces if n == 0 else ()
            result, new = project(
                attention, weights, streamed, out_weight, given, z, name, deps, now
            )
            hold(now, new)
            deps = [result]
            results.append(result)
        return results

    def sent(results):
        return [across(result, k) for k, result in zip(far, results)]

    def rows_of(n, first, rows, pool, deps, pieces):
        (piece, *pool_out), new = attend(
            table, res_len, query_rows, new_kv, pool, n == 0, first, rows, z, deps,
            **bringing(pieces),
        )
        hold(pieces, new)
        return piece, pool_out[0] if n == 0 else pool

    counts = (z.batch // 2, z.batch // 4, z.batch // 4)
    low, high, every = (0, 1), (2, 3), (0, 1, 2, 3)

    a, pool = rows_of(0, 0, counts[0], res_pool, [], gives(far, low) + keeps(far, low))
    given, mate = give([a], far, low, "give", [])
    (sends, tail), new = pack(
        src_table, mig_dest, out_pool, query_rows, new_kv, z, [given], **bringing(gives(far, (2,)))
    )
    hold(gives(far, (2,)), new)
    arriving = lax.all_to_all(sends, "inst", split_axis=0, concat_axis=0, tiled=True)
    kept = keep([a], far, low, mate, "keep", [tail], gives(far, (3,)))
    got_low = sent(kept)
    tails = [lax.ppermute(tail, "inst", perm) for perm in from_inst]
    given, mate = give([a], far, high, "give", [kept[-1]])
    b, _ = rows_of(1, counts[0], counts[1], pool, [given], keeps(far, high))
    kept = keep([a], far, high, mate, "keep", [b])
    got_high = sent(kept)
    served, _ = serve(src_table, mig_len, mig_dest, out_pool, tails, z, [kept[-1]])
    back = [lax.ppermute(served, "inst", perm) for perm in from_inst]
    given, mate = give([b], far, every, "give", [served] + got_low)
    c, _ = rows_of(2, counts[0] + counts[1], counts[2], pool, [given], [])
    kept = keep([b], far, every, mate, "keep", [c])
    got_b = sent(kept)
    c, _ = merge(mig_dest, c, back, z, [kept[-1]])
    given, mate = give([c], far, every, "give", got_high)
    own_given, own_mate = give([a, b, c], [0], every, "give_own", [given])
    kept = keep([c], far, every, mate, "keep", [own_given])
    got_c = sent(kept)
    own = keep([a, b, c], [0], every, own_mate, "keep_own", [kept[-1]])[0]
    arrived = assemble(mig_dest, mig_len, arriving, z, [own])

    hidden = finish(None, own, got_low, 0, 0, z, [])
    hidden = finish(hidden, own, got_high, z.features // 2, 0, z, [])
    hidden = finish(hidden, own, got_b, 0, counts[0] * z.steps, z, [])
    hidden = finish(hidden, own, got_c, 0, (counts[0] + counts[1]) * z.steps, z, [])
    return (arrived, hidden)


def solution(mesh):
    placed = (
        P(("groups", "inst"), "tp", None, None, None),
        P(("groups", "inst"), None, None),
        P(("groups", "inst"), None),
        P(("groups", "inst"), "tp", None, None, None),
        P(("groups", "inst"), None, None),
        P("groups"),
        P("groups"),
        P(("groups", "inst"), None, "tp", None),
        P(("groups", "inst"), None, "tp", None),
        P("tp", None),
    )
    return jax.shard_map(
        shards,
        mesh=mesh,
        in_specs=placed,
        out_specs=(P(("groups", "inst"), None, "tp", None, None), P("tp", ("groups", "inst"))),
        check_vma=False,
    )
```

```python
import functools
import math

import jax
import jax.numpy as jnp
from jax import lax
from jax.experimental import pallas as pl
from jax.experimental.pallas import tpu as pltpu
from jax.sharding import PartitionSpec as P

CORES = 2
LOW = -1e30
MIB = 1 << 20
LANES = 128
GROUP = 16
TOGETHER = 8


def dot_t(left, right):
    return lax.dot_general(
        left, right, (((1,), (1,)), ((), ())), preferred_element_type=jnp.float32
    )


def row_plan(dest_ref, inst, cap):
    requests = [jnp.int32(-1)] * cap
    seen = jnp.int32(0)
    for g in range(dest_ref.shape[0]):
        here = dest_ref[g] == inst
        requests = [jnp.where(here & (seen == a), g, requests[a]) for a in range(cap)]
        seen = seen + here.astype(jnp.int32)
    return requests


VMEM = pl.BlockSpec(memory_space=pltpu.VMEM)
ANY = pl.BlockSpec(memory_space=pl.ANY)
HBM = pl.BlockSpec(memory_space=pltpu.HBM)


class Sizes:
    def __init__(self, queries, res_pool, res_table, src_table, mig_dest, out_weight):
        self.batch, self.steps, self.heads, self.width = queries.shape
        self.slots = res_pool.shape[1]
        self.block = res_pool.shape[3]
        self.resident, self.blocks = res_table.shape[1:]
        self.mig_per, self.mig_blocks = src_table.shape[1:]
        self.requests = mig_dest.shape[0]
        self.insts = lax.axis_size("inst")
        self.tps = lax.axis_size("tp")
        self.chips = self.tps // CORES
        self.cap = self.insts - 1
        self.per = self.steps * self.heads
        self.per_kv = self.steps * self.slots
        self.depth = out_weight.shape[0]
        self.features = out_weight.shape[1] // self.tps
        self.quarter = self.features // 4
        self.tail_q = self.insts * self.per
        self.tail_kv = self.insts * self.per_kv


def piece_columns(piece, sizes):
    ahead, mine, part = piece
    tp = lax.axis_index("tp")
    core = lax.rem(tp, CORES)
    chip = lax.rem(tp // CORES + ahead, sizes.chips)
    owner = chip * CORES + (core if mine else 1 - core)
    return owner * sizes.features + part * sizes.quarter


def run(kernel, tables, operands, in_specs, deps, out_shapes, out_specs, name, sizes,
        pieces=(), weight=None, limit=16, grid=(), scratch=(), aliases=None):
    inputs, outputs, many = len(operands), len(out_shapes), len(tables)
    count = len(deps)
    fetches = len(pieces)
    extra_in = [weight] if fetches else []
    limit = max(limit, 36) if fetches else limit

    def call(*refs):
        table_in, refs = refs[:many], refs[many:]
        own_in = refs[:inputs]
        position = inputs + len(extra_in) + count
        own_out = refs[position : position + outputs]
        fetched = refs[position + outputs : position + outputs + fetches]
        rest = list(refs[position + outputs + fetches :])
        copies, reads = [], []
        if fetches:
            source, sems = refs[inputs], rest.pop()
            for n, piece in enumerate(pieces):
                first = pl.multiple_of(piece_columns(piece, sizes), LANES)
                copies.append(
                    pltpu.make_async_copy(
                        source.at[:, pl.ds(first, sizes.quarter)], fetched[n], sems.at[n]
                    )
                )
        table_refs = []
        if many:
            sems = rest.pop()
            table_refs = rest[len(rest) - many :]
            rest = rest[: len(rest) - many]
            reads = [
                pltpu.make_async_copy(source, target, sems.at[n])
                for n, (source, target) in enumerate(zip(table_in, table_refs))
            ]

        def ready():
            for read in reads:
                read.wait()

        def launch():
            for copy in copies:
                copy.start()

        def each(step, action):
            if not grid:
                action()
            else:
                pl.when(pl.program_id(0) == step)(action)

        def begin():
            for read in reads:
                read.start()

        def end():
            for copy in copies:
                copy.wait()

        if reads:
            each(0, begin)
        kernel(ready, launch, *table_refs, *own_in, *own_out, *rest)
        if copies:
            each(grid[0] - 1 if grid else 0, end)

    result = pl.pallas_call(
        call,
        grid_spec=pltpu.PrefetchScalarGridSpec(
            num_scalar_prefetch=0,
            grid=grid,
            in_specs=[HBM] * many + list(in_specs) + [HBM] * len(extra_in) + [ANY] * count,
            out_specs=list(out_specs) + [ANY] * fetches,
            scratch_shapes=list(scratch)
            + [pltpu.SMEM(t.shape, t.dtype) for t in tables]
            + ([pltpu.SemaphoreType.DMA((many,))] if many else [])
            + ([pltpu.SemaphoreType.DMA((fetches,))] if fetches else []),
        ),
        out_shape=list(out_shapes)
        + [jax.ShapeDtypeStruct((sizes.depth, sizes.quarter), jnp.bfloat16)] * fetches,
        input_output_aliases=aliases or {},
        compiler_params=pltpu.CompilerParams(vmem_limit_bytes=limit * MIB),
        cost_estimate=pl.CostEstimate(flops=0, bytes_accessed=1024, transcendentals=0),
        name=name,
    )(*tables, *operands, *extra_in, *deps)
    return result[:outputs], result[outputs:]


def pack_kernel(ready, launch, table_ref, dest_ref, pool_ref, send_ref, *, sizes):
    inst = lax.axis_index("inst")
    ready()
    for m in range(sizes.mig_per):
        dest = dest_ref[inst * sizes.mig_per + m]

        def copy_block(b, carry, m=m, dest=dest):
            block = table_ref[0, m, b]
            for s in range(sizes.slots):
                send_ref[dest, s, b] = pool_ref[0, s, block]
            return carry

        lax.fori_loop(0, sizes.mig_blocks, copy_block, 0, unroll=8)


def pack(src_table, mig_dest, out_pool, sizes):
    z = sizes
    shape = (z.insts, z.slots, z.mig_blocks, z.block, 2 * z.width)
    result, _ = run(
        functools.partial(pack_kernel, sizes=z),
        [src_table, mig_dest], [out_pool], [VMEM], [],
        [jax.ShapeDtypeStruct(shape, out_pool.dtype)], [VMEM], "pack", z,
    )
    return result[0]


def arrived_kernel(ready, launch, dest_ref, len_ref, got_ref, out_ref, *, sizes):
    ready()
    inst = lax.axis_index("inst")
    block = sizes.block
    requests = row_plan(dest_ref, inst, sizes.cap)
    place = lax.broadcasted_iota(jnp.int32, (block, 2 * sizes.width), 0)
    for a in range(sizes.cap):
        known = jnp.maximum(requests[a], 0)
        length = jnp.where(requests[a] >= 0, len_ref[known], 0)
        source = known // sizes.mig_per

        def one(b, carry, a=a, source=source, length=length):
            inside = place + b * block < length
            at = pl.ds(pl.multiple_of(b * block, block), block)
            for s in range(sizes.slots):
                value = got_ref[source, s, b].astype(jnp.float32)
                out_ref[0, a, s, at, :] = jnp.where(inside, value, 0.0).astype(jnp.bfloat16)
            return carry

        lax.fori_loop(0, sizes.mig_blocks, one, 0, unroll=4)


def assemble(mig_dest, mig_len, got, sizes, deps):
    z = sizes
    shape = (1, z.cap, z.slots, z.mig_blocks * z.block, 2 * z.width)
    result, _ = run(
        functools.partial(arrived_kernel, sizes=z),
        [mig_dest, mig_len], [got], [VMEM], deps,
        [jax.ShapeDtypeStruct(shape, jnp.bfloat16)], [VMEM], "assemble", z,
    )
    return result[0]


def fresh_code(rows, keys, sizes):
    index = lax.broadcasted_iota(jnp.int32, (rows, keys), 0)
    key = lax.broadcasted_iota(jnp.int32, (rows, keys), 1)
    step = index // sizes.heads
    slot = lax.rem(index, sizes.heads) // (sizes.heads // sizes.slots)
    in_row = lax.rem(key, sizes.per_kv)
    seen = (in_row // sizes.slots <= step) & (lax.rem(in_row, sizes.slots) == slot)
    return jnp.where(seen, key // sizes.per_kv, -1)


def slot_index(extent, sizes):
    index = lax.broadcasted_iota(jnp.int32, (sizes.per, extent), 0)
    return lax.rem(index, sizes.heads) // (sizes.heads // sizes.slots)


def own_scores(scores, slot_of, slots):
    extent = scores.shape[1] // slots
    own = scores[:, :extent]
    for s in range(1, slots):
        own = jnp.where(slot_of == s, scores[:, s * extent : (s + 1) * extent], own)
    return own


def weigh(own, length, fresh, fresh_seen, scale):
    place = lax.broadcasted_iota(jnp.int32, own.shape, 1)
    own = jnp.where(place < length, own, LOW)
    fresh = jnp.where(fresh_seen, fresh, LOW)
    if own.shape == fresh.shape:
        largest = jnp.max(jnp.maximum(own, fresh), axis=1, keepdims=True)
    else:
        largest = jnp.maximum(
            jnp.max(own, axis=1, keepdims=True), jnp.max(fresh, axis=1, keepdims=True)
        )
    return jnp.exp2((own - largest) * scale), jnp.exp2((fresh - largest) * scale)


def spread(own, slot_of, slots):
    if slots == 1:
        return own.astype(jnp.bfloat16)
    parts = [jnp.where(slot_of == s, own, 0.0) for s in range(slots)]
    return jnp.concatenate(parts, axis=1).astype(jnp.bfloat16)


def gather_blocks(pool_ref, slots, ids):
    tiles = [pool_ref[0, s, block] for s in range(slots) for block in ids]
    return jnp.concatenate(tiles, axis=0)


def with_ones(values):
    return jnp.concatenate([values, jnp.ones_like(values)], axis=1)


def dot(left, right):
    return jnp.dot(left, right, preferred_element_type=jnp.float32)


def attend_kernel(
    ready, launch, table_ref, len_ref, query_hbm, kv_hbm, pool_ref, out_ref, query_all, kv_all,
    fresh_ref, pf_ref, blend_ref, done_ref, sems, *, first_row, steps_in_all, sizes,
):
    z = sizes
    width, per = z.width, z.per
    rows = GROUP
    step = pl.program_id(0)
    extent = z.blocks * z.block
    start = first_row + step * rows
    scale = math.log2(math.e) / math.sqrt(width)

    def copies(n):
        begin = first_row + n * rows
        return (
            pltpu.make_async_copy(
                query_hbm.at[pl.ds(pl.multiple_of(begin * per, rows * per), rows * per)],
                query_all.at[n], sems.at[0, n],
            ),
            pltpu.make_async_copy(kv_hbm.at[pl.ds(begin, rows)], kv_all.at[n], sems.at[1, n]),
        )

    @pl.when(step == 0)
    def _():
        for n in range(steps_in_all):
            for copy in copies(n):
                copy.start()
        launch()
        ready()

    for copy in copies(step):
        copy.wait()

    query_ref = query_all.at[step]
    new_kv = kv_all[step].reshape(rows * z.per_kv, 2 * width)
    fresh_ref[...] = dot_t(query_ref[...], new_kv[:, :width])
    code = fresh_code(per, rows * z.per_kv, z)
    slot_of = slot_index(extent, z)
    together = min(TOGETHER, rows)
    for begin in range(0, rows, together):
        group = range(begin, begin + together)
        at = [slice(r * per, (r + 1) * per) for r in group]
        known = [jnp.minimum(start + r, z.resident - 1) for r in group]
        length = [
            jnp.where(start + r < z.resident, len_ref[0, k], 0) for r, k in zip(group, known)
        ]
        both = [
            gather_blocks(pool_ref, z.slots, [table_ref[j, k] for j in range(z.blocks)])
            for k in known
        ]
        fresh = [fresh_ref[a, :] for a in at]
        scores = [dot_t(query_ref[a, :], b[:, :width]) for a, b in zip(at, both)]
        weights = [
            weigh(own_scores(s, slot_of, z.slots), n, f, code == r, scale)
            for s, n, f, r in zip(scores, length, fresh, group)
        ]
        context = [
            dot(spread(w[0], slot_of, z.slots), with_ones(b[:, width:]))
            for w, b in zip(weights, both)
        ]
        for a, c, w in zip(at, context, weights):
            blend_ref[a, :] = c
            pf_ref[a, :] = w[1].astype(jnp.bfloat16)

    done = blend_ref[...] + dot(pf_ref[...], with_ones(new_kv[:, width:]))
    done_ref[...] = done[:, :width] / done[:, width:]
    for h in range(z.heads):
        column = done_ref[pl.ds(h, rows * z.steps, stride=z.heads), :]
        out_ref[:, h * width : (h + 1) * width] = column.astype(jnp.bfloat16)


def attend(table, lengths, queries, new_kv, pool, first_row, rows, sizes, deps, **fetch):
    z = sizes
    groups = rows // GROUP
    tokens = rows * z.steps
    result, pieces = run(
        functools.partial(
            attend_kernel, first_row=first_row, steps_in_all=groups, sizes=z
        ),
        [table, lengths],
        [queries, new_kv, pool],
        [HBM, HBM, VMEM],
        deps,
        [jax.ShapeDtypeStruct((tokens, z.heads * z.width), jnp.bfloat16)],
        [pl.BlockSpec((GROUP * z.steps, z.heads * z.width), lambda i: (i, 0))],
        "attend", z, limit=36,
        grid=(groups,),
        scratch=[
            pltpu.VMEM((groups, GROUP * z.per, z.width), jnp.bfloat16),
            pltpu.VMEM((groups, GROUP) + new_kv.shape[1:], jnp.bfloat16),
            pltpu.VMEM((GROUP * z.per, GROUP * z.per_kv), jnp.float32),
            pltpu.VMEM((GROUP * z.per, GROUP * z.per_kv), jnp.bfloat16),
            pltpu.VMEM((GROUP * z.per, 2 * z.width), jnp.float32),
            pltpu.VMEM((GROUP * z.per, z.width), jnp.float32),
            pltpu.SemaphoreType.DMA((2, groups)),
        ],
        **fetch,
    )
    return result[0], pieces


def settle_kernel(
    ready, launch, dest_ref, len_ref, got_ref, query_ref, kv_ref, old_ref, out_ref, last_ref,
    rows_ref, *, sizes
):
    z = sizes
    ready()
    inst = lax.axis_index("inst")
    requests = row_plan(dest_ref, inst, z.cap)
    extent = z.mig_blocks * z.block
    new_kv = kv_ref[...].reshape(z.tail_kv, 2 * z.width)
    code = fresh_code(z.per, z.tail_kv, z)
    slot_of = slot_index(extent, z)
    scale = math.log2(math.e) / math.sqrt(z.width)
    tokens = z.insts * z.steps
    row = lax.broadcasted_iota(jnp.int32, (tokens, z.width), 0) // z.steps
    filled = row < 0
    rows_ref[: z.per, :] = jnp.zeros((z.per, z.width), jnp.float32)
    for a in range(z.cap):
        at = slice((a + 1) * z.per, (a + 2) * z.per)
        known = jnp.maximum(requests[a], 0)
        source = known // z.mig_per
        both = jnp.concatenate(
            [got_ref[source, s].reshape(extent, 2 * z.width) for s in range(z.slots)], axis=0
        )
        own = own_scores(dot_t(query_ref[at, :], both[:, : z.width]), slot_of, z.slots)
        fresh = dot_t(query_ref[at, :], new_kv[:, : z.width])
        own, fresh = weigh(own, len_ref[known], fresh, code == a + 1, scale)
        done = dot(spread(own, slot_of, z.slots), with_ones(both[:, z.width :]))
        done = done + dot(fresh.astype(jnp.bfloat16), with_ones(new_kv[:, z.width :]))
        rows_ref[at, :] = done[:, : z.width] / done[:, z.width :]
        filled = filled | ((row == a + 1) & (requests[a] >= 0))
    for h in range(z.heads):
        at = slice(h * z.width, (h + 1) * z.width)
        column = rows_ref[pl.ds(h, tokens, stride=z.heads), :]
        old = old_ref[:, at].astype(jnp.float32)
        value = jnp.where(filled, column, old).astype(jnp.bfloat16)
        out_ref[:, at] = value
        last_ref[:, at] = value


def settle(mig_dest, mig_len, got, query_rows, new_kv, attention, sizes, deps):
    z = sizes
    tokens = z.insts * z.steps
    last = attention.shape[0] // tokens - 1
    last_q = query_rows.shape[0] // z.tail_q - 1
    last_kv = z.batch // z.insts - 1
    spec = pl.BlockSpec((tokens, attention.shape[1]), lambda i: (last, 0))
    result, _ = run(
        functools.partial(settle_kernel, sizes=z),
        [mig_dest, mig_len], [got, query_rows, new_kv, attention],
        [
            VMEM,
            pl.BlockSpec((z.tail_q, z.width), lambda i: (last_q, 0)),
            pl.BlockSpec((z.insts,) + new_kv.shape[1:], lambda i: (last_kv, 0, 0, 0)),
            spec,
        ],
        deps,
        [
            jax.ShapeDtypeStruct(attention.shape, jnp.bfloat16),
            jax.ShapeDtypeStruct((tokens, attention.shape[1]), jnp.bfloat16),
        ],
        [spec, VMEM], "settle", z, grid=(1,),
        scratch=[pltpu.VMEM((z.insts * z.per, z.width), jnp.float32)],
        aliases={5: 0},
    )
    return result


def project_kernel(
    ready, launch, *refs, parts, count, streamed, added, joined, kept, sizes
):
    launch()
    attention, weights = refs[:parts], list(refs[parts : parts + count])
    position = parts + count
    extra = refs[position : position + added]
    position += added
    source = refs[position]
    position += bool(streamed)
    outs = 1 if joined else count + len(streamed)
    out_refs = refs[position : position + outs]
    copies = [None] * count
    if streamed:
        if kept:
            buffers = refs[position + outs : position + outs + len(streamed)]
        else:
            buffers = [refs[-2].at[n] for n in range(len(streamed))]
        for n, piece in enumerate(streamed):
            first = pl.multiple_of(piece_columns(piece, sizes), LANES)
            copy = pltpu.make_async_copy(
                source.at[:, pl.ds(first, sizes.quarter)], buffers[n], refs[-1].at[n]
            )
            copy.start()
            copies.append(copy)
            weights.append(buffers[n])
    width = sizes.quarter
    tile = min(width, 256)
    for n, (weight, copy) in enumerate(zip(weights, copies)):
        if copy is not None:
            copy.wait()

        def one(j, carry, n=n, weight=weight):
            at = pl.ds(pl.multiple_of(j * tile, tile), tile)
            begin = 0
            for part in attention:
                tokens = part.shape[0]
                rows = slice(begin, begin + tokens)
                result = dot(part[...], weight[:, at])
                to = pl.ds(pl.multiple_of(n * width + j * tile, tile), tile)
                if added == 1:
                    result = result + extra[0][rows, to].astype(jnp.float32)
                elif added:
                    result = result + extra[n][rows, at].astype(jnp.float32)
                if joined:
                    out_refs[0][rows, to] = result.astype(jnp.bfloat16)
                else:
                    out_refs[n][rows, at] = result.astype(jnp.bfloat16)
                begin += tokens
            return carry

        lax.fori_loop(0, width // tile, one, 0)


def project(attention, weights, streamed, out_weight, mates, joined, kept, sizes, name, deps,
            pieces=()):
    tokens = sum(a.shape[0] for a in attention)
    count = len(weights) + len(streamed)
    if joined:
        shapes = [jax.ShapeDtypeStruct((tokens, count * sizes.quarter), jnp.bfloat16)]
    else:
        shapes = [jax.ShapeDtypeStruct((tokens, sizes.quarter), jnp.bfloat16)] * count
    results = len(shapes)
    operands = attention + weights + mates
    specs = [VMEM] * len(operands)
    scratch = []
    piece = (sizes.depth, sizes.quarter)
    if streamed:
        operands = operands + [out_weight]
        specs = specs + [HBM]
        if kept:
            shapes = shapes + [jax.ShapeDtypeStruct(piece, jnp.bfloat16)] * len(streamed)
        else:
            scratch.append(pltpu.VMEM((len(streamed),) + piece, jnp.bfloat16))
        scratch.append(pltpu.SemaphoreType.DMA((len(streamed),)))
    result, new = run(
        functools.partial(
            project_kernel, parts=len(attention), count=len(weights), streamed=streamed,
            added=len(mates), joined=joined, kept=kept, sizes=sizes,
        ),
        [], operands, specs, deps, shapes, [VMEM] * len(shapes), name, sizes,
        limit=36 if streamed or pieces else 16, scratch=scratch,
        pieces=pieces, weight=out_weight,
    )
    return result[:results], result[results:], new


def finish_kernel(ready, launch, part_ref, *refs, count):
    got, late, out_ref = refs[:count], refs[count:-1], refs[-1]
    sums = part_ref[...].astype(jnp.float32)
    for n, ref in enumerate(got):
        arrived = ref[...]
        if late:
            rows = late[n].shape[0]
            arrived = jnp.concatenate([arrived[:-rows], late[n][...]], axis=0)
        sums = sums + arrived.astype(jnp.float32)
    out_ref[...] = sums.T.astype(jnp.bfloat16)


def finish(hidden, own, got, late, row, column, sizes, deps):
    count, height = got[0].shape
    tile = min(height, 512)
    first = row // tile
    block = column // count
    spec = pl.BlockSpec((tile, count), lambda j: (first + j, block))
    operands = [own] + got + late
    in_specs = [pl.BlockSpec((count, tile), lambda j: (block, first + j))]
    in_specs += [pl.BlockSpec((count, tile), lambda j: (0, j))] * len(got)
    in_specs += [pl.BlockSpec((x.shape[0], tile), lambda j: (0, first + j)) for x in late]
    aliases = None
    if hidden is not None:
        aliases = {len(operands): 0}
        deps = [hidden] + deps
    result, _ = run(
        functools.partial(finish_kernel, count=len(got)), [], operands, in_specs, deps,
        [jax.ShapeDtypeStruct(own.shape[::-1], jnp.bfloat16)], [spec], "finish", sizes,
        grid=(height // tile,), aliases=aliases,
    )
    return result[0]


def shards(
    res_pool,
    res_table,
    res_len,
    out_pool,
    src_table,
    mig_len,
    mig_dest,
    queries,
    new_kv,
    out_weight,
):
    z = Sizes(queries, res_pool, res_table, src_table, mig_dest, out_weight)
    tps, chips = z.tps, z.chips
    table = res_table[0].T
    query_rows = queries.reshape(z.batch * z.per, z.width)

    to_mate = [(i, i + 1 - 2 * (i % CORES)) for i in range(tps)]
    far = range(1, chips)
    held = {}

    def mate_of(x):
        return lax.ppermute(x, "tp", to_mate)

    def across(x, ahead):
        shift = ahead * CORES
        return lax.ppermute(x, "tp", [(i, (i + shift) % tps) for i in range(tps)])

    def bringing(pieces):
        return dict(pieces=pieces, weight=out_weight)

    def gives(ks, parts):
        return [(k, False, part) for k in ks for part in parts]

    def keeps(ks, parts):
        return [(k, True, part) for k in ks for part in parts]

    def at_hand(pieces):
        here = [held[piece] for piece in pieces if piece in held]
        return here, [piece for piece in pieces if piece not in held]

    def hold(pieces, arrays):
        held.update(zip(pieces, arrays))

    def give(attention, ks, parts, name, deps, pieces=(), kept=True, joined=False):
        weights, streamed = at_hand(gives(ks, parts))
        results, mine, new = project(
            attention, weights, streamed, out_weight, [], joined, kept, z, name, deps, pieces
        )
        if kept:
            hold(streamed, mine)
        hold(pieces, new)
        return results[0], [mate_of(result) for result in results]

    def keep(attention, ks, parts, mates, name, deps, kept=True):
        results = []
        for n, k in enumerate(ks):
            weights, streamed = at_hand(keeps([k], parts))
            if len(mates) == 1:
                width = mates[0].shape[1] // len(ks)
                now = [mates[0][:, n * width : (n + 1) * width] if len(ks) > 1 else mates[0]]
            else:
                now = mates[n * len(parts) : (n + 1) * len(parts)]
            result, mine, _ = project(
                attention, weights, streamed, out_weight, now, True, kept, z, name, deps
            )
            if kept:
                hold(streamed, mine)
            deps = [result[0]]
            results.append(result[0])
        return results

    def sent(results):
        return [across(result, k) for k, result in zip(far, results)]

    half = z.batch // 2
    low, high, every = (0, 1), (2, 3), (0, 1, 2, 3)

    sends = pack(src_table, mig_dest, out_pool, z)
    arriving = lax.all_to_all(sends, "inst", split_axis=0, concat_axis=0, tiled=True)

    a, new = attend(
        table, res_len, query_rows, new_kv, res_pool, 0, half, z, [sends],
        **bringing(gives(far, low) + keeps(far, low)),
    )
    hold(gives(far, low) + keeps(far, low), new)
    given, mates = give([a], far, low, "give", [])
    kept = keep([a], far, low, mates, "keep", [given])
    got_a_low = sent(kept)
    given, mates = give([a], far, high, "give", kept[-1:])
    kept = keep([a], far, high, mates, "keep", [given])
    got_a_high = sent(kept)
    b, _ = attend(
        table, res_len, query_rows, new_kv, res_pool, half, half, z, kept[-1:],
    )
    given, mates = give([b], far, every, "give", got_a_low)
    kept = keep([b], far, every, mates, "keep", [given])
    got_b = sent(kept)
    b, d = settle(mig_dest, mig_len, arriving, query_rows, new_kv, b, z, kept[-1:])
    given, mates = give([d], far, every, "give_last", got_a_high, joined=True)
    given, own_mates = give([a, b], [0], every, "give_own", [given], kept=False)
    kept = keep([d], far, every, mates, "keep_last", [given])
    got_d = sent(kept)
    own = keep([a, b], [0], every, own_mates, "keep_own", kept[-1:], kept=False)[0]

    arrived = assemble(mig_dest, mig_len, arriving, z, [own])
    tokens = half * z.steps
    hidden = finish(None, own, got_a_low, [], 0, 0, z, [])
    hidden = finish(hidden, own, got_a_high, [], z.features // 2, 0, z, [])
    hidden = finish(hidden, own, got_b, got_d, 0, tokens, z, [])
    return (arrived, hidden)


def solution(mesh):
    placed = (
        P(("groups", "inst"), "tp", None, None, None),
        P(("groups", "inst"), None, None),
        P(("groups", "inst"), None),
        P(("groups", "inst"), "tp", None, None, None),
        P(("groups", "inst"), None, None),
        P("groups"),
        P("groups"),
        P(("groups", "inst"), None, "tp", None),
        P(("groups", "inst"), None, "tp", None),
        P("tp", None),
    )
    return jax.shard_map(
        shards,
        mesh=mesh,
        in_specs=placed,
        out_specs=(P(("groups", "inst"), None, "tp", None, None), P("tp", ("groups", "inst"))),
        check_vma=False,
    )
```

```python
import functools
import math

import jax
import jax.numpy as jnp
from jax import lax
from jax.experimental import pallas as pl
from jax.experimental.pallas import tpu as pltpu
from jax.sharding import PartitionSpec as P

CORES = 2
LOW = -1e30
MIB = 1 << 20
LANES = 128
GROUP = 16
TOGETHER = 8
LARGE_FIRST = 40


def dot_t(left, right):
    return lax.dot_general(
        left, right, (((1,), (1,)), ((), ())), preferred_element_type=jnp.float32
    )


def row_plan(dest_ref, inst, cap):
    requests = [jnp.int32(-1)] * cap
    seen = jnp.int32(0)
    for g in range(dest_ref.shape[0]):
        here = dest_ref[g] == inst
        requests = [jnp.where(here & (seen == a), g, requests[a]) for a in range(cap)]
        seen = seen + here.astype(jnp.int32)
    return requests


VMEM = pl.BlockSpec(memory_space=pltpu.VMEM)
ANY = pl.BlockSpec(memory_space=pl.ANY)
HBM = pl.BlockSpec(memory_space=pltpu.HBM)


class Sizes:
    def __init__(self, queries, res_pool, res_table, src_table, mig_dest, out_weight):
        self.batch, self.steps, self.heads, self.width = queries.shape
        self.slots = res_pool.shape[1]
        self.block = res_pool.shape[3]
        self.resident, self.blocks = res_table.shape[1:]
        self.mig_per, self.mig_blocks = src_table.shape[1:]
        self.requests = mig_dest.shape[0]
        self.insts = lax.axis_size("inst")
        self.tps = lax.axis_size("tp")
        self.chips = self.tps // CORES
        self.cap = self.insts - 1
        self.per = self.steps * self.heads
        self.per_kv = self.steps * self.slots
        self.depth = out_weight.shape[0]
        self.features = out_weight.shape[1] // self.tps
        self.quarter = self.features // 4
        self.tail_q = self.insts * self.per
        self.tail_kv = self.insts * self.per_kv


def piece_columns(piece, sizes):
    ahead, mine, part = piece
    tp = lax.axis_index("tp")
    core = lax.rem(tp, CORES)
    chip = lax.rem(tp // CORES + ahead, sizes.chips)
    owner = chip * CORES + (core if mine else 1 - core)
    return owner * sizes.features + part * sizes.quarter


def run(kernel, tables, operands, in_specs, deps, out_shapes, out_specs, name, sizes,
        pieces=(), weight=None, limit=16, grid=(), scratch=(), aliases=None):
    inputs, outputs, many = len(operands), len(out_shapes), len(tables)
    count = len(deps)
    fetches = len(pieces)
    extra_in = [weight] if fetches else []
    limit = max(limit, 36) if fetches else limit

    def call(*refs):
        table_in, refs = refs[:many], refs[many:]
        own_in = refs[:inputs]
        position = inputs + len(extra_in) + count
        own_out = refs[position : position + outputs]
        fetched = refs[position + outputs : position + outputs + fetches]
        rest = list(refs[position + outputs + fetches :])
        copies, reads = [], []
        if fetches:
            source, sems = refs[inputs], rest.pop()
            for n, piece in enumerate(pieces):
                first = pl.multiple_of(piece_columns(piece, sizes), LANES)
                copies.append(
                    pltpu.make_async_copy(
                        source.at[:, pl.ds(first, sizes.quarter)], fetched[n], sems.at[n]
                    )
                )
        table_refs = []
        if many:
            sems = rest.pop()
            table_refs = rest[len(rest) - many :]
            rest = rest[: len(rest) - many]
            reads = [
                pltpu.make_async_copy(source, target, sems.at[n])
                for n, (source, target) in enumerate(zip(table_in, table_refs))
            ]

        def ready():
            for read in reads:
                read.wait()

        def launch():
            for copy in copies:
                copy.start()

        def each(step, action):
            if not grid:
                action()
            else:
                pl.when(pl.program_id(0) == step)(action)

        def begin():
            for read in reads:
                read.start()

        def end():
            for copy in copies:
                copy.wait()

        if reads:
            each(0, begin)
        kernel(ready, launch, *table_refs, *own_in, *own_out, *rest)
        if copies:
            each(grid[0] - 1 if grid else 0, end)

    result = pl.pallas_call(
        call,
        grid_spec=pltpu.PrefetchScalarGridSpec(
            num_scalar_prefetch=0,
            grid=grid,
            in_specs=[HBM] * many + list(in_specs) + [HBM] * len(extra_in) + [ANY] * count,
            out_specs=list(out_specs) + [ANY] * fetches,
            scratch_shapes=list(scratch)
            + [pltpu.SMEM(t.shape, t.dtype) for t in tables]
            + ([pltpu.SemaphoreType.DMA((many,))] if many else [])
            + ([pltpu.SemaphoreType.DMA((fetches,))] if fetches else []),
        ),
        out_shape=list(out_shapes)
        + [jax.ShapeDtypeStruct((sizes.depth, sizes.quarter), jnp.bfloat16)] * fetches,
        input_output_aliases=aliases or {},
        compiler_params=pltpu.CompilerParams(vmem_limit_bytes=limit * MIB),
        cost_estimate=pl.CostEstimate(flops=0, bytes_accessed=1024, transcendentals=0),
        name=name,
    )(*tables, *operands, *extra_in, *deps)
    return result[:outputs], result[outputs:]


def pack_kernel(ready, launch, table_ref, dest_ref, pool_ref, send_ref, *, sizes):
    inst = lax.axis_index("inst")
    ready()
    for m in range(sizes.mig_per):
        dest = dest_ref[inst * sizes.mig_per + m]

        def copy_block(b, carry, m=m, dest=dest):
            block = table_ref[0, m, b]
            for s in range(sizes.slots):
                send_ref[dest, s, b] = pool_ref[0, s, block]
            return carry

        lax.fori_loop(0, sizes.mig_blocks, copy_block, 0, unroll=8)


def pack(src_table, mig_dest, out_pool, sizes):
    z = sizes
    shape = (z.insts, z.slots, z.mig_blocks, z.block, 2 * z.width)
    result, _ = run(
        functools.partial(pack_kernel, sizes=z),
        [src_table, mig_dest], [out_pool], [VMEM], [],
        [jax.ShapeDtypeStruct(shape, out_pool.dtype)], [VMEM], "pack", z, limit=60,
    )
    return result[0]


def fresh_code(rows, keys, sizes):
    index = lax.broadcasted_iota(jnp.int32, (rows, keys), 0)
    key = lax.broadcasted_iota(jnp.int32, (rows, keys), 1)
    step = index // sizes.heads
    slot = lax.rem(index, sizes.heads) // (sizes.heads // sizes.slots)
    in_row = lax.rem(key, sizes.per_kv)
    seen = (in_row // sizes.slots <= step) & (lax.rem(in_row, sizes.slots) == slot)
    return jnp.where(seen, key // sizes.per_kv, -1)


def slot_index(extent, sizes):
    index = lax.broadcasted_iota(jnp.int32, (sizes.per, extent), 0)
    return lax.rem(index, sizes.heads) // (sizes.heads // sizes.slots)


def own_scores(scores, slot_of, slots):
    extent = scores.shape[1] // slots
    own = scores[:, :extent]
    for s in range(1, slots):
        own = jnp.where(slot_of == s, scores[:, s * extent : (s + 1) * extent], own)
    return own


def weigh(own, length, fresh, fresh_seen, scale):
    place = lax.broadcasted_iota(jnp.int32, own.shape, 1)
    own = jnp.where(place < length, own, LOW)
    fresh = jnp.where(fresh_seen, fresh, LOW)
    if own.shape == fresh.shape:
        largest = jnp.max(jnp.maximum(own, fresh), axis=1, keepdims=True)
    else:
        largest = jnp.maximum(
            jnp.max(own, axis=1, keepdims=True), jnp.max(fresh, axis=1, keepdims=True)
        )
    return jnp.exp2((own - largest) * scale), jnp.exp2((fresh - largest) * scale)


def spread(own, slot_of, slots):
    if slots == 1:
        return own.astype(jnp.bfloat16)
    parts = [jnp.where(slot_of == s, own, 0.0) for s in range(slots)]
    return jnp.concatenate(parts, axis=1).astype(jnp.bfloat16)


def gather_blocks(pool_ref, slots, ids):
    tiles = [pool_ref[0, s, block] for s in range(slots) for block in ids]
    return jnp.concatenate(tiles, axis=0)


def with_ones(values):
    return jnp.concatenate([values, jnp.ones_like(values)], axis=1)


def dot(left, right):
    return jnp.dot(left, right, preferred_element_type=jnp.float32)


def attend_kernel(
    ready, launch, table_ref, len_ref, query_hbm, kv_hbm, pool_ref, out_ref, query_all, kv_all,
    fresh_ref, pf_ref, blend_ref, done_ref, sems, *, first_row, steps_in_all, sizes,
):
    z = sizes
    width, per = z.width, z.per
    rows = GROUP
    step = pl.program_id(0)
    extent = z.blocks * z.block
    start = first_row + step * rows
    scale = math.log2(math.e) / math.sqrt(width)

    def copies(n):
        begin = first_row + n * rows
        return (
            pltpu.make_async_copy(
                query_hbm.at[pl.ds(pl.multiple_of(begin * per, rows * per), rows * per)],
                query_all.at[n], sems.at[0, n],
            ),
            pltpu.make_async_copy(kv_hbm.at[pl.ds(begin, rows)], kv_all.at[n], sems.at[1, n]),
        )

    @pl.when(step == 0)
    def _():
        for n in range(steps_in_all):
            for copy in copies(n):
                copy.start()
        launch()
        ready()

    for copy in copies(step):
        copy.wait()

    query_ref = query_all.at[step]
    new_kv = kv_all[step].reshape(rows * z.per_kv, 2 * width)
    fresh_ref[...] = dot_t(query_ref[...], new_kv[:, :width])
    code = fresh_code(per, rows * z.per_kv, z)
    slot_of = slot_index(extent, z)
    together = min(TOGETHER, rows)
    for begin in range(0, rows, together):
        group = range(begin, begin + together)
        at = [slice(r * per, (r + 1) * per) for r in group]
        known = [jnp.minimum(start + r, z.resident - 1) for r in group]
        length = [
            jnp.where(start + r < z.resident, len_ref[0, k], 0) for r, k in zip(group, known)
        ]
        both = [
            gather_blocks(pool_ref, z.slots, [table_ref[j, k] for j in range(z.blocks)])
            for k in known
        ]
        fresh = [fresh_ref[a, :] for a in at]
        scores = [dot_t(query_ref[a, :], b[:, :width]) for a, b in zip(at, both)]
        weights = [
            weigh(own_scores(s, slot_of, z.slots), n, f, code == r, scale)
            for s, n, f, r in zip(scores, length, fresh, group)
        ]
        context = [
            dot(spread(w[0], slot_of, z.slots), with_ones(b[:, width:]))
            for w, b in zip(weights, both)
        ]
        for a, c, w in zip(at, context, weights):
            blend_ref[a, :] = c
            pf_ref[a, :] = w[1].astype(jnp.bfloat16)

    done = blend_ref[...] + dot(pf_ref[...], with_ones(new_kv[:, width:]))
    done_ref[...] = done[:, :width] / done[:, width:]
    for h in range(z.heads):
        column = done_ref[pl.ds(h, rows * z.steps, stride=z.heads), :]
        out_ref[:, h * width : (h + 1) * width] = column.astype(jnp.bfloat16)


def attend(table, lengths, queries, new_kv, pool, first_row, rows, sizes, deps, limit=12, **fetch):
    z = sizes
    groups = rows // GROUP
    tokens = rows * z.steps
    result, pieces = run(
        functools.partial(
            attend_kernel, first_row=first_row, steps_in_all=groups, sizes=z
        ),
        [table, lengths],
        [queries, new_kv, pool],
        [HBM, HBM, VMEM],
        deps,
        [jax.ShapeDtypeStruct((tokens, z.heads * z.width), jnp.bfloat16)],
        [pl.BlockSpec((GROUP * z.steps, z.heads * z.width), lambda i: (i, 0))],
        "attend", z, limit=limit,
        grid=(groups,),
        scratch=[
            pltpu.VMEM((groups, GROUP * z.per, z.width), jnp.bfloat16),
            pltpu.VMEM((groups, GROUP) + new_kv.shape[1:], jnp.bfloat16),
            pltpu.VMEM((GROUP * z.per, GROUP * z.per_kv), jnp.float32),
            pltpu.VMEM((GROUP * z.per, GROUP * z.per_kv), jnp.bfloat16),
            pltpu.VMEM((GROUP * z.per, 2 * z.width), jnp.float32),
            pltpu.VMEM((GROUP * z.per, z.width), jnp.float32),
            pltpu.SemaphoreType.DMA((2, groups)),
        ],
        **fetch,
    )
    return result[0], pieces


def settle_kernel(
    ready, launch, dest_ref, len_ref, got_hbm, query_ref, kv_ref, old_ref, out_ref, last_ref,
    arrived_hbm, rows_ref, got_ref, keep_ref, sems, *, sizes
):
    z = sizes
    launch()
    ready()
    inst = lax.axis_index("inst")
    requests = row_plan(dest_ref, inst, z.cap)
    known = [jnp.maximum(request, 0) for request in requests]
    extent = z.mig_blocks * z.block
    reads = [
        pltpu.make_async_copy(got_hbm.at[known[a] // z.mig_per], got_ref.at[a], sems.at[0, a])
        for a in range(z.cap)
    ]
    writes = [
        pltpu.make_async_copy(keep_ref.at[a], arrived_hbm.at[0, a], sems.at[1, a])
        for a in range(z.cap)
    ]
    for read in reads:
        read.start()
    new_kv = kv_ref[...].reshape(z.tail_kv, 2 * z.width)
    code = fresh_code(z.per, z.tail_kv, z)
    slot_of = slot_index(extent, z)
    scale = math.log2(math.e) / math.sqrt(z.width)
    tokens = z.insts * z.steps
    row = lax.broadcasted_iota(jnp.int32, (tokens, z.width), 0) // z.steps
    place = lax.broadcasted_iota(jnp.int32, (z.block, 2 * z.width), 0)
    filled = row < 0
    rows_ref[: z.per, :] = jnp.zeros((z.per, z.width), jnp.float32)
    for a in range(z.cap):
        length = jnp.where(requests[a] >= 0, len_ref[known[a]], 0)
        reads[a].wait()

        def one(b, carry, a=a, length=length):
            inside = place + b * z.block < length
            at = pl.ds(pl.multiple_of(b * z.block, z.block), z.block)
            for s in range(z.slots):
                value = got_ref[a, s, b].astype(jnp.float32)
                keep_ref[a, s, at, :] = jnp.where(inside, value, 0.0).astype(jnp.bfloat16)
            return carry

        lax.fori_loop(0, z.mig_blocks, one, 0, unroll=8)
        writes[a].start()
        at = slice((a + 1) * z.per, (a + 2) * z.per)
        both = jnp.concatenate([keep_ref[a, s] for s in range(z.slots)], axis=0)
        own = own_scores(dot_t(query_ref[at, :], both[:, : z.width]), slot_of, z.slots)
        fresh = dot_t(query_ref[at, :], new_kv[:, : z.width])
        own, fresh = weigh(own, length, fresh, code == a + 1, scale)
        done = dot(spread(own, slot_of, z.slots), with_ones(both[:, z.width :]))
        done = done + dot(fresh.astype(jnp.bfloat16), with_ones(new_kv[:, z.width :]))
        rows_ref[at, :] = done[:, : z.width] / done[:, z.width :]
        filled = filled | ((row == a + 1) & (requests[a] >= 0))
    for h in range(z.heads):
        at = slice(h * z.width, (h + 1) * z.width)
        column = rows_ref[pl.ds(h, tokens, stride=z.heads), :]
        old = old_ref[:, at].astype(jnp.float32)
        value = jnp.where(filled, column, old).astype(jnp.bfloat16)
        out_ref[:, at] = value
        last_ref[:, at] = value
    for write in writes:
        write.wait()


def settle(mig_dest, mig_len, got, query_rows, new_kv, attention, sizes, deps, **fetch):
    z = sizes
    tokens = z.insts * z.steps
    last = attention.shape[0] // tokens - 1
    last_q = query_rows.shape[0] // z.tail_q - 1
    last_kv = z.batch // z.insts - 1
    spec = pl.BlockSpec((tokens, attention.shape[1]), lambda i: (last, 0))
    cache = (z.slots, z.mig_blocks * z.block, 2 * z.width)
    return run(
        functools.partial(settle_kernel, sizes=z),
        [mig_dest, mig_len], [got, query_rows, new_kv, attention],
        [
            HBM,
            pl.BlockSpec((z.tail_q, z.width), lambda i: (last_q, 0)),
            pl.BlockSpec((z.insts,) + new_kv.shape[1:], lambda i: (last_kv, 0, 0, 0)),
            spec,
        ],
        deps,
        [
            jax.ShapeDtypeStruct(attention.shape, jnp.bfloat16),
            jax.ShapeDtypeStruct((tokens, attention.shape[1]), jnp.bfloat16),
            jax.ShapeDtypeStruct((1, z.cap) + cache, jnp.bfloat16),
        ],
        [spec, VMEM, ANY], "settle", z, grid=(1,),
        scratch=[
            pltpu.VMEM((z.insts * z.per, z.width), jnp.float32),
            pltpu.VMEM((z.cap,) + got.shape[1:], jnp.bfloat16),
            pltpu.VMEM((z.cap,) + cache, jnp.bfloat16),
            pltpu.SemaphoreType.DMA((2, z.cap)),
        ],
        aliases={5: 0}, **fetch,
    )


def project_kernel(
    ready, launch, *refs, parts, count, streamed, added, joined, kept, sizes
):
    launch()
    attention, weights = refs[:parts], list(refs[parts : parts + count])
    position = parts + count
    extra = refs[position : position + added]
    position += added
    source = refs[position]
    position += bool(streamed)
    outs = 1 if joined else count + len(streamed)
    out_refs = refs[position : position + outs]
    copies = [None] * count
    if streamed:
        if kept:
            buffers = refs[position + outs : position + outs + len(streamed)]
        else:
            buffers = [refs[-2].at[n] for n in range(len(streamed))]
        for n, piece in enumerate(streamed):
            first = pl.multiple_of(piece_columns(piece, sizes), LANES)
            copy = pltpu.make_async_copy(
                source.at[:, pl.ds(first, sizes.quarter)], buffers[n], refs[-1].at[n]
            )
            copy.start()
            copies.append(copy)
            weights.append(buffers[n])
    width = sizes.quarter
    tile = min(width, 256)
    for n, (weight, copy) in enumerate(zip(weights, copies)):
        if copy is not None:
            copy.wait()

        def one(j, carry, n=n, weight=weight):
            at = pl.ds(pl.multiple_of(j * tile, tile), tile)
            begin = 0
            for part in attention:
                tokens = part.shape[0]
                rows = slice(begin, begin + tokens)
                result = dot(part[...], weight[:, at])
                to = pl.ds(pl.multiple_of(n * width + j * tile, tile), tile)
                if added == 1:
                    result = result + extra[0][rows, to].astype(jnp.float32)
                elif added:
                    result = result + extra[n][rows, at].astype(jnp.float32)
                if joined:
                    out_refs[0][rows, to] = result.astype(jnp.bfloat16)
                else:
                    out_refs[n][rows, at] = result.astype(jnp.bfloat16)
                begin += tokens
            return carry

        lax.fori_loop(0, width // tile, one, 0)


def project(attention, weights, streamed, out_weight, mates, joined, kept, sizes, name, deps,
            pieces=()):
    tokens = sum(a.shape[0] for a in attention)
    count = len(weights) + len(streamed)
    if joined:
        shapes = [jax.ShapeDtypeStruct((tokens, count * sizes.quarter), jnp.bfloat16)]
    else:
        shapes = [jax.ShapeDtypeStruct((tokens, sizes.quarter), jnp.bfloat16)] * count
    results = len(shapes)
    operands = attention + weights + mates
    specs = [VMEM] * len(operands)
    scratch = []
    piece = (sizes.depth, sizes.quarter)
    if streamed:
        operands = operands + [out_weight]
        specs = specs + [HBM]
        if kept:
            shapes = shapes + [jax.ShapeDtypeStruct(piece, jnp.bfloat16)] * len(streamed)
        else:
            scratch.append(pltpu.VMEM((len(streamed),) + piece, jnp.bfloat16))
        scratch.append(pltpu.SemaphoreType.DMA((len(streamed),)))
    result, new = run(
        functools.partial(
            project_kernel, parts=len(attention), count=len(weights), streamed=streamed,
            added=len(mates), joined=joined, kept=kept, sizes=sizes,
        ),
        [], operands, specs, deps, shapes, [VMEM] * len(shapes), name, sizes,
        limit=36 if streamed or pieces else 16, scratch=scratch,
        pieces=pieces, weight=out_weight,
    )
    return result[:results], result[results:], new


def final_kernel(ready, launch, *refs, parts, count, streamed, mates, fars, sizes):
    z = sizes
    refs = list(refs)

    def take(n):
        taken = refs[:n]
        del refs[:n]
        return taken

    attention, weights, extra = take(parts), take(count), take(mates)
    low, high, second, late = take(fars), take(fars), take(fars), take(fars)
    source = take(bool(streamed))
    (out_hbm,) = take(1)
    block_ref, block_sems = take(2)
    copies = [None] * count
    for n, piece in enumerate(streamed):
        first = pl.multiple_of(piece_columns(piece, z), LANES)
        copy = pltpu.make_async_copy(
            source[0].at[:, pl.ds(first, z.quarter)], refs[0].at[n], refs[1].at[n]
        )
        copy.start()
        copies.append(copy)
        weights.append(refs[0].at[n])
    tile = min(z.quarter, 256)
    writes = []
    for n, (weight, copy) in enumerate(zip(weights, copies)):
        if copy is not None:
            copy.wait()

        def one(j, carry, n=n, weight=weight):
            start = pl.multiple_of(j * tile, tile)
            at = pl.ds(start, tile)
            whole = pl.ds(n * z.quarter + start, tile)
            half = pl.ds((n % 2) * z.quarter + start, tile)
            begin = 0
            for p, part in enumerate(attention):
                tokens = part.shape[0]
                rows = slice(begin, begin + tokens)
                sums = dot(part[...], weight[:, at]) + extra[n][rows, at].astype(jnp.float32)
                for k in range(fars):
                    if p == 0:
                        arrived = (low if n < 2 else high)[k][:, half]
                    else:
                        count = late[k].shape[0]
                        arrived = jnp.concatenate(
                            [second[k][: tokens - count, whole], late[k][:, whole]], axis=0
                        )
                    sums = sums + arrived.astype(jnp.float32)
                block_ref[n, at, rows] = sums.T.astype(jnp.bfloat16)
                begin += tokens
            return carry

        lax.fori_loop(0, z.quarter // tile, one, 0)
        write = pltpu.make_async_copy(
            block_ref.at[n], out_hbm.at[pl.ds(n * z.quarter, z.quarter)], block_sems.at[n]
        )
        write.start()
        writes.append(write)
    for write in writes:
        write.wait()


def final(attention, weights, streamed, out_weight, mates, low, high, second, late, sizes, deps):
    z = sizes
    tokens = sum(a.shape[0] for a in attention)
    operands = attention + weights + mates + low + high + second + late
    specs = [VMEM] * len(operands)
    scratch = [
        pltpu.VMEM((4, z.quarter, tokens), jnp.bfloat16), pltpu.SemaphoreType.DMA((4,))
    ]
    if streamed:
        operands = operands + [out_weight]
        specs = specs + [HBM]
        scratch += [
            pltpu.VMEM((len(streamed), z.depth, z.quarter), jnp.bfloat16),
            pltpu.SemaphoreType.DMA((len(streamed),)),
        ]
    result, _ = run(
        functools.partial(
            final_kernel, parts=len(attention), count=len(weights), streamed=streamed,
            mates=len(mates), fars=len(low), sizes=z,
        ),
        [], operands, specs, deps,
        [jax.ShapeDtypeStruct((z.features, tokens), jnp.bfloat16)], [ANY], "final", z,
        limit=36 if streamed else 24, scratch=scratch,
    )
    return result[0]


def shards(
    res_pool,
    res_table,
    res_len,
    out_pool,
    src_table,
    mig_len,
    mig_dest,
    queries,
    new_kv,
    out_weight,
):
    z = Sizes(queries, res_pool, res_table, src_table, mig_dest, out_weight)
    tps, chips = z.tps, z.chips
    table = res_table[0].T
    query_rows = queries.reshape(z.batch * z.per, z.width)

    to_mate = [(i, i + 1 - 2 * (i % CORES)) for i in range(tps)]
    far = range(1, chips)
    held = {}

    def mate_of(x):
        return lax.ppermute(x, "tp", to_mate)

    def across(x, ahead):
        shift = ahead * CORES
        return lax.ppermute(x, "tp", [(i, (i + shift) % tps) for i in range(tps)])

    def bringing(pieces):
        return dict(pieces=pieces, weight=out_weight)

    def gives(ks, parts):
        return [(k, False, part) for k in ks for part in parts]

    def keeps(ks, parts):
        return [(k, True, part) for k in ks for part in parts]

    def at_hand(pieces):
        here = [held[piece] for piece in pieces if piece in held]
        return here, [piece for piece in pieces if piece not in held]

    def hold(pieces, arrays):
        held.update(zip(pieces, arrays))

    def give(attention, ks, parts, name, deps, pieces=(), kept=True, joined=False):
        weights, streamed = at_hand(gives(ks, parts))
        results, mine, new = project(
            attention, weights, streamed, out_weight, [], joined, kept, z, name, deps, pieces
        )
        if kept:
            hold(streamed, mine)
        hold(pieces, new)
        return results[0], [mate_of(result) for result in results]

    def keep(attention, ks, parts, mates, name, deps, kept=True):
        results = []
        for n, k in enumerate(ks):
            weights, streamed = at_hand(keeps([k], parts))
            if len(mates) == 1:
                width = mates[0].shape[1] // len(ks)
                now = [mates[0][:, n * width : (n + 1) * width] if len(ks) > 1 else mates[0]]
            else:
                now = mates[n * len(parts) : (n + 1) * len(parts)]
            result, mine, _ = project(
                attention, weights, streamed, out_weight, now, True, kept, z, name, deps
            )
            if kept:
                hold(streamed, mine)
            deps = [result[0]]
            results.append(result[0])
        return results

    def sent(results):
        return [across(result, k) for k, result in zip(far, results)]

    half = z.batch // 2
    low, high, every = (0, 1), (2, 3), (0, 1, 2, 3)

    sends = pack(src_table, mig_dest, out_pool, z)
    arriving = lax.all_to_all(sends, "inst", split_axis=0, concat_axis=0, tiled=True)

    a, new = attend(
        table, res_len, query_rows, new_kv, res_pool, 0, half, z, [sends], limit=LARGE_FIRST,
        **bringing(gives(far, low) + keeps(far, low)),
    )
    hold(gives(far, low) + keeps(far, low), new)
    given, mates = give([a], far, low, "give", [])
    kept = keep([a], far, low, mates, "keep", [given])
    got_low = sent(kept)
    given, mates = give([a], far, high, "give", kept[-1:])
    kept = keep([a], far, high, mates, "keep", [given])
    got_high = sent(kept)
    b, new = attend(
        table, res_len, query_rows, new_kv, res_pool, half, half, z, kept[-1:],
        **bringing(gives([0], every)),
    )
    hold(gives([0], every), new)
    given, mates = give([b], far, every, "give", got_low)
    kept = keep([b], far, every, mates, "keep", [given] + got_high)
    got_second = sent(kept)
    (b, d, arrived), new = settle(
        mig_dest, mig_len, arriving, query_rows, new_kv, b, z, kept[-1:]
    )
    given, mates = give([d], far, every, "give_last", [], joined=True)
    given, own_mates = give([a, b], [0], every, "give_own", [given])
    kept = keep([d], far, every, mates, "keep_last", [given])
    got_late = sent(kept)
    weights, streamed = at_hand(keeps([0], every))
    hidden = final(
        [a, b], weights, streamed, out_weight, own_mates, got_low, got_high, got_second, got_late,
        z, kept[-1:],
    )
    return (arrived, hidden)


def solution(mesh):
    placed = (
        P(("groups", "inst"), "tp", None, None, None),
        P(("groups", "inst"), None, None),
        P(("groups", "inst"), None),
        P(("groups", "inst"), "tp", None, None, None),
        P(("groups", "inst"), None, None),
        P("groups"),
        P("groups"),
        P(("groups", "inst"), None, "tp", None),
        P(("groups", "inst"), None, "tp", None),
        P("tp", None),
    )
    return jax.shard_map(
        shards,
        mesh=mesh,
        in_specs=placed,
        out_specs=(P(("groups", "inst"), None, "tp", None, None), P("tp", ("groups", "inst"))),
        check_vma=False,
    )
```

```python
import functools
import math

import jax
import jax.numpy as jnp
from jax import lax
from jax.experimental import pallas as pl
from jax.experimental.pallas import tpu as pltpu
from jax.sharding import PartitionSpec as P

CORES = 2
LOW = -1e30
MIB = 1 << 20
LANES = 128
GROUP = 16
TOGETHER = 8
LARGE_FIRST = 40
FETCHING = 33


def dot_t(left, right):
    return lax.dot_general(
        left, right, (((1,), (1,)), ((), ())), preferred_element_type=jnp.float32
    )


def row_plan(dest_ref, inst, cap):
    requests = [jnp.int32(-1)] * cap
    seen = jnp.int32(0)
    for g in range(dest_ref.shape[0]):
        here = dest_ref[g] == inst
        requests = [jnp.where(here & (seen == a), g, requests[a]) for a in range(cap)]
        seen = seen + here.astype(jnp.int32)
    return requests


VMEM = pl.BlockSpec(memory_space=pltpu.VMEM)
ANY = pl.BlockSpec(memory_space=pl.ANY)
HBM = pl.BlockSpec(memory_space=pltpu.HBM)


class Sizes:
    def __init__(self, queries, res_pool, res_table, src_table, mig_dest, out_weight):
        self.batch, self.steps, self.heads, self.width = queries.shape
        self.slots = res_pool.shape[1]
        self.block = res_pool.shape[3]
        self.resident, self.blocks = res_table.shape[1:]
        self.mig_per, self.mig_blocks = src_table.shape[1:]
        self.requests = mig_dest.shape[0]
        self.insts = lax.axis_size("inst")
        self.tps = lax.axis_size("tp")
        self.chips = self.tps // CORES
        self.cap = self.insts - 1
        self.per = self.steps * self.heads
        self.per_kv = self.steps * self.slots
        self.depth = out_weight.shape[0]
        self.features = out_weight.shape[1] // self.tps
        self.quarter = self.features // 4
        self.tail_q = self.insts * self.per
        self.tail_kv = self.insts * self.per_kv


def piece_columns(piece, sizes):
    ahead, mine, part = piece
    tp = lax.axis_index("tp")
    core = lax.rem(tp, CORES)
    chip = lax.rem(tp // CORES + ahead, sizes.chips)
    owner = chip * CORES + (core if mine else 1 - core)
    return owner * sizes.features + part * sizes.quarter


def run(kernel, tables, operands, in_specs, deps, out_shapes, out_specs, name, sizes,
        pieces=(), weight=None, limit=16, grid=(), scratch=(), aliases=None):
    inputs, outputs, many = len(operands), len(out_shapes), len(tables)
    count = len(deps)
    fetches = len(pieces)
    extra_in = [weight] if fetches else []
    limit = max(limit, FETCHING) if fetches else limit

    def call(*refs):
        table_in, refs = refs[:many], refs[many:]
        own_in = refs[:inputs]
        position = inputs + len(extra_in) + count
        own_out = refs[position : position + outputs]
        fetched = refs[position + outputs : position + outputs + fetches]
        rest = list(refs[position + outputs + fetches :])
        copies, reads = [], []
        if fetches:
            source, sems = refs[inputs], rest.pop()
            for n, piece in enumerate(pieces):
                first = pl.multiple_of(piece_columns(piece, sizes), LANES)
                copies.append(
                    pltpu.make_async_copy(
                        source.at[:, pl.ds(first, sizes.quarter)], fetched[n], sems.at[n]
                    )
                )
        table_refs = []
        if many:
            sems = rest.pop()
            table_refs = rest[len(rest) - many :]
            rest = rest[: len(rest) - many]
            reads = [
                pltpu.make_async_copy(source, target, sems.at[n])
                for n, (source, target) in enumerate(zip(table_in, table_refs))
            ]

        def ready():
            for read in reads:
                read.wait()

        def launch():
            for copy in copies:
                copy.start()

        def each(step, action):
            if not grid:
                action()
            else:
                pl.when(pl.program_id(0) == step)(action)

        def begin():
            for read in reads:
                read.start()

        def end():
            for copy in copies:
                copy.wait()

        if reads:
            each(0, begin)
        kernel(ready, launch, *table_refs, *own_in, *own_out, *rest)
        if copies:
            each(grid[0] - 1 if grid else 0, end)

    result = pl.pallas_call(
        call,
        grid_spec=pltpu.PrefetchScalarGridSpec(
            num_scalar_prefetch=0,
            grid=grid,
            in_specs=[HBM] * many + list(in_specs) + [HBM] * len(extra_in) + [ANY] * count,
            out_specs=list(out_specs) + [ANY] * fetches,
            scratch_shapes=list(scratch)
            + [pltpu.SMEM(t.shape, t.dtype) for t in tables]
            + ([pltpu.SemaphoreType.DMA((many,))] if many else [])
            + ([pltpu.SemaphoreType.DMA((fetches,))] if fetches else []),
        ),
        out_shape=list(out_shapes)
        + [jax.ShapeDtypeStruct((sizes.depth, sizes.quarter), jnp.bfloat16)] * fetches,
        input_output_aliases=aliases or {},
        compiler_params=pltpu.CompilerParams(vmem_limit_bytes=limit * MIB),
        cost_estimate=pl.CostEstimate(flops=0, bytes_accessed=1024, transcendentals=0),
        name=name,
    )(*tables, *operands, *extra_in, *deps)
    return result[:outputs], result[outputs:]


def pack_kernel(
    ready, launch, table_ref, dest_ref, pool_ref, query_ref, kv_ref, send_ref, tail_q_ref,
    tail_kv_ref, *, sizes
):
    inst = lax.axis_index("inst")
    launch()
    tail_q_ref[...] = query_ref[...]
    tail_kv_ref[...] = kv_ref[...].reshape(sizes.tail_kv, 2 * sizes.width)
    ready()
    for m in range(sizes.mig_per):
        dest = dest_ref[inst * sizes.mig_per + m]

        def copy_block(b, carry, m=m, dest=dest):
            block = table_ref[0, m, b]
            for s in range(sizes.slots):
                send_ref[dest, s, b] = pool_ref[0, s, block]
            return carry

        lax.fori_loop(0, sizes.mig_blocks, copy_block, 0, unroll=8)


def pack(src_table, mig_dest, out_pool, query_rows, new_kv, sizes):
    z = sizes
    last_q = query_rows.shape[0] // z.tail_q - 1
    last_kv = z.batch // z.insts - 1
    result, _ = run(
        functools.partial(pack_kernel, sizes=z),
        [src_table, mig_dest], [out_pool, query_rows, new_kv],
        [
            VMEM,
            pl.BlockSpec((z.tail_q, z.width), lambda i: (last_q, 0)),
            pl.BlockSpec((z.insts,) + new_kv.shape[1:], lambda i: (last_kv, 0, 0, 0)),
        ],
        [],
        [
            jax.ShapeDtypeStruct(
                (z.insts, z.slots, z.mig_blocks, z.block, 2 * z.width), out_pool.dtype
            ),
            jax.ShapeDtypeStruct((z.tail_q, z.width), out_pool.dtype),
            jax.ShapeDtypeStruct((z.tail_kv, 2 * z.width), out_pool.dtype),
        ],
        [VMEM] * 3, "pack", z, limit=60, grid=(1,),
    )
    return result


def fresh_code(rows, keys, sizes):
    index = lax.broadcasted_iota(jnp.int32, (rows, keys), 0)
    key = lax.broadcasted_iota(jnp.int32, (rows, keys), 1)
    step = index // sizes.heads
    slot = lax.rem(index, sizes.heads) // (sizes.heads // sizes.slots)
    in_row = lax.rem(key, sizes.per_kv)
    seen = (in_row // sizes.slots <= step) & (lax.rem(in_row, sizes.slots) == slot)
    return jnp.where(seen, key // sizes.per_kv, -1)


def slot_index(extent, sizes):
    index = lax.broadcasted_iota(jnp.int32, (sizes.per, extent), 0)
    return lax.rem(index, sizes.heads) // (sizes.heads // sizes.slots)


def own_scores(scores, slot_of, slots):
    extent = scores.shape[1] // slots
    own = scores[:, :extent]
    for s in range(1, slots):
        own = jnp.where(slot_of == s, scores[:, s * extent : (s + 1) * extent], own)
    return own


def weigh(own, length, fresh, fresh_seen, scale):
    place = lax.broadcasted_iota(jnp.int32, own.shape, 1)
    own = jnp.where(place < length, own, LOW)
    fresh = jnp.where(fresh_seen, fresh, LOW)
    if own.shape == fresh.shape:
        largest = jnp.max(jnp.maximum(own, fresh), axis=1, keepdims=True)
    else:
        largest = jnp.maximum(
            jnp.max(own, axis=1, keepdims=True), jnp.max(fresh, axis=1, keepdims=True)
        )
    return jnp.exp2((own - largest) * scale), jnp.exp2((fresh - largest) * scale)


def spread(own, slot_of, slots):
    if slots == 1:
        return own.astype(jnp.bfloat16)
    parts = [jnp.where(slot_of == s, own, 0.0) for s in range(slots)]
    return jnp.concatenate(parts, axis=1).astype(jnp.bfloat16)


def gather_blocks(pool_ref, slots, ids):
    tiles = [pool_ref[0, s, block] for s in range(slots) for block in ids]
    return jnp.concatenate(tiles, axis=0)


def with_ones(values):
    return jnp.concatenate([values, jnp.ones_like(values)], axis=1)


def dot(left, right):
    return jnp.dot(left, right, preferred_element_type=jnp.float32)


def attend_kernel(
    ready, launch, table_ref, len_ref, query_hbm, kv_hbm, pool_ref, *refs, first_row,
    steps_in_all, sizes,
):
    z = sizes
    out_ref, query_all, kv_all, fresh_ref, pf_ref, blend_ref, done_ref, sems = refs
    width, per = z.width, z.per
    rows = GROUP
    step = pl.program_id(0)
    extent = z.blocks * z.block
    start = first_row + step * rows
    scale = math.log2(math.e) / math.sqrt(width)

    def copies(n):
        begin = first_row + n * rows
        return (
            pltpu.make_async_copy(
                query_hbm.at[pl.ds(pl.multiple_of(begin * per, rows * per), rows * per)],
                query_all.at[n], sems.at[0, n],
            ),
            pltpu.make_async_copy(kv_hbm.at[pl.ds(begin, rows)], kv_all.at[n], sems.at[1, n]),
        )

    @pl.when(step == 0)
    def _():
        for n in range(steps_in_all):
            for copy in copies(n):
                copy.start()
        launch()
        ready()

    for copy in copies(step):
        copy.wait()

    query_ref = query_all.at[step]
    new_kv = kv_all[step].reshape(rows * z.per_kv, 2 * width)
    fresh_ref[...] = dot_t(query_ref[...], new_kv[:, :width])
    code = fresh_code(per, rows * z.per_kv, z)
    slot_of = slot_index(extent, z)
    together = min(TOGETHER, rows)
    for begin in range(0, rows, together):
        group = range(begin, begin + together)
        at = [slice(r * per, (r + 1) * per) for r in group]
        known = [jnp.minimum(start + r, z.resident - 1) for r in group]
        length = [
            jnp.where(start + r < z.resident, len_ref[0, k], 0) for r, k in zip(group, known)
        ]
        both = [
            gather_blocks(pool_ref, z.slots, [table_ref[j, k] for j in range(z.blocks)])
            for k in known
        ]
        fresh = [fresh_ref[a, :] for a in at]
        scores = [dot_t(query_ref[a, :], b[:, :width]) for a, b in zip(at, both)]
        weights = [
            weigh(own_scores(s, slot_of, z.slots), n, f, code == r, scale)
            for s, n, f, r in zip(scores, length, fresh, group)
        ]
        context = [
            dot(spread(w[0], slot_of, z.slots), with_ones(b[:, width:]))
            for w, b in zip(weights, both)
        ]
        for a, c, w in zip(at, context, weights):
            blend_ref[a, :] = c
            pf_ref[a, :] = w[1].astype(jnp.bfloat16)

    done = blend_ref[...] + dot(pf_ref[...], with_ones(new_kv[:, width:]))
    done_ref[...] = done[:, :width] / done[:, width:]
    for h in range(z.heads):
        column = done_ref[pl.ds(h, rows * z.steps, stride=z.heads), :]
        out_ref[:, h * width : (h + 1) * width] = column.astype(jnp.bfloat16)


def attend(table, lengths, queries, new_kv, pool, into, first_row, rows, sizes, deps, limit=12,
           **fetch):
    z = sizes
    groups = rows // GROUP
    first = first_row // GROUP
    tokens = z.batch * z.steps
    aliases = {}
    if into is not None:
        deps = [into] + deps
        aliases = {5 + (1 if fetch else 0): 0}
    result, pieces = run(
        functools.partial(
            attend_kernel, first_row=first_row, steps_in_all=groups, sizes=z
        ),
        [table, lengths],
        [queries, new_kv, pool],
        [HBM, HBM, VMEM],
        deps,
        [jax.ShapeDtypeStruct((tokens, z.heads * z.width), jnp.bfloat16)],
        [pl.BlockSpec((GROUP * z.steps, z.heads * z.width), lambda i: (first + i, 0))],
        "attend", z, limit=limit,
        grid=(groups,),
        scratch=[
            pltpu.VMEM((groups, GROUP * z.per, z.width), jnp.bfloat16),
            pltpu.VMEM((groups, GROUP) + new_kv.shape[1:], jnp.bfloat16),
            pltpu.VMEM((GROUP * z.per, GROUP * z.per_kv), jnp.float32),
            pltpu.VMEM((GROUP * z.per, GROUP * z.per_kv), jnp.bfloat16),
            pltpu.VMEM((GROUP * z.per, 2 * z.width), jnp.float32),
            pltpu.VMEM((GROUP * z.per, z.width), jnp.float32),
            pltpu.SemaphoreType.DMA((2, groups)),
        ],
        aliases=aliases, **fetch,
    )
    return result[0], pieces


def settle_kernel(
    ready, launch, dest_ref, len_ref, got_hbm, query_ref, kv_ref, old_ref, out_ref, last_ref,
    arrived_hbm, rows_ref, got_ref, keep_ref, sems, *, sizes
):
    z = sizes
    launch()
    ready()
    inst = lax.axis_index("inst")
    requests = row_plan(dest_ref, inst, z.cap)
    known = [jnp.maximum(request, 0) for request in requests]
    extent = z.mig_blocks * z.block
    reads = [
        pltpu.make_async_copy(got_hbm.at[known[a] // z.mig_per], got_ref.at[a], sems.at[0, a])
        for a in range(z.cap)
    ]
    writes = [
        pltpu.make_async_copy(keep_ref.at[a], arrived_hbm.at[0, a], sems.at[1, a])
        for a in range(z.cap)
    ]
    for read in reads:
        read.start()
    new_kv = kv_ref[...]
    code = fresh_code(z.per, z.tail_kv, z)
    slot_of = slot_index(extent, z)
    scale = math.log2(math.e) / math.sqrt(z.width)
    tokens = z.insts * z.steps
    row = lax.broadcasted_iota(jnp.int32, (tokens, z.width), 0) // z.steps
    place = lax.broadcasted_iota(jnp.int32, (z.block, 2 * z.width), 0)
    filled = row < 0
    rows_ref[: z.per, :] = jnp.zeros((z.per, z.width), jnp.float32)
    for a in range(z.cap):
        length = jnp.where(requests[a] >= 0, len_ref[known[a]], 0)
        reads[a].wait()

        def one(b, carry, a=a, length=length):
            inside = place + b * z.block < length
            at = pl.ds(pl.multiple_of(b * z.block, z.block), z.block)
            for s in range(z.slots):
                value = got_ref[a, s, b].astype(jnp.float32)
                keep_ref[a, s, at, :] = jnp.where(inside, value, 0.0).astype(jnp.bfloat16)
            return carry

        lax.fori_loop(0, z.mig_blocks, one, 0, unroll=8)
        writes[a].start()
        at = slice((a + 1) * z.per, (a + 2) * z.per)
        both = jnp.concatenate([keep_ref[a, s] for s in range(z.slots)], axis=0)
        own = own_scores(dot_t(query_ref[at, :], both[:, : z.width]), slot_of, z.slots)
        fresh = dot_t(query_ref[at, :], new_kv[:, : z.width])
        own, fresh = weigh(own, length, fresh, code == a + 1, scale)
        done = dot(spread(own, slot_of, z.slots), with_ones(both[:, z.width :]))
        done = done + dot(fresh.astype(jnp.bfloat16), with_ones(new_kv[:, z.width :]))
        rows_ref[at, :] = done[:, : z.width] / done[:, z.width :]
        filled = filled | ((row == a + 1) & (requests[a] >= 0))
    for h in range(z.heads):
        at = slice(h * z.width, (h + 1) * z.width)
        column = rows_ref[pl.ds(h, tokens, stride=z.heads), :]
        old = old_ref[:, at].astype(jnp.float32)
        value = jnp.where(filled, column, old).astype(jnp.bfloat16)
        out_ref[:, at] = value
        last_ref[:, at] = value
    for write in writes:
        write.wait()


def settle(mig_dest, mig_len, got, tail_q, tail_kv, attention, sizes, deps, **fetch):
    z = sizes
    tokens = z.insts * z.steps
    last = attention.shape[0] // tokens - 1
    spec = pl.BlockSpec((tokens, attention.shape[1]), lambda i: (last, 0))
    cache = (z.slots, z.mig_blocks * z.block, 2 * z.width)
    return run(
        functools.partial(settle_kernel, sizes=z),
        [mig_dest, mig_len], [got, tail_q, tail_kv, attention],
        [HBM, VMEM, VMEM, spec],
        deps,
        [
            jax.ShapeDtypeStruct(attention.shape, jnp.bfloat16),
            jax.ShapeDtypeStruct((tokens, attention.shape[1]), jnp.bfloat16),
            jax.ShapeDtypeStruct((1, z.cap) + cache, jnp.bfloat16),
        ],
        [spec, VMEM, ANY], "settle", z, grid=(1,),
        scratch=[
            pltpu.VMEM((z.insts * z.per, z.width), jnp.float32),
            pltpu.VMEM((z.cap,) + got.shape[1:], jnp.bfloat16),
            pltpu.VMEM((z.cap,) + cache, jnp.bfloat16),
            pltpu.SemaphoreType.DMA((2, z.cap)),
        ],
        aliases={5: 0}, **fetch,
    )


def project_kernel(
    ready, launch, attention, *refs, first, tokens, count, streamed, added, joined, kept, sizes
):
    launch()
    weights = list(refs[:count])
    position = count
    extra = refs[position : position + added]
    position += added
    source = refs[position]
    position += bool(streamed)
    outs = 1 if joined else count + len(streamed)
    out_refs = refs[position : position + outs]
    copies = [None] * count
    if streamed:
        if kept:
            buffers = refs[position + outs : position + outs + len(streamed)]
        else:
            buffers = [refs[-2].at[n] for n in range(len(streamed))]
        for n, piece in enumerate(streamed):
            first = pl.multiple_of(piece_columns(piece, sizes), LANES)
            copy = pltpu.make_async_copy(
                source.at[:, pl.ds(first, sizes.quarter)], buffers[n], refs[-1].at[n]
            )
            copy.start()
            copies.append(copy)
            weights.append(buffers[n])
    width = sizes.quarter
    tile = min(width, 256)
    for n, (weight, copy) in enumerate(zip(weights, copies)):
        if copy is not None:
            copy.wait()

        def one(j, carry, n=n, weight=weight):
            at = pl.ds(pl.multiple_of(j * tile, tile), tile)
            to = pl.ds(pl.multiple_of(n * width + j * tile, tile), tile)
            result = dot(attention[first : first + tokens, :], weight[:, at])
            if added == 1:
                result = result + extra[0][:, to].astype(jnp.float32)
            elif added:
                result = result + extra[n][:, at].astype(jnp.float32)
            if joined:
                out_refs[0][:, to] = result.astype(jnp.bfloat16)
            else:
                out_refs[n][:, at] = result.astype(jnp.bfloat16)
            return carry

        lax.fori_loop(0, width // tile, one, 0)


def project(attention, weights, streamed, out_weight, mates, joined, kept, sizes, name, deps,
            pieces=()):
    attention, first, tokens = attention
    count = len(weights) + len(streamed)
    if joined:
        shapes = [jax.ShapeDtypeStruct((tokens, count * sizes.quarter), jnp.bfloat16)]
    else:
        shapes = [jax.ShapeDtypeStruct((tokens, sizes.quarter), jnp.bfloat16)] * count
    results = len(shapes)
    operands = [attention] + weights + mates
    specs = [VMEM] * len(operands)
    scratch = []
    piece = (sizes.depth, sizes.quarter)
    if streamed:
        operands = operands + [out_weight]
        specs = specs + [HBM]
        if kept:
            shapes = shapes + [jax.ShapeDtypeStruct(piece, jnp.bfloat16)] * len(streamed)
        else:
            scratch.append(pltpu.VMEM((len(streamed),) + piece, jnp.bfloat16))
        scratch.append(pltpu.SemaphoreType.DMA((len(streamed),)))
    result, new = run(
        functools.partial(
            project_kernel, first=first, tokens=tokens, count=len(weights), streamed=streamed,
            added=len(mates), joined=joined, kept=kept, sizes=sizes,
        ),
        [], operands, specs, deps, shapes, [VMEM] * len(shapes), name, sizes,
        limit=FETCHING if streamed or pieces else 16, scratch=scratch,
        pieces=pieces, weight=out_weight,
    )
    return result[:results], result[results:], new


def final_kernel(ready, launch, attention, *refs, count, streamed, mates, fars, sizes):
    z = sizes
    refs = list(refs)

    def take(n):
        taken = refs[:n]
        del refs[:n]
        return taken

    weights, extra = take(count), take(mates)
    low, second, high, late = take(fars), take(fars), take(fars), take(fars)
    source = take(bool(streamed))
    (out_hbm,) = take(1)
    block_ref, block_sems = take(2)
    copies = [None] * count
    for n, piece in enumerate(streamed):
        first = pl.multiple_of(piece_columns(piece, z), LANES)
        copy = pltpu.make_async_copy(
            source[0].at[:, pl.ds(first, z.quarter)], refs[0].at[n], refs[1].at[n]
        )
        copy.start()
        copies.append(copy)
        weights.append(refs[0].at[n])
    tile = min(z.quarter, 256)
    writes = []
    for n, (weight, copy) in enumerate(zip(weights, copies)):
        if copy is not None:
            copy.wait()

        def one(j, carry, n=n, weight=weight):
            start = pl.multiple_of(j * tile, tile)
            at = pl.ds(start, tile)
            whole = pl.ds(n * z.quarter + start, tile)
            half = pl.ds((n % 2) * z.quarter + start, tile)
            sums = dot(attention[...], weight[:, at]) + extra[n][:, at].astype(jnp.float32)
            for k in range(fars):
                if n < 2:
                    parts = [low[k][:, half], second[k][:, half]]
                else:
                    parts = [high[k][:, half]]
                rows = late[k].shape[0]
                parts = parts[:-1] + [parts[-1][:-rows], late[k][:, whole]]
                sums = sums + jnp.concatenate(parts, axis=0).astype(jnp.float32)
            block_ref[n, at, :] = sums.T.astype(jnp.bfloat16)
            return carry

        lax.fori_loop(0, z.quarter // tile, one, 0)
        write = pltpu.make_async_copy(
            block_ref.at[n], out_hbm.at[pl.ds(n * z.quarter, z.quarter)], block_sems.at[n]
        )
        write.start()
        writes.append(write)
    for write in writes:
        write.wait()


def final(attention, weights, streamed, out_weight, mates, low, second, high, late, sizes, deps):
    z = sizes
    tokens = attention.shape[0]
    operands = [attention] + weights + mates + low + second + high + late
    specs = [VMEM] * len(operands)
    scratch = [
        pltpu.VMEM((4, z.quarter, tokens), jnp.bfloat16), pltpu.SemaphoreType.DMA((4,))
    ]
    if streamed:
        operands = operands + [out_weight]
        specs = specs + [HBM]
        scratch += [
            pltpu.VMEM((len(streamed), z.depth, z.quarter), jnp.bfloat16),
            pltpu.SemaphoreType.DMA((len(streamed),)),
        ]
    result, _ = run(
        functools.partial(
            final_kernel, count=len(weights), streamed=streamed, mates=len(mates),
            fars=len(low), sizes=z,
        ),
        [], operands, specs, deps,
        [jax.ShapeDtypeStruct((z.features, tokens), jnp.bfloat16)], [ANY], "final", z,
        limit=FETCHING if streamed else 24, scratch=scratch,
    )
    return result[0]


def fetch_kernel(ready, launch, out_ref):
    launch()
    out_ref[...] = jnp.zeros_like(out_ref)


def fetch_pieces(pieces, out_weight, sizes, deps):
    _, new = run(
        fetch_kernel, [], [], [], deps, [jax.ShapeDtypeStruct((8, LANES), jnp.float32)], [VMEM],
        "fetch", sizes, pieces=pieces, weight=out_weight,
    )
    return new


def shards(
    res_pool,
    res_table,
    res_len,
    out_pool,
    src_table,
    mig_len,
    mig_dest,
    queries,
    new_kv,
    out_weight,
):
    z = Sizes(queries, res_pool, res_table, src_table, mig_dest, out_weight)
    tps, chips = z.tps, z.chips
    table = res_table[0].T
    query_rows = queries.reshape(z.batch * z.per, z.width)

    to_mate = [(i, i + 1 - 2 * (i % CORES)) for i in range(tps)]
    far = range(1, chips)
    held = {}

    def mate_of(x):
        return lax.ppermute(x, "tp", to_mate)

    def across(x, ahead):
        shift = ahead * CORES
        return lax.ppermute(x, "tp", [(i, (i + shift) % tps) for i in range(tps)])

    def bringing(pieces):
        return dict(pieces=pieces, weight=out_weight)

    def gives(ks, parts):
        return [(k, False, part) for k in ks for part in parts]

    def keeps(ks, parts):
        return [(k, True, part) for k in ks for part in parts]

    def at_hand(pieces):
        here = [held[piece] for piece in pieces if piece in held]
        return here, [piece for piece in pieces if piece not in held]

    def hold(pieces, arrays):
        held.update(zip(pieces, arrays))

    def give(attention, ks, parts, name, deps, pieces=(), kept=True, joined=False):
        weights, streamed = at_hand(gives(ks, parts))
        results, mine, new = project(
            attention, weights, streamed, out_weight, [], joined, kept, z, name, deps, pieces
        )
        if kept:
            hold(streamed, mine)
        hold(pieces, new)
        return results[0], [mate_of(result) for result in results]

    def keep(attention, ks, parts, mates, name, deps, kept=True):
        results = []
        for n, k in enumerate(ks):
            weights, streamed = at_hand(keeps([k], parts))
            if len(mates) == 1:
                width = mates[0].shape[1] // len(ks)
                now = [mates[0][:, n * width : (n + 1) * width] if len(ks) > 1 else mates[0]]
            else:
                now = mates[n * len(parts) : (n + 1) * len(parts)]
            result, mine, _ = project(
                attention, weights, streamed, out_weight, now, True, kept, z, name, deps
            )
            if kept:
                hold(streamed, mine)
            deps = [result[0]]
            results.append(result[0])
        return results

    def sent(results):
        return [across(result, k) for k, result in zip(far, results)]

    half = z.batch // 2
    low, high, every = (0, 1), (2, 3), (0, 1, 2, 3)

    sends, tail_q, tail_kv = pack(src_table, mig_dest, out_pool, query_rows, new_kv, z)
    arriving = lax.all_to_all(sends, "inst", split_axis=0, concat_axis=0, tiled=True)

    tokens = half * z.steps
    pieces = gives(far, low) + keeps(far, low)
    rows, new = attend(
        table, res_len, query_rows, new_kv, res_pool, None, 0, half, z, [sends],
        limit=LARGE_FIRST, **bringing(pieces),
    )
    hold(pieces, new)
    given, mates = give((rows, 0, tokens), far, low, "give", [])
    kept = keep((rows, 0, tokens), far, low, mates, "keep", [given])
    got_low = sent(kept)
    pieces = gives(far, high) + keeps(far, high)
    rows, new = attend(
        table, res_len, query_rows, new_kv, res_pool, rows, half, half, z, kept[-1:],
        **bringing(pieces),
    )
    hold(pieces, new)
    given, mates_low = give((rows, tokens, tokens), far, low, "give", [])
    given, mates = give((rows, 0, 2 * tokens), far, high, "give", [given])
    kept = keep((rows, tokens, tokens), far, low, mates_low, "keep", [given] + got_low)
    got_second = sent(kept)
    kept = keep((rows, 0, 2 * tokens), far, high, mates, "keep", kept[-1:])
    got_high = sent(kept)
    early = gives([0], every)
    new = fetch_pieces(early, out_weight, z, kept[-1:])
    hold(early, new)
    (rows, last, arrived), _ = settle(
        mig_dest, mig_len, arriving, tail_q, tail_kv, rows, z, new[:1]
    )
    late = (last, 0, last.shape[0])
    given, mates = give(late, far, every, "give_last", [], joined=True)
    kept = keep(late, far, every, mates, "keep_last", [given])
    got_late = sent(kept)
    whole = (rows, 0, 2 * tokens)
    given, own_low = give(whole, [0], low, "give_own", kept[-1:] + got_second)
    given, own_high = give(whole, [0], high, "give_own", [given] + got_late)
    weights, streamed = at_hand(keeps([0], every))
    hidden = final(
        rows, weights, streamed, out_weight, own_low + own_high, got_low, got_second, got_high,
        got_late, z, [given],
    )
    return (arrived, hidden)


def solution(mesh):
    placed = (
        P(("groups", "inst"), "tp", None, None, None),
        P(("groups", "inst"), None, None),
        P(("groups", "inst"), None),
        P(("groups", "inst"), "tp", None, None, None),
        P(("groups", "inst"), None, None),
        P("groups"),
        P("groups"),
        P(("groups", "inst"), None, "tp", None),
        P(("groups", "inst"), None, "tp", None),
        P("tp", None),
    )
    return jax.shard_map(
        shards,
        mesh=mesh,
        in_specs=placed,
        out_specs=(P(("groups", "inst"), None, "tp", None, None), P("tp", ("groups", "inst"))),
        check_vma=False,
    )
```

```python
import functools
import math

import jax
import jax.numpy as jnp
from jax import lax
from jax.experimental import pallas as pl
from jax.experimental.pallas import tpu as pltpu
from jax.sharding import PartitionSpec as P

CORES = 2
LOW = -1e30
MIB = 1 << 20
LANES = 128
GROUP = 16
TOGETHER = 8
LARGE_FIRST = 12
FETCHING = 16


def dot_t(left, right):
    return lax.dot_general(
        left, right, (((1,), (1,)), ((), ())), preferred_element_type=jnp.float32
    )


def row_plan(dest_ref, inst, cap):
    requests = [jnp.int32(-1)] * cap
    seen = jnp.int32(0)
    for g in range(dest_ref.shape[0]):
        here = dest_ref[g] == inst
        requests = [jnp.where(here & (seen == a), g, requests[a]) for a in range(cap)]
        seen = seen + here.astype(jnp.int32)
    return requests


VMEM = pl.BlockSpec(memory_space=pltpu.VMEM)
ANY = pl.BlockSpec(memory_space=pl.ANY)
HBM = pl.BlockSpec(memory_space=pltpu.HBM)


class Sizes:
    def __init__(self, queries, res_pool, res_table, src_table, mig_dest, out_weight):
        self.batch, self.steps, self.heads, self.width = queries.shape
        self.slots = res_pool.shape[1]
        self.block = res_pool.shape[3]
        self.resident, self.blocks = res_table.shape[1:]
        self.mig_per, self.mig_blocks = src_table.shape[1:]
        self.requests = mig_dest.shape[0]
        self.insts = lax.axis_size("inst")
        self.tps = lax.axis_size("tp")
        self.chips = self.tps // CORES
        self.cap = self.insts - 1
        self.per = self.steps * self.heads
        self.per_kv = self.steps * self.slots
        self.depth = out_weight.shape[0]
        self.features = out_weight.shape[1] // self.tps
        self.quarter = self.features // 4
        self.tail_q = self.insts * self.per
        self.tail_kv = self.insts * self.per_kv


def piece_columns(piece, sizes):
    ahead, mine, part = piece
    tp = lax.axis_index("tp")
    core = lax.rem(tp, CORES)
    chip = lax.rem(tp // CORES + ahead, sizes.chips)
    owner = chip * CORES + (core if mine else 1 - core)
    return owner * sizes.features + part * sizes.quarter


def run(kernel, tables, operands, in_specs, deps, out_shapes, out_specs, name, sizes,
        pieces=(), weight=None, limit=16, grid=(), scratch=(), aliases=None):
    inputs, outputs, many = len(operands), len(out_shapes), len(tables)
    count = len(deps)
    fetches = len(pieces)
    extra_in = [weight] if fetches else []
    limit = max(limit, FETCHING) if fetches else limit

    def call(*refs):
        table_in, refs = refs[:many], refs[many:]
        own_in = refs[:inputs]
        position = inputs + len(extra_in) + count
        own_out = refs[position : position + outputs]
        fetched = refs[position + outputs : position + outputs + fetches]
        rest = list(refs[position + outputs + fetches :])
        copies, reads = [], []
        if fetches:
            source, sems = refs[inputs], rest.pop()
            for n, piece in enumerate(pieces):
                first = pl.multiple_of(piece_columns(piece, sizes), LANES)
                copies.append(
                    pltpu.make_async_copy(
                        source.at[:, pl.ds(first, sizes.quarter)], fetched[n], sems.at[n]
                    )
                )
        table_refs = []
        if many:
            sems = rest.pop()
            table_refs = rest[len(rest) - many :]
            rest = rest[: len(rest) - many]
            reads = [
                pltpu.make_async_copy(source, target, sems.at[n])
                for n, (source, target) in enumerate(zip(table_in, table_refs))
            ]

        def ready():
            for read in reads:
                read.wait()

        def launch():
            for copy in copies:
                copy.start()

        def each(step, action):
            if not grid:
                action()
            else:
                pl.when(pl.program_id(0) == step)(action)

        def begin():
            for read in reads:
                read.start()

        def end():
            for copy in copies:
                copy.wait()

        if reads:
            each(0, begin)
        kernel(ready, launch, *table_refs, *own_in, *own_out, *rest)
        if copies:
            each(grid[0] - 1 if grid else 0, end)

    result = pl.pallas_call(
        call,
        grid_spec=pltpu.PrefetchScalarGridSpec(
            num_scalar_prefetch=0,
            grid=grid,
            in_specs=[HBM] * many + list(in_specs) + [HBM] * len(extra_in) + [ANY] * count,
            out_specs=list(out_specs) + [ANY] * fetches,
            scratch_shapes=list(scratch)
            + [pltpu.SMEM(t.shape, t.dtype) for t in tables]
            + ([pltpu.SemaphoreType.DMA((many,))] if many else [])
            + ([pltpu.SemaphoreType.DMA((fetches,))] if fetches else []),
        ),
        out_shape=list(out_shapes)
        + [jax.ShapeDtypeStruct((sizes.depth, sizes.quarter), jnp.bfloat16)] * fetches,
        input_output_aliases=aliases or {},
        compiler_params=pltpu.CompilerParams(vmem_limit_bytes=limit * MIB),
        cost_estimate=pl.CostEstimate(flops=0, bytes_accessed=1024, transcendentals=0),
        name=name,
    )(*tables, *operands, *extra_in, *deps)
    return result[:outputs], result[outputs:]


def pack_kernel(
    ready, launch, table_ref, dest_ref, pool_ref, query_ref, kv_ref, send_ref, tail_q_ref,
    tail_kv_ref, *, sizes
):
    inst = lax.axis_index("inst")
    launch()
    tail_q_ref[...] = query_ref[...]
    tail_kv_ref[...] = kv_ref[...].reshape(sizes.tail_kv, 2 * sizes.width)
    ready()
    for m in range(sizes.mig_per):
        dest = dest_ref[inst * sizes.mig_per + m]

        def copy_block(b, carry, m=m, dest=dest):
            block = table_ref[0, m, b]
            for s in range(sizes.slots):
                send_ref[dest, s, b] = pool_ref[0, s, block]
            return carry

        lax.fori_loop(0, sizes.mig_blocks, copy_block, 0, unroll=8)


def pack(src_table, mig_dest, out_pool, query_rows, new_kv, sizes):
    z = sizes
    last_q = query_rows.shape[0] // z.tail_q - 1
    last_kv = z.batch // z.insts - 1
    result, _ = run(
        functools.partial(pack_kernel, sizes=z),
        [src_table, mig_dest], [out_pool, query_rows, new_kv],
        [
            VMEM,
            pl.BlockSpec((z.tail_q, z.width), lambda i: (last_q, 0)),
            pl.BlockSpec((z.insts,) + new_kv.shape[1:], lambda i: (last_kv, 0, 0, 0)),
        ],
        [],
        [
            pltpu.HBM((z.insts, z.slots, z.mig_blocks, z.block, 2 * z.width), out_pool.dtype),
            jax.ShapeDtypeStruct((z.tail_q, z.width), out_pool.dtype),
            jax.ShapeDtypeStruct((z.tail_kv, 2 * z.width), out_pool.dtype),
        ],
        [VMEM] * 3, "pack", z, limit=16, grid=(1,),
    )
    return result


def fresh_code(rows, keys, sizes):
    index = lax.broadcasted_iota(jnp.int32, (rows, keys), 0)
    key = lax.broadcasted_iota(jnp.int32, (rows, keys), 1)
    step = index // sizes.heads
    slot = lax.rem(index, sizes.heads) // (sizes.heads // sizes.slots)
    in_row = lax.rem(key, sizes.per_kv)
    seen = (in_row // sizes.slots <= step) & (lax.rem(in_row, sizes.slots) == slot)
    return jnp.where(seen, key // sizes.per_kv, -1)


def slot_index(extent, sizes):
    index = lax.broadcasted_iota(jnp.int32, (sizes.per, extent), 0)
    return lax.rem(index, sizes.heads) // (sizes.heads // sizes.slots)


def own_scores(scores, slot_of, slots):
    extent = scores.shape[1] // slots
    own = scores[:, :extent]
    for s in range(1, slots):
        own = jnp.where(slot_of == s, scores[:, s * extent : (s + 1) * extent], own)
    return own


def weigh(own, length, fresh, fresh_seen, scale):
    place = lax.broadcasted_iota(jnp.int32, own.shape, 1)
    own = jnp.where(place < length, own, LOW)
    fresh = jnp.where(fresh_seen, fresh, LOW)
    if own.shape == fresh.shape:
        largest = jnp.max(jnp.maximum(own, fresh), axis=1, keepdims=True)
    else:
        largest = jnp.maximum(
            jnp.max(own, axis=1, keepdims=True), jnp.max(fresh, axis=1, keepdims=True)
        )
    return jnp.exp2((own - largest) * scale), jnp.exp2((fresh - largest) * scale)


def spread(own, slot_of, slots):
    if slots == 1:
        return own.astype(jnp.bfloat16)
    parts = [jnp.where(slot_of == s, own, 0.0) for s in range(slots)]
    return jnp.concatenate(parts, axis=1).astype(jnp.bfloat16)


def gather_blocks(pool_ref, slots, ids):
    tiles = [pool_ref[0, s, block] for s in range(slots) for block in ids]
    return jnp.concatenate(tiles, axis=0)


def with_ones(values):
    return jnp.concatenate([values, jnp.ones_like(values)], axis=1)


def dot(left, right):
    return jnp.dot(left, right, preferred_element_type=jnp.float32)


def attend_kernel(
    ready, launch, table_ref, len_ref, query_hbm, kv_hbm, pool_ref, *refs, first_row,
    steps_in_all, sizes,
):
    z = sizes
    out_ref, query_all, kv_all, fresh_ref, pf_ref, blend_ref, done_ref, sems = refs
    width, per = z.width, z.per
    rows = GROUP
    step = pl.program_id(0)
    extent = z.blocks * z.block
    start = first_row + step * rows
    scale = math.log2(math.e) / math.sqrt(width)

    def copies(n):
        begin = first_row + n * rows
        return (
            pltpu.make_async_copy(
                query_hbm.at[pl.ds(pl.multiple_of(begin * per, rows * per), rows * per)],
                query_all.at[n], sems.at[0, n],
            ),
            pltpu.make_async_copy(kv_hbm.at[pl.ds(begin, rows)], kv_all.at[n], sems.at[1, n]),
        )

    @pl.when(step == 0)
    def _():
        for n in range(steps_in_all):
            for copy in copies(n):
                copy.start()
        launch()
        ready()

    for copy in copies(step):
        copy.wait()

    query_ref = query_all.at[step]
    new_kv = kv_all[step].reshape(rows * z.per_kv, 2 * width)
    fresh_ref[...] = dot_t(query_ref[...], new_kv[:, :width])
    code = fresh_code(per, rows * z.per_kv, z)
    slot_of = slot_index(extent, z)
    together = min(TOGETHER, rows)
    for begin in range(0, rows, together):
        group = range(begin, begin + together)
        at = [slice(r * per, (r + 1) * per) for r in group]
        known = [jnp.minimum(start + r, z.resident - 1) for r in group]
        length = [
            jnp.where(start + r < z.resident, len_ref[0, k], 0) for r, k in zip(group, known)
        ]
        both = [
            gather_blocks(pool_ref, z.slots, [table_ref[j, k] for j in range(z.blocks)])
            for k in known
        ]
        fresh = [fresh_ref[a, :] for a in at]
        scores = [dot_t(query_ref[a, :], b[:, :width]) for a, b in zip(at, both)]
        weights = [
            weigh(own_scores(s, slot_of, z.slots), n, f, code == r, scale)
            for s, n, f, r in zip(scores, length, fresh, group)
        ]
        context = [
            dot(spread(w[0], slot_of, z.slots), with_ones(b[:, width:]))
            for w, b in zip(weights, both)
        ]
        for a, c, w in zip(at, context, weights):
            blend_ref[a, :] = c
            pf_ref[a, :] = w[1].astype(jnp.bfloat16)

    done = blend_ref[...] + dot(pf_ref[...], with_ones(new_kv[:, width:]))
    done_ref[...] = done[:, :width] / done[:, width:]
    for h in range(z.heads):
        column = done_ref[pl.ds(h, rows * z.steps, stride=z.heads), :]
        out_ref[:, h * width : (h + 1) * width] = column.astype(jnp.bfloat16)


def attend(table, lengths, queries, new_kv, pool, into, first_row, rows, sizes, deps, limit=12,
           **fetch):
    z = sizes
    groups = rows // GROUP
    first = first_row // GROUP
    tokens = z.batch * z.steps
    aliases = {}
    if into is not None:
        deps = [into] + deps
        aliases = {5 + (1 if fetch else 0): 0}
    result, pieces = run(
        functools.partial(
            attend_kernel, first_row=first_row, steps_in_all=groups, sizes=z
        ),
        [table, lengths],
        [queries, new_kv, pool],
        [HBM, HBM, VMEM],
        deps,
        [jax.ShapeDtypeStruct((tokens, z.heads * z.width), jnp.bfloat16)],
        [pl.BlockSpec((GROUP * z.steps, z.heads * z.width), lambda i: (first + i, 0))],
        "attend", z, limit=limit,
        grid=(groups,),
        scratch=[
            pltpu.VMEM((groups, GROUP * z.per, z.width), jnp.bfloat16),
            pltpu.VMEM((groups, GROUP) + new_kv.shape[1:], jnp.bfloat16),
            pltpu.VMEM((GROUP * z.per, GROUP * z.per_kv), jnp.float32),
            pltpu.VMEM((GROUP * z.per, GROUP * z.per_kv), jnp.bfloat16),
            pltpu.VMEM((GROUP * z.per, 2 * z.width), jnp.float32),
            pltpu.VMEM((GROUP * z.per, z.width), jnp.float32),
            pltpu.SemaphoreType.DMA((2, groups)),
        ],
        aliases=aliases, **fetch,
    )
    return result[0], pieces


def settle_kernel(
    ready, launch, dest_ref, len_ref, got_hbm, query_ref, kv_ref, old_ref, last_ref, arrived_hbm,
    rows_ref, got_ref, keep_ref, sems, *, sizes
):
    z = sizes
    launch()
    ready()
    inst = lax.axis_index("inst")
    requests = row_plan(dest_ref, inst, z.cap)
    known = [jnp.maximum(request, 0) for request in requests]
    extent = z.mig_blocks * z.block
    reads = [
        pltpu.make_async_copy(got_hbm.at[known[a] // z.mig_per], got_ref.at[a], sems.at[0, a])
        for a in range(z.cap)
    ]
    writes = [
        pltpu.make_async_copy(keep_ref.at[a], arrived_hbm.at[0, a], sems.at[1, a])
        for a in range(z.cap)
    ]
    for read in reads:
        read.start()
    new_kv = kv_ref[...]
    code = fresh_code(z.per, z.tail_kv, z)
    slot_of = slot_index(extent, z)
    scale = math.log2(math.e) / math.sqrt(z.width)
    tokens = z.insts * z.steps
    row = lax.broadcasted_iota(jnp.int32, (tokens, z.width), 0) // z.steps
    place = lax.broadcasted_iota(jnp.int32, (z.block, 2 * z.width), 0)
    filled = row < 0
    rows_ref[: z.per, :] = jnp.zeros((z.per, z.width), jnp.float32)
    for a in range(z.cap):
        length = jnp.where(requests[a] >= 0, len_ref[known[a]], 0)
        reads[a].wait()

        def one(b, carry, a=a, length=length):
            inside = place + b * z.block < length
            at = pl.ds(pl.multiple_of(b * z.block, z.block), z.block)
            for s in range(z.slots):
                value = got_ref[a, s, b].astype(jnp.float32)
                keep_ref[a, s, at, :] = jnp.where(inside, value, 0.0).astype(jnp.bfloat16)
            return carry

        lax.fori_loop(0, z.mig_blocks, one, 0, unroll=8)
        writes[a].start()
        at = slice((a + 1) * z.per, (a + 2) * z.per)
        both = jnp.concatenate([keep_ref[a, s] for s in range(z.slots)], axis=0)
        own = own_scores(dot_t(query_ref[at, :], both[:, : z.width]), slot_of, z.slots)
        fresh = dot_t(query_ref[at, :], new_kv[:, : z.width])
        own, fresh = weigh(own, length, fresh, code == a + 1, scale)
        done = dot(spread(own, slot_of, z.slots), with_ones(both[:, z.width :]))
        done = done + dot(fresh.astype(jnp.bfloat16), with_ones(new_kv[:, z.width :]))
        rows_ref[at, :] = done[:, : z.width] / done[:, z.width :]
        filled = filled | ((row == a + 1) & (requests[a] >= 0))
    for h in range(z.heads):
        at = slice(h * z.width, (h + 1) * z.width)
        column = rows_ref[pl.ds(h, tokens, stride=z.heads), :]
        old = old_ref[:, at].astype(jnp.float32)
        last_ref[:, at] = jnp.where(filled, column, old).astype(jnp.bfloat16)
    for write in writes:
        write.wait()


def settle(mig_dest, mig_len, got, tail_q, tail_kv, attention, sizes, deps, **fetch):
    z = sizes
    tokens = z.insts * z.steps
    last = attention.shape[0] // tokens - 1
    spec = pl.BlockSpec((tokens, attention.shape[1]), lambda i: (last, 0))
    cache = (z.slots, z.mig_blocks * z.block, 2 * z.width)
    return run(
        functools.partial(settle_kernel, sizes=z),
        [mig_dest, mig_len], [got, tail_q, tail_kv, attention],
        [HBM, VMEM, VMEM, spec],
        deps,
        [
            jax.ShapeDtypeStruct((tokens, attention.shape[1]), jnp.bfloat16),
            jax.ShapeDtypeStruct((1, z.cap) + cache, jnp.bfloat16),
        ],
        [VMEM, ANY], "settle", z, grid=(1,),
        scratch=[
            pltpu.VMEM((z.insts * z.per, z.width), jnp.float32),
            pltpu.VMEM((z.cap,) + got.shape[1:], jnp.bfloat16),
            pltpu.VMEM((z.cap,) + cache, jnp.bfloat16),
            pltpu.SemaphoreType.DMA((2, z.cap)),
        ],
        **fetch,
    )


def project_kernel(ready, launch, attention, *refs, first, tokens, count, added, joined, sizes):
    launch()
    weights, extra, out_refs = refs[:count], refs[count : count + added], refs[count + added :]
    width = sizes.quarter
    tile = min(width, 256)
    for n, weight in enumerate(weights):

        def one(j, carry, n=n, weight=weight):
            at = pl.ds(pl.multiple_of(j * tile, tile), tile)
            to = pl.ds(pl.multiple_of(n * width + j * tile, tile), tile)
            result = dot(attention[first : first + tokens, :], weight[:, at])
            if added == 1:
                result = result + extra[0][:, to].astype(jnp.float32)
            elif added:
                result = result + extra[n][:, at].astype(jnp.float32)
            if joined:
                out_refs[0][:, to] = result.astype(out_refs[0].dtype)
            else:
                out_refs[n][:, at] = result.astype(out_refs[n].dtype)
            return carry

        lax.fori_loop(0, width // tile, one, 0)


def project(attention, weights, mates, joined, dtype, sizes, name, deps, **fetch):
    attention, first, tokens = attention
    count = len(weights)
    if joined:
        shapes = [jax.ShapeDtypeStruct((tokens, count * sizes.quarter), dtype)]
    else:
        shapes = [jax.ShapeDtypeStruct((tokens, sizes.quarter), dtype)] * count
    operands = [attention] + weights + mates
    return run(
        functools.partial(
            project_kernel, first=first, tokens=tokens, count=count, added=len(mates),
            joined=joined, sizes=sizes,
        ),
        [], operands, [VMEM] * len(operands), deps, shapes, [VMEM] * len(shapes), name, sizes,
        **fetch,
    )


def finish_kernel(ready, launch, own, own_late, *refs, fars, sizes):
    z = sizes
    refs = list(refs)

    def take(n):
        taken = refs[:n]
        del refs[:n]
        return taken

    low, high, second, late = take(fars), take(fars), take(fars), take(fars)
    out_hbm, block_ref, sems = refs
    rows = own_late.shape[0]
    tile = min(z.quarter, 256)
    writes = []
    for n in range(4):

        def one(j, carry, n=n):
            start = pl.multiple_of(j * tile, tile)
            at = pl.ds(n * z.quarter + start, tile)
            half = pl.ds((n % 2) * z.quarter + start, tile)
            begin = low[0].shape[0]
            first = own[:begin, at]
            rest = own[begin:-rows, at]
            last = own_late[:, at]
            for k in range(fars):
                first = first + (low if n < 2 else high)[k][:, half].astype(jnp.float32)
                rest = rest + second[k][:-rows, at].astype(jnp.float32)
                last = last + late[k][:, at].astype(jnp.float32)
            sums = jnp.concatenate([first, rest, last], axis=0)
            block_ref[n, pl.ds(start, tile), :] = sums.T.astype(jnp.bfloat16)
            return carry

        lax.fori_loop(0, z.quarter // tile, one, 0)
        write = pltpu.make_async_copy(
            block_ref.at[n], out_hbm.at[pl.ds(n * z.quarter, z.quarter)], sems.at[n]
        )
        write.start()
        writes.append(write)
    for write in writes:
        write.wait()


def finish(own, own_late, low, high, second, late, sizes, deps):
    z = sizes
    tokens = own.shape[0]
    operands = [own, own_late] + low + high + second + late
    result, _ = run(
        functools.partial(finish_kernel, fars=len(low), sizes=z),
        [], operands, [VMEM] * len(operands), deps,
        [jax.ShapeDtypeStruct((z.features, tokens), jnp.bfloat16)], [ANY], "finish", z,
        scratch=[
            pltpu.VMEM((4, z.quarter, tokens), jnp.bfloat16), pltpu.SemaphoreType.DMA((4,))
        ],
    )
    return result[0]


def shards(
    res_pool,
    res_table,
    res_len,
    out_pool,
    src_table,
    mig_len,
    mig_dest,
    queries,
    new_kv,
    out_weight,
):
    z = Sizes(queries, res_pool, res_table, src_table, mig_dest, out_weight)
    tps, chips = z.tps, z.chips
    table = res_table[0].T
    out_weight, res_pool, out_pool, new_kv, query_rows, table, res_len, src_table, mig_dest, mig_len = (
        pltpu.with_memory_space_constraint(x, pltpu.HBM)
        for x in (
            out_weight, res_pool, out_pool, new_kv, queries.reshape(z.batch * z.per, z.width),
            table, res_len, src_table, mig_dest, mig_len,
        )
    )
    to_mate = [(i, i + 1 - 2 * (i % CORES)) for i in range(tps)]
    far = range(1, chips)
    held = {}

    def mate_of(x):
        return lax.ppermute(x, "tp", to_mate)

    def across(x, ahead):
        shift = ahead * CORES
        return lax.ppermute(x, "tp", [(i, (i + shift) % tps) for i in range(tps)])

    def bringing(pieces):
        return dict(pieces=pieces, weight=out_weight)

    def gives(ks, parts):
        return [(k, False, part) for k in ks for part in parts]

    def keeps(ks, parts):
        return [(k, True, part) for k in ks for part in parts]

    def hold(pieces, arrays):
        held.update(zip(pieces, arrays))

    def give(attention, ks, parts, name, deps, pieces=(), joined=False):
        weights = [held[piece] for piece in gives(ks, parts)]
        results, new = project(
            attention, weights, [], joined, jnp.bfloat16, z, name, deps, **bringing(pieces)
        )
        hold(pieces, new)
        return results[0], [mate_of(result) for result in results]

    def keep(attention, ks, parts, mates, name, deps, pieces=(), dtype=jnp.bfloat16):
        results = []
        for n, k in enumerate(ks):
            weights = [held[piece] for piece in keeps([k], parts)]
            if len(mates) == 1:
                width = mates[0].shape[1] // len(ks)
                now = [mates[0][:, n * width : (n + 1) * width] if len(ks) > 1 else mates[0]]
            else:
                now = mates[n * len(parts) : (n + 1) * len(parts)]
            bring = pieces if n == 0 else ()
            result, new = project(
                attention, weights, now, True, dtype, z, name, deps, **bringing(bring)
            )
            hold(bring, new)
            deps = [result[0]]
            results.append(result[0])
        return results

    def sent(results):
        return [across(result, k) for k, result in zip(far, results)]

    half = z.batch // 2
    low, high, every = (0, 1), (2, 3), (0, 1, 2, 3)

    sends, tail_q, tail_kv = pack(src_table, mig_dest, out_pool, query_rows, new_kv, z)
    arriving = lax.all_to_all(sends, "inst", split_axis=0, concat_axis=0, tiled=True)

    tokens = half * z.steps
    pieces = gives(far, low) + keeps(far, low)
    rows, new = attend(
        table, res_len, query_rows, new_kv, res_pool, None, 0, half, z, [sends],
        **bringing(pieces),
    )
    hold(pieces, new)
    a, b, whole = (rows, 0, tokens), None, None
    given, mates = give(a, far, low, "give", [], gives(far, (2,)))
    kept = keep(a, far, low, mates, "keep", [given], gives(far, (3,)))
    got_low = sent(kept)
    given, mates = give(a, far, high, "give", kept[-1:], keeps(far, high))
    kept = keep(a, far, high, mates, "keep", [given])
    got_high = sent(kept)
    rows, new = attend(
        table, res_len, query_rows, new_kv, res_pool, rows, half, half, z, kept[-1:],
        **bringing(gives([0], every)),
    )
    hold(gives([0], every), new)
    b, whole = (rows, tokens, tokens), (rows, 0, 2 * tokens)
    given, mates = give(b, far, every, "give", got_low, keeps([0], low))
    kept = keep(b, far, every, mates, "keep", [given] + got_high, keeps([0], high))
    got_second = sent(kept)

    given, mates = give(whole, [0], every, "give_own", kept[-1:])
    own = keep(whole, [0], every, mates, "keep_own", [given], dtype=jnp.float32)

    (last, arrived), _ = settle(
        mig_dest, mig_len, arriving, tail_q, tail_kv, rows, z, own
    )
    late = (last, 0, last.shape[0])
    given, mates = give(late, far, every, "give_last", [], joined=True)
    given, own_mates = give(late, [0], every, "give_last", [given], joined=True)
    kept = keep(late, far, every, mates, "keep_last", [given])
    got_late = sent(kept)
    own_late = keep(late, [0], every, own_mates, "keep_last", kept[-1:], dtype=jnp.float32)
    hidden = finish(own[0], own_late[0], got_low, got_high, got_second, got_late, z, [])
    return (arrived, hidden)


def solution(mesh):
    placed = (
        P(("groups", "inst"), "tp", None, None, None),
        P(("groups", "inst"), None, None),
        P(("groups", "inst"), None),
        P(("groups", "inst"), "tp", None, None, None),
        P(("groups", "inst"), None, None),
        P("groups"),
        P("groups"),
        P(("groups", "inst"), None, "tp", None),
        P(("groups", "inst"), None, "tp", None),
        P("tp", None),
    )
    return jax.shard_map(
        shards,
        mesh=mesh,
        in_specs=placed,
        out_specs=(P(("groups", "inst"), None, "tp", None, None), P("tp", ("groups", "inst"))),
        check_vma=False,
    )
```

```python
import functools
import math

import jax
import jax.numpy as jnp
from jax import lax
from jax.experimental import pallas as pl
from jax.experimental.pallas import tpu as pltpu
from jax.sharding import PartitionSpec as P

CORES = 2
LOW = -1e30
MIB = 1 << 20
LANES = 128
GROUP = 16
TOGETHER = 8
LARGE_FIRST = 12
FETCHING = 16


def dot_t(left, right):
    return lax.dot_general(
        left, right, (((1,), (1,)), ((), ())), preferred_element_type=jnp.float32
    )


def row_plan(dest_ref, inst, cap):
    requests = [jnp.int32(-1)] * cap
    seen = jnp.int32(0)
    for g in range(dest_ref.shape[0]):
        here = dest_ref[g] == inst
        requests = [jnp.where(here & (seen == a), g, requests[a]) for a in range(cap)]
        seen = seen + here.astype(jnp.int32)
    return requests


VMEM = pl.BlockSpec(memory_space=pltpu.VMEM)
ANY = pl.BlockSpec(memory_space=pl.ANY)
HBM = pl.BlockSpec(memory_space=pltpu.HBM)


class Sizes:
    def __init__(self, queries, res_pool, res_table, src_table, mig_dest, out_weight):
        self.batch, self.steps, self.heads, self.width = queries.shape
        self.slots = res_pool.shape[1]
        self.block = res_pool.shape[3]
        self.resident, self.blocks = res_table.shape[1:]
        self.mig_per, self.mig_blocks = src_table.shape[1:]
        self.requests = mig_dest.shape[0]
        self.insts = lax.axis_size("inst")
        self.tps = lax.axis_size("tp")
        self.chips = self.tps // CORES
        self.cap = self.insts - 1
        self.per = self.steps * self.heads
        self.per_kv = self.steps * self.slots
        self.depth = out_weight.shape[0]
        self.features = out_weight.shape[1] // self.tps
        self.quarter = self.features // 4
        self.tail_q = self.insts * self.per
        self.tail_kv = self.insts * self.per_kv


def piece_columns(piece, sizes):
    ahead, mine, part = piece
    tp = lax.axis_index("tp")
    core = lax.rem(tp, CORES)
    chip = lax.rem(tp // CORES + ahead, sizes.chips)
    owner = chip * CORES + (core if mine else 1 - core)
    return owner * sizes.features + part * sizes.quarter


def run(kernel, tables, operands, in_specs, deps, out_shapes, out_specs, name, sizes,
        pieces=(), weight=None, limit=16, grid=(), scratch=(), aliases=None):
    inputs, outputs, many = len(operands), len(out_shapes), len(tables)
    count = len(deps)
    fetches = len(pieces)
    extra_in = [weight] if fetches else []
    limit = max(limit, FETCHING) if fetches else limit

    def call(*refs):
        table_in, refs = refs[:many], refs[many:]
        own_in = refs[:inputs]
        position = inputs + len(extra_in) + count
        own_out = refs[position : position + outputs]
        fetched = refs[position + outputs : position + outputs + fetches]
        rest = list(refs[position + outputs + fetches :])
        copies, reads = [], []
        if fetches:
            source, sems = refs[inputs], rest.pop()
            for n, piece in enumerate(pieces):
                first = pl.multiple_of(piece_columns(piece, sizes), LANES)
                copies.append(
                    pltpu.make_async_copy(
                        source.at[:, pl.ds(first, sizes.quarter)], fetched[n], sems.at[n]
                    )
                )
        table_refs = []
        if many:
            sems = rest.pop()
            table_refs = rest[len(rest) - many :]
            rest = rest[: len(rest) - many]
            reads = [
                pltpu.make_async_copy(source, target, sems.at[n])
                for n, (source, target) in enumerate(zip(table_in, table_refs))
            ]

        def ready():
            for read in reads:
                read.wait()

        def launch():
            for copy in copies:
                copy.start()

        def each(step, action):
            if not grid:
                action()
            else:
                pl.when(pl.program_id(0) == step)(action)

        def begin():
            for read in reads:
                read.start()

        def end():
            for copy in copies:
                copy.wait()

        if reads:
            each(0, begin)
        kernel(ready, launch, *table_refs, *own_in, *own_out, *rest)
        if copies:
            each(grid[0] - 1 if grid else 0, end)

    result = pl.pallas_call(
        call,
        grid_spec=pltpu.PrefetchScalarGridSpec(
            num_scalar_prefetch=0,
            grid=grid,
            in_specs=[HBM] * many + list(in_specs) + [HBM] * len(extra_in) + [ANY] * count,
            out_specs=list(out_specs) + [ANY] * fetches,
            scratch_shapes=list(scratch)
            + [pltpu.SMEM(t.shape, t.dtype) for t in tables]
            + ([pltpu.SemaphoreType.DMA((many,))] if many else [])
            + ([pltpu.SemaphoreType.DMA((fetches,))] if fetches else []),
        ),
        out_shape=list(out_shapes)
        + [pltpu.VMEM((sizes.depth, sizes.quarter), jnp.bfloat16)] * fetches,
        input_output_aliases=aliases or {},
        compiler_params=pltpu.CompilerParams(vmem_limit_bytes=limit * MIB),
        cost_estimate=pl.CostEstimate(flops=0, bytes_accessed=1024, transcendentals=0),
        name=name,
    )(*tables, *operands, *extra_in, *deps)
    return result[:outputs], result[outputs:]


def pack_kernel(
    ready, launch, table_ref, dest_ref, pool_ref, query_ref, kv_ref, send_ref, tail_q_ref,
    tail_kv_ref, *, sizes
):
    inst = lax.axis_index("inst")
    launch()
    tail_q_ref[...] = query_ref[...]
    tail_kv_ref[...] = kv_ref[...].reshape(sizes.tail_kv, 2 * sizes.width)
    ready()
    for m in range(sizes.mig_per):
        dest = dest_ref[inst * sizes.mig_per + m]

        def copy_block(b, carry, m=m, dest=dest):
            block = table_ref[0, m, b]
            for s in range(sizes.slots):
                send_ref[dest, s, b] = pool_ref[0, s, block]
            return carry

        lax.fori_loop(0, sizes.mig_blocks, copy_block, 0, unroll=8)


def pack(src_table, mig_dest, out_pool, query_rows, new_kv, sizes):
    z = sizes
    last_q = query_rows.shape[0] // z.tail_q - 1
    last_kv = z.batch // z.insts - 1
    result, _ = run(
        functools.partial(pack_kernel, sizes=z),
        [src_table, mig_dest], [out_pool, query_rows, new_kv],
        [
            VMEM,
            pl.BlockSpec((z.tail_q, z.width), lambda i: (last_q, 0)),
            pl.BlockSpec((z.insts,) + new_kv.shape[1:], lambda i: (last_kv, 0, 0, 0)),
        ],
        [],
        [
            jax.ShapeDtypeStruct(
                (z.insts, z.slots, z.mig_blocks, z.block, 2 * z.width), out_pool.dtype
            ),
            jax.ShapeDtypeStruct((z.tail_q, z.width), out_pool.dtype),
            jax.ShapeDtypeStruct((z.tail_kv, 2 * z.width), out_pool.dtype),
        ],
        [VMEM] * 3, "pack", z, limit=60, grid=(1,),
    )
    return result


def fresh_code(rows, keys, sizes):
    index = lax.broadcasted_iota(jnp.int32, (rows, keys), 0)
    key = lax.broadcasted_iota(jnp.int32, (rows, keys), 1)
    step = index // sizes.heads
    slot = lax.rem(index, sizes.heads) // (sizes.heads // sizes.slots)
    in_row = lax.rem(key, sizes.per_kv)
    seen = (in_row // sizes.slots <= step) & (lax.rem(in_row, sizes.slots) == slot)
    return jnp.where(seen, key // sizes.per_kv, -1)


def slot_index(extent, sizes):
    index = lax.broadcasted_iota(jnp.int32, (sizes.per, extent), 0)
    return lax.rem(index, sizes.heads) // (sizes.heads // sizes.slots)


def own_scores(scores, slot_of, slots):
    extent = scores.shape[1] // slots
    own = scores[:, :extent]
    for s in range(1, slots):
        own = jnp.where(slot_of == s, scores[:, s * extent : (s + 1) * extent], own)
    return own


def weigh(own, length, fresh, fresh_seen, scale):
    place = lax.broadcasted_iota(jnp.int32, own.shape, 1)
    own = jnp.where(place < length, own, LOW)
    fresh = jnp.where(fresh_seen, fresh, LOW)
    if own.shape == fresh.shape:
        largest = jnp.max(jnp.maximum(own, fresh), axis=1, keepdims=True)
    else:
        largest = jnp.maximum(
            jnp.max(own, axis=1, keepdims=True), jnp.max(fresh, axis=1, keepdims=True)
        )
    return jnp.exp2((own - largest) * scale), jnp.exp2((fresh - largest) * scale)


def spread(own, slot_of, slots):
    if slots == 1:
        return own.astype(jnp.bfloat16)
    parts = [jnp.where(slot_of == s, own, 0.0) for s in range(slots)]
    return jnp.concatenate(parts, axis=1).astype(jnp.bfloat16)


def gather_blocks(pool_ref, slots, ids):
    tiles = [pool_ref[0, s, block] for s in range(slots) for block in ids]
    return jnp.concatenate(tiles, axis=0)


def with_ones(values):
    return jnp.concatenate([values, jnp.ones_like(values)], axis=1)


def dot(left, right):
    return jnp.dot(left, right, preferred_element_type=jnp.float32)


def attend_kernel(
    ready, launch, table_ref, len_ref, query_hbm, kv_hbm, pool_ref, *refs, first_row,
    steps_in_all, sizes,
):
    z = sizes
    out_ref, query_all, kv_all, fresh_ref, pf_ref, blend_ref, done_ref, sems = refs
    width, per = z.width, z.per
    rows = GROUP
    step = pl.program_id(0)
    extent = z.blocks * z.block
    start = first_row + step * rows
    scale = math.log2(math.e) / math.sqrt(width)

    def copies(n):
        begin = first_row + n * rows
        return (
            pltpu.make_async_copy(
                query_hbm.at[pl.ds(pl.multiple_of(begin * per, rows * per), rows * per)],
                query_all.at[n], sems.at[0, n],
            ),
            pltpu.make_async_copy(kv_hbm.at[pl.ds(begin, rows)], kv_all.at[n], sems.at[1, n]),
        )

    @pl.when(step == 0)
    def _():
        for n in range(steps_in_all):
            for copy in copies(n):
                copy.start()
        launch()
        ready()

    for copy in copies(step):
        copy.wait()

    query_ref = query_all.at[step]
    new_kv = kv_all[step].reshape(rows * z.per_kv, 2 * width)
    fresh_ref[...] = dot_t(query_ref[...], new_kv[:, :width])
    code = fresh_code(per, rows * z.per_kv, z)
    slot_of = slot_index(extent, z)
    together = min(TOGETHER, rows)
    for begin in range(0, rows, together):
        group = range(begin, begin + together)
        at = [slice(r * per, (r + 1) * per) for r in group]
        known = [jnp.minimum(start + r, z.resident - 1) for r in group]
        length = [
            jnp.where(start + r < z.resident, len_ref[0, k], 0) for r, k in zip(group, known)
        ]
        both = [
            gather_blocks(pool_ref, z.slots, [table_ref[j, k] for j in range(z.blocks)])
            for k in known
        ]
        fresh = [fresh_ref[a, :] for a in at]
        scores = [dot_t(query_ref[a, :], b[:, :width]) for a, b in zip(at, both)]
        weights = [
            weigh(own_scores(s, slot_of, z.slots), n, f, code == r, scale)
            for s, n, f, r in zip(scores, length, fresh, group)
        ]
        context = [
            dot(spread(w[0], slot_of, z.slots), with_ones(b[:, width:]))
            for w, b in zip(weights, both)
        ]
        for a, c, w in zip(at, context, weights):
            blend_ref[a, :] = c
            pf_ref[a, :] = w[1].astype(jnp.bfloat16)

    done = blend_ref[...] + dot(pf_ref[...], with_ones(new_kv[:, width:]))
    done_ref[...] = done[:, :width] / done[:, width:]
    for h in range(z.heads):
        column = done_ref[pl.ds(h, rows * z.steps, stride=z.heads), :]
        out_ref[:, h * width : (h + 1) * width] = column.astype(jnp.bfloat16)


def attend(table, lengths, queries, new_kv, pool, into, first_row, rows, sizes, deps, limit=12,
           **fetch):
    z = sizes
    groups = rows // GROUP
    first = first_row // GROUP
    tokens = z.batch * z.steps
    aliases = {}
    if into is not None:
        deps = [into] + deps
        aliases = {5 + (1 if fetch else 0): 0}
    result, pieces = run(
        functools.partial(
            attend_kernel, first_row=first_row, steps_in_all=groups, sizes=z
        ),
        [table, lengths],
        [queries, new_kv, pool],
        [HBM, HBM, VMEM],
        deps,
        [jax.ShapeDtypeStruct((tokens, z.heads * z.width), jnp.bfloat16)],
        [pl.BlockSpec((GROUP * z.steps, z.heads * z.width), lambda i: (first + i, 0))],
        "attend", z, limit=limit,
        grid=(groups,),
        scratch=[
            pltpu.VMEM((groups, GROUP * z.per, z.width), jnp.bfloat16),
            pltpu.VMEM((groups, GROUP) + new_kv.shape[1:], jnp.bfloat16),
            pltpu.VMEM((GROUP * z.per, GROUP * z.per_kv), jnp.float32),
            pltpu.VMEM((GROUP * z.per, GROUP * z.per_kv), jnp.bfloat16),
            pltpu.VMEM((GROUP * z.per, 2 * z.width), jnp.float32),
            pltpu.VMEM((GROUP * z.per, z.width), jnp.float32),
            pltpu.SemaphoreType.DMA((2, groups)),
        ],
        aliases=aliases, **fetch,
    )
    return result[0], pieces


def settle_kernel(
    ready, launch, dest_ref, len_ref, got_hbm, query_ref, kv_ref, old_ref, last_ref, arrived_hbm,
    rows_ref, got_ref, keep_ref, sems, *, sizes
):
    z = sizes
    launch()
    ready()
    inst = lax.axis_index("inst")
    requests = row_plan(dest_ref, inst, z.cap)
    known = [jnp.maximum(request, 0) for request in requests]
    extent = z.mig_blocks * z.block
    reads = [
        pltpu.make_async_copy(got_hbm.at[known[a] // z.mig_per], got_ref.at[a], sems.at[0, a])
        for a in range(z.cap)
    ]
    writes = [
        pltpu.make_async_copy(keep_ref.at[a], arrived_hbm.at[0, a], sems.at[1, a])
        for a in range(z.cap)
    ]
    for read in reads:
        read.start()
    new_kv = kv_ref[...]
    code = fresh_code(z.per, z.tail_kv, z)
    slot_of = slot_index(extent, z)
    scale = math.log2(math.e) / math.sqrt(z.width)
    tokens = z.insts * z.steps
    row = lax.broadcasted_iota(jnp.int32, (tokens, z.width), 0) // z.steps
    place = lax.broadcasted_iota(jnp.int32, (z.block, 2 * z.width), 0)
    filled = row < 0
    rows_ref[: z.per, :] = jnp.zeros((z.per, z.width), jnp.float32)
    for a in range(z.cap):
        length = jnp.where(requests[a] >= 0, len_ref[known[a]], 0)
        reads[a].wait()

        def one(b, carry, a=a, length=length):
            inside = place + b * z.block < length
            at = pl.ds(pl.multiple_of(b * z.block, z.block), z.block)
            for s in range(z.slots):
                value = got_ref[a, s, b].astype(jnp.float32)
                keep_ref[a, s, at, :] = jnp.where(inside, value, 0.0).astype(jnp.bfloat16)
            return carry

        lax.fori_loop(0, z.mig_blocks, one, 0, unroll=8)
        writes[a].start()
        at = slice((a + 1) * z.per, (a + 2) * z.per)
        both = jnp.concatenate([keep_ref[a, s] for s in range(z.slots)], axis=0)
        own = own_scores(dot_t(query_ref[at, :], both[:, : z.width]), slot_of, z.slots)
        fresh = dot_t(query_ref[at, :], new_kv[:, : z.width])
        own, fresh = weigh(own, length, fresh, code == a + 1, scale)
        done = dot(spread(own, slot_of, z.slots), with_ones(both[:, z.width :]))
        done = done + dot(fresh.astype(jnp.bfloat16), with_ones(new_kv[:, z.width :]))
        rows_ref[at, :] = done[:, : z.width] / done[:, z.width :]
        filled = filled | ((row == a + 1) & (requests[a] >= 0))
    for h in range(z.heads):
        at = slice(h * z.width, (h + 1) * z.width)
        column = rows_ref[pl.ds(h, tokens, stride=z.heads), :]
        old = old_ref[:, at].astype(jnp.float32)
        last_ref[:, at] = jnp.where(filled, column, old).astype(jnp.bfloat16)
    for write in writes:
        write.wait()


def settle(mig_dest, mig_len, got, tail_q, tail_kv, attention, sizes, deps, **fetch):
    z = sizes
    tokens = z.insts * z.steps
    last = attention.shape[0] // tokens - 1
    spec = pl.BlockSpec((tokens, attention.shape[1]), lambda i: (last, 0))
    cache = (z.slots, z.mig_blocks * z.block, 2 * z.width)
    return run(
        functools.partial(settle_kernel, sizes=z),
        [mig_dest, mig_len], [got, tail_q, tail_kv, attention],
        [HBM, VMEM, VMEM, spec],
        deps,
        [
            jax.ShapeDtypeStruct((tokens, attention.shape[1]), jnp.bfloat16),
            jax.ShapeDtypeStruct((1, z.cap) + cache, jnp.bfloat16),
        ],
        [VMEM, ANY], "settle", z, grid=(1,),
        scratch=[
            pltpu.VMEM((z.insts * z.per, z.width), jnp.float32),
            pltpu.VMEM((z.cap,) + got.shape[1:], jnp.bfloat16),
            pltpu.VMEM((z.cap,) + cache, jnp.bfloat16),
            pltpu.SemaphoreType.DMA((2, z.cap)),
        ],
        **fetch,
    )


def project_kernel(ready, launch, attention, *refs, first, tokens, count, added, joined, sizes):
    launch()
    weights, extra, out_refs = refs[:count], refs[count : count + added], refs[count + added :]
    width = sizes.quarter
    tile = min(width, 256)
    for n, weight in enumerate(weights):

        def one(j, carry, n=n, weight=weight):
            at = pl.ds(pl.multiple_of(j * tile, tile), tile)
            to = pl.ds(pl.multiple_of(n * width + j * tile, tile), tile)
            result = dot(attention[first : first + tokens, :], weight[:, at])
            if added == 1:
                result = result + extra[0][:, to].astype(jnp.float32)
            elif added:
                result = result + extra[n][:, at].astype(jnp.float32)
            if joined:
                out_refs[0][:, to] = result.astype(out_refs[0].dtype)
            else:
                out_refs[n][:, at] = result.astype(out_refs[n].dtype)
            return carry

        lax.fori_loop(0, width // tile, one, 0)


def project(attention, weights, mates, joined, dtype, sizes, name, deps, **fetch):
    attention, first, tokens = attention
    count = len(weights)
    if dtype == jnp.float32:
        shapes = [pltpu.VMEM((tokens, count * sizes.quarter), dtype)]
    elif joined:
        shapes = [jax.ShapeDtypeStruct((tokens, count * sizes.quarter), dtype)]
    else:
        shapes = [jax.ShapeDtypeStruct((tokens, sizes.quarter), dtype)] * count
    operands = [attention] + weights + mates
    return run(
        functools.partial(
            project_kernel, first=first, tokens=tokens, count=count, added=len(mates),
            joined=joined, sizes=sizes,
        ),
        [], operands, [VMEM] * len(operands), deps, shapes, [VMEM] * len(shapes), name, sizes,
        **fetch,
    )


def finish_kernel(ready, launch, own_low, own_high, own_late, *refs, fars, sizes):
    z = sizes
    refs = list(refs)

    def take(n):
        taken = refs[:n]
        del refs[:n]
        return taken

    low, high, second, late = take(fars), take(fars), take(fars), take(fars)
    out_hbm, block_ref, sems = refs
    rows = own_late.shape[0]
    tile = min(z.quarter, 256)
    writes = []
    for n in range(4):

        def one(j, carry, n=n):
            start = pl.multiple_of(j * tile, tile)
            at = pl.ds(n * z.quarter + start, tile)
            half = pl.ds((n % 2) * z.quarter + start, tile)
            begin = low[0].shape[0]
            own = own_low if n < 2 else own_high
            first = own[:begin, half]
            rest = own[begin:-rows, half]
            last = own_late[:, at]
            for k in range(fars):
                first = first + (low if n < 2 else high)[k][:, half].astype(jnp.float32)
                rest = rest + second[k][:-rows, at].astype(jnp.float32)
                last = last + late[k][:, at].astype(jnp.float32)
            sums = jnp.concatenate([first, rest, last], axis=0)
            block_ref[n, pl.ds(start, tile), :] = sums.T.astype(jnp.bfloat16)
            return carry

        lax.fori_loop(0, z.quarter // tile, one, 0)
        write = pltpu.make_async_copy(
            block_ref.at[n], out_hbm.at[pl.ds(n * z.quarter, z.quarter)], sems.at[n]
        )
        write.start()
        writes.append(write)
    for write in writes:
        write.wait()


def finish(own, own_late, low, high, second, late, sizes, deps):
    z = sizes
    tokens = own[0].shape[0]
    operands = own + [own_late] + low + high + second + late
    result, _ = run(
        functools.partial(finish_kernel, fars=len(low), sizes=z),
        [], operands, [VMEM] * len(operands), deps,
        [jax.ShapeDtypeStruct((z.features, tokens), jnp.bfloat16)], [ANY], "finish", z,
        scratch=[
            pltpu.VMEM((4, z.quarter, tokens), jnp.bfloat16), pltpu.SemaphoreType.DMA((4,))
        ],
    )
    return result[0]


def shards(
    res_pool,
    res_table,
    res_len,
    out_pool,
    src_table,
    mig_len,
    mig_dest,
    queries,
    new_kv,
    out_weight,
):
    z = Sizes(queries, res_pool, res_table, src_table, mig_dest, out_weight)
    tps, chips = z.tps, z.chips
    table = res_table[0].T
    out_weight, res_pool, out_pool, new_kv, query_rows, table, res_len, src_table, mig_dest, mig_len = (
        pltpu.with_memory_space_constraint(x, pltpu.HBM)
        for x in (
            out_weight, res_pool, out_pool, new_kv, queries.reshape(z.batch * z.per, z.width),
            table, res_len, src_table, mig_dest, mig_len,
        )
    )
    to_mate = [(i, i + 1 - 2 * (i % CORES)) for i in range(tps)]
    far = range(1, chips)
    held = {}

    def mate_of(x):
        return lax.ppermute(x, "tp", to_mate)

    def across(x, ahead):
        shift = ahead * CORES
        return lax.ppermute(x, "tp", [(i, (i + shift) % tps) for i in range(tps)])

    def bringing(pieces):
        return dict(pieces=pieces, weight=out_weight)

    def gives(ks, parts):
        return [(k, False, part) for k in ks for part in parts]

    def keeps(ks, parts):
        return [(k, True, part) for k in ks for part in parts]

    def hold(pieces, arrays):
        held.update(zip(pieces, arrays))

    def give(attention, ks, parts, name, deps, pieces=(), joined=False):
        weights = [held[piece] for piece in gives(ks, parts)]
        results, new = project(
            attention, weights, [], joined, jnp.bfloat16, z, name, deps, **bringing(pieces)
        )
        hold(pieces, new)
        return results[0], [mate_of(result) for result in results]

    def keep(attention, ks, parts, mates, name, deps, pieces=(), dtype=jnp.bfloat16):
        results = []
        for n, k in enumerate(ks):
            weights = [held[piece] for piece in keeps([k], parts)]
            if len(mates) == 1:
                width = mates[0].shape[1] // len(ks)
                now = [mates[0][:, n * width : (n + 1) * width] if len(ks) > 1 else mates[0]]
            else:
                now = mates[n * len(parts) : (n + 1) * len(parts)]
            bring = pieces if n == 0 else ()
            result, new = project(
                attention, weights, now, True, dtype, z, name, deps, **bringing(bring)
            )
            hold(bring, new)
            deps = [result[0]]
            results.append(result[0])
        return results

    def sent(results):
        return [across(result, k) for k, result in zip(far, results)]

    half = z.batch // 2
    low, high, every = (0, 1), (2, 3), (0, 1, 2, 3)

    sends, tail_q, tail_kv = pack(src_table, mig_dest, out_pool, query_rows, new_kv, z)
    arriving = lax.all_to_all(sends, "inst", split_axis=0, concat_axis=0, tiled=True)

    tokens = half * z.steps
    pieces = gives(far, low) + keeps(far, low)
    rows, new = attend(
        table, res_len, query_rows, new_kv, res_pool, None, 0, half, z, [sends],
        **bringing(pieces),
    )
    hold(pieces, new)
    a, b, whole = (rows, 0, tokens), None, None
    given, mates = give(a, far, low, "give", [], gives(far, (2,)))
    kept = keep(a, far, low, mates, "keep", [given], gives(far, (3,)))
    got_low = sent(kept)
    given, mates = give(a, far, high, "give", kept[-1:], keeps(far, high))
    kept = keep(a, far, high, mates, "keep", [given])
    got_high = sent(kept)
    rows, new = attend(
        table, res_len, query_rows, new_kv, res_pool, rows, half, half, z, kept[-1:],
        **bringing(gives([0], every)),
    )
    hold(gives([0], every), new)
    b, whole = (rows, tokens, tokens), (rows, 0, 2 * tokens)
    given, mates = give(b, far, every, "give", got_low, keeps([0], low))
    kept = keep(b, far, every, mates, "keep", [given], keeps([0], high))
    got_second = sent(kept)

    given, mates_low = give(whole, [0], low, "give_own", kept[-1:] + got_high)
    given, mates_high = give(whole, [0], high, "give_own", [given])
    own = keep(whole, [0], low, mates_low, "keep_own", [given], dtype=jnp.float32)
    own += keep(whole, [0], high, mates_high, "keep_own", own, dtype=jnp.float32)

    (last, arrived), _ = settle(
        mig_dest, mig_len, arriving, tail_q, tail_kv, rows, z, own[-1:]
    )
    late = (last, 0, last.shape[0])
    given, mates = give(late, far, every, "give_last", [], joined=True)
    given, own_mates = give(late, [0], every, "give_last", [given], joined=True)
    kept = keep(late, far, every, mates, "keep_last", [given])
    got_late = sent(kept)
    own_late = keep(late, [0], every, own_mates, "keep_last", kept[-1:], dtype=jnp.float32)
    hidden = finish(own, own_late[0], got_low, got_high, got_second, got_late, z, [])
    return (arrived, hidden)


def solution(mesh):
    placed = (
        P(("groups", "inst"), "tp", None, None, None),
        P(("groups", "inst"), None, None),
        P(("groups", "inst"), None),
        P(("groups", "inst"), "tp", None, None, None),
        P(("groups", "inst"), None, None),
        P("groups"),
        P("groups"),
        P(("groups", "inst"), None, "tp", None),
        P(("groups", "inst"), None, "tp", None),
        P("tp", None),
    )
    return jax.shard_map(
        shards,
        mesh=mesh,
        in_specs=placed,
        out_specs=(P(("groups", "inst"), None, "tp", None, None), P("tp", ("groups", "inst"))),
        check_vma=False,
    )
```

```python
import functools
import math

import jax
import jax.numpy as jnp
from jax import lax
from jax.experimental import pallas as pl
from jax.experimental.pallas import tpu as pltpu
from jax.sharding import PartitionSpec as P

CORES = 2
LOW = -1e30
MIB = 1 << 20
LANES = 128
GROUP = 16
TOGETHER = 8
LARGE_FIRST = 12
FETCHING = 16


def dot_t(left, right):
    return lax.dot_general(
        left, right, (((1,), (1,)), ((), ())), preferred_element_type=jnp.float32
    )


def row_plan(dest_ref, inst, cap):
    requests = [jnp.int32(-1)] * cap
    seen = jnp.int32(0)
    for g in range(dest_ref.shape[0]):
        here = dest_ref[g] == inst
        requests = [jnp.where(here & (seen == a), g, requests[a]) for a in range(cap)]
        seen = seen + here.astype(jnp.int32)
    return requests


VMEM = pl.BlockSpec(memory_space=pltpu.VMEM)
ANY = pl.BlockSpec(memory_space=pl.ANY)
HBM = pl.BlockSpec(memory_space=pltpu.HBM)


class Sizes:
    def __init__(self, queries, res_pool, res_table, src_table, mig_dest, out_weight):
        self.batch, self.steps, self.heads, self.width = queries.shape
        self.slots = res_pool.shape[1]
        self.block = res_pool.shape[3]
        self.resident, self.blocks = res_table.shape[1:]
        self.mig_per, self.mig_blocks = src_table.shape[1:]
        self.requests = mig_dest.shape[0]
        self.insts = lax.axis_size("inst")
        self.tps = lax.axis_size("tp")
        self.chips = self.tps // CORES
        self.cap = self.insts - 1
        self.per = self.steps * self.heads
        self.per_kv = self.steps * self.slots
        self.depth = out_weight.shape[0]
        self.features = out_weight.shape[1] // self.tps
        self.quarter = self.features // 4
        self.tail_q = self.insts * self.per
        self.tail_kv = self.insts * self.per_kv


def piece_columns(piece, sizes):
    ahead, mine, part = piece
    tp = lax.axis_index("tp")
    core = lax.rem(tp, CORES)
    chip = lax.rem(tp // CORES + ahead, sizes.chips)
    owner = chip * CORES + (core if mine else 1 - core)
    return owner * sizes.features + part * sizes.quarter


def run(kernel, tables, operands, in_specs, deps, out_shapes, out_specs, name, sizes,
        pieces=(), weight=None, limit=16, grid=(), scratch=(), aliases=None):
    inputs, outputs, many = len(operands), len(out_shapes), len(tables)
    count = len(deps)
    fetches = len(pieces)
    extra_in = [weight] if fetches else []
    limit = max(limit, FETCHING) if fetches else limit

    def call(*refs):
        table_in, refs = refs[:many], refs[many:]
        own_in = refs[:inputs]
        position = inputs + len(extra_in) + count
        own_out = refs[position : position + outputs]
        fetched = refs[position + outputs : position + outputs + fetches]
        rest = list(refs[position + outputs + fetches :])
        copies, reads = [], []
        if fetches:
            source, sems = refs[inputs], rest.pop()
            for n, piece in enumerate(pieces):
                first = pl.multiple_of(piece_columns(piece, sizes), LANES)
                copies.append(
                    pltpu.make_async_copy(
                        source.at[:, pl.ds(first, sizes.quarter)], fetched[n], sems.at[n]
                    )
                )
        table_refs = []
        if many:
            sems = rest.pop()
            table_refs = rest[len(rest) - many :]
            rest = rest[: len(rest) - many]
            reads = [
                pltpu.make_async_copy(source, target, sems.at[n])
                for n, (source, target) in enumerate(zip(table_in, table_refs))
            ]

        def ready():
            for read in reads:
                read.wait()

        def launch():
            for copy in copies:
                copy.start()

        def each(step, action):
            if not grid:
                action()
            else:
                pl.when(pl.program_id(0) == step)(action)

        def begin():
            for read in reads:
                read.start()

        def end():
            for copy in copies:
                copy.wait()

        if reads:
            each(0, begin)
        kernel(ready, launch, *table_refs, *own_in, *own_out, *rest)
        if copies:
            each(grid[0] - 1 if grid else 0, end)

    result = pl.pallas_call(
        call,
        grid_spec=pltpu.PrefetchScalarGridSpec(
            num_scalar_prefetch=0,
            grid=grid,
            in_specs=[HBM] * many + list(in_specs) + [HBM] * len(extra_in) + [ANY] * count,
            out_specs=list(out_specs) + [ANY] * fetches,
            scratch_shapes=list(scratch)
            + [pltpu.SMEM(t.shape, t.dtype) for t in tables]
            + ([pltpu.SemaphoreType.DMA((many,))] if many else [])
            + ([pltpu.SemaphoreType.DMA((fetches,))] if fetches else []),
        ),
        out_shape=list(out_shapes)
        + [pltpu.VMEM((sizes.depth, sizes.quarter), jnp.bfloat16)] * fetches,
        input_output_aliases=aliases or {},
        compiler_params=pltpu.CompilerParams(vmem_limit_bytes=limit * MIB),
        cost_estimate=pl.CostEstimate(flops=0, bytes_accessed=1024, transcendentals=0),
        name=name,
    )(*tables, *operands, *extra_in, *deps)
    return result[:outputs], result[outputs:]


def pack_kernel(
    ready, launch, table_ref, dest_ref, pool_ref, query_ref, kv_ref, send_ref, tail_q_ref,
    tail_kv_ref, *, sizes
):
    inst = lax.axis_index("inst")
    launch()
    tail_q_ref[...] = query_ref[...]
    tail_kv_ref[...] = kv_ref[...].reshape(sizes.tail_kv, 2 * sizes.width)
    ready()
    for m in range(sizes.mig_per):
        dest = dest_ref[inst * sizes.mig_per + m]

        def copy_block(b, carry, m=m, dest=dest):
            block = table_ref[0, m, b]
            for s in range(sizes.slots):
                send_ref[dest, s, b] = pool_ref[0, s, block]
            return carry

        lax.fori_loop(0, sizes.mig_blocks, copy_block, 0, unroll=8)


def pack(src_table, mig_dest, out_pool, query_rows, new_kv, sizes):
    z = sizes
    last_q = query_rows.shape[0] // z.tail_q - 1
    last_kv = z.batch // z.insts - 1
    result, _ = run(
        functools.partial(pack_kernel, sizes=z),
        [src_table, mig_dest], [out_pool, query_rows, new_kv],
        [
            VMEM,
            pl.BlockSpec((z.tail_q, z.width), lambda i: (last_q, 0)),
            pl.BlockSpec((z.insts,) + new_kv.shape[1:], lambda i: (last_kv, 0, 0, 0)),
        ],
        [],
        [
            jax.ShapeDtypeStruct(
                (z.insts, z.slots, z.mig_blocks, z.block, 2 * z.width), out_pool.dtype
            ),
            jax.ShapeDtypeStruct((z.tail_q, z.width), out_pool.dtype),
            jax.ShapeDtypeStruct((z.tail_kv, 2 * z.width), out_pool.dtype),
        ],
        [VMEM] * 3, "pack", z, limit=60, grid=(1,),
    )
    return result


def fresh_code(rows, keys, sizes):
    index = lax.broadcasted_iota(jnp.int32, (rows, keys), 0)
    key = lax.broadcasted_iota(jnp.int32, (rows, keys), 1)
    step = index // sizes.heads
    slot = lax.rem(index, sizes.heads) // (sizes.heads // sizes.slots)
    in_row = lax.rem(key, sizes.per_kv)
    seen = (in_row // sizes.slots <= step) & (lax.rem(in_row, sizes.slots) == slot)
    return jnp.where(seen, key // sizes.per_kv, -1)


def slot_index(extent, sizes):
    index = lax.broadcasted_iota(jnp.int32, (sizes.per, extent), 0)
    return lax.rem(index, sizes.heads) // (sizes.heads // sizes.slots)


def own_scores(scores, slot_of, slots):
    extent = scores.shape[1] // slots
    own = scores[:, :extent]
    for s in range(1, slots):
        own = jnp.where(slot_of == s, scores[:, s * extent : (s + 1) * extent], own)
    return own


def weigh(own, length, fresh, fresh_seen, scale):
    place = lax.broadcasted_iota(jnp.int32, own.shape, 1)
    own = jnp.where(place < length, own, LOW)
    fresh = jnp.where(fresh_seen, fresh, LOW)
    if own.shape == fresh.shape:
        largest = jnp.max(jnp.maximum(own, fresh), axis=1, keepdims=True)
    else:
        largest = jnp.maximum(
            jnp.max(own, axis=1, keepdims=True), jnp.max(fresh, axis=1, keepdims=True)
        )
    return jnp.exp2((own - largest) * scale), jnp.exp2((fresh - largest) * scale)


def spread(own, slot_of, slots):
    if slots == 1:
        return own.astype(jnp.bfloat16)
    parts = [jnp.where(slot_of == s, own, 0.0) for s in range(slots)]
    return jnp.concatenate(parts, axis=1).astype(jnp.bfloat16)


def gather_blocks(pool_ref, slots, ids):
    tiles = [pool_ref[0, s, block] for s in range(slots) for block in ids]
    return jnp.concatenate(tiles, axis=0)


def with_ones(values):
    return jnp.concatenate([values, jnp.ones_like(values)], axis=1)


def dot(left, right):
    return jnp.dot(left, right, preferred_element_type=jnp.float32)


def attend_kernel(
    ready, launch, table_ref, len_ref, query_hbm, kv_hbm, pool_ref, *refs, first_row,
    steps_in_all, sizes,
):
    z = sizes
    out_ref, query_all, kv_all, fresh_ref, pf_ref, blend_ref, done_ref, sems = refs
    width, per = z.width, z.per
    rows = GROUP
    step = pl.program_id(0)
    extent = z.blocks * z.block
    start = first_row + step * rows
    scale = math.log2(math.e) / math.sqrt(width)

    def copies(n):
        begin = first_row + n * rows
        return (
            pltpu.make_async_copy(
                query_hbm.at[pl.ds(pl.multiple_of(begin * per, rows * per), rows * per)],
                query_all.at[n], sems.at[0, n],
            ),
            pltpu.make_async_copy(kv_hbm.at[pl.ds(begin, rows)], kv_all.at[n], sems.at[1, n]),
        )

    @pl.when(step == 0)
    def _():
        for n in range(steps_in_all):
            for copy in copies(n):
                copy.start()
        launch()
        ready()

    for copy in copies(step):
        copy.wait()

    query_ref = query_all.at[step]
    new_kv = kv_all[step].reshape(rows * z.per_kv, 2 * width)
    fresh_ref[...] = dot_t(query_ref[...], new_kv[:, :width])
    code = fresh_code(per, rows * z.per_kv, z)
    slot_of = slot_index(extent, z)
    together = min(TOGETHER, rows)
    for begin in range(0, rows, together):
        group = range(begin, begin + together)
        at = [slice(r * per, (r + 1) * per) for r in group]
        known = [jnp.minimum(start + r, z.resident - 1) for r in group]
        length = [
            jnp.where(start + r < z.resident, len_ref[0, k], 0) for r, k in zip(group, known)
        ]
        both = [
            gather_blocks(pool_ref, z.slots, [table_ref[j, k] for j in range(z.blocks)])
            for k in known
        ]
        fresh = [fresh_ref[a, :] for a in at]
        scores = [dot_t(query_ref[a, :], b[:, :width]) for a, b in zip(at, both)]
        weights = [
            weigh(own_scores(s, slot_of, z.slots), n, f, code == r, scale)
            for s, n, f, r in zip(scores, length, fresh, group)
        ]
        context = [
            dot(spread(w[0], slot_of, z.slots), with_ones(b[:, width:]))
            for w, b in zip(weights, both)
        ]
        for a, c, w in zip(at, context, weights):
            blend_ref[a, :] = c
            pf_ref[a, :] = w[1].astype(jnp.bfloat16)

    done = blend_ref[...] + dot(pf_ref[...], with_ones(new_kv[:, width:]))
    done_ref[...] = done[:, :width] / done[:, width:]
    for h in range(z.heads):
        column = done_ref[pl.ds(h, rows * z.steps, stride=z.heads), :]
        out_ref[:, h * width : (h + 1) * width] = column.astype(jnp.bfloat16)


def attend(table, lengths, queries, new_kv, pool, into, first_row, rows, sizes, deps, limit=12,
           **fetch):
    z = sizes
    groups = rows // GROUP
    first = first_row // GROUP
    tokens = z.batch * z.steps
    aliases = {}
    if into is not None:
        deps = [into] + deps
        aliases = {5 + (1 if fetch else 0): 0}
    result, pieces = run(
        functools.partial(
            attend_kernel, first_row=first_row, steps_in_all=groups, sizes=z
        ),
        [table, lengths],
        [queries, new_kv, pool],
        [HBM, HBM, VMEM],
        deps,
        [jax.ShapeDtypeStruct((tokens, z.heads * z.width), jnp.bfloat16)],
        [pl.BlockSpec((GROUP * z.steps, z.heads * z.width), lambda i: (first + i, 0))],
        "attend", z, limit=limit,
        grid=(groups,),
        scratch=[
            pltpu.VMEM((groups, GROUP * z.per, z.width), jnp.bfloat16),
            pltpu.VMEM((groups, GROUP) + new_kv.shape[1:], jnp.bfloat16),
            pltpu.VMEM((GROUP * z.per, GROUP * z.per_kv), jnp.float32),
            pltpu.VMEM((GROUP * z.per, GROUP * z.per_kv), jnp.bfloat16),
            pltpu.VMEM((GROUP * z.per, 2 * z.width), jnp.float32),
            pltpu.VMEM((GROUP * z.per, z.width), jnp.float32),
            pltpu.SemaphoreType.DMA((2, groups)),
        ],
        aliases=aliases, **fetch,
    )
    return result[0], pieces


def settle_kernel(
    ready, launch, dest_ref, len_ref, got_hbm, query_ref, kv_ref, old_ref, last_ref, arrived_hbm,
    rows_ref, got_ref, keep_ref, sems, *, sizes
):
    z = sizes
    ready()
    inst = lax.axis_index("inst")
    requests = row_plan(dest_ref, inst, z.cap)
    known = [jnp.maximum(request, 0) for request in requests]
    extent = z.mig_blocks * z.block
    reads = [
        pltpu.make_async_copy(got_hbm.at[known[a] // z.mig_per], got_ref.at[a], sems.at[0, a])
        for a in range(z.cap)
    ]
    writes = [
        pltpu.make_async_copy(keep_ref.at[a], arrived_hbm.at[0, a], sems.at[1, a])
        for a in range(z.cap)
    ]
    for read in reads:
        read.start()
    launch()
    new_kv = kv_ref[...]
    code = fresh_code(z.per, z.tail_kv, z)
    slot_of = slot_index(extent, z)
    scale = math.log2(math.e) / math.sqrt(z.width)
    tokens = z.insts * z.steps
    row = lax.broadcasted_iota(jnp.int32, (tokens, z.width), 0) // z.steps
    place = lax.broadcasted_iota(jnp.int32, (z.block, 2 * z.width), 0)
    filled = row < 0
    rows_ref[: z.per, :] = jnp.zeros((z.per, z.width), jnp.float32)
    for a in range(z.cap):
        length = jnp.where(requests[a] >= 0, len_ref[known[a]], 0)
        reads[a].wait()

        def one(b, carry, a=a, length=length):
            inside = place + b * z.block < length
            at = pl.ds(pl.multiple_of(b * z.block, z.block), z.block)
            for s in range(z.slots):
                value = got_ref[a, s, b].astype(jnp.float32)
                keep_ref[a, s, at, :] = jnp.where(inside, value, 0.0).astype(jnp.bfloat16)
            return carry

        lax.fori_loop(0, z.mig_blocks, one, 0, unroll=8)
        writes[a].start()
        at = slice((a + 1) * z.per, (a + 2) * z.per)
        both = jnp.concatenate([keep_ref[a, s] for s in range(z.slots)], axis=0)
        own = own_scores(dot_t(query_ref[at, :], both[:, : z.width]), slot_of, z.slots)
        fresh = dot_t(query_ref[at, :], new_kv[:, : z.width])
        own, fresh = weigh(own, length, fresh, code == a + 1, scale)
        done = dot(spread(own, slot_of, z.slots), with_ones(both[:, z.width :]))
        done = done + dot(fresh.astype(jnp.bfloat16), with_ones(new_kv[:, z.width :]))
        rows_ref[at, :] = done[:, : z.width] / done[:, z.width :]
        filled = filled | ((row == a + 1) & (requests[a] >= 0))
    for h in range(z.heads):
        at = slice(h * z.width, (h + 1) * z.width)
        column = rows_ref[pl.ds(h, tokens, stride=z.heads), :]
        old = old_ref[:, at].astype(jnp.float32)
        last_ref[:, at] = jnp.where(filled, column, old).astype(jnp.bfloat16)
    for write in writes:
        write.wait()


def settle(mig_dest, mig_len, got, tail_q, tail_kv, attention, sizes, deps, **fetch):
    z = sizes
    tokens = z.insts * z.steps
    last = attention.shape[0] // tokens - 1
    spec = pl.BlockSpec((tokens, attention.shape[1]), lambda i: (last, 0))
    cache = (z.slots, z.mig_blocks * z.block, 2 * z.width)
    return run(
        functools.partial(settle_kernel, sizes=z),
        [mig_dest, mig_len], [got, tail_q, tail_kv, attention],
        [HBM, VMEM, VMEM, spec],
        deps,
        [
            jax.ShapeDtypeStruct((tokens, attention.shape[1]), jnp.bfloat16),
            jax.ShapeDtypeStruct((1, z.cap) + cache, jnp.bfloat16),
        ],
        [VMEM, ANY], "settle", z, grid=(1,),
        scratch=[
            pltpu.VMEM((z.insts * z.per, z.width), jnp.float32),
            pltpu.VMEM((z.cap,) + got.shape[1:], jnp.bfloat16),
            pltpu.VMEM((z.cap,) + cache, jnp.bfloat16),
            pltpu.SemaphoreType.DMA((2, z.cap)),
        ],
        **fetch,
    )


def project_kernel(ready, launch, attention, *refs, first, tokens, count, added, joined, sizes):
    launch()
    weights, extra, out_refs = refs[:count], refs[count : count + added], refs[count + added :]
    width = sizes.quarter
    tile = min(width, 256)
    for n, weight in enumerate(weights):

        def one(j, carry, n=n, weight=weight):
            at = pl.ds(pl.multiple_of(j * tile, tile), tile)
            to = pl.ds(pl.multiple_of(n * width + j * tile, tile), tile)
            result = dot(attention[first : first + tokens, :], weight[:, at])
            if added == 1:
                result = result + extra[0][:, to].astype(jnp.float32)
            elif added:
                result = result + extra[n][:, at].astype(jnp.float32)
            if joined:
                out_refs[0][:, to] = result.astype(out_refs[0].dtype)
            else:
                out_refs[n][:, at] = result.astype(out_refs[n].dtype)
            return carry

        lax.fori_loop(0, width // tile, one, 0)


def project(attention, weights, mates, joined, dtype, sizes, name, deps, place=None, **fetch):
    attention, first, tokens = attention
    count = len(weights)
    if place is not None:
        shapes = [place((tokens, count * sizes.quarter), dtype)]
    elif joined:
        shapes = [jax.ShapeDtypeStruct((tokens, count * sizes.quarter), dtype)]
    else:
        shapes = [jax.ShapeDtypeStruct((tokens, sizes.quarter), dtype)] * count
    operands = [attention] + weights + mates
    return run(
        functools.partial(
            project_kernel, first=first, tokens=tokens, count=count, added=len(mates),
            joined=joined, sizes=sizes,
        ),
        [], operands, [VMEM] * len(operands), deps, shapes, [VMEM] * len(shapes), name, sizes,
        **fetch,
    )


def finish_kernel(ready, launch, own_low, own_high, own_late, *refs, fars, sizes):
    z = sizes
    refs = list(refs)

    def take(n):
        taken = refs[:n]
        del refs[:n]
        return taken

    low, high, second, late = take(fars), take(fars), take(fars), take(fars)
    out_hbm, block_ref, sems = refs
    rows = own_late.shape[0]
    tile = min(z.quarter, 256)
    writes = []
    for n in range(4):

        def one(j, carry, n=n):
            start = pl.multiple_of(j * tile, tile)
            at = pl.ds(n * z.quarter + start, tile)
            half = pl.ds((n % 2) * z.quarter + start, tile)
            begin = low[0].shape[0]
            own = own_low if n < 2 else own_high
            first = own[:begin, half].astype(jnp.float32)
            rest = own[begin:-rows, half].astype(jnp.float32)
            last = own_late[:, at]
            for k in range(fars):
                first = first + (low if n < 2 else high)[k][:, half].astype(jnp.float32)
                rest = rest + second[k][:-rows, at].astype(jnp.float32)
                last = last + late[k][:, at].astype(jnp.float32)
            sums = jnp.concatenate([first, rest, last], axis=0)
            block_ref[n, pl.ds(start, tile), :] = sums.T.astype(jnp.bfloat16)
            return carry

        lax.fori_loop(0, z.quarter // tile, one, 0)
        write = pltpu.make_async_copy(
            block_ref.at[n], out_hbm.at[pl.ds(n * z.quarter, z.quarter)], sems.at[n]
        )
        write.start()
        writes.append(write)
    for write in writes:
        write.wait()


def finish(own, own_late, low, high, second, late, sizes, deps):
    z = sizes
    tokens = own[0].shape[0]
    operands = own + [own_late] + low + high + second + late
    result, _ = run(
        functools.partial(finish_kernel, fars=len(low), sizes=z),
        [], operands, [VMEM] * len(operands), deps,
        [jax.ShapeDtypeStruct((z.features, tokens), jnp.bfloat16)], [ANY], "finish", z,
        scratch=[
            pltpu.VMEM((4, z.quarter, tokens), jnp.bfloat16), pltpu.SemaphoreType.DMA((4,))
        ],
    )
    return result[0]


def shards(
    res_pool,
    res_table,
    res_len,
    out_pool,
    src_table,
    mig_len,
    mig_dest,
    queries,
    new_kv,
    out_weight,
):
    z = Sizes(queries, res_pool, res_table, src_table, mig_dest, out_weight)
    tps, chips = z.tps, z.chips
    table = res_table[0].T
    out_weight, res_pool, out_pool, new_kv, query_rows, table, res_len, src_table, mig_dest, mig_len = (
        pltpu.with_memory_space_constraint(x, pltpu.HBM)
        for x in (
            out_weight, res_pool, out_pool, new_kv, queries.reshape(z.batch * z.per, z.width),
            table, res_len, src_table, mig_dest, mig_len,
        )
    )
    to_mate = [(i, i + 1 - 2 * (i % CORES)) for i in range(tps)]
    far = range(1, chips)
    held = {}

    def mate_of(x):
        return lax.ppermute(x, "tp", to_mate)

    def across(x, ahead):
        shift = ahead * CORES
        return lax.ppermute(x, "tp", [(i, (i + shift) % tps) for i in range(tps)])

    def bringing(pieces):
        return dict(pieces=pieces, weight=out_weight)

    def gives(ks, parts):
        return [(k, False, part) for k in ks for part in parts]

    def keeps(ks, parts):
        return [(k, True, part) for k in ks for part in parts]

    def in_hbm(arrays):
        return [pltpu.with_memory_space_constraint(x, pltpu.HBM) for x in arrays]

    def hold(pieces, arrays):
        held.update(zip(pieces, arrays))

    def give(attention, ks, parts, name, deps, pieces=(), joined=False):
        weights = [held[piece] for piece in gives(ks, parts)]
        results, new = project(
            attention, weights, [], joined, jnp.bfloat16, z, name, deps, **bringing(pieces)
        )
        hold(pieces, new)
        return results[0], [mate_of(result) for result in results]

    def keep(attention, ks, parts, mates, name, deps, pieces=(), dtype=jnp.bfloat16, place=None):
        results = []
        for n, k in enumerate(ks):
            weights = [held[piece] for piece in keeps([k], parts)]
            if len(mates) == 1:
                width = mates[0].shape[1] // len(ks)
                now = [mates[0][:, n * width : (n + 1) * width] if len(ks) > 1 else mates[0]]
            else:
                now = mates[n * len(parts) : (n + 1) * len(parts)]
            bring = pieces if n == 0 else ()
            result, new = project(
                attention, weights, now, True, dtype, z, name, deps, place, **bringing(bring)
            )
            hold(bring, new)
            deps = [result[0]]
            results.append(result[0])
        return results

    def sent(results):
        return [across(result, k) for k, result in zip(far, results)]

    half = z.batch // 2
    low, high, every = (0, 1), (2, 3), (0, 1, 2, 3)

    sends, tail_q, tail_kv = pack(src_table, mig_dest, out_pool, query_rows, new_kv, z)
    arriving = lax.all_to_all(sends, "inst", split_axis=0, concat_axis=0, tiled=True)

    tokens = half * z.steps
    pieces = gives(far, low) + keeps(far, low)
    rows, new = attend(
        table, res_len, query_rows, new_kv, res_pool, None, 0, half, z, [sends],
        **bringing(pieces),
    )
    hold(pieces, new)
    a, b, whole = (rows, 0, tokens), None, None
    given, mates = give(a, far, low, "give", [], gives(far, (2,)))
    kept = keep(a, far, low, mates, "keep", [given], gives(far, (3,)))
    got_low = sent(kept)
    given, mates = give(a, far, high, "give", kept[-1:], keeps(far, high))
    kept = keep(a, far, high, mates, "keep", [given])
    got_high = sent(kept)
    rows, new = attend(
        table, res_len, query_rows, new_kv, res_pool, rows, half, half, z, kept[-1:],
        **bringing(gives([0], every)),
    )
    hold(gives([0], every), new)
    b, whole = (rows, tokens, tokens), (rows, 0, 2 * tokens)
    given, mates = give(b, far, every, "give", got_low, keeps([0], low))
    kept = keep(b, far, every, mates, "keep", [given] + got_high, keeps([0], high))
    got_second = sent(kept)

    given, mates_low = give(whole, [0], low, "give_own", kept[-1:])
    given, mates_high = give(whole, [0], high, "give_own", [given])
    own = keep(whole, [0], low, mates_low, "keep_own", [given], place=pltpu.HBM)
    own += keep(whole, [0], high, mates_high, "keep_own", in_hbm(own), place=pltpu.HBM)

    pieces = gives(far, every) + gives([0], every)
    (last, arrived), new = settle(
        mig_dest, mig_len, arriving, tail_q, tail_kv, rows, z, in_hbm(own[-1:]), **bringing(pieces)
    )
    hold(pieces, new)
    late = (last, 0, last.shape[0])
    given, mates = give(late, far, every, "give_last", [], keeps(far, every), joined=True)
    given, own_mates = give(late, [0], every, "give_last", [given], joined=True)
    kept = keep(late, far, every, mates, "keep_last", [given], keeps([0], every))
    got_late = sent(kept)
    own_late = keep(late, [0], every, own_mates, "keep_last", kept[-1:], dtype=jnp.float32)
    hidden = finish(own, own_late[0], got_low, got_high, got_second, got_late, z, [])
    return (arrived, hidden)


def solution(mesh):
    placed = (
        P(("groups", "inst"), "tp", None, None, None),
        P(("groups", "inst"), None, None),
        P(("groups", "inst"), None),
        P(("groups", "inst"), "tp", None, None, None),
        P(("groups", "inst"), None, None),
        P("groups"),
        P("groups"),
        P(("groups", "inst"), None, "tp", None),
        P(("groups", "inst"), None, "tp", None),
        P("tp", None),
    )
    return jax.shard_map(
        shards,
        mesh=mesh,
        in_specs=placed,
        out_specs=(P(("groups", "inst"), None, "tp", None, None), P("tp", ("groups", "inst"))),
        check_vma=False,
    )
```

```python
import functools
import math

import jax
import jax.numpy as jnp
from jax import lax
from jax.experimental import pallas as pl
from jax.experimental.pallas import tpu as pltpu
from jax.sharding import PartitionSpec as P

CORES = 2
LOW = -1e30
MIB = 1 << 20
LANES = 128
GROUP = 16
TOGETHER = 8
LARGE_FIRST = 12
FETCHING = 16


def dot_t(left, right):
    return lax.dot_general(
        left, right, (((1,), (1,)), ((), ())), preferred_element_type=jnp.float32
    )


def row_plan(dest_ref, inst, cap):
    requests = [jnp.int32(-1)] * cap
    seen = jnp.int32(0)
    for g in range(dest_ref.shape[0]):
        here = dest_ref[g] == inst
        requests = [jnp.where(here & (seen == a), g, requests[a]) for a in range(cap)]
        seen = seen + here.astype(jnp.int32)
    return requests


VMEM = pl.BlockSpec(memory_space=pltpu.VMEM)
ANY = pl.BlockSpec(memory_space=pl.ANY)
HBM = pl.BlockSpec(memory_space=pltpu.HBM)


class Sizes:
    def __init__(self, queries, res_pool, res_table, src_table, mig_dest, out_weight):
        self.batch, self.steps, self.heads, self.width = queries.shape
        self.slots = res_pool.shape[1]
        self.block = res_pool.shape[3]
        self.resident, self.blocks = res_table.shape[1:]
        self.mig_per, self.mig_blocks = src_table.shape[1:]
        self.requests = mig_dest.shape[0]
        self.insts = lax.axis_size("inst")
        self.tps = lax.axis_size("tp")
        self.chips = self.tps // CORES
        self.cap = self.insts - 1
        self.per = self.steps * self.heads
        self.per_kv = self.steps * self.slots
        self.depth = out_weight.shape[0]
        self.features = out_weight.shape[1] // self.tps
        self.quarter = self.features // 4
        self.tail_q = self.insts * self.per
        self.tail_kv = self.insts * self.per_kv


def piece_columns(piece, sizes):
    ahead, mine, part = piece
    tp = lax.axis_index("tp")
    core = lax.rem(tp, CORES)
    chip = lax.rem(tp // CORES + ahead, sizes.chips)
    owner = chip * CORES + (core if mine else 1 - core)
    return owner * sizes.features + part * sizes.quarter


def run(kernel, tables, operands, in_specs, deps, out_shapes, out_specs, name, sizes,
        pieces=(), weight=None, limit=16, grid=(), scratch=(), aliases=None):
    inputs, outputs, many = len(operands), len(out_shapes), len(tables)
    count = len(deps)
    fetches = len(pieces)
    extra_in = [weight] if fetches else []
    limit = max(limit, FETCHING) if fetches else limit

    def call(*refs):
        table_in, refs = refs[:many], refs[many:]
        own_in = refs[:inputs]
        position = inputs + len(extra_in) + count
        own_out = refs[position : position + outputs]
        fetched = refs[position + outputs : position + outputs + fetches]
        rest = list(refs[position + outputs + fetches :])
        copies, reads = [], []
        if fetches:
            source, sems = refs[inputs], rest.pop()
            for n, piece in enumerate(pieces):
                first = pl.multiple_of(piece_columns(piece, sizes), LANES)
                copies.append(
                    pltpu.make_async_copy(
                        source.at[:, pl.ds(first, sizes.quarter)], fetched[n], sems.at[n]
                    )
                )
        table_refs = []
        if many:
            sems = rest.pop()
            table_refs = rest[len(rest) - many :]
            rest = rest[: len(rest) - many]
            reads = [
                pltpu.make_async_copy(source, target, sems.at[n])
                for n, (source, target) in enumerate(zip(table_in, table_refs))
            ]

        def ready():
            for read in reads:
                read.wait()

        def launch():
            for copy in copies:
                copy.start()

        def each(step, action):
            if not grid:
                action()
            else:
                pl.when(pl.program_id(0) == step)(action)

        def begin():
            for read in reads:
                read.start()

        def end():
            for copy in copies:
                copy.wait()

        if reads:
            each(0, begin)
        kernel(ready, launch, *table_refs, *own_in, *own_out, *rest)
        if copies:
            each(grid[0] - 1 if grid else 0, end)

    result = pl.pallas_call(
        call,
        grid_spec=pltpu.PrefetchScalarGridSpec(
            num_scalar_prefetch=0,
            grid=grid,
            in_specs=[HBM] * many + list(in_specs) + [HBM] * len(extra_in) + [ANY] * count,
            out_specs=list(out_specs) + [ANY] * fetches,
            scratch_shapes=list(scratch)
            + [pltpu.SMEM(t.shape, t.dtype) for t in tables]
            + ([pltpu.SemaphoreType.DMA((many,))] if many else [])
            + ([pltpu.SemaphoreType.DMA((fetches,))] if fetches else []),
        ),
        out_shape=list(out_shapes)
        + [pltpu.VMEM((sizes.depth, sizes.quarter), jnp.bfloat16)] * fetches,
        input_output_aliases=aliases or {},
        compiler_params=pltpu.CompilerParams(vmem_limit_bytes=limit * MIB),
        cost_estimate=pl.CostEstimate(flops=0, bytes_accessed=1024, transcendentals=0),
        name=name,
    )(*tables, *operands, *extra_in, *deps)
    return result[:outputs], result[outputs:]


def pack_kernel(
    ready, launch, table_ref, dest_ref, pool_hbm, query_ref, kv_ref, send_hbm, tail_q_ref,
    tail_kv_ref, sems, *, sizes
):
    inst = lax.axis_index("inst")
    ready()
    dests = [dest_ref[inst * sizes.mig_per + m] for m in range(sizes.mig_per)]
    for m, dest in enumerate(dests):

        def copy_block(b, carry, m=m, dest=dest):
            block = table_ref[0, m, b]
            for s in range(sizes.slots):
                pltpu.make_async_copy(
                    pool_hbm.at[0, s, block], send_hbm.at[dest, s, b], sems.at[m]
                ).start()
            return carry

        lax.fori_loop(0, sizes.mig_blocks, copy_block, 0, unroll=8)
    tail_q_ref[...] = query_ref[...]
    tail_kv_ref[...] = kv_ref[...].reshape(sizes.tail_kv, 2 * sizes.width)
    for m, dest in enumerate(dests):
        pltpu.make_async_copy(send_hbm.at[dest], send_hbm.at[dest], sems.at[m]).wait()


def pack(src_table, mig_dest, out_pool, query_rows, new_kv, sizes):
    z = sizes
    last_q = query_rows.shape[0] // z.tail_q - 1
    last_kv = z.batch // z.insts - 1
    result, _ = run(
        functools.partial(pack_kernel, sizes=z),
        [src_table, mig_dest], [out_pool, query_rows, new_kv],
        [
            HBM,
            pl.BlockSpec((z.tail_q, z.width), lambda i: (last_q, 0)),
            pl.BlockSpec((z.insts,) + new_kv.shape[1:], lambda i: (last_kv, 0, 0, 0)),
        ],
        [],
        [
            pltpu.HBM((z.insts, z.slots, z.mig_blocks, z.block, 2 * z.width), out_pool.dtype),
            jax.ShapeDtypeStruct((z.tail_q, z.width), out_pool.dtype),
            jax.ShapeDtypeStruct((z.tail_kv, 2 * z.width), out_pool.dtype),
        ],
        [ANY, VMEM, VMEM], "pack", z, limit=60, grid=(1,),
        scratch=[pltpu.SemaphoreType.DMA((z.mig_per,))],
    )
    return result


def fresh_code(rows, keys, sizes):
    index = lax.broadcasted_iota(jnp.int32, (rows, keys), 0)
    key = lax.broadcasted_iota(jnp.int32, (rows, keys), 1)
    step = index // sizes.heads
    slot = lax.rem(index, sizes.heads) // (sizes.heads // sizes.slots)
    in_row = lax.rem(key, sizes.per_kv)
    seen = (in_row // sizes.slots <= step) & (lax.rem(in_row, sizes.slots) == slot)
    return jnp.where(seen, key // sizes.per_kv, -1)


def slot_index(extent, sizes):
    index = lax.broadcasted_iota(jnp.int32, (sizes.per, extent), 0)
    return lax.rem(index, sizes.heads) // (sizes.heads // sizes.slots)


def own_scores(scores, slot_of, slots):
    extent = scores.shape[1] // slots
    own = scores[:, :extent]
    for s in range(1, slots):
        own = jnp.where(slot_of == s, scores[:, s * extent : (s + 1) * extent], own)
    return own


def weigh(own, length, fresh, fresh_seen, scale):
    place = lax.broadcasted_iota(jnp.int32, own.shape, 1)
    own = jnp.where(place < length, own, LOW)
    fresh = jnp.where(fresh_seen, fresh, LOW)
    if own.shape == fresh.shape:
        largest = jnp.max(jnp.maximum(own, fresh), axis=1, keepdims=True)
    else:
        largest = jnp.maximum(
            jnp.max(own, axis=1, keepdims=True), jnp.max(fresh, axis=1, keepdims=True)
        )
    return jnp.exp2((own - largest) * scale), jnp.exp2((fresh - largest) * scale)


def spread(own, slot_of, slots):
    if slots == 1:
        return own.astype(jnp.bfloat16)
    parts = [jnp.where(slot_of == s, own, 0.0) for s in range(slots)]
    return jnp.concatenate(parts, axis=1).astype(jnp.bfloat16)


def gather_blocks(pool_ref, slots, ids):
    tiles = [pool_ref[0, s, block] for s in range(slots) for block in ids]
    return jnp.concatenate(tiles, axis=0)


def with_ones(values):
    return jnp.concatenate([values, jnp.ones_like(values)], axis=1)


def dot(left, right):
    return jnp.dot(left, right, preferred_element_type=jnp.float32)


def attend_kernel(
    ready, launch, table_ref, len_ref, query_hbm, kv_hbm, pool_ref, *refs, first_row,
    steps_in_all, sizes,
):
    z = sizes
    out_ref, query_all, kv_all, fresh_ref, pf_ref, blend_ref, done_ref, sems = refs
    width, per = z.width, z.per
    rows = GROUP
    step = pl.program_id(0)
    extent = z.blocks * z.block
    start = first_row + step * rows
    scale = math.log2(math.e) / math.sqrt(width)

    def copies(n):
        begin = first_row + n * rows
        return (
            pltpu.make_async_copy(
                query_hbm.at[pl.ds(pl.multiple_of(begin * per, rows * per), rows * per)],
                query_all.at[n], sems.at[0, n],
            ),
            pltpu.make_async_copy(kv_hbm.at[pl.ds(begin, rows)], kv_all.at[n], sems.at[1, n]),
        )

    @pl.when(step == 0)
    def _():
        for n in range(steps_in_all):
            for copy in copies(n):
                copy.start()
        launch()
        ready()

    for copy in copies(step):
        copy.wait()

    query_ref = query_all.at[step]
    new_kv = kv_all[step].reshape(rows * z.per_kv, 2 * width)
    fresh_ref[...] = dot_t(query_ref[...], new_kv[:, :width])
    code = fresh_code(per, rows * z.per_kv, z)
    slot_of = slot_index(extent, z)
    together = min(TOGETHER, rows)
    for begin in range(0, rows, together):
        group = range(begin, begin + together)
        at = [slice(r * per, (r + 1) * per) for r in group]
        known = [jnp.minimum(start + r, z.resident - 1) for r in group]
        length = [
            jnp.where(start + r < z.resident, len_ref[0, k], 0) for r, k in zip(group, known)
        ]
        both = [
            gather_blocks(pool_ref, z.slots, [table_ref[j, k] for j in range(z.blocks)])
            for k in known
        ]
        fresh = [fresh_ref[a, :] for a in at]
        scores = [dot_t(query_ref[a, :], b[:, :width]) for a, b in zip(at, both)]
        weights = [
            weigh(own_scores(s, slot_of, z.slots), n, f, code == r, scale)
            for s, n, f, r in zip(scores, length, fresh, group)
        ]
        context = [
            dot(spread(w[0], slot_of, z.slots), with_ones(b[:, width:]))
            for w, b in zip(weights, both)
        ]
        for a, c, w in zip(at, context, weights):
            blend_ref[a, :] = c
            pf_ref[a, :] = w[1].astype(jnp.bfloat16)

    done = blend_ref[...] + dot(pf_ref[...], with_ones(new_kv[:, width:]))
    done_ref[...] = done[:, :width] / done[:, width:]
    for h in range(z.heads):
        column = done_ref[pl.ds(h, rows * z.steps, stride=z.heads), :]
        out_ref[:, h * width : (h + 1) * width] = column.astype(jnp.bfloat16)


def attend(table, lengths, queries, new_kv, pool, into, first_row, rows, sizes, deps, limit=12,
           **fetch):
    z = sizes
    groups = rows // GROUP
    first = first_row // GROUP
    tokens = z.batch * z.steps
    aliases = {}
    if into is not None:
        deps = [into] + deps
        aliases = {5 + (1 if fetch else 0): 0}
    result, pieces = run(
        functools.partial(
            attend_kernel, first_row=first_row, steps_in_all=groups, sizes=z
        ),
        [table, lengths],
        [queries, new_kv, pool],
        [HBM, HBM, VMEM],
        deps,
        [jax.ShapeDtypeStruct((tokens, z.heads * z.width), jnp.bfloat16)],
        [pl.BlockSpec((GROUP * z.steps, z.heads * z.width), lambda i: (first + i, 0))],
        "attend", z, limit=limit,
        grid=(groups,),
        scratch=[
            pltpu.VMEM((groups, GROUP * z.per, z.width), jnp.bfloat16),
            pltpu.VMEM((groups, GROUP) + new_kv.shape[1:], jnp.bfloat16),
            pltpu.VMEM((GROUP * z.per, GROUP * z.per_kv), jnp.float32),
            pltpu.VMEM((GROUP * z.per, GROUP * z.per_kv), jnp.bfloat16),
            pltpu.VMEM((GROUP * z.per, 2 * z.width), jnp.float32),
            pltpu.VMEM((GROUP * z.per, z.width), jnp.float32),
            pltpu.SemaphoreType.DMA((2, groups)),
        ],
        aliases=aliases, **fetch,
    )
    return result[0], pieces


def settle_kernel(
    ready, launch, dest_ref, len_ref, got_hbm, query_ref, kv_ref, old_ref, out_ref, last_ref,
    arrived_hbm, rows_ref, got_ref, keep_ref, sems, *, sizes
):
    z = sizes
    ready()
    inst = lax.axis_index("inst")
    requests = row_plan(dest_ref, inst, z.cap)
    known = [jnp.maximum(request, 0) for request in requests]
    extent = z.mig_blocks * z.block
    reads = [
        pltpu.make_async_copy(got_hbm.at[known[a] // z.mig_per], got_ref.at[a], sems.at[0, a])
        for a in range(z.cap)
    ]
    writes = [
        pltpu.make_async_copy(keep_ref.at[a], arrived_hbm.at[0, a], sems.at[1, a])
        for a in range(z.cap)
    ]
    for read in reads:
        read.start()
    launch()
    new_kv = kv_ref[...]
    code = fresh_code(z.per, z.tail_kv, z)
    slot_of = slot_index(extent, z)
    scale = math.log2(math.e) / math.sqrt(z.width)
    tokens = z.insts * z.steps
    row = lax.broadcasted_iota(jnp.int32, (tokens, z.width), 0) // z.steps
    place = lax.broadcasted_iota(jnp.int32, (z.block, 2 * z.width), 0)
    filled = row < 0
    rows_ref[: z.per, :] = jnp.zeros((z.per, z.width), jnp.float32)
    for a in range(z.cap):
        length = jnp.where(requests[a] >= 0, len_ref[known[a]], 0)
        reads[a].wait()

        def one(b, carry, a=a, length=length):
            inside = place + b * z.block < length
            at = pl.ds(pl.multiple_of(b * z.block, z.block), z.block)
            for s in range(z.slots):
                value = got_ref[a, s, b].astype(jnp.float32)
                keep_ref[a, s, at, :] = jnp.where(inside, value, 0.0).astype(jnp.bfloat16)
            return carry

        lax.fori_loop(0, z.mig_blocks, one, 0, unroll=8)
        writes[a].start()
        at = slice((a + 1) * z.per, (a + 2) * z.per)
        both = jnp.concatenate([keep_ref[a, s] for s in range(z.slots)], axis=0)
        own = own_scores(dot_t(query_ref[at, :], both[:, : z.width]), slot_of, z.slots)
        fresh = dot_t(query_ref[at, :], new_kv[:, : z.width])
        own, fresh = weigh(own, length, fresh, code == a + 1, scale)
        done = dot(spread(own, slot_of, z.slots), with_ones(both[:, z.width :]))
        done = done + dot(fresh.astype(jnp.bfloat16), with_ones(new_kv[:, z.width :]))
        rows_ref[at, :] = done[:, : z.width] / done[:, z.width :]
        filled = filled | ((row == a + 1) & (requests[a] >= 0))
    for h in range(z.heads):
        at = slice(h * z.width, (h + 1) * z.width)
        column = rows_ref[pl.ds(h, tokens, stride=z.heads), :]
        old = old_ref[:, at].astype(jnp.float32)
        value = jnp.where(filled, column, old).astype(jnp.bfloat16)
        out_ref[:, at] = value
        last_ref[:, at] = value
    for write in writes:
        write.wait()


def settle(mig_dest, mig_len, got, tail_q, tail_kv, attention, sizes, deps, **fetch):
    z = sizes
    tokens = z.insts * z.steps
    last = attention.shape[0] // tokens - 1
    spec = pl.BlockSpec((tokens, attention.shape[1]), lambda i: (last, 0))
    cache = (z.slots, z.mig_blocks * z.block, 2 * z.width)
    return run(
        functools.partial(settle_kernel, sizes=z),
        [mig_dest, mig_len], [got, tail_q, tail_kv, attention],
        [HBM, VMEM, VMEM, spec],
        deps,
        [
            jax.ShapeDtypeStruct(attention.shape, jnp.bfloat16),
            jax.ShapeDtypeStruct((tokens, attention.shape[1]), jnp.bfloat16),
            jax.ShapeDtypeStruct((1, z.cap) + cache, jnp.bfloat16),
        ],
        [spec, VMEM, ANY], "settle", z, grid=(1,),
        scratch=[
            pltpu.VMEM((z.insts * z.per, z.width), jnp.float32),
            pltpu.VMEM((z.cap,) + got.shape[1:], jnp.bfloat16),
            pltpu.VMEM((z.cap,) + cache, jnp.bfloat16),
            pltpu.SemaphoreType.DMA((2, z.cap)),
        ],
        aliases={5: 0}, **fetch,
    )


def project_kernel(ready, launch, attention, *refs, first, tokens, count, added, joined, sizes):
    launch()
    weights, extra, out_refs = refs[:count], refs[count : count + added], refs[count + added :]
    width = sizes.quarter
    tile = min(width, 256)
    for n, weight in enumerate(weights):

        def one(j, carry, n=n, weight=weight):
            at = pl.ds(pl.multiple_of(j * tile, tile), tile)
            to = pl.ds(pl.multiple_of(n * width + j * tile, tile), tile)
            result = dot(attention[first : first + tokens, :], weight[:, at])
            if added == 1:
                result = result + extra[0][:, to].astype(jnp.float32)
            elif added:
                result = result + extra[n][:, at].astype(jnp.float32)
            if joined:
                out_refs[0][:, to] = result.astype(out_refs[0].dtype)
            else:
                out_refs[n][:, at] = result.astype(out_refs[n].dtype)
            return carry

        lax.fori_loop(0, width // tile, one, 0)


def project(attention, weights, mates, joined, dtype, sizes, name, deps, place=None, **fetch):
    attention, first, tokens = attention
    count = len(weights)
    if place is not None:
        shapes = [place((tokens, count * sizes.quarter), dtype)]
    elif joined:
        shapes = [jax.ShapeDtypeStruct((tokens, count * sizes.quarter), dtype)]
    else:
        shapes = [jax.ShapeDtypeStruct((tokens, sizes.quarter), dtype)] * count
    operands = [attention] + weights + mates
    return run(
        functools.partial(
            project_kernel, first=first, tokens=tokens, count=count, added=len(mates),
            joined=joined, sizes=sizes,
        ),
        [], operands, [VMEM] * len(operands), deps, shapes, [VMEM] * len(shapes), name, sizes,
        **fetch,
    )


def finish_kernel(ready, launch, own_low, own_high, *refs, fars, sizes):
    z = sizes
    refs = list(refs)

    def take(n):
        taken = refs[:n]
        del refs[:n]
        return taken

    low, high, second, late = take(fars), take(fars), take(fars), take(fars)
    out_hbm, block_ref, sems = refs
    tile = min(z.quarter, 256)
    writes = []
    for n in range(4):

        def one(j, carry, n=n):
            start = pl.multiple_of(j * tile, tile)
            at = pl.ds(n * z.quarter + start, tile)
            half = pl.ds((n % 2) * z.quarter + start, tile)
            sums = (own_low if n < 2 else own_high)[:, half]
            for k in range(fars):
                rows = late[k].shape[0]
                arrived = jnp.concatenate(
                    [
                        (low if n < 2 else high)[k][:, half],
                        second[k][:-rows, at],
                        late[k][:, at],
                    ],
                    axis=0,
                )
                sums = sums + arrived.astype(jnp.float32)
            block_ref[n, pl.ds(start, tile), :] = sums.T.astype(jnp.bfloat16)
            return carry

        lax.fori_loop(0, z.quarter // tile, one, 0)
        write = pltpu.make_async_copy(
            block_ref.at[n], out_hbm.at[pl.ds(n * z.quarter, z.quarter)], sems.at[n]
        )
        write.start()
        writes.append(write)
    for write in writes:
        write.wait()


def finish(own, low, high, second, late, sizes, deps):
    z = sizes
    tokens = own[0].shape[0]
    operands = own + low + high + second + late
    result, _ = run(
        functools.partial(finish_kernel, fars=len(low), sizes=z),
        [], operands, [VMEM] * len(operands), deps,
        [jax.ShapeDtypeStruct((z.features, tokens), jnp.bfloat16)], [ANY], "finish", z,
        scratch=[
            pltpu.VMEM((4, z.quarter, tokens), jnp.bfloat16), pltpu.SemaphoreType.DMA((4,))
        ],
    )
    return result[0]


def shards(
    res_pool,
    res_table,
    res_len,
    out_pool,
    src_table,
    mig_len,
    mig_dest,
    queries,
    new_kv,
    out_weight,
):
    z = Sizes(queries, res_pool, res_table, src_table, mig_dest, out_weight)
    tps, chips = z.tps, z.chips
    table = res_table[0].T
    out_weight, res_pool, out_pool, new_kv, query_rows, table, res_len, src_table, mig_dest, mig_len = (
        pltpu.with_memory_space_constraint(x, pltpu.HBM)
        for x in (
            out_weight, res_pool, out_pool, new_kv, queries.reshape(z.batch * z.per, z.width),
            table, res_len, src_table, mig_dest, mig_len,
        )
    )
    to_mate = [(i, i + 1 - 2 * (i % CORES)) for i in range(tps)]
    far = range(1, chips)
    held = {}

    def mate_of(x):
        return lax.ppermute(x, "tp", to_mate)

    def across(x, ahead):
        shift = ahead * CORES
        return lax.ppermute(x, "tp", [(i, (i + shift) % tps) for i in range(tps)])

    def bringing(pieces):
        return dict(pieces=pieces, weight=out_weight)

    def gives(ks, parts):
        return [(k, False, part) for k in ks for part in parts]

    def keeps(ks, parts):
        return [(k, True, part) for k in ks for part in parts]

    def hold(pieces, arrays):
        held.update(zip(pieces, arrays))

    def give(attention, ks, parts, name, deps, pieces=(), joined=False):
        weights = [held[piece] for piece in gives(ks, parts)]
        results, new = project(
            attention, weights, [], joined, jnp.bfloat16, z, name, deps, **bringing(pieces)
        )
        hold(pieces, new)
        return results[0], [mate_of(result) for result in results]

    def keep(attention, ks, parts, mates, name, deps, pieces=(), dtype=jnp.bfloat16, place=None):
        results = []
        for n, k in enumerate(ks):
            weights = [held[piece] for piece in keeps([k], parts)]
            if len(mates) == 1:
                width = mates[0].shape[1] // len(ks)
                now = [mates[0][:, n * width : (n + 1) * width] if len(ks) > 1 else mates[0]]
            else:
                now = mates[n * len(parts) : (n + 1) * len(parts)]
            bring = pieces if n == 0 else ()
            result, new = project(
                attention, weights, now, True, dtype, z, name, deps, place, **bringing(bring)
            )
            hold(bring, new)
            deps = [result[0]]
            results.append(result[0])
        return results

    def sent(results):
        return [across(result, k) for k, result in zip(far, results)]

    half = z.batch // 2
    low, high, every = (0, 1), (2, 3), (0, 1, 2, 3)

    sends, tail_q, tail_kv = pack(src_table, mig_dest, out_pool, query_rows, new_kv, z)
    arriving = lax.all_to_all(sends, "inst", split_axis=0, concat_axis=0, tiled=True)

    tokens = half * z.steps
    pieces = gives(far, low) + keeps(far, low) + gives(far, high)
    rows, new = attend(
        table, res_len, query_rows, new_kv, res_pool, None, 0, half, z, [sends],
        **bringing(pieces),
    )
    hold(pieces, new)
    a = (rows, 0, tokens)
    given, mates_low = give(a, far, low, "give", [], keeps(far, high))
    given, mates_high = give(a, far, high, "give", [given])
    kept = keep(a, far, low, mates_low, "keep", [given])
    got_low = sent(kept)
    kept = keep(a, far, high, mates_high, "keep", kept[-1:])
    got_high = sent(kept)
    rows, _ = attend(
        table, res_len, query_rows, new_kv, res_pool, rows, half, half, z, kept[-1:],
    )
    b = (rows, tokens, tokens)
    given, mates = give(b, far, every, "give", [])
    kept = keep(b, far, every, mates, "keep", [given] + got_low)
    got_second = sent(kept)

    pieces = gives(far, every) + keeps(far, (0,))
    (rows, last, arrived), new = settle(
        mig_dest, mig_len, arriving, tail_q, tail_kv, rows, z, kept[-1:] + got_high,
        **bringing(pieces),
    )
    hold(pieces, new)
    late, whole = (last, 0, last.shape[0]), (rows, 0, 2 * tokens)
    given, mates = give(late, far, every, "give_last", [], gives([0], low), joined=True)
    given, mates_low = give(whole, [0], low, "give_own", [given], keeps(far, (1, 2, 3)))
    kept = keep(late, far, every, mates, "keep_last", [given], gives([0], high))
    got_late = sent(kept)
    pieces = keeps([0], (0, 1, 2))
    given, mates_high = give(whole, [0], high, "give_own", kept[-1:], pieces)
    own = keep(whole, [0], low, mates_low, "keep_own", [given], keeps([0], (3,)), jnp.float32)
    own += keep(whole, [0], high, mates_high, "keep_own", own, (), jnp.float32)
    hidden = finish(own, got_low, got_high, got_second, got_late, z, [])
    return (arrived, hidden)


def solution(mesh):
    placed = (
        P(("groups", "inst"), "tp", None, None, None),
        P(("groups", "inst"), None, None),
        P(("groups", "inst"), None),
        P(("groups", "inst"), "tp", None, None, None),
        P(("groups", "inst"), None, None),
        P("groups"),
        P("groups"),
        P(("groups", "inst"), None, "tp", None),
        P(("groups", "inst"), None, "tp", None),
        P("tp", None),
    )
    return jax.shard_map(
        shards,
        mesh=mesh,
        in_specs=placed,
        out_specs=(P(("groups", "inst"), None, "tp", None, None), P("tp", ("groups", "inst"))),
        check_vma=False,
    )
```

```python
import functools
import math

import jax
import jax.numpy as jnp
from jax import lax
from jax.experimental import pallas as pl
from jax.experimental.pallas import tpu as pltpu
from jax.sharding import PartitionSpec as P

CORES = 2
LOW = -1e30
MIB = 1 << 20
LANES = 128
GROUP = 16
TOGETHER = 8
LARGE_FIRST = 12
FETCHING = 16


def dot_t(left, right):
    return lax.dot_general(
        left, right, (((1,), (1,)), ((), ())), preferred_element_type=jnp.float32
    )


def row_plan(dest_ref, inst, cap):
    requests = [jnp.int32(-1)] * cap
    seen = jnp.int32(0)
    for g in range(dest_ref.shape[0]):
        here = dest_ref[g] == inst
        requests = [jnp.where(here & (seen == a), g, requests[a]) for a in range(cap)]
        seen = seen + here.astype(jnp.int32)
    return requests


VMEM = pl.BlockSpec(memory_space=pltpu.VMEM)
ANY = pl.BlockSpec(memory_space=pl.ANY)
HBM = pl.BlockSpec(memory_space=pltpu.HBM)


class Sizes:
    def __init__(self, queries, res_pool, res_table, src_table, mig_dest, out_weight):
        self.batch, self.steps, self.heads, self.width = queries.shape
        self.slots = res_pool.shape[1]
        self.block = res_pool.shape[3]
        self.resident, self.blocks = res_table.shape[1:]
        self.mig_per, self.mig_blocks = src_table.shape[1:]
        self.requests = mig_dest.shape[0]
        self.insts = lax.axis_size("inst")
        self.tps = lax.axis_size("tp")
        self.chips = self.tps // CORES
        self.cap = self.insts - 1
        self.per = self.steps * self.heads
        self.per_kv = self.steps * self.slots
        self.depth = out_weight.shape[0]
        self.features = out_weight.shape[1] // self.tps
        self.quarter = self.features // 4
        self.tail_q = self.insts * self.per
        self.tail_kv = self.insts * self.per_kv


def piece_columns(piece, sizes):
    ahead, mine, part = piece
    tp = lax.axis_index("tp")
    core = lax.rem(tp, CORES)
    chip = lax.rem(tp // CORES + ahead, sizes.chips)
    owner = chip * CORES + (core if mine else 1 - core)
    return owner * sizes.features + part * sizes.quarter


def run(kernel, tables, operands, in_specs, deps, out_shapes, out_specs, name, sizes,
        pieces=(), weight=None, limit=16, grid=(), scratch=(), aliases=None):
    inputs, outputs, many = len(operands), len(out_shapes), len(tables)
    count = len(deps)
    fetches = len(pieces)
    extra_in = [weight] if fetches else []
    limit = max(limit, FETCHING) if fetches else limit

    def call(*refs):
        table_in, refs = refs[:many], refs[many:]
        own_in = refs[:inputs]
        position = inputs + len(extra_in) + count
        own_out = refs[position : position + outputs]
        fetched = refs[position + outputs : position + outputs + fetches]
        rest = list(refs[position + outputs + fetches :])
        copies, reads = [], []
        if fetches:
            source, sems = refs[inputs], rest.pop()
            for n, piece in enumerate(pieces):
                first = pl.multiple_of(piece_columns(piece, sizes), LANES)
                copies.append(
                    pltpu.make_async_copy(
                        source.at[:, pl.ds(first, sizes.quarter)], fetched[n], sems.at[n]
                    )
                )
        table_refs = []
        if many:
            sems = rest.pop()
            table_refs = rest[len(rest) - many :]
            rest = rest[: len(rest) - many]
            reads = [
                pltpu.make_async_copy(source, target, sems.at[n])
                for n, (source, target) in enumerate(zip(table_in, table_refs))
            ]

        def ready():
            for read in reads:
                read.wait()

        def launch():
            for copy in copies:
                copy.start()

        def each(step, action):
            if not grid:
                action()
            else:
                pl.when(pl.program_id(0) == step)(action)

        def begin():
            for read in reads:
                read.start()

        def end():
            for copy in copies:
                copy.wait()

        if reads:
            each(0, begin)
        kernel(ready, launch, *table_refs, *own_in, *own_out, *rest)
        if copies:
            each(grid[0] - 1 if grid else 0, end)

    result = pl.pallas_call(
        call,
        grid_spec=pltpu.PrefetchScalarGridSpec(
            num_scalar_prefetch=0,
            grid=grid,
            in_specs=[HBM] * many + list(in_specs) + [HBM] * len(extra_in) + [ANY] * count,
            out_specs=list(out_specs) + [ANY] * fetches,
            scratch_shapes=list(scratch)
            + [pltpu.SMEM(t.shape, t.dtype) for t in tables]
            + ([pltpu.SemaphoreType.DMA((many,))] if many else [])
            + ([pltpu.SemaphoreType.DMA((fetches,))] if fetches else []),
        ),
        out_shape=list(out_shapes)
        + [pltpu.VMEM((sizes.depth, sizes.quarter), jnp.bfloat16)] * fetches,
        input_output_aliases=aliases or {},
        compiler_params=pltpu.CompilerParams(vmem_limit_bytes=limit * MIB),
        cost_estimate=pl.CostEstimate(flops=0, bytes_accessed=1024, transcendentals=0),
        name=name,
    )(*tables, *operands, *extra_in, *deps)
    return result[:outputs], result[outputs:]


def pack_kernel(
    ready, launch, table_ref, dest_ref, pool_ref, query_ref, kv_ref, send_hbm, tail_q_ref,
    tail_kv_ref, pack_ref, sems, *, sizes
):
    inst = lax.axis_index("inst")
    ready()
    copies = []
    for m in range(sizes.mig_per):
        dest = dest_ref[inst * sizes.mig_per + m]

        def copy_block(b, carry, m=m):
            block = table_ref[0, m, b]
            for s in range(sizes.slots):
                pack_ref[m, s, b] = pool_ref[0, s, block]
            return carry

        lax.fori_loop(0, sizes.mig_blocks, copy_block, 0, unroll=8)
        copies.append(pltpu.make_async_copy(pack_ref.at[m], send_hbm.at[dest], sems.at[m]))
        copies[-1].start()
    tail_q_ref[...] = query_ref[...]
    tail_kv_ref[...] = kv_ref[...].reshape(sizes.tail_kv, 2 * sizes.width)
    for copy in copies:
        copy.wait()


def pack(src_table, mig_dest, out_pool, query_rows, new_kv, sizes):
    z = sizes
    last_q = query_rows.shape[0] // z.tail_q - 1
    last_kv = z.batch // z.insts - 1
    request = (z.slots, z.mig_blocks, z.block, 2 * z.width)
    result, _ = run(
        functools.partial(pack_kernel, sizes=z),
        [src_table, mig_dest], [out_pool, query_rows, new_kv],
        [
            VMEM,
            pl.BlockSpec((z.tail_q, z.width), lambda i: (last_q, 0)),
            pl.BlockSpec((z.insts,) + new_kv.shape[1:], lambda i: (last_kv, 0, 0, 0)),
        ],
        [],
        [
            pltpu.HBM((z.insts,) + request, out_pool.dtype),
            pltpu.HBM((z.tail_q, z.width), out_pool.dtype),
            pltpu.HBM((z.tail_kv, 2 * z.width), out_pool.dtype),
        ],
        [ANY, VMEM, VMEM], "pack", z, limit=60, grid=(1,),
        scratch=[
            pltpu.VMEM((z.mig_per,) + request, out_pool.dtype),
            pltpu.SemaphoreType.DMA((z.mig_per,)),
        ],
    )
    return result


def fresh_code(rows, keys, sizes):
    index = lax.broadcasted_iota(jnp.int32, (rows, keys), 0)
    key = lax.broadcasted_iota(jnp.int32, (rows, keys), 1)
    step = index // sizes.heads
    slot = lax.rem(index, sizes.heads) // (sizes.heads // sizes.slots)
    in_row = lax.rem(key, sizes.per_kv)
    seen = (in_row // sizes.slots <= step) & (lax.rem(in_row, sizes.slots) == slot)
    return jnp.where(seen, key // sizes.per_kv, -1)


def slot_index(extent, sizes):
    index = lax.broadcasted_iota(jnp.int32, (sizes.per, extent), 0)
    return lax.rem(index, sizes.heads) // (sizes.heads // sizes.slots)


def own_scores(scores, slot_of, slots):
    extent = scores.shape[1] // slots
    own = scores[:, :extent]
    for s in range(1, slots):
        own = jnp.where(slot_of == s, scores[:, s * extent : (s + 1) * extent], own)
    return own


def weigh(own, length, fresh, fresh_seen, scale):
    place = lax.broadcasted_iota(jnp.int32, own.shape, 1)
    own = jnp.where(place < length, own, LOW)
    fresh = jnp.where(fresh_seen, fresh, LOW)
    if own.shape == fresh.shape:
        largest = jnp.max(jnp.maximum(own, fresh), axis=1, keepdims=True)
    else:
        largest = jnp.maximum(
            jnp.max(own, axis=1, keepdims=True), jnp.max(fresh, axis=1, keepdims=True)
        )
    return jnp.exp2((own - largest) * scale), jnp.exp2((fresh - largest) * scale)


def spread(own, slot_of, slots):
    if slots == 1:
        return own.astype(jnp.bfloat16)
    parts = [jnp.where(slot_of == s, own, 0.0) for s in range(slots)]
    return jnp.concatenate(parts, axis=1).astype(jnp.bfloat16)


def gather_blocks(pool_ref, slots, ids):
    tiles = [pool_ref[0, s, block] for s in range(slots) for block in ids]
    return jnp.concatenate(tiles, axis=0)


def with_ones(values):
    return jnp.concatenate([values, jnp.ones_like(values)], axis=1)


def dot(left, right):
    return jnp.dot(left, right, preferred_element_type=jnp.float32)


def attend_kernel(
    ready, launch, table_ref, len_ref, query_hbm, kv_hbm, pool_ref, *refs, first_row,
    steps_in_all, sizes,
):
    z = sizes
    out_ref, query_all, kv_all, fresh_ref, pf_ref, blend_ref, done_ref, sems = refs
    width, per = z.width, z.per
    rows = GROUP
    step = pl.program_id(0)
    extent = z.blocks * z.block
    start = first_row + step * rows
    scale = math.log2(math.e) / math.sqrt(width)

    def copies(n):
        begin = first_row + n * rows
        return (
            pltpu.make_async_copy(
                query_hbm.at[pl.ds(pl.multiple_of(begin * per, rows * per), rows * per)],
                query_all.at[n], sems.at[0, n],
            ),
            pltpu.make_async_copy(kv_hbm.at[pl.ds(begin, rows)], kv_all.at[n], sems.at[1, n]),
        )

    @pl.when(step == 0)
    def _():
        for n in range(steps_in_all):
            for copy in copies(n):
                copy.start()
        launch()
        ready()

    for copy in copies(step):
        copy.wait()

    query_ref = query_all.at[step]
    new_kv = kv_all[step].reshape(rows * z.per_kv, 2 * width)
    fresh_ref[...] = dot_t(query_ref[...], new_kv[:, :width])
    code = fresh_code(per, rows * z.per_kv, z)
    slot_of = slot_index(extent, z)
    together = min(TOGETHER, rows)
    for begin in range(0, rows, together):
        group = range(begin, begin + together)
        at = [slice(r * per, (r + 1) * per) for r in group]
        known = [jnp.minimum(start + r, z.resident - 1) for r in group]
        length = [
            jnp.where(start + r < z.resident, len_ref[0, k], 0) for r, k in zip(group, known)
        ]
        both = [
            gather_blocks(pool_ref, z.slots, [table_ref[j, k] for j in range(z.blocks)])
            for k in known
        ]
        fresh = [fresh_ref[a, :] for a in at]
        scores = [dot_t(query_ref[a, :], b[:, :width]) for a, b in zip(at, both)]
        weights = [
            weigh(own_scores(s, slot_of, z.slots), n, f, code == r, scale)
            for s, n, f, r in zip(scores, length, fresh, group)
        ]
        context = [
            dot(spread(w[0], slot_of, z.slots), with_ones(b[:, width:]))
            for w, b in zip(weights, both)
        ]
        for a, c, w in zip(at, context, weights):
            blend_ref[a, :] = c
            pf_ref[a, :] = w[1].astype(jnp.bfloat16)

    done = blend_ref[...] + dot(pf_ref[...], with_ones(new_kv[:, width:]))
    done_ref[...] = done[:, :width] / done[:, width:]
    for h in range(z.heads):
        column = done_ref[pl.ds(h, rows * z.steps, stride=z.heads), :]
        out_ref[:, h * width : (h + 1) * width] = column.astype(jnp.bfloat16)


def attend(table, lengths, queries, new_kv, pool, into, first_row, rows, sizes, deps, limit=12,
           **fetch):
    z = sizes
    groups = rows // GROUP
    first = first_row // GROUP
    tokens = z.batch * z.steps
    aliases = {}
    if into is not None:
        deps = [into] + deps
        aliases = {5 + (1 if fetch else 0): 0}
    result, pieces = run(
        functools.partial(
            attend_kernel, first_row=first_row, steps_in_all=groups, sizes=z
        ),
        [table, lengths],
        [queries, new_kv, pool],
        [HBM, HBM, VMEM],
        deps,
        [jax.ShapeDtypeStruct((tokens, z.heads * z.width), jnp.bfloat16)],
        [pl.BlockSpec((GROUP * z.steps, z.heads * z.width), lambda i: (first + i, 0))],
        "attend", z, limit=limit,
        grid=(groups,),
        scratch=[
            pltpu.VMEM((groups, GROUP * z.per, z.width), jnp.bfloat16),
            pltpu.VMEM((groups, GROUP) + new_kv.shape[1:], jnp.bfloat16),
            pltpu.VMEM((GROUP * z.per, GROUP * z.per_kv), jnp.float32),
            pltpu.VMEM((GROUP * z.per, GROUP * z.per_kv), jnp.bfloat16),
            pltpu.VMEM((GROUP * z.per, 2 * z.width), jnp.float32),
            pltpu.VMEM((GROUP * z.per, z.width), jnp.float32),
            pltpu.SemaphoreType.DMA((2, groups)),
        ],
        aliases=aliases, **fetch,
    )
    return result[0], pieces


def settle_kernel(
    ready, launch, dest_ref, len_ref, got_hbm, query_ref, kv_ref, old_ref, out_ref, last_ref,
    arrived_hbm, rows_ref, got_ref, keep_ref, sems, *, sizes
):
    z = sizes
    ready()
    inst = lax.axis_index("inst")
    requests = row_plan(dest_ref, inst, z.cap)
    known = [jnp.maximum(request, 0) for request in requests]
    extent = z.mig_blocks * z.block
    reads = [
        pltpu.make_async_copy(got_hbm.at[known[a] // z.mig_per], got_ref.at[a], sems.at[0, a])
        for a in range(z.cap)
    ]
    writes = [
        pltpu.make_async_copy(keep_ref.at[a], arrived_hbm.at[0, a], sems.at[1, a])
        for a in range(z.cap)
    ]
    for read in reads:
        read.start()
    launch()
    new_kv = kv_ref[...]
    code = fresh_code(z.per, z.tail_kv, z)
    slot_of = slot_index(extent, z)
    scale = math.log2(math.e) / math.sqrt(z.width)
    tokens = z.insts * z.steps
    row = lax.broadcasted_iota(jnp.int32, (tokens, z.width), 0) // z.steps
    place = lax.broadcasted_iota(jnp.int32, (z.block, 2 * z.width), 0)
    filled = row < 0
    rows_ref[: z.per, :] = jnp.zeros((z.per, z.width), jnp.float32)
    for a in range(z.cap):
        length = jnp.where(requests[a] >= 0, len_ref[known[a]], 0)
        reads[a].wait()

        def one(b, carry, a=a, length=length):
            inside = place + b * z.block < length
            at = pl.ds(pl.multiple_of(b * z.block, z.block), z.block)
            for s in range(z.slots):
                value = got_ref[a, s, b].astype(jnp.float32)
                keep_ref[a, s, at, :] = jnp.where(inside, value, 0.0).astype(jnp.bfloat16)
            return carry

        lax.fori_loop(0, z.mig_blocks, one, 0, unroll=8)
        writes[a].start()
        at = slice((a + 1) * z.per, (a + 2) * z.per)
        both = jnp.concatenate([keep_ref[a, s] for s in range(z.slots)], axis=0)
        own = own_scores(dot_t(query_ref[at, :], both[:, : z.width]), slot_of, z.slots)
        fresh = dot_t(query_ref[at, :], new_kv[:, : z.width])
        own, fresh = weigh(own, length, fresh, code == a + 1, scale)
        done = dot(spread(own, slot_of, z.slots), with_ones(both[:, z.width :]))
        done = done + dot(fresh.astype(jnp.bfloat16), with_ones(new_kv[:, z.width :]))
        rows_ref[at, :] = done[:, : z.width] / done[:, z.width :]
        filled = filled | ((row == a + 1) & (requests[a] >= 0))
    for h in range(z.heads):
        at = slice(h * z.width, (h + 1) * z.width)
        column = rows_ref[pl.ds(h, tokens, stride=z.heads), :]
        old = old_ref[:, at].astype(jnp.float32)
        value = jnp.where(filled, column, old).astype(jnp.bfloat16)
        out_ref[:, at] = value
        last_ref[:, at] = value
    for write in writes:
        write.wait()


def settle(mig_dest, mig_len, got, tail_q, tail_kv, attention, sizes, deps, **fetch):
    z = sizes
    tokens = z.insts * z.steps
    last = attention.shape[0] // tokens - 1
    spec = pl.BlockSpec((tokens, attention.shape[1]), lambda i: (last, 0))
    cache = (z.slots, z.mig_blocks * z.block, 2 * z.width)
    return run(
        functools.partial(settle_kernel, sizes=z),
        [mig_dest, mig_len], [got, tail_q, tail_kv, attention],
        [HBM, VMEM, VMEM, spec],
        deps,
        [
            jax.ShapeDtypeStruct(attention.shape, jnp.bfloat16),
            jax.ShapeDtypeStruct((tokens, attention.shape[1]), jnp.bfloat16),
            jax.ShapeDtypeStruct((1, z.cap) + cache, jnp.bfloat16),
        ],
        [spec, VMEM, ANY], "settle", z, grid=(1,),
        scratch=[
            pltpu.VMEM((z.insts * z.per, z.width), jnp.float32),
            pltpu.VMEM((z.cap,) + got.shape[1:], jnp.bfloat16),
            pltpu.VMEM((z.cap,) + cache, jnp.bfloat16),
            pltpu.SemaphoreType.DMA((2, z.cap)),
        ],
        aliases={5: 0}, **fetch,
    )


def project_kernel(ready, launch, attention, *refs, first, tokens, count, added, joined, sizes):
    launch()
    weights, extra, out_refs = refs[:count], refs[count : count + added], refs[count + added :]
    width = sizes.quarter
    tile = min(width, 256)
    for n, weight in enumerate(weights):

        def one(j, carry, n=n, weight=weight):
            at = pl.ds(pl.multiple_of(j * tile, tile), tile)
            to = pl.ds(pl.multiple_of(n * width + j * tile, tile), tile)
            result = dot(attention[first : first + tokens, :], weight[:, at])
            if added == 1:
                result = result + extra[0][:, to].astype(jnp.float32)
            elif added:
                result = result + extra[n][:, at].astype(jnp.float32)
            if joined:
                out_refs[0][:, to] = result.astype(out_refs[0].dtype)
            else:
                out_refs[n][:, at] = result.astype(out_refs[n].dtype)
            return carry

        lax.fori_loop(0, width // tile, one, 0)


def project(attention, weights, mates, joined, dtype, sizes, name, deps, place=None, **fetch):
    attention, first, tokens = attention
    count = len(weights)
    if place is not None:
        shapes = [place((tokens, count * sizes.quarter), dtype)]
    elif joined:
        shapes = [jax.ShapeDtypeStruct((tokens, count * sizes.quarter), dtype)]
    else:
        shapes = [jax.ShapeDtypeStruct((tokens, sizes.quarter), dtype)] * count
    operands = [attention] + weights + mates
    return run(
        functools.partial(
            project_kernel, first=first, tokens=tokens, count=count, added=len(mates),
            joined=joined, sizes=sizes,
        ),
        [], operands, [VMEM] * len(operands), deps, shapes, [VMEM] * len(shapes), name, sizes,
        **fetch,
    )


def final_kernel(ready, launch, attention, *refs, count, streamed, mates, fars, sizes):
    z = sizes
    refs = list(refs)

    def take(n):
        taken = refs[:n]
        del refs[:n]
        return taken

    weights, extra = take(count), take(mates)
    low, high, second, late = take(fars), take(fars), take(fars), take(fars)
    source = take(bool(streamed))
    (out_hbm,) = take(1)
    block_ref, block_sems = take(2)
    copies = [None] * count
    for n, piece in enumerate(streamed):
        begin = pl.multiple_of(piece_columns(piece, z), LANES)
        copy = pltpu.make_async_copy(
            source[0].at[:, pl.ds(begin, z.quarter)], refs[0].at[n], refs[1].at[n]
        )
        copy.start()
        copies.append(copy)
        weights.append(refs[0].at[n])
    tile = min(z.quarter, 256)
    writes = []
    for n, (weight, copy) in enumerate(zip(weights, copies)):
        if copy is not None:
            copy.wait()

        def one(j, carry, n=n, weight=weight):
            start = pl.multiple_of(j * tile, tile)
            at = pl.ds(start, tile)
            whole = pl.ds(n * z.quarter + start, tile)
            sums = dot(attention[...], weight[:, at]) + extra[n][:, at].astype(jnp.float32)
            for k in range(fars):
                rows = late[k].shape[0]
                arrived = jnp.concatenate(
                    [
                        low[k][:, whole] if n < 3 else high[k][:, at],
                        second[k][:-rows, whole],
                        late[k][:, whole],
                    ],
                    axis=0,
                )
                sums = sums + arrived.astype(jnp.float32)
            block_ref[n, at, :] = sums.T.astype(jnp.bfloat16)
            return carry

        lax.fori_loop(0, z.quarter // tile, one, 0)
        write = pltpu.make_async_copy(
            block_ref.at[n], out_hbm.at[pl.ds(n * z.quarter, z.quarter)], block_sems.at[n]
        )
        write.start()
        writes.append(write)
    for write in writes:
        write.wait()


def final(attention, weights, streamed, out_weight, mates, low, high, second, late, sizes, deps):
    z = sizes
    tokens = attention.shape[0]
    operands = [attention] + weights + mates + low + high + second + late + [out_weight]
    specs = [VMEM] * (len(operands) - 1) + [HBM]
    result, _ = run(
        functools.partial(
            final_kernel, count=len(weights), streamed=streamed, mates=len(mates),
            fars=len(low), sizes=z,
        ),
        [], operands, specs, deps,
        [jax.ShapeDtypeStruct((z.features, tokens), jnp.bfloat16)], [ANY], "final", z,
        scratch=[
            pltpu.VMEM((4, z.quarter, tokens), jnp.bfloat16), pltpu.SemaphoreType.DMA((4,)),
            pltpu.VMEM((len(streamed), z.depth, z.quarter), jnp.bfloat16),
            pltpu.SemaphoreType.DMA((len(streamed),)),
        ],
    )
    return result[0]


def shards(
    res_pool,
    res_table,
    res_len,
    out_pool,
    src_table,
    mig_len,
    mig_dest,
    queries,
    new_kv,
    out_weight,
):
    z = Sizes(queries, res_pool, res_table, src_table, mig_dest, out_weight)
    tps, chips = z.tps, z.chips
    table = res_table[0].T
    out_weight, res_pool, out_pool, new_kv, query_rows, table, res_len, src_table, mig_dest, mig_len = (
        pltpu.with_memory_space_constraint(x, pltpu.HBM)
        for x in (
            out_weight, res_pool, out_pool, new_kv, queries.reshape(z.batch * z.per, z.width),
            table, res_len, src_table, mig_dest, mig_len,
        )
    )
    to_mate = [(i, i + 1 - 2 * (i % CORES)) for i in range(tps)]
    far = range(1, chips)
    held = {}

    def mate_of(x):
        return lax.ppermute(x, "tp", to_mate)

    def across(x, ahead):
        shift = ahead * CORES
        return lax.ppermute(x, "tp", [(i, (i + shift) % tps) for i in range(tps)])

    def bringing(pieces):
        return dict(pieces=pieces, weight=out_weight)

    def gives(ks, parts):
        return [(k, False, part) for k in ks for part in parts]

    def keeps(ks, parts):
        return [(k, True, part) for k in ks for part in parts]

    def hold(pieces, arrays):
        held.update(zip(pieces, arrays))

    def give(attention, ks, parts, name, deps, pieces=(), joined=False):
        weights = [held[piece] for piece in gives(ks, parts)]
        results, new = project(
            attention, weights, [], joined, jnp.bfloat16, z, name, deps, **bringing(pieces)
        )
        hold(pieces, new)
        return results[0], [mate_of(result) for result in results]

    def keep(attention, ks, parts, mates, name, deps, pieces=(), dtype=jnp.bfloat16, place=None):
        results = []
        for n, k in enumerate(ks):
            weights = [held[piece] for piece in keeps([k], parts)]
            if len(mates) == 1:
                width = mates[0].shape[1] // len(ks)
                now = [mates[0][:, n * width : (n + 1) * width] if len(ks) > 1 else mates[0]]
            else:
                now = mates[n * len(parts) : (n + 1) * len(parts)]
            bring = pieces if n == 0 else ()
            result, new = project(
                attention, weights, now, True, dtype, z, name, deps, place, **bringing(bring)
            )
            hold(bring, new)
            deps = [result[0]]
            results.append(result[0])
        return results

    def sent(results):
        return [across(result, k) for k, result in zip(far, results)]

    half = z.batch // 2
    low, high, every = (0, 1), (2, 3), (0, 1, 2, 3)

    sends, tail_q, tail_kv = pack(src_table, mig_dest, out_pool, query_rows, new_kv, z)
    arriving = lax.all_to_all(sends, "inst", split_axis=0, concat_axis=0, tiled=True)

    tokens = half * z.steps
    pieces = gives(far, low) + keeps(far, low) + gives(far, high)
    rows, new = attend(
        table, res_len, query_rows, new_kv, res_pool, None, 0, half, z, [sends],
        **bringing(pieces),
    )
    hold(pieces, new)
    a = (rows, 0, tokens)
    given, mates_low = give(a, far, low, "give", [], keeps(far, high))
    given, mates_high = give(a, far, high, "give", [given])
    mates = [mates_low[2 * n : 2 * n + 2] + mates_high[2 * n : 2 * n + 2] for n in range(chips - 1)]
    kept = keep(a, far, (0, 1, 2), sum((m[:3] for m in mates), []), "keep", [given])
    got_low = sent(kept)
    kept = keep(a, far, (3,), sum((m[3:] for m in mates), []), "keep", kept[-1:])
    got_high = sent(kept)
    rows, _ = attend(
        table, res_len, query_rows, new_kv, res_pool, rows, half, half, z, kept[-1:],
    )
    b = (rows, tokens, tokens)
    given, mates = give(b, far, every, "give", [])
    kept = keep(b, far, every, mates, "keep", [given] + got_low)
    got_second = sent(kept)

    pieces = gives(far, every) + keeps(far, (0,))
    tail_q, tail_kv = (
        pltpu.with_memory_space_constraint(x, pltpu.HBM) for x in (tail_q, tail_kv)
    )
    (rows, last, arrived), new = settle(
        mig_dest, mig_len, arriving, tail_q, tail_kv, rows, z, kept[-1:] + got_high,
        **bringing(pieces),
    )
    hold(pieces, new)
    late, whole = (last, 0, last.shape[0]), (rows, 0, 2 * tokens)
    given, mates = give(late, far, every, "give_last", [], gives([0], low), joined=True)
    given, mates_low = give(whole, [0], low, "give_own", [given], keeps(far, (1, 2, 3)))
    kept = keep(late, far, every, mates, "keep_last", [given], gives([0], high))
    got_late = sent(kept)
    pieces = keeps([0], (0, 1, 2))
    given, mates_high = give(whole, [0], high, "give_own", kept[-1:], pieces)
    weights = [held[piece] for piece in pieces]
    hidden = final(
        rows, weights, keeps([0], (3,)), out_weight, mates_low + mates_high, got_low, got_high,
        got_second, got_late, z, [given],
    )
    return (arrived, hidden)


def solution(mesh):
    placed = (
        P(("groups", "inst"), "tp", None, None, None),
        P(("groups", "inst"), None, None),
        P(("groups", "inst"), None),
        P(("groups", "inst"), "tp", None, None, None),
        P(("groups", "inst"), None, None),
        P("groups"),
        P("groups"),
        P(("groups", "inst"), None, "tp", None),
        P(("groups", "inst"), None, "tp", None),
        P("tp", None),
    )
    return jax.shard_map(
        shards,
        mesh=mesh,
        in_specs=placed,
        out_specs=(P(("groups", "inst"), None, "tp", None, None), P("tp", ("groups", "inst"))),
        check_vma=False,
    )
```

```python
import functools
import math

import jax
import jax.numpy as jnp
from jax import lax
from jax.experimental import pallas as pl
from jax.experimental.pallas import tpu as pltpu
from jax.sharding import PartitionSpec as P

CORES = 2
LOW = -1e30
MIB = 1 << 20
LANES = 128
GROUP = 16
TOGETHER = 8
LARGE_FIRST = 12
FETCHING = 16


def dot_t(left, right):
    return lax.dot_general(
        left, right, (((1,), (1,)), ((), ())), preferred_element_type=jnp.float32
    )


def row_plan(dest_ref, inst, cap):
    requests = [jnp.int32(-1)] * cap
    seen = jnp.int32(0)
    for g in range(dest_ref.shape[0]):
        here = dest_ref[g] == inst
        requests = [jnp.where(here & (seen == a), g, requests[a]) for a in range(cap)]
        seen = seen + here.astype(jnp.int32)
    return requests


VMEM = pl.BlockSpec(memory_space=pltpu.VMEM)
ANY = pl.BlockSpec(memory_space=pl.ANY)
HBM = pl.BlockSpec(memory_space=pltpu.HBM)


class Sizes:
    def __init__(self, queries, res_pool, res_table, src_table, mig_dest, out_weight):
        self.batch, self.steps, self.heads, self.width = queries.shape
        self.slots = res_pool.shape[1]
        self.block = res_pool.shape[3]
        self.resident, self.blocks = res_table.shape[1:]
        self.mig_per, self.mig_blocks = src_table.shape[1:]
        self.requests = mig_dest.shape[0]
        self.insts = lax.axis_size("inst")
        self.tps = lax.axis_size("tp")
        self.chips = self.tps // CORES
        self.cap = self.insts - 1
        self.per = self.steps * self.heads
        self.per_kv = self.steps * self.slots
        self.depth = out_weight.shape[0]
        self.features = out_weight.shape[1] // self.tps
        self.quarter = self.features // 4
        self.tail_q = self.insts * self.per
        self.tail_kv = self.insts * self.per_kv


def piece_columns(piece, sizes):
    ahead, mine, part = piece
    tp = lax.axis_index("tp")
    core = lax.rem(tp, CORES)
    chip = lax.rem(tp // CORES + ahead, sizes.chips)
    owner = chip * CORES + (core if mine else 1 - core)
    return owner * sizes.features + part * sizes.quarter


def run(kernel, tables, operands, in_specs, deps, out_shapes, out_specs, name, sizes,
        pieces=(), weight=None, limit=16, grid=(), scratch=(), aliases=None):
    inputs, outputs, many = len(operands), len(out_shapes), len(tables)
    count = len(deps)
    fetches = len(pieces)
    extra_in = [weight] if fetches else []
    limit = max(limit, FETCHING) if fetches else limit

    def call(*refs):
        table_in, refs = refs[:many], refs[many:]
        own_in = refs[:inputs]
        position = inputs + len(extra_in) + count
        own_out = refs[position : position + outputs]
        fetched = refs[position + outputs : position + outputs + fetches]
        rest = list(refs[position + outputs + fetches :])
        copies, reads = [], []
        if fetches:
            source, sems = refs[inputs], rest.pop()
            for n, piece in enumerate(pieces):
                first = pl.multiple_of(piece_columns(piece, sizes), LANES)
                copies.append(
                    pltpu.make_async_copy(
                        source.at[:, pl.ds(first, sizes.quarter)], fetched[n], sems.at[n]
                    )
                )
        table_refs = []
        if many:
            sems = rest.pop()
            table_refs = rest[len(rest) - many :]
            rest = rest[: len(rest) - many]
            reads = [
                pltpu.make_async_copy(source, target, sems.at[n])
                for n, (source, target) in enumerate(zip(table_in, table_refs))
            ]

        def ready():
            for read in reads:
                read.wait()

        def launch():
            for copy in copies:
                copy.start()

        def each(step, action):
            if not grid:
                action()
            else:
                pl.when(pl.program_id(0) == step)(action)

        def begin():
            for read in reads:
                read.start()

        def end():
            for copy in copies:
                copy.wait()

        if reads:
            each(0, begin)
        kernel(ready, launch, *table_refs, *own_in, *own_out, *rest)
        if copies:
            each(grid[0] - 1 if grid else 0, end)

    result = pl.pallas_call(
        call,
        grid_spec=pltpu.PrefetchScalarGridSpec(
            num_scalar_prefetch=0,
            grid=grid,
            in_specs=[HBM] * many + list(in_specs) + [HBM] * len(extra_in) + [ANY] * count,
            out_specs=list(out_specs) + [ANY] * fetches,
            scratch_shapes=list(scratch)
            + [pltpu.SMEM(t.shape, t.dtype) for t in tables]
            + ([pltpu.SemaphoreType.DMA((many,))] if many else [])
            + ([pltpu.SemaphoreType.DMA((fetches,))] if fetches else []),
        ),
        out_shape=list(out_shapes)
        + [pltpu.VMEM((sizes.depth, sizes.quarter), jnp.bfloat16)] * fetches,
        input_output_aliases=aliases or {},
        compiler_params=pltpu.CompilerParams(vmem_limit_bytes=limit * MIB),
        cost_estimate=pl.CostEstimate(flops=0, bytes_accessed=1024, transcendentals=0),
        name=name,
    )(*tables, *operands, *extra_in, *deps)
    return result[:outputs], result[outputs:]


def pack_kernel(
    ready, launch, table_ref, dest_ref, pool_ref, query_ref, kv_ref, send_hbm, tail_q_ref,
    tail_kv_ref, pack_ref, sems, *, sizes
):
    inst = lax.axis_index("inst")
    ready()
    copies = []
    for m in range(sizes.mig_per):
        dest = dest_ref[inst * sizes.mig_per + m]

        def copy_block(b, carry, m=m):
            block = table_ref[0, m, b]
            for s in range(sizes.slots):
                pack_ref[m, s, b] = pool_ref[0, s, block]
            return carry

        lax.fori_loop(0, sizes.mig_blocks, copy_block, 0, unroll=8)
        copies.append(pltpu.make_async_copy(pack_ref.at[m], send_hbm.at[dest], sems.at[m]))
        copies[-1].start()
    tail_q_ref[...] = query_ref[...]
    tail_kv_ref[...] = kv_ref[...].reshape(sizes.tail_kv, 2 * sizes.width)
    for copy in copies:
        copy.wait()


def pack(src_table, mig_dest, out_pool, query_rows, new_kv, sizes):
    z = sizes
    last_q = query_rows.shape[0] // z.tail_q - 1
    last_kv = z.batch // z.insts - 1
    request = (z.slots, z.mig_blocks, z.block, 2 * z.width)
    result, _ = run(
        functools.partial(pack_kernel, sizes=z),
        [src_table, mig_dest], [out_pool, query_rows, new_kv],
        [
            VMEM,
            pl.BlockSpec((z.tail_q, z.width), lambda i: (last_q, 0)),
            pl.BlockSpec((z.insts,) + new_kv.shape[1:], lambda i: (last_kv, 0, 0, 0)),
        ],
        [],
        [
            pltpu.HBM((z.insts,) + request, out_pool.dtype),
            pltpu.HBM((z.tail_q, z.width), out_pool.dtype),
            pltpu.HBM((z.tail_kv, 2 * z.width), out_pool.dtype),
        ],
        [ANY, VMEM, VMEM], "pack", z, limit=60, grid=(1,),
        scratch=[
            pltpu.VMEM((z.mig_per,) + request, out_pool.dtype),
            pltpu.SemaphoreType.DMA((z.mig_per,)),
        ],
    )
    return result


def fresh_code(rows, keys, sizes):
    index = lax.broadcasted_iota(jnp.int32, (rows, keys), 0)
    key = lax.broadcasted_iota(jnp.int32, (rows, keys), 1)
    step = index // sizes.heads
    slot = lax.rem(index, sizes.heads) // (sizes.heads // sizes.slots)
    in_row = lax.rem(key, sizes.per_kv)
    seen = (in_row // sizes.slots <= step) & (lax.rem(in_row, sizes.slots) == slot)
    return jnp.where(seen, key // sizes.per_kv, -1)


def slot_index(extent, sizes):
    index = lax.broadcasted_iota(jnp.int32, (sizes.per, extent), 0)
    return lax.rem(index, sizes.heads) // (sizes.heads // sizes.slots)


def own_scores(scores, slot_of, slots):
    extent = scores.shape[1] // slots
    own = scores[:, :extent]
    for s in range(1, slots):
        own = jnp.where(slot_of == s, scores[:, s * extent : (s + 1) * extent], own)
    return own


def weigh(own, length, fresh, fresh_seen, scale):
    place = lax.broadcasted_iota(jnp.int32, own.shape, 1)
    own = jnp.where(place < length, own, LOW)
    fresh = jnp.where(fresh_seen, fresh, LOW)
    if own.shape == fresh.shape:
        largest = jnp.max(jnp.maximum(own, fresh), axis=1, keepdims=True)
    else:
        largest = jnp.maximum(
            jnp.max(own, axis=1, keepdims=True), jnp.max(fresh, axis=1, keepdims=True)
        )
    return jnp.exp2((own - largest) * scale), jnp.exp2((fresh - largest) * scale)


def spread(own, slot_of, slots):
    if slots == 1:
        return own.astype(jnp.bfloat16)
    parts = [jnp.where(slot_of == s, own, 0.0) for s in range(slots)]
    return jnp.concatenate(parts, axis=1).astype(jnp.bfloat16)


def gather_blocks(pool_ref, slots, ids):
    tiles = [pool_ref[0, s, block] for s in range(slots) for block in ids]
    return jnp.concatenate(tiles, axis=0)


def with_ones(values):
    return jnp.concatenate([values, jnp.ones_like(values)], axis=1)


def dot(left, right):
    return jnp.dot(left, right, preferred_element_type=jnp.float32)


def attend_kernel(
    ready, launch, table_ref, len_ref, query_hbm, kv_hbm, pool_ref, *refs, first_row,
    steps_in_all, sizes,
):
    z = sizes
    out_ref, query_all, kv_all, fresh_ref, pf_ref, blend_ref, done_ref, sems = refs
    width, per = z.width, z.per
    rows = GROUP
    step = pl.program_id(0)
    extent = z.blocks * z.block
    start = first_row + step * rows
    scale = math.log2(math.e) / math.sqrt(width)

    def copies(n):
        begin = first_row + n * rows
        return (
            pltpu.make_async_copy(
                query_hbm.at[pl.ds(pl.multiple_of(begin * per, rows * per), rows * per)],
                query_all.at[n], sems.at[0, n],
            ),
            pltpu.make_async_copy(kv_hbm.at[pl.ds(begin, rows)], kv_all.at[n], sems.at[1, n]),
        )

    @pl.when(step == 0)
    def _():
        for n in range(steps_in_all):
            for copy in copies(n):
                copy.start()
        launch()
        ready()

    for copy in copies(step):
        copy.wait()

    query_ref = query_all.at[step]
    new_kv = kv_all[step].reshape(rows * z.per_kv, 2 * width)
    fresh_ref[...] = dot_t(query_ref[...], new_kv[:, :width])
    code = fresh_code(per, rows * z.per_kv, z)
    slot_of = slot_index(extent, z)
    together = min(TOGETHER, rows)
    for begin in range(0, rows, together):
        group = range(begin, begin + together)
        at = [slice(r * per, (r + 1) * per) for r in group]
        known = [jnp.minimum(start + r, z.resident - 1) for r in group]
        length = [
            jnp.where(start + r < z.resident, len_ref[0, k], 0) for r, k in zip(group, known)
        ]
        both = [
            gather_blocks(pool_ref, z.slots, [table_ref[j, k] for j in range(z.blocks)])
            for k in known
        ]
        fresh = [fresh_ref[a, :] for a in at]
        scores = [dot_t(query_ref[a, :], b[:, :width]) for a, b in zip(at, both)]
        weights = [
            weigh(own_scores(s, slot_of, z.slots), n, f, code == r, scale)
            for s, n, f, r in zip(scores, length, fresh, group)
        ]
        context = [
            dot(spread(w[0], slot_of, z.slots), with_ones(b[:, width:]))
            for w, b in zip(weights, both)
        ]
        for a, c, w in zip(at, context, weights):
            blend_ref[a, :] = c
            pf_ref[a, :] = w[1].astype(jnp.bfloat16)

    done = blend_ref[...] + dot(pf_ref[...], with_ones(new_kv[:, width:]))
    done_ref[...] = done[:, :width] / done[:, width:]
    for h in range(z.heads):
        column = done_ref[pl.ds(h, rows * z.steps, stride=z.heads), :]
        out_ref[:, h * width : (h + 1) * width] = column.astype(jnp.bfloat16)


def attend(table, lengths, queries, new_kv, pool, into, first_row, rows, sizes, deps, limit=12,
           **fetch):
    z = sizes
    groups = rows // GROUP
    first = first_row // GROUP
    tokens = z.batch * z.steps
    aliases = {}
    if into is not None:
        deps = [into] + deps
        aliases = {5 + (1 if fetch else 0): 0}
    result, pieces = run(
        functools.partial(
            attend_kernel, first_row=first_row, steps_in_all=groups, sizes=z
        ),
        [table, lengths],
        [queries, new_kv, pool],
        [HBM, HBM, VMEM],
        deps,
        [jax.ShapeDtypeStruct((tokens, z.heads * z.width), jnp.bfloat16)],
        [pl.BlockSpec((GROUP * z.steps, z.heads * z.width), lambda i: (first + i, 0))],
        "attend", z, limit=limit,
        grid=(groups,),
        scratch=[
            pltpu.VMEM((groups, GROUP * z.per, z.width), jnp.bfloat16),
            pltpu.VMEM((groups, GROUP) + new_kv.shape[1:], jnp.bfloat16),
            pltpu.VMEM((GROUP * z.per, GROUP * z.per_kv), jnp.float32),
            pltpu.VMEM((GROUP * z.per, GROUP * z.per_kv), jnp.bfloat16),
            pltpu.VMEM((GROUP * z.per, 2 * z.width), jnp.float32),
            pltpu.VMEM((GROUP * z.per, z.width), jnp.float32),
            pltpu.SemaphoreType.DMA((2, groups)),
        ],
        aliases=aliases, **fetch,
    )
    return result[0], pieces


def settle_kernel(
    ready, launch, dest_ref, len_ref, got_hbm, query_ref, kv_ref, old_ref, out_ref, last_ref,
    arrived_hbm, rows_ref, got_ref, keep_ref, sems, *, sizes
):
    z = sizes
    ready()
    inst = lax.axis_index("inst")
    requests = row_plan(dest_ref, inst, z.cap)
    known = [jnp.maximum(request, 0) for request in requests]
    extent = z.mig_blocks * z.block
    reads = [
        pltpu.make_async_copy(got_hbm.at[known[a] // z.mig_per], got_ref.at[a], sems.at[0, a])
        for a in range(z.cap)
    ]
    writes = [
        pltpu.make_async_copy(keep_ref.at[a], arrived_hbm.at[0, a], sems.at[1, a])
        for a in range(z.cap)
    ]
    for read in reads:
        read.start()
    launch()
    new_kv = kv_ref[...]
    code = fresh_code(z.per, z.tail_kv, z)
    slot_of = slot_index(extent, z)
    scale = math.log2(math.e) / math.sqrt(z.width)
    tokens = z.insts * z.steps
    row = lax.broadcasted_iota(jnp.int32, (tokens, z.width), 0) // z.steps
    place = lax.broadcasted_iota(jnp.int32, (z.block, 2 * z.width), 0)
    filled = row < 0
    rows_ref[: z.per, :] = jnp.zeros((z.per, z.width), jnp.float32)
    for a in range(z.cap):
        length = jnp.where(requests[a] >= 0, len_ref[known[a]], 0)
        reads[a].wait()

        def one(b, carry, a=a, length=length):
            inside = place + b * z.block < length
            at = pl.ds(pl.multiple_of(b * z.block, z.block), z.block)
            for s in range(z.slots):
                value = got_ref[a, s, b].astype(jnp.float32)
                keep_ref[a, s, at, :] = jnp.where(inside, value, 0.0).astype(jnp.bfloat16)
            return carry

        lax.fori_loop(0, z.mig_blocks, one, 0, unroll=8)
        writes[a].start()
        at = slice((a + 1) * z.per, (a + 2) * z.per)
        both = jnp.concatenate([keep_ref[a, s] for s in range(z.slots)], axis=0)
        own = own_scores(dot_t(query_ref[at, :], both[:, : z.width]), slot_of, z.slots)
        fresh = dot_t(query_ref[at, :], new_kv[:, : z.width])
        own, fresh = weigh(own, length, fresh, code == a + 1, scale)
        done = dot(spread(own, slot_of, z.slots), with_ones(both[:, z.width :]))
        done = done + dot(fresh.astype(jnp.bfloat16), with_ones(new_kv[:, z.width :]))
        rows_ref[at, :] = done[:, : z.width] / done[:, z.width :]
        filled = filled | ((row == a + 1) & (requests[a] >= 0))
    for h in range(z.heads):
        at = slice(h * z.width, (h + 1) * z.width)
        column = rows_ref[pl.ds(h, tokens, stride=z.heads), :]
        old = old_ref[:, at].astype(jnp.float32)
        value = jnp.where(filled, column, old).astype(jnp.bfloat16)
        out_ref[:, at] = value
        last_ref[:, at] = value
    for write in writes:
        write.wait()


def settle(mig_dest, mig_len, got, tail_q, tail_kv, attention, sizes, deps, **fetch):
    z = sizes
    tokens = z.insts * z.steps
    last = attention.shape[0] // tokens - 1
    spec = pl.BlockSpec((tokens, attention.shape[1]), lambda i: (last, 0))
    cache = (z.slots, z.mig_blocks * z.block, 2 * z.width)
    return run(
        functools.partial(settle_kernel, sizes=z),
        [mig_dest, mig_len], [got, tail_q, tail_kv, attention],
        [HBM, VMEM, VMEM, spec],
        deps,
        [
            jax.ShapeDtypeStruct(attention.shape, jnp.bfloat16),
            jax.ShapeDtypeStruct((tokens, attention.shape[1]), jnp.bfloat16),
            jax.ShapeDtypeStruct((1, z.cap) + cache, jnp.bfloat16),
        ],
        [spec, VMEM, ANY], "settle", z, grid=(1,),
        scratch=[
            pltpu.VMEM((z.insts * z.per, z.width), jnp.float32),
            pltpu.VMEM((z.cap,) + got.shape[1:], jnp.bfloat16),
            pltpu.VMEM((z.cap,) + cache, jnp.bfloat16),
            pltpu.SemaphoreType.DMA((2, z.cap)),
        ],
        aliases={5: 0}, **fetch,
    )


def project_kernel(ready, launch, attention, *refs, first, tokens, count, added, joined, sizes):
    launch()
    weights, extra, out_refs = refs[:count], refs[count : count + added], refs[count + added :]
    width = sizes.quarter
    tile = min(width, 256)
    for n, weight in enumerate(weights):

        def one(j, carry, n=n, weight=weight):
            at = pl.ds(pl.multiple_of(j * tile, tile), tile)
            to = pl.ds(pl.multiple_of(n * width + j * tile, tile), tile)
            result = dot(attention[first : first + tokens, :], weight[:, at])
            if added == 1:
                result = result + extra[0][:, to].astype(jnp.float32)
            elif added:
                result = result + extra[n][:, at].astype(jnp.float32)
            if joined:
                out_refs[0][:, to] = result.astype(out_refs[0].dtype)
            else:
                out_refs[n][:, at] = result.astype(out_refs[n].dtype)
            return carry

        lax.fori_loop(0, width // tile, one, 0)


def project(attention, weights, mates, joined, dtype, sizes, name, deps, place=None, **fetch):
    attention, first, tokens = attention
    count = len(weights)
    if place is not None:
        shapes = [place((tokens, count * sizes.quarter), dtype)]
    elif joined:
        shapes = [jax.ShapeDtypeStruct((tokens, count * sizes.quarter), dtype)]
    else:
        shapes = [jax.ShapeDtypeStruct((tokens, sizes.quarter), dtype)] * count
    operands = [attention] + weights + mates
    return run(
        functools.partial(
            project_kernel, first=first, tokens=tokens, count=count, added=len(mates),
            joined=joined, sizes=sizes,
        ),
        [], operands, [VMEM] * len(operands), deps, shapes, [VMEM] * len(shapes), name, sizes,
        **fetch,
    )


def final_kernel(ready, launch, attention, *refs, count, streamed, mates, fars, sizes):
    z = sizes
    refs = list(refs)

    def take(n):
        taken = refs[:n]
        del refs[:n]
        return taken

    weights, extra = take(count), take(mates)
    low, high, second, late = take(fars), take(fars), take(fars), take(fars)
    source = take(bool(streamed))
    (out_hbm,) = take(1)
    block_ref, block_sems = take(2)
    copies = [None] * count
    for n, piece in enumerate(streamed):
        begin = pl.multiple_of(piece_columns(piece, z), LANES)
        copy = pltpu.make_async_copy(
            source[0].at[:, pl.ds(begin, z.quarter)], refs[0].at[n], refs[1].at[n]
        )
        copy.start()
        copies.append(copy)
        weights.append(refs[0].at[n])
    tile = min(z.quarter, 256)
    writes = []
    for n, (weight, copy) in enumerate(zip(weights, copies)):
        if copy is not None:
            copy.wait()

        def one(j, carry, n=n, weight=weight):
            start = pl.multiple_of(j * tile, tile)
            at = pl.ds(start, tile)
            whole = pl.ds(n * z.quarter + start, tile)
            half = pl.ds((n % 2) * z.quarter + start, tile)
            sums = dot(attention[...], weight[:, at]) + extra[n][:, at].astype(jnp.float32)
            for k in range(fars):
                rows = late[k].shape[0]
                arrived = jnp.concatenate(
                    [
                        (low if n < 2 else high)[k][:, half],
                        second[k][:-rows, whole],
                        late[k][:, whole],
                    ],
                    axis=0,
                )
                sums = sums + arrived.astype(jnp.float32)
            block_ref[n, at, :] = sums.T.astype(jnp.bfloat16)
            return carry

        lax.fori_loop(0, z.quarter // tile, one, 0)
        write = pltpu.make_async_copy(
            block_ref.at[n], out_hbm.at[pl.ds(n * z.quarter, z.quarter)], block_sems.at[n]
        )
        write.start()
        writes.append(write)
    for write in writes:
        write.wait()


def final(attention, weights, streamed, out_weight, mates, low, high, second, late, sizes, deps):
    z = sizes
    tokens = attention.shape[0]
    operands = [attention] + weights + mates + low + high + second + late + [out_weight]
    specs = [VMEM] * (len(operands) - 1) + [HBM]
    result, _ = run(
        functools.partial(
            final_kernel, count=len(weights), streamed=streamed, mates=len(mates),
            fars=len(low), sizes=z,
        ),
        [], operands, specs, deps,
        [jax.ShapeDtypeStruct((z.features, tokens), jnp.bfloat16)], [ANY], "final", z,
        scratch=[
            pltpu.VMEM((4, z.quarter, tokens), jnp.bfloat16), pltpu.SemaphoreType.DMA((4,)),
            pltpu.VMEM((len(streamed), z.depth, z.quarter), jnp.bfloat16),
            pltpu.SemaphoreType.DMA((len(streamed),)),
        ],
    )
    return result[0]


def shards(
    res_pool,
    res_table,
    res_len,
    out_pool,
    src_table,
    mig_len,
    mig_dest,
    queries,
    new_kv,
    out_weight,
):
    z = Sizes(queries, res_pool, res_table, src_table, mig_dest, out_weight)
    tps, chips = z.tps, z.chips
    table = res_table[0].T
    out_weight, res_pool, out_pool, new_kv, query_rows, table, res_len, src_table, mig_dest, mig_len = (
        pltpu.with_memory_space_constraint(x, pltpu.HBM)
        for x in (
            out_weight, res_pool, out_pool, new_kv, queries.reshape(z.batch * z.per, z.width),
            table, res_len, src_table, mig_dest, mig_len,
        )
    )
    to_mate = [(i, i + 1 - 2 * (i % CORES)) for i in range(tps)]
    far = range(1, chips)
    held = {}

    def mate_of(x):
        return lax.ppermute(x, "tp", to_mate)

    def across(x, ahead):
        shift = ahead * CORES
        return lax.ppermute(x, "tp", [(i, (i + shift) % tps) for i in range(tps)])

    def bringing(pieces):
        return dict(pieces=pieces, weight=out_weight)

    def gives(ks, parts):
        return [(k, False, part) for k in ks for part in parts]

    def keeps(ks, parts):
        return [(k, True, part) for k in ks for part in parts]

    def hold(pieces, arrays):
        held.update(zip(pieces, arrays))

    def give(attention, ks, parts, name, deps, pieces=(), joined=False):
        weights = [held[piece] for piece in gives(ks, parts)]
        results, new = project(
            attention, weights, [], joined, jnp.bfloat16, z, name, deps, **bringing(pieces)
        )
        hold(pieces, new)
        return results[0], [mate_of(result) for result in results]

    def keep(attention, ks, parts, mates, name, deps, pieces=(), dtype=jnp.bfloat16, place=None):
        results = []
        for n, k in enumerate(ks):
            weights = [held[piece] for piece in keeps([k], parts)]
            if len(mates) == 1:
                width = mates[0].shape[1] // len(ks)
                now = [mates[0][:, n * width : (n + 1) * width] if len(ks) > 1 else mates[0]]
            else:
                now = mates[n * len(parts) : (n + 1) * len(parts)]
            bring = pieces if n == 0 else ()
            result, new = project(
                attention, weights, now, True, dtype, z, name, deps, place, **bringing(bring)
            )
            hold(bring, new)
            deps = [result[0]]
            results.append(result[0])
        return results

    def sent(results):
        return [across(result, k) for k, result in zip(far, results)]

    half = z.batch // 2
    low, high, every = (0, 1), (2, 3), (0, 1, 2, 3)

    sends, tail_q, tail_kv = pack(src_table, mig_dest, out_pool, query_rows, new_kv, z)
    arriving = lax.all_to_all(sends, "inst", split_axis=0, concat_axis=0, tiled=True)

    tokens = half * z.steps
    pieces = gives(far, low) + keeps(far, low) + gives(far, high)
    rows, new = attend(
        table, res_len, query_rows, new_kv, res_pool, None, 0, half, z, [sends],
        **bringing(pieces),
    )
    hold(pieces, new)
    a = (rows, 0, tokens)
    given, mates_low = give(a, far, low, "give", [], keeps(far, high))
    given, mates_high = give(a, far, high, "give", [given])
    kept = keep(a, far, low, mates_low, "keep", [given])
    got_low = sent(kept)
    kept = keep(a, far, high, mates_high, "keep", kept[-1:])
    got_high = sent(kept)
    rows, _ = attend(
        table, res_len, query_rows, new_kv, res_pool, rows, half, half, z, kept[-1:],
    )
    b = (rows, tokens, tokens)
    given, mates = give(b, far, every, "give", [])
    kept = keep(b, far, every, mates, "keep", [given] + got_low)
    got_second = sent(kept)

    pieces = gives(far, every) + keeps(far, (0,))
    tail_q, tail_kv = (
        pltpu.with_memory_space_constraint(x, pltpu.HBM) for x in (tail_q, tail_kv)
    )
    (rows, last, arrived), new = settle(
        mig_dest, mig_len, arriving, tail_q, tail_kv, rows, z, kept[-1:] + got_high,
        **bringing(pieces),
    )
    hold(pieces, new)
    late, whole = (last, 0, last.shape[0]), (rows, 0, 2 * tokens)
    given, mates = give(late, far, every, "give_last", [], gives([0], low), joined=True)
    given, mates_low = give(whole, [0], low, "give_own", [given], keeps(far, (1, 2, 3)))
    kept = keep(late, far, every, mates, "keep_last", [given], gives([0], high))
    got_late = sent(kept)
    pieces = keeps([0], (0, 1, 2))
    given, mates_high = give(whole, [0], high, "give_own", kept[-1:], pieces)
    weights = [held[piece] for piece in pieces]
    hidden = final(
        rows, weights, keeps([0], (3,)), out_weight, mates_low + mates_high, got_low, got_high,
        got_second, got_late, z, [given],
    )
    return (arrived, hidden)


def solution(mesh):
    placed = (
        P(("groups", "inst"), "tp", None, None, None),
        P(("groups", "inst"), None, None),
        P(("groups", "inst"), None),
        P(("groups", "inst"), "tp", None, None, None),
        P(("groups", "inst"), None, None),
        P("groups"),
        P("groups"),
        P(("groups", "inst"), None, "tp", None),
        P(("groups", "inst"), None, "tp", None),
        P("tp", None),
    )
    return jax.shard_map(
        shards,
        mesh=mesh,
        in_specs=placed,
        out_specs=(P(("groups", "inst"), None, "tp", None, None), P("tp", ("groups", "inst"))),
        check_vma=False,
    )
```

```python
import functools
import math

import jax
import jax.numpy as jnp
from jax import lax
from jax.experimental import pallas as pl
from jax.experimental.pallas import tpu as pltpu
from jax.sharding import PartitionSpec as P

CORES = 2
LOW = -1e30
MIB = 1 << 20
LANES = 128
GROUP = 16
TOGETHER = 8
LARGE_FIRST = 12
FETCHING = 16


def dot_t(left, right):
    return lax.dot_general(
        left, right, (((1,), (1,)), ((), ())), preferred_element_type=jnp.float32
    )


def row_plan(dest_ref, inst, cap):
    requests = [jnp.int32(-1)] * cap
    seen = jnp.int32(0)
    for g in range(dest_ref.shape[0]):
        here = dest_ref[g] == inst
        requests = [jnp.where(here & (seen == a), g, requests[a]) for a in range(cap)]
        seen = seen + here.astype(jnp.int32)
    return requests


VMEM = pl.BlockSpec(memory_space=pltpu.VMEM)
ANY = pl.BlockSpec(memory_space=pl.ANY)
HBM = pl.BlockSpec(memory_space=pltpu.HBM)


class Sizes:
    def __init__(self, queries, res_pool, res_table, src_table, mig_dest, out_weight):
        self.batch, self.steps, self.heads, self.width = queries.shape
        self.slots = res_pool.shape[1]
        self.block = res_pool.shape[3]
        self.resident, self.blocks = res_table.shape[1:]
        self.mig_per, self.mig_blocks = src_table.shape[1:]
        self.requests = mig_dest.shape[0]
        self.insts = lax.axis_size("inst")
        self.tps = lax.axis_size("tp")
        self.chips = self.tps // CORES
        self.cap = self.insts - 1
        self.per = self.steps * self.heads
        self.per_kv = self.steps * self.slots
        self.depth = out_weight.shape[0]
        self.features = out_weight.shape[1] // self.tps
        self.quarter = self.features // 4
        self.tail_q = self.insts * self.per
        self.tail_kv = self.insts * self.per_kv


def piece_columns(piece, sizes):
    ahead, mine, part = piece
    tp = lax.axis_index("tp")
    core = lax.rem(tp, CORES)
    chip = lax.rem(tp // CORES + ahead, sizes.chips)
    owner = chip * CORES + (core if mine else 1 - core)
    return owner * sizes.features + part * sizes.quarter


def run(kernel, tables, operands, in_specs, deps, out_shapes, out_specs, name, sizes,
        pieces=(), weight=None, limit=16, grid=(), scratch=(), aliases=None):
    inputs, outputs, many = len(operands), len(out_shapes), len(tables)
    count = len(deps)
    fetches = len(pieces)
    extra_in = [weight] if fetches else []
    limit = max(limit, FETCHING) if fetches else limit

    def call(*refs):
        table_in, refs = refs[:many], refs[many:]
        own_in = refs[:inputs]
        position = inputs + len(extra_in) + count
        own_out = refs[position : position + outputs]
        fetched = refs[position + outputs : position + outputs + fetches]
        rest = list(refs[position + outputs + fetches :])
        copies, reads = [], []
        if fetches:
            source, sems = refs[inputs], rest.pop()
            for n, piece in enumerate(pieces):
                first = pl.multiple_of(piece_columns(piece, sizes), LANES)
                copies.append(
                    pltpu.make_async_copy(
                        source.at[:, pl.ds(first, sizes.quarter)], fetched[n], sems.at[n]
                    )
                )
        table_refs = []
        if many:
            sems = rest.pop()
            table_refs = rest[len(rest) - many :]
            rest = rest[: len(rest) - many]
            reads = [
                pltpu.make_async_copy(source, target, sems.at[n])
                for n, (source, target) in enumerate(zip(table_in, table_refs))
            ]

        def ready():
            for read in reads:
                read.wait()

        def launch():
            for copy in copies:
                copy.start()

        def each(step, action):
            if not grid:
                action()
            else:
                pl.when(pl.program_id(0) == step)(action)

        def begin():
            for read in reads:
                read.start()

        def end():
            for copy in copies:
                copy.wait()

        if reads:
            each(0, begin)
        kernel(ready, launch, *table_refs, *own_in, *own_out, *rest)
        if copies:
            each(grid[0] - 1 if grid else 0, end)

    result = pl.pallas_call(
        call,
        grid_spec=pltpu.PrefetchScalarGridSpec(
            num_scalar_prefetch=0,
            grid=grid,
            in_specs=[HBM] * many + list(in_specs) + [HBM] * len(extra_in) + [ANY] * count,
            out_specs=list(out_specs) + [ANY] * fetches,
            scratch_shapes=list(scratch)
            + [pltpu.SMEM(t.shape, t.dtype) for t in tables]
            + ([pltpu.SemaphoreType.DMA((many,))] if many else [])
            + ([pltpu.SemaphoreType.DMA((fetches,))] if fetches else []),
        ),
        out_shape=list(out_shapes)
        + [pltpu.VMEM((sizes.depth, sizes.quarter), jnp.bfloat16)] * fetches,
        input_output_aliases=aliases or {},
        compiler_params=pltpu.CompilerParams(vmem_limit_bytes=limit * MIB),
        cost_estimate=pl.CostEstimate(flops=0, bytes_accessed=1024, transcendentals=0),
        name=name,
    )(*tables, *operands, *extra_in, *deps)
    return result[:outputs], result[outputs:]


def pack_kernel(
    ready, launch, table_ref, dest_ref, pool_ref, query_ref, kv_ref, send_hbm, tail_q_ref,
    tail_kv_ref, pack_ref, sems, *, sizes
):
    inst = lax.axis_index("inst")
    ready()
    copies = []
    for m in range(sizes.mig_per):
        dest = dest_ref[inst * sizes.mig_per + m]

        def copy_block(b, carry, m=m):
            block = table_ref[0, m, b]
            for s in range(sizes.slots):
                pack_ref[m, s, b] = pool_ref[0, s, block]
            return carry

        lax.fori_loop(0, sizes.mig_blocks, copy_block, 0, unroll=8)
        copies.append(pltpu.make_async_copy(pack_ref.at[m], send_hbm.at[dest], sems.at[m]))
        copies[-1].start()
    tail_q_ref[...] = query_ref[...]
    tail_kv_ref[...] = kv_ref[...].reshape(sizes.tail_kv, 2 * sizes.width)
    for copy in copies:
        copy.wait()


def pack(src_table, mig_dest, out_pool, query_rows, new_kv, sizes):
    z = sizes
    last_q = query_rows.shape[0] // z.tail_q - 1
    last_kv = z.batch // z.insts - 1
    request = (z.slots, z.mig_blocks, z.block, 2 * z.width)
    result, _ = run(
        functools.partial(pack_kernel, sizes=z),
        [src_table, mig_dest], [out_pool, query_rows, new_kv],
        [
            VMEM,
            pl.BlockSpec((z.tail_q, z.width), lambda i: (last_q, 0)),
            pl.BlockSpec((z.insts,) + new_kv.shape[1:], lambda i: (last_kv, 0, 0, 0)),
        ],
        [],
        [
            pltpu.HBM((z.insts,) + request, out_pool.dtype),
            pltpu.HBM((z.tail_q, z.width), out_pool.dtype),
            pltpu.HBM((z.tail_kv, 2 * z.width), out_pool.dtype),
        ],
        [ANY, VMEM, VMEM], "pack", z, limit=60, grid=(1,),
        scratch=[
            pltpu.VMEM((z.mig_per,) + request, out_pool.dtype),
            pltpu.SemaphoreType.DMA((z.mig_per,)),
        ],
    )
    return result


def fresh_code(rows, keys, sizes):
    index = lax.broadcasted_iota(jnp.int32, (rows, keys), 0)
    key = lax.broadcasted_iota(jnp.int32, (rows, keys), 1)
    step = index // sizes.heads
    slot = lax.rem(index, sizes.heads) // (sizes.heads // sizes.slots)
    in_row = lax.rem(key, sizes.per_kv)
    seen = (in_row // sizes.slots <= step) & (lax.rem(in_row, sizes.slots) == slot)
    return jnp.where(seen, key // sizes.per_kv, -1)


def slot_index(extent, sizes):
    index = lax.broadcasted_iota(jnp.int32, (sizes.per, extent), 0)
    return lax.rem(index, sizes.heads) // (sizes.heads // sizes.slots)


def own_scores(scores, slot_of, slots):
    extent = scores.shape[1] // slots
    own = scores[:, :extent]
    for s in range(1, slots):
        own = jnp.where(slot_of == s, scores[:, s * extent : (s + 1) * extent], own)
    return own


def weigh(own, length, fresh, fresh_seen, scale):
    place = lax.broadcasted_iota(jnp.int32, own.shape, 1)
    own = jnp.where(place < length, own, LOW)
    fresh = jnp.where(fresh_seen, fresh, LOW)
    if own.shape == fresh.shape:
        largest = jnp.max(jnp.maximum(own, fresh), axis=1, keepdims=True)
    else:
        largest = jnp.maximum(
            jnp.max(own, axis=1, keepdims=True), jnp.max(fresh, axis=1, keepdims=True)
        )
    return jnp.exp2((own - largest) * scale), jnp.exp2((fresh - largest) * scale)


def spread(own, slot_of, slots):
    if slots == 1:
        return own.astype(jnp.bfloat16)
    parts = [jnp.where(slot_of == s, own, 0.0) for s in range(slots)]
    return jnp.concatenate(parts, axis=1).astype(jnp.bfloat16)


def gather_blocks(pool_ref, slots, ids):
    tiles = [pool_ref[0, s, block] for s in range(slots) for block in ids]
    return jnp.concatenate(tiles, axis=0)


def with_ones(values):
    return jnp.concatenate([values, jnp.ones_like(values)], axis=1)


def dot(left, right):
    return jnp.dot(left, right, preferred_element_type=jnp.float32)


def attend_kernel(
    ready, launch, table_ref, len_ref, query_hbm, kv_hbm, pool_ref, *refs, first_row,
    steps_in_all, sizes,
):
    z = sizes
    out_ref, query_all, kv_all, fresh_ref, pf_ref, blend_ref, done_ref, sems = refs
    width, per = z.width, z.per
    rows = GROUP
    step = pl.program_id(0)
    extent = z.blocks * z.block
    start = first_row + step * rows
    scale = math.log2(math.e) / math.sqrt(width)

    def copies(n):
        begin = first_row + n * rows
        return (
            pltpu.make_async_copy(
                query_hbm.at[pl.ds(pl.multiple_of(begin * per, rows * per), rows * per)],
                query_all.at[n], sems.at[0, n],
            ),
            pltpu.make_async_copy(kv_hbm.at[pl.ds(begin, rows)], kv_all.at[n], sems.at[1, n]),
        )

    @pl.when(step == 0)
    def _():
        for n in range(steps_in_all):
            for copy in copies(n):
                copy.start()
        launch()
        ready()

    for copy in copies(step):
        copy.wait()

    query_ref = query_all.at[step]
    new_kv = kv_all[step].reshape(rows * z.per_kv, 2 * width)
    fresh_ref[...] = dot_t(query_ref[...], new_kv[:, :width])
    code = fresh_code(per, rows * z.per_kv, z)
    slot_of = slot_index(extent, z)
    together = min(TOGETHER, rows)
    for begin in range(0, rows, together):
        group = range(begin, begin + together)
        at = [slice(r * per, (r + 1) * per) for r in group]
        known = [jnp.minimum(start + r, z.resident - 1) for r in group]
        length = [
            jnp.where(start + r < z.resident, len_ref[0, k], 0) for r, k in zip(group, known)
        ]
        both = [
            gather_blocks(pool_ref, z.slots, [table_ref[j, k] for j in range(z.blocks)])
            for k in known
        ]
        fresh = [fresh_ref[a, :] for a in at]
        scores = [dot_t(query_ref[a, :], b[:, :width]) for a, b in zip(at, both)]
        weights = [
            weigh(own_scores(s, slot_of, z.slots), n, f, code == r, scale)
            for s, n, f, r in zip(scores, length, fresh, group)
        ]
        context = [
            dot(spread(w[0], slot_of, z.slots), with_ones(b[:, width:]))
            for w, b in zip(weights, both)
        ]
        for a, c, w in zip(at, context, weights):
            blend_ref[a, :] = c
            pf_ref[a, :] = w[1].astype(jnp.bfloat16)

    done = blend_ref[...] + dot(pf_ref[...], with_ones(new_kv[:, width:]))
    done_ref[...] = done[:, :width] / done[:, width:]
    for h in range(z.heads):
        column = done_ref[pl.ds(h, rows * z.steps, stride=z.heads), :]
        out_ref[:, h * width : (h + 1) * width] = column.astype(jnp.bfloat16)


def attend(table, lengths, queries, new_kv, pool, into, first_row, rows, sizes, deps, limit=12,
           **fetch):
    z = sizes
    groups = rows // GROUP
    first = first_row // GROUP
    tokens = z.batch * z.steps
    aliases = {}
    if into is not None:
        deps = [into] + deps
        aliases = {5 + (1 if fetch else 0): 0}
    result, pieces = run(
        functools.partial(
            attend_kernel, first_row=first_row, steps_in_all=groups, sizes=z
        ),
        [table, lengths],
        [queries, new_kv, pool],
        [HBM, HBM, VMEM],
        deps,
        [jax.ShapeDtypeStruct((tokens, z.heads * z.width), jnp.bfloat16)],
        [pl.BlockSpec((GROUP * z.steps, z.heads * z.width), lambda i: (first + i, 0))],
        "attend", z, limit=limit,
        grid=(groups,),
        scratch=[
            pltpu.VMEM((groups, GROUP * z.per, z.width), jnp.bfloat16),
            pltpu.VMEM((groups, GROUP) + new_kv.shape[1:], jnp.bfloat16),
            pltpu.VMEM((GROUP * z.per, GROUP * z.per_kv), jnp.float32),
            pltpu.VMEM((GROUP * z.per, GROUP * z.per_kv), jnp.bfloat16),
            pltpu.VMEM((GROUP * z.per, 2 * z.width), jnp.float32),
            pltpu.VMEM((GROUP * z.per, z.width), jnp.float32),
            pltpu.SemaphoreType.DMA((2, groups)),
        ],
        aliases=aliases, **fetch,
    )
    return result[0], pieces


def settle_kernel(
    ready, launch, dest_ref, len_ref, got_hbm, query_ref, kv_ref, old_ref, out_ref, last_ref,
    arrived_hbm, rows_ref, got_ref, keep_ref, sems, *, sizes
):
    z = sizes
    ready()
    inst = lax.axis_index("inst")
    requests = row_plan(dest_ref, inst, z.cap)
    known = [jnp.maximum(request, 0) for request in requests]
    extent = z.mig_blocks * z.block
    reads = [
        pltpu.make_async_copy(got_hbm.at[known[a] // z.mig_per], got_ref.at[a], sems.at[0, a])
        for a in range(z.cap)
    ]
    writes = [
        pltpu.make_async_copy(keep_ref.at[a], arrived_hbm.at[0, a], sems.at[1, a])
        for a in range(z.cap)
    ]
    for read in reads:
        read.start()
    launch()
    new_kv = kv_ref[...]
    code = fresh_code(z.per, z.tail_kv, z)
    slot_of = slot_index(extent, z)
    scale = math.log2(math.e) / math.sqrt(z.width)
    tokens = z.insts * z.steps
    row = lax.broadcasted_iota(jnp.int32, (tokens, z.width), 0) // z.steps
    place = lax.broadcasted_iota(jnp.int32, (z.block, 2 * z.width), 0)
    filled = row < 0
    rows_ref[: z.per, :] = jnp.zeros((z.per, z.width), jnp.float32)
    for a in range(z.cap):
        length = jnp.where(requests[a] >= 0, len_ref[known[a]], 0)
        reads[a].wait()

        def one(b, carry, a=a, length=length):
            inside = place + b * z.block < length
            at = pl.ds(pl.multiple_of(b * z.block, z.block), z.block)
            for s in range(z.slots):
                value = got_ref[a, s, b].astype(jnp.float32)
                keep_ref[a, s, at, :] = jnp.where(inside, value, 0.0).astype(jnp.bfloat16)
            return carry

        lax.fori_loop(0, z.mig_blocks, one, 0, unroll=8)
        writes[a].start()
        at = slice((a + 1) * z.per, (a + 2) * z.per)
        both = jnp.concatenate([keep_ref[a, s] for s in range(z.slots)], axis=0)
        own = own_scores(dot_t(query_ref[at, :], both[:, : z.width]), slot_of, z.slots)
        fresh = dot_t(query_ref[at, :], new_kv[:, : z.width])
        own, fresh = weigh(own, length, fresh, code == a + 1, scale)
        done = dot(spread(own, slot_of, z.slots), with_ones(both[:, z.width :]))
        done = done + dot(fresh.astype(jnp.bfloat16), with_ones(new_kv[:, z.width :]))
        rows_ref[at, :] = done[:, : z.width] / done[:, z.width :]
        filled = filled | ((row == a + 1) & (requests[a] >= 0))
    for h in range(z.heads):
        at = slice(h * z.width, (h + 1) * z.width)
        column = rows_ref[pl.ds(h, tokens, stride=z.heads), :]
        old = old_ref[:, at].astype(jnp.float32)
        value = jnp.where(filled, column, old).astype(jnp.bfloat16)
        out_ref[:, at] = value
        last_ref[:, at] = value
    for write in writes:
        write.wait()


def settle(mig_dest, mig_len, got, tail_q, tail_kv, attention, sizes, deps, **fetch):
    z = sizes
    tokens = z.insts * z.steps
    last = attention.shape[0] // tokens - 1
    spec = pl.BlockSpec((tokens, attention.shape[1]), lambda i: (last, 0))
    cache = (z.slots, z.mig_blocks * z.block, 2 * z.width)
    return run(
        functools.partial(settle_kernel, sizes=z),
        [mig_dest, mig_len], [got, tail_q, tail_kv, attention],
        [HBM, VMEM, VMEM, spec],
        deps,
        [
            jax.ShapeDtypeStruct(attention.shape, jnp.bfloat16),
            jax.ShapeDtypeStruct((tokens, attention.shape[1]), jnp.bfloat16),
            jax.ShapeDtypeStruct((1, z.cap) + cache, jnp.bfloat16),
        ],
        [spec, VMEM, ANY], "settle", z, grid=(1,),
        scratch=[
            pltpu.VMEM((z.insts * z.per, z.width), jnp.float32),
            pltpu.VMEM((z.cap,) + got.shape[1:], jnp.bfloat16),
            pltpu.VMEM((z.cap,) + cache, jnp.bfloat16),
            pltpu.SemaphoreType.DMA((2, z.cap)),
        ],
        aliases={5: 0}, **fetch,
    )


def project_kernel(ready, launch, attention, *refs, first, tokens, count, added, joined, sizes):
    launch()
    weights, extra, out_refs = refs[:count], refs[count : count + added], refs[count + added :]
    width = sizes.quarter
    tile = min(width, 256)
    for n, weight in enumerate(weights):

        def one(j, carry, n=n, weight=weight):
            at = pl.ds(pl.multiple_of(j * tile, tile), tile)
            to = pl.ds(pl.multiple_of(n * width + j * tile, tile), tile)
            result = dot(attention[first : first + tokens, :], weight[:, at])
            if added == 1:
                result = result + extra[0][:, to].astype(jnp.float32)
            elif added:
                result = result + extra[n][:, at].astype(jnp.float32)
            if joined:
                out_refs[0][:, to] = result.astype(out_refs[0].dtype)
            else:
                out_refs[n][:, at] = result.astype(out_refs[n].dtype)
            return carry

        lax.fori_loop(0, width // tile, one, 0)


def project(attention, weights, mates, joined, dtype, sizes, name, deps, place=None, **fetch):
    attention, first, tokens = attention
    count = len(weights)
    if place is not None:
        shapes = [place((tokens, count * sizes.quarter), dtype)]
    elif joined:
        shapes = [jax.ShapeDtypeStruct((tokens, count * sizes.quarter), dtype)]
    else:
        shapes = [jax.ShapeDtypeStruct((tokens, sizes.quarter), dtype)] * count
    operands = [attention] + weights + mates
    return run(
        functools.partial(
            project_kernel, first=first, tokens=tokens, count=count, added=len(mates),
            joined=joined, sizes=sizes,
        ),
        [], operands, [VMEM] * len(operands), deps, shapes, [VMEM] * len(shapes), name, sizes,
        **fetch,
    )


def finish_kernel(ready, launch, own_low, own_high, *refs, fars, sizes):
    z = sizes
    refs = list(refs)

    def take(n):
        taken = refs[:n]
        del refs[:n]
        return taken

    low, high, second, late = take(fars), take(fars), take(fars), take(fars)
    out_hbm, block_ref, sems = refs
    tile = min(z.quarter, 256)
    writes = []
    for n in range(4):

        def one(j, carry, n=n):
            start = pl.multiple_of(j * tile, tile)
            at = pl.ds(n * z.quarter + start, tile)
            half = pl.ds((n % 2) * z.quarter + start, tile)
            sums = (own_low if n < 2 else own_high)[:, half]
            for k in range(fars):
                rows = late[k].shape[0]
                arrived = jnp.concatenate(
                    [
                        (low if n < 2 else high)[k][:, half],
                        second[k][:-rows, at],
                        late[k][:, at],
                    ],
                    axis=0,
                )
                sums = sums + arrived.astype(jnp.float32)
            block_ref[n, pl.ds(start, tile), :] = sums.T.astype(jnp.bfloat16)
            return carry

        lax.fori_loop(0, z.quarter // tile, one, 0)
        write = pltpu.make_async_copy(
            block_ref.at[n], out_hbm.at[pl.ds(n * z.quarter, z.quarter)], sems.at[n]
        )
        write.start()
        writes.append(write)
    for write in writes:
        write.wait()


def finish(own, low, high, second, late, sizes, deps):
    z = sizes
    tokens = own[0].shape[0]
    operands = own + low + high + second + late
    result, _ = run(
        functools.partial(finish_kernel, fars=len(low), sizes=z),
        [], operands, [VMEM] * len(operands), deps,
        [jax.ShapeDtypeStruct((z.features, tokens), jnp.bfloat16)], [ANY], "finish", z,
        scratch=[
            pltpu.VMEM((4, z.quarter, tokens), jnp.bfloat16), pltpu.SemaphoreType.DMA((4,))
        ],
    )
    return result[0]


def shards(
    res_pool,
    res_table,
    res_len,
    out_pool,
    src_table,
    mig_len,
    mig_dest,
    queries,
    new_kv,
    out_weight,
):
    z = Sizes(queries, res_pool, res_table, src_table, mig_dest, out_weight)
    tps, chips = z.tps, z.chips
    table = res_table[0].T
    out_weight, res_pool, out_pool, new_kv, query_rows, table, res_len, src_table, mig_dest, mig_len = (
        pltpu.with_memory_space_constraint(x, pltpu.HBM)
        for x in (
            out_weight, res_pool, out_pool, new_kv, queries.reshape(z.batch * z.per, z.width),
            table, res_len, src_table, mig_dest, mig_len,
        )
    )
    to_mate = [(i, i + 1 - 2 * (i % CORES)) for i in range(tps)]
    far = range(1, chips)
    held = {}

    def mate_of(x):
        return lax.ppermute(x, "tp", to_mate)

    def across(x, ahead):
        shift = ahead * CORES
        return lax.ppermute(x, "tp", [(i, (i + shift) % tps) for i in range(tps)])

    def bringing(pieces):
        return dict(pieces=pieces, weight=out_weight)

    def gives(ks, parts):
        return [(k, False, part) for k in ks for part in parts]

    def keeps(ks, parts):
        return [(k, True, part) for k in ks for part in parts]

    def hold(pieces, arrays):
        held.update(zip(pieces, arrays))

    def give(attention, ks, parts, name, deps, pieces=(), joined=False):
        weights = [held[piece] for piece in gives(ks, parts)]
        results, new = project(
            attention, weights, [], joined, jnp.bfloat16, z, name, deps, **bringing(pieces)
        )
        hold(pieces, new)
        return results[0], [mate_of(result) for result in results]

    def keep(attention, ks, parts, mates, name, deps, pieces=(), dtype=jnp.bfloat16, place=None):
        results = []
        for n, k in enumerate(ks):
            weights = [held[piece] for piece in keeps([k], parts)]
            if len(mates) == 1:
                width = mates[0].shape[1] // len(ks)
                now = [mates[0][:, n * width : (n + 1) * width] if len(ks) > 1 else mates[0]]
            else:
                now = mates[n * len(parts) : (n + 1) * len(parts)]
            bring = pieces if n == 0 else ()
            result, new = project(
                attention, weights, now, True, dtype, z, name, deps, place, **bringing(bring)
            )
            hold(bring, new)
            deps = [result[0]]
            results.append(result[0])
        return results

    def sent(results):
        return [across(result, k) for k, result in zip(far, results)]

    half = z.batch // 2
    low, high, every = (0, 1), (2, 3), (0, 1, 2, 3)

    sends, tail_q, tail_kv = pack(src_table, mig_dest, out_pool, query_rows, new_kv, z)
    arriving = lax.all_to_all(sends, "inst", split_axis=0, concat_axis=0, tiled=True)

    tokens = half * z.steps
    pieces = gives(far, low) + keeps(far, low) + gives(far, high)
    rows, new = attend(
        table, res_len, query_rows, new_kv, res_pool, None, 0, half, z, [sends],
        **bringing(pieces),
    )
    hold(pieces, new)
    a = (rows, 0, tokens)
    given, mates_low = give(a, far, low, "give", [], keeps(far, high))
    given, mates_high = give(a, far, high, "give", [given])
    kept = keep(a, far, low, mates_low, "keep", [given])
    got_low = sent(kept)
    kept = keep(a, far, high, mates_high, "keep", kept[-1:])
    got_high = sent(kept)
    rows, _ = attend(
        table, res_len, query_rows, new_kv, res_pool, rows, half, half, z, kept[-1:],
    )
    b = (rows, tokens, tokens)
    given, mates = give(b, far, every, "give", [])
    kept = keep(b, far, every, mates, "keep", [given] + got_low)
    got_second = sent(kept)

    tail_q, tail_kv = (
        pltpu.with_memory_space_constraint(x, pltpu.HBM) for x in (tail_q, tail_kv)
    )
    pieces = gives([0], low) + gives(far, (0,))
    (rows, last, arrived), new = settle(
        mig_dest, mig_len, arriving, tail_q, tail_kv, rows, z, kept[-1:] + got_high,
        **bringing(pieces),
    )
    hold(pieces, new)
    late, whole = (last, 0, last.shape[0]), (rows, 0, 2 * tokens)
    given, mates_low = give(whole, [0], low, "give_own", [], gives(far, (1, 2, 3)))
    given, mates = give(late, far, every, "give_last", [given], gives([0], high), joined=True)
    given, mates_high = give(whole, [0], high, "give_own", [given], keeps(far, every))
    kept = keep(late, far, every, mates, "keep_last", [given], keeps([0], low))
    got_late = sent(kept)
    own = keep(
        whole, [0], low, mates_low, "keep_own", kept[-1:], keeps([0], high), jnp.float32
    )
    own += keep(whole, [0], high, mates_high, "keep_own", own, (), jnp.float32)
    hidden = finish(own, got_low, got_high, got_second, got_late, z, [])
    return (arrived, hidden)


def solution(mesh):
    placed = (
        P(("groups", "inst"), "tp", None, None, None),
        P(("groups", "inst"), None, None),
        P(("groups", "inst"), None),
        P(("groups", "inst"), "tp", None, None, None),
        P(("groups", "inst"), None, None),
        P("groups"),
        P("groups"),
        P(("groups", "inst"), None, "tp", None),
        P(("groups", "inst"), None, "tp", None),
        P("tp", None),
    )
    return jax.shard_map(
        shards,
        mesh=mesh,
        in_specs=placed,
        out_specs=(P(("groups", "inst"), None, "tp", None, None), P("tp", ("groups", "inst"))),
        check_vma=False,
    )
```

```python
import functools
import math

import jax
import jax.numpy as jnp
from jax import lax
from jax.experimental import pallas as pl
from jax.experimental.pallas import tpu as pltpu
from jax.sharding import PartitionSpec as P

CORES = 2
LOW = -1e30
MIB = 1 << 20
LANES = 128
GROUP = 16
TOGETHER = 8
LARGE_FIRST = 12
FETCHING = 16


def dot_t(left, right):
    return lax.dot_general(
        left, right, (((1,), (1,)), ((), ())), preferred_element_type=jnp.float32
    )


def row_plan(dest_ref, inst, cap):
    requests = [jnp.int32(-1)] * cap
    seen = jnp.int32(0)
    for g in range(dest_ref.shape[0]):
        here = dest_ref[g] == inst
        requests = [jnp.where(here & (seen == a), g, requests[a]) for a in range(cap)]
        seen = seen + here.astype(jnp.int32)
    return requests


VMEM = pl.BlockSpec(memory_space=pltpu.VMEM)
ANY = pl.BlockSpec(memory_space=pl.ANY)
HBM = pl.BlockSpec(memory_space=pltpu.HBM)


class Sizes:
    def __init__(self, queries, res_pool, res_table, src_table, mig_dest, out_weight):
        self.batch, self.steps, self.heads, self.width = queries.shape
        self.slots = res_pool.shape[1]
        self.block = res_pool.shape[3]
        self.resident, self.blocks = res_table.shape[1:]
        self.mig_per, self.mig_blocks = src_table.shape[1:]
        self.requests = mig_dest.shape[0]
        self.insts = lax.axis_size("inst")
        self.tps = lax.axis_size("tp")
        self.chips = self.tps // CORES
        self.cap = self.insts - 1
        self.per = self.steps * self.heads
        self.per_kv = self.steps * self.slots
        self.depth = out_weight.shape[0]
        self.features = out_weight.shape[1] // self.tps
        self.quarter = self.features // 4
        self.tail_q = self.insts * self.per
        self.tail_kv = self.insts * self.per_kv


def piece_columns(piece, sizes):
    ahead, mine, part = piece
    tp = lax.axis_index("tp")
    core = lax.rem(tp, CORES)
    chip = lax.rem(tp // CORES + ahead, sizes.chips)
    owner = chip * CORES + (core if mine else 1 - core)
    return owner * sizes.features + part * sizes.quarter


def run(kernel, tables, operands, in_specs, deps, out_shapes, out_specs, name, sizes,
        pieces=(), weight=None, limit=16, grid=(), scratch=(), aliases=None):
    inputs, outputs, many = len(operands), len(out_shapes), len(tables)
    count = len(deps)
    fetches = len(pieces)
    extra_in = [weight] if fetches else []
    limit = max(limit, FETCHING) if fetches else limit

    def call(*refs):
        table_in, refs = refs[:many], refs[many:]
        own_in = refs[:inputs]
        position = inputs + len(extra_in) + count
        own_out = refs[position : position + outputs]
        fetched = refs[position + outputs : position + outputs + fetches]
        rest = list(refs[position + outputs + fetches :])
        copies, reads = [], []
        if fetches:
            source, sems = refs[inputs], rest.pop()
            for n, piece in enumerate(pieces):
                first = pl.multiple_of(piece_columns(piece, sizes), LANES)
                copies.append(
                    pltpu.make_async_copy(
                        source.at[:, pl.ds(first, sizes.quarter)], fetched[n], sems.at[n]
                    )
                )
        table_refs = []
        if many:
            sems = rest.pop()
            table_refs = rest[len(rest) - many :]
            rest = rest[: len(rest) - many]
            reads = [
                pltpu.make_async_copy(source, target, sems.at[n])
                for n, (source, target) in enumerate(zip(table_in, table_refs))
            ]

        def ready():
            for read in reads:
                read.wait()

        def launch():
            for copy in copies:
                copy.start()

        def each(step, action):
            if not grid:
                action()
            else:
                pl.when(pl.program_id(0) == step)(action)

        def begin():
            for read in reads:
                read.start()

        def end():
            for copy in copies:
                copy.wait()

        if reads:
            each(0, begin)
        kernel(ready, launch, *table_refs, *own_in, *own_out, *rest)
        if copies:
            each(grid[0] - 1 if grid else 0, end)

    result = pl.pallas_call(
        call,
        grid_spec=pltpu.PrefetchScalarGridSpec(
            num_scalar_prefetch=0,
            grid=grid,
            in_specs=[HBM] * many + list(in_specs) + [HBM] * len(extra_in) + [ANY] * count,
            out_specs=list(out_specs) + [ANY] * fetches,
            scratch_shapes=list(scratch)
            + [pltpu.SMEM(t.shape, t.dtype) for t in tables]
            + ([pltpu.SemaphoreType.DMA((many,))] if many else [])
            + ([pltpu.SemaphoreType.DMA((fetches,))] if fetches else []),
        ),
        out_shape=list(out_shapes)
        + [pltpu.VMEM((sizes.depth, sizes.quarter), jnp.bfloat16)] * fetches,
        input_output_aliases=aliases or {},
        compiler_params=pltpu.CompilerParams(vmem_limit_bytes=limit * MIB),
        cost_estimate=pl.CostEstimate(flops=0, bytes_accessed=1024, transcendentals=0),
        name=name,
    )(*tables, *operands, *extra_in, *deps)
    return result[:outputs], result[outputs:]


def pack_kernel(
    ready, launch, table_ref, dest_ref, pool_hbm, query_ref, kv_ref, send_hbm, tail_q_ref,
    tail_kv_ref, pool_ref, pack_ref, sems, *, sizes
):
    inst = lax.axis_index("inst")
    pool_copy = pltpu.make_async_copy(pool_hbm, pool_ref, sems.at[sizes.mig_per])
    pool_copy.start()
    ready()
    pool_copy.wait()
    copies = []
    for m in range(sizes.mig_per):
        dest = dest_ref[inst * sizes.mig_per + m]

        def copy_block(b, carry, m=m):
            block = table_ref[0, m, b]
            for s in range(sizes.slots):
                pack_ref[m, s, b] = pool_ref[0, s, block]
            return carry

        lax.fori_loop(0, sizes.mig_blocks, copy_block, 0, unroll=8)
        copies.append(pltpu.make_async_copy(pack_ref.at[m], send_hbm.at[dest], sems.at[m]))
        copies[-1].start()
    tail_q_ref[...] = query_ref[...]
    tail_kv_ref[...] = kv_ref[...].reshape(sizes.tail_kv, 2 * sizes.width)
    for copy in copies:
        copy.wait()


def pack(src_table, mig_dest, out_pool, query_rows, new_kv, sizes):
    z = sizes
    last_q = query_rows.shape[0] // z.tail_q - 1
    last_kv = z.batch // z.insts - 1
    request = (z.slots, z.mig_blocks, z.block, 2 * z.width)
    result, _ = run(
        functools.partial(pack_kernel, sizes=z),
        [src_table, mig_dest], [out_pool, query_rows, new_kv],
        [
            HBM,
            pl.BlockSpec((z.tail_q, z.width), lambda i: (last_q, 0)),
            pl.BlockSpec((z.insts,) + new_kv.shape[1:], lambda i: (last_kv, 0, 0, 0)),
        ],
        [],
        [
            pltpu.HBM((z.insts,) + request, out_pool.dtype),
            pltpu.HBM((z.tail_q, z.width), out_pool.dtype),
            pltpu.HBM((z.tail_kv, 2 * z.width), out_pool.dtype),
        ],
        [ANY, VMEM, VMEM], "pack", z, limit=60, grid=(1,),
        scratch=[
            pltpu.VMEM(out_pool.shape, out_pool.dtype),
            pltpu.VMEM((z.mig_per,) + request, out_pool.dtype),
            pltpu.SemaphoreType.DMA((z.mig_per + 1,)),
        ],
    )
    return result


def fresh_code(rows, keys, sizes):
    index = lax.broadcasted_iota(jnp.int32, (rows, keys), 0)
    key = lax.broadcasted_iota(jnp.int32, (rows, keys), 1)
    step = index // sizes.heads
    slot = lax.rem(index, sizes.heads) // (sizes.heads // sizes.slots)
    in_row = lax.rem(key, sizes.per_kv)
    seen = (in_row // sizes.slots <= step) & (lax.rem(in_row, sizes.slots) == slot)
    return jnp.where(seen, key // sizes.per_kv, -1)


def slot_index(extent, sizes):
    index = lax.broadcasted_iota(jnp.int32, (sizes.per, extent), 0)
    return lax.rem(index, sizes.heads) // (sizes.heads // sizes.slots)


def own_scores(scores, slot_of, slots):
    extent = scores.shape[1] // slots
    own = scores[:, :extent]
    for s in range(1, slots):
        own = jnp.where(slot_of == s, scores[:, s * extent : (s + 1) * extent], own)
    return own


def weigh(own, length, fresh, fresh_seen, scale):
    place = lax.broadcasted_iota(jnp.int32, own.shape, 1)
    own = jnp.where(place < length, own, LOW)
    fresh = jnp.where(fresh_seen, fresh, LOW)
    if own.shape == fresh.shape:
        largest = jnp.max(jnp.maximum(own, fresh), axis=1, keepdims=True)
    else:
        largest = jnp.maximum(
            jnp.max(own, axis=1, keepdims=True), jnp.max(fresh, axis=1, keepdims=True)
        )
    return jnp.exp2((own - largest) * scale), jnp.exp2((fresh - largest) * scale)


def spread(own, slot_of, slots):
    if slots == 1:
        return own.astype(jnp.bfloat16)
    parts = [jnp.where(slot_of == s, own, 0.0) for s in range(slots)]
    return jnp.concatenate(parts, axis=1).astype(jnp.bfloat16)


def gather_blocks(pool_ref, slots, ids):
    tiles = [pool_ref[0, s, block] for s in range(slots) for block in ids]
    return jnp.concatenate(tiles, axis=0)


def with_ones(values):
    return jnp.concatenate([values, jnp.ones_like(values)], axis=1)


def dot(left, right):
    return jnp.dot(left, right, preferred_element_type=jnp.float32)


def attend_kernel(
    ready, launch, table_ref, len_ref, query_hbm, kv_hbm, pool_ref, *refs, first_row,
    steps_in_all, sizes,
):
    z = sizes
    out_ref, query_all, kv_all, fresh_ref, pf_ref, blend_ref, done_ref, sems = refs
    width, per = z.width, z.per
    rows = GROUP
    step = pl.program_id(0)
    extent = z.blocks * z.block
    start = first_row + step * rows
    scale = math.log2(math.e) / math.sqrt(width)

    def copies(n):
        begin = first_row + n * rows
        return (
            pltpu.make_async_copy(
                query_hbm.at[pl.ds(pl.multiple_of(begin * per, rows * per), rows * per)],
                query_all.at[n], sems.at[0, n],
            ),
            pltpu.make_async_copy(kv_hbm.at[pl.ds(begin, rows)], kv_all.at[n], sems.at[1, n]),
        )

    @pl.when(step == 0)
    def _():
        for n in range(steps_in_all):
            for copy in copies(n):
                copy.start()
        launch()
        ready()

    for copy in copies(step):
        copy.wait()

    query_ref = query_all.at[step]
    new_kv = kv_all[step].reshape(rows * z.per_kv, 2 * width)
    fresh_ref[...] = dot_t(query_ref[...], new_kv[:, :width])
    code = fresh_code(per, rows * z.per_kv, z)
    slot_of = slot_index(extent, z)
    together = min(TOGETHER, rows)
    for begin in range(0, rows, together):
        group = range(begin, begin + together)
        at = [slice(r * per, (r + 1) * per) for r in group]
        known = [jnp.minimum(start + r, z.resident - 1) for r in group]
        length = [
            jnp.where(start + r < z.resident, len_ref[0, k], 0) for r, k in zip(group, known)
        ]
        both = [
            gather_blocks(pool_ref, z.slots, [table_ref[j, k] for j in range(z.blocks)])
            for k in known
        ]
        fresh = [fresh_ref[a, :] for a in at]
        scores = [dot_t(query_ref[a, :], b[:, :width]) for a, b in zip(at, both)]
        weights = [
            weigh(own_scores(s, slot_of, z.slots), n, f, code == r, scale)
            for s, n, f, r in zip(scores, length, fresh, group)
        ]
        context = [
            dot(spread(w[0], slot_of, z.slots), with_ones(b[:, width:]))
            for w, b in zip(weights, both)
        ]
        for a, c, w in zip(at, context, weights):
            blend_ref[a, :] = c
            pf_ref[a, :] = w[1].astype(jnp.bfloat16)

    done = blend_ref[...] + dot(pf_ref[...], with_ones(new_kv[:, width:]))
    done_ref[...] = done[:, :width] / done[:, width:]
    for h in range(z.heads):
        column = done_ref[pl.ds(h, rows * z.steps, stride=z.heads), :]
        out_ref[:, h * width : (h + 1) * width] = column.astype(jnp.bfloat16)


def attend(table, lengths, queries, new_kv, pool, into, first_row, rows, sizes, deps, limit=12,
           **fetch):
    z = sizes
    groups = rows // GROUP
    first = first_row // GROUP
    tokens = z.batch * z.steps
    aliases = {}
    if into is not None:
        deps = [into] + deps
        aliases = {5 + (1 if fetch else 0): 0}
    result, pieces = run(
        functools.partial(
            attend_kernel, first_row=first_row, steps_in_all=groups, sizes=z
        ),
        [table, lengths],
        [queries, new_kv, pool],
        [HBM, HBM, VMEM],
        deps,
        [jax.ShapeDtypeStruct((tokens, z.heads * z.width), jnp.bfloat16)],
        [pl.BlockSpec((GROUP * z.steps, z.heads * z.width), lambda i: (first + i, 0))],
        "attend", z, limit=limit,
        grid=(groups,),
        scratch=[
            pltpu.VMEM((groups, GROUP * z.per, z.width), jnp.bfloat16),
            pltpu.VMEM((groups, GROUP) + new_kv.shape[1:], jnp.bfloat16),
            pltpu.VMEM((GROUP * z.per, GROUP * z.per_kv), jnp.float32),
            pltpu.VMEM((GROUP * z.per, GROUP * z.per_kv), jnp.bfloat16),
            pltpu.VMEM((GROUP * z.per, 2 * z.width), jnp.float32),
            pltpu.VMEM((GROUP * z.per, z.width), jnp.float32),
            pltpu.SemaphoreType.DMA((2, groups)),
        ],
        aliases=aliases, **fetch,
    )
    return result[0], pieces


def settle_kernel(
    ready, launch, dest_ref, len_ref, got_hbm, query_ref, kv_ref, old_ref, out_ref, last_ref,
    arrived_hbm, rows_ref, got_ref, keep_ref, sems, *, sizes
):
    z = sizes
    inst = lax.axis_index("inst")
    extent = z.mig_blocks * z.block
    reads = [
        pltpu.make_async_copy(
            got_hbm.at[lax.rem(inst + k, z.insts)], got_ref.at[k - 1], sems.at[0, k - 1]
        )
        for k in range(1, z.insts)
    ]
    writes = [
        pltpu.make_async_copy(keep_ref.at[a], arrived_hbm.at[0, a], sems.at[1, a])
        for a in range(z.cap)
    ]
    for read in reads:
        read.start()
    launch()
    ready()
    requests = row_plan(dest_ref, inst, z.cap)
    known = [jnp.maximum(request, 0) for request in requests]
    new_kv = kv_ref[...]
    code = fresh_code(z.per, z.tail_kv, z)
    slot_of = slot_index(extent, z)
    scale = math.log2(math.e) / math.sqrt(z.width)
    tokens = z.insts * z.steps
    row = lax.broadcasted_iota(jnp.int32, (tokens, z.width), 0) // z.steps
    place = lax.broadcasted_iota(jnp.int32, (z.block, 2 * z.width), 0)
    filled = row < 0
    rows_ref[: z.per, :] = jnp.zeros((z.per, z.width), jnp.float32)
    for read in reads:
        read.wait()
    for a in range(z.cap):
        length = jnp.where(requests[a] >= 0, len_ref[known[a]], 0)
        ahead = lax.rem(known[a] // z.mig_per - inst + z.insts, z.insts)
        at_hand = jnp.maximum(ahead - 1, 0)

        def one(b, carry, a=a, length=length, at_hand=at_hand):
            inside = place + b * z.block < length
            at = pl.ds(pl.multiple_of(b * z.block, z.block), z.block)
            for s in range(z.slots):
                value = got_ref[at_hand, s, b].astype(jnp.float32)
                keep_ref[a, s, at, :] = jnp.where(inside, value, 0.0).astype(jnp.bfloat16)
            return carry

        lax.fori_loop(0, z.mig_blocks, one, 0, unroll=8)
        writes[a].start()
        at = slice((a + 1) * z.per, (a + 2) * z.per)
        both = jnp.concatenate([keep_ref[a, s] for s in range(z.slots)], axis=0)
        own = own_scores(dot_t(query_ref[at, :], both[:, : z.width]), slot_of, z.slots)
        fresh = dot_t(query_ref[at, :], new_kv[:, : z.width])
        own, fresh = weigh(own, length, fresh, code == a + 1, scale)
        done = dot(spread(own, slot_of, z.slots), with_ones(both[:, z.width :]))
        done = done + dot(fresh.astype(jnp.bfloat16), with_ones(new_kv[:, z.width :]))
        rows_ref[at, :] = done[:, : z.width] / done[:, z.width :]
        filled = filled | ((row == a + 1) & (requests[a] >= 0))
    for h in range(z.heads):
        at = slice(h * z.width, (h + 1) * z.width)
        column = rows_ref[pl.ds(h, tokens, stride=z.heads), :]
        old = old_ref[:, at].astype(jnp.float32)
        value = jnp.where(filled, column, old).astype(jnp.bfloat16)
        out_ref[:, at] = value
        last_ref[:, at] = value
    for write in writes:
        write.wait()


def settle(mig_dest, mig_len, got, tail_q, tail_kv, attention, sizes, deps, **fetch):
    z = sizes
    tokens = z.insts * z.steps
    last = attention.shape[0] // tokens - 1
    spec = pl.BlockSpec((tokens, attention.shape[1]), lambda i: (last, 0))
    cache = (z.slots, z.mig_blocks * z.block, 2 * z.width)
    return run(
        functools.partial(settle_kernel, sizes=z),
        [mig_dest, mig_len], [got, tail_q, tail_kv, attention],
        [HBM, VMEM, VMEM, spec],
        deps,
        [
            jax.ShapeDtypeStruct(attention.shape, jnp.bfloat16),
            jax.ShapeDtypeStruct((tokens, attention.shape[1]), jnp.bfloat16),
            jax.ShapeDtypeStruct((1, z.cap) + cache, jnp.bfloat16),
        ],
        [spec, VMEM, ANY], "settle", z, grid=(1,),
        scratch=[
            pltpu.VMEM((z.insts * z.per, z.width), jnp.float32),
            pltpu.VMEM((z.cap,) + got.shape[1:], jnp.bfloat16),
            pltpu.VMEM((z.cap,) + cache, jnp.bfloat16),
            pltpu.SemaphoreType.DMA((2, z.cap)),
        ],
        aliases={5: 0}, **fetch,
    )


def project_kernel(ready, launch, attention, *refs, first, tokens, count, added, joined, sizes):
    launch()
    weights, extra, out_refs = refs[:count], refs[count : count + added], refs[count + added :]
    width = sizes.quarter
    tile = min(width, 256)
    for n, weight in enumerate(weights):

        def one(j, carry, n=n, weight=weight):
            at = pl.ds(pl.multiple_of(j * tile, tile), tile)
            to = pl.ds(pl.multiple_of(n * width + j * tile, tile), tile)
            result = dot(attention[first : first + tokens, :], weight[:, at])
            if added == 1:
                result = result + extra[0][:, to].astype(jnp.float32)
            elif added:
                result = result + extra[n][:, at].astype(jnp.float32)
            if joined:
                out_refs[0][:, to] = result.astype(out_refs[0].dtype)
            else:
                out_refs[n][:, at] = result.astype(out_refs[n].dtype)
            return carry

        lax.fori_loop(0, width // tile, one, 0)


def project(attention, weights, mates, joined, dtype, sizes, name, deps, place=None, **fetch):
    attention, first, tokens = attention
    count = len(weights)
    if place is not None:
        shapes = [place((tokens, count * sizes.quarter), dtype)]
    elif joined:
        shapes = [jax.ShapeDtypeStruct((tokens, count * sizes.quarter), dtype)]
    else:
        shapes = [jax.ShapeDtypeStruct((tokens, sizes.quarter), dtype)] * count
    operands = [attention] + weights + mates
    return run(
        functools.partial(
            project_kernel, first=first, tokens=tokens, count=count, added=len(mates),
            joined=joined, sizes=sizes,
        ),
        [], operands, [VMEM] * len(operands), deps, shapes, [VMEM] * len(shapes), name, sizes,
        **fetch,
    )


def finish_kernel(ready, launch, own_low, own_high, *refs, fars, sizes):
    z = sizes
    refs = list(refs)

    def take(n):
        taken = refs[:n]
        del refs[:n]
        return taken

    low, high, second, late = take(fars), take(fars), take(fars), take(fars)
    out_hbm, block_ref, sems = refs
    tile = min(z.quarter, 256)
    writes = []
    for n in range(4):

        def one(j, carry, n=n):
            start = pl.multiple_of(j * tile, tile)
            at = pl.ds(n * z.quarter + start, tile)
            half = pl.ds((n % 2) * z.quarter + start, tile)
            sums = (own_low if n < 2 else own_high)[:, half]
            for k in range(fars):
                rows = late[k].shape[0]
                arrived = jnp.concatenate(
                    [
                        (low if n < 2 else high)[k][:, half],
                        second[k][:-rows, at],
                        late[k][:, at],
                    ],
                    axis=0,
                )
                sums = sums + arrived.astype(jnp.float32)
            block_ref[n, pl.ds(start, tile), :] = sums.T.astype(jnp.bfloat16)
            return carry

        lax.fori_loop(0, z.quarter // tile, one, 0)
        write = pltpu.make_async_copy(
            block_ref.at[n], out_hbm.at[pl.ds(n * z.quarter, z.quarter)], sems.at[n]
        )
        write.start()
        writes.append(write)
    for write in writes:
        write.wait()


def finish(own, low, high, second, late, sizes, deps):
    z = sizes
    tokens = own[0].shape[0]
    operands = own + low + high + second + late
    result, _ = run(
        functools.partial(finish_kernel, fars=len(low), sizes=z),
        [], operands, [VMEM] * len(operands), deps,
        [jax.ShapeDtypeStruct((z.features, tokens), jnp.bfloat16)], [ANY], "finish", z,
        scratch=[
            pltpu.VMEM((4, z.quarter, tokens), jnp.bfloat16), pltpu.SemaphoreType.DMA((4,))
        ],
    )
    return result[0]


def shards(
    res_pool,
    res_table,
    res_len,
    out_pool,
    src_table,
    mig_len,
    mig_dest,
    queries,
    new_kv,
    out_weight,
):
    z = Sizes(queries, res_pool, res_table, src_table, mig_dest, out_weight)
    tps, chips = z.tps, z.chips
    table = res_table[0].T
    out_weight, res_pool, out_pool, new_kv, query_rows, table, res_len, src_table, mig_dest, mig_len = (
        pltpu.with_memory_space_constraint(x, pltpu.HBM)
        for x in (
            out_weight, res_pool, out_pool, new_kv, queries.reshape(z.batch * z.per, z.width),
            table, res_len, src_table, mig_dest, mig_len,
        )
    )
    to_mate = [(i, i + 1 - 2 * (i % CORES)) for i in range(tps)]
    far = range(1, chips)
    held = {}

    def mate_of(x):
        return lax.ppermute(x, "tp", to_mate)

    def across(x, ahead):
        shift = ahead * CORES
        return lax.ppermute(x, "tp", [(i, (i + shift) % tps) for i in range(tps)])

    def bringing(pieces):
        return dict(pieces=pieces, weight=out_weight)

    def gives(ks, parts):
        return [(k, False, part) for k in ks for part in parts]

    def keeps(ks, parts):
        return [(k, True, part) for k in ks for part in parts]

    def hold(pieces, arrays):
        held.update(zip(pieces, arrays))

    def give(attention, ks, parts, name, deps, pieces=(), joined=False):
        weights = [held[piece] for piece in gives(ks, parts)]
        results, new = project(
            attention, weights, [], joined, jnp.bfloat16, z, name, deps, **bringing(pieces)
        )
        hold(pieces, new)
        return results[0], [mate_of(result) for result in results]

    def keep(attention, ks, parts, mates, name, deps, pieces=(), dtype=jnp.bfloat16, place=None):
        results = []
        for n, k in enumerate(ks):
            weights = [held[piece] for piece in keeps([k], parts)]
            if len(mates) == 1:
                width = mates[0].shape[1] // len(ks)
                now = [mates[0][:, n * width : (n + 1) * width] if len(ks) > 1 else mates[0]]
            else:
                now = mates[n * len(parts) : (n + 1) * len(parts)]
            bring = pieces if n == 0 else ()
            result, new = project(
                attention, weights, now, True, dtype, z, name, deps, place, **bringing(bring)
            )
            hold(bring, new)
            deps = [result[0]]
            results.append(result[0])
        return results

    def sent(results):
        return [across(result, k) for k, result in zip(far, results)]

    half = z.batch // 2
    low, high, every = (0, 1), (2, 3), (0, 1, 2, 3)

    sends, tail_q, tail_kv = pack(src_table, mig_dest, out_pool, query_rows, new_kv, z)
    arriving = lax.all_to_all(sends, "inst", split_axis=0, concat_axis=0, tiled=True)

    tokens = half * z.steps
    pieces = gives(far, low) + keeps(far, low) + gives(far, high)
    rows, new = attend(
        table, res_len, query_rows, new_kv, res_pool, None, 0, half, z, [sends],
        **bringing(pieces),
    )
    hold(pieces, new)
    a = (rows, 0, tokens)
    given, mates_low = give(a, far, low, "give", [], keeps(far, high))
    given, mates_high = give(a, far, high, "give", [given])
    kept = keep(a, far, low, mates_low, "keep", [given])
    got_low = sent(kept)
    kept = keep(a, far, high, mates_high, "keep", kept[-1:])
    got_high = sent(kept)
    rows, _ = attend(
        table, res_len, query_rows, new_kv, res_pool, rows, half, half, z, kept[-1:],
    )
    b = (rows, tokens, tokens)
    given, mates = give(b, far, every, "give", [])
    kept = keep(b, far, every, mates, "keep", [given] + got_low + got_high)
    got_second = sent(kept)

    tail_q, tail_kv = (
        pltpu.with_memory_space_constraint(x, pltpu.HBM) for x in (tail_q, tail_kv)
    )
    pieces = gives([0], low) + gives(far, (0,))
    (rows, last, arrived), new = settle(
        mig_dest, mig_len, arriving, tail_q, tail_kv, rows, z, kept[-1:],
        **bringing(pieces),
    )
    hold(pieces, new)
    late, whole = (last, 0, last.shape[0]), (rows, 0, 2 * tokens)
    given, mates_low = give(whole, [0], low, "give_own", [], gives(far, (1, 2, 3)))
    given, mates = give(late, far, every, "give_last", [given], gives([0], high), joined=True)
    given, mates_high = give(whole, [0], high, "give_own", [given], keeps(far, every))
    kept = keep(late, far, every, mates, "keep_last", [given], keeps([0], low))
    got_late = sent(kept)
    own = keep(
        whole, [0], low, mates_low, "keep_own", kept[-1:], keeps([0], high), jnp.float32
    )
    own += keep(whole, [0], high, mates_high, "keep_own", own, (), jnp.float32)
    hidden = finish(own, got_low, got_high, got_second, got_late, z, [])
    return (arrived, hidden)


def solution(mesh):
    placed = (
        P(("groups", "inst"), "tp", None, None, None),
        P(("groups", "inst"), None, None),
        P(("groups", "inst"), None),
        P(("groups", "inst"), "tp", None, None, None),
        P(("groups", "inst"), None, None),
        P("groups"),
        P("groups"),
        P(("groups", "inst"), None, "tp", None),
        P(("groups", "inst"), None, "tp", None),
        P("tp", None),
    )
    return jax.shard_map(
        shards,
        mesh=mesh,
        in_specs=placed,
        out_specs=(P(("groups", "inst"), None, "tp", None, None), P("tp", ("groups", "inst"))),
        check_vma=False,
    )
```

```python
import functools
import math

import jax
import jax.numpy as jnp
from jax import lax
from jax.experimental import pallas as pl
from jax.experimental.pallas import tpu as pltpu
from jax.sharding import PartitionSpec as P

CORES = 2
LOW = -1e30
MIB = 1 << 20
LANES = 128
GROUP = 16
TOGETHER = 8
LARGE_FIRST = 12
FETCHING = 16


def dot_t(left, right):
    return lax.dot_general(
        left, right, (((1,), (1,)), ((), ())), preferred_element_type=jnp.float32
    )


def row_plan(dest_ref, inst, cap):
    requests = [jnp.int32(-1)] * cap
    seen = jnp.int32(0)
    for g in range(dest_ref.shape[0]):
        here = dest_ref[g] == inst
        requests = [jnp.where(here & (seen == a), g, requests[a]) for a in range(cap)]
        seen = seen + here.astype(jnp.int32)
    return requests


VMEM = pl.BlockSpec(memory_space=pltpu.VMEM)
ANY = pl.BlockSpec(memory_space=pl.ANY)
HBM = pl.BlockSpec(memory_space=pltpu.HBM)


class Sizes:
    def __init__(self, queries, res_pool, res_table, src_table, mig_dest, out_weight):
        self.batch, self.steps, self.heads, self.width = queries.shape
        self.slots = res_pool.shape[1]
        self.block = res_pool.shape[3]
        self.resident, self.blocks = res_table.shape[1:]
        self.mig_per, self.mig_blocks = src_table.shape[1:]
        self.requests = mig_dest.shape[0]
        self.insts = lax.axis_size("inst")
        self.tps = lax.axis_size("tp")
        self.chips = self.tps // CORES
        self.cap = self.insts - 1
        self.per = self.steps * self.heads
        self.per_kv = self.steps * self.slots
        self.depth = out_weight.shape[0]
        self.features = out_weight.shape[1] // self.tps
        self.quarter = self.features // 4
        self.tail_q = self.insts * self.per
        self.tail_kv = self.insts * self.per_kv


def piece_columns(piece, sizes):
    ahead, mine, part = piece
    tp = lax.axis_index("tp")
    core = lax.rem(tp, CORES)
    chip = lax.rem(tp // CORES + ahead, sizes.chips)
    owner = chip * CORES + (core if mine else 1 - core)
    return owner * sizes.features + part * sizes.quarter


def run(kernel, tables, operands, in_specs, deps, out_shapes, out_specs, name, sizes,
        pieces=(), weight=None, limit=16, grid=(), scratch=(), aliases=None):
    inputs, outputs, many = len(operands), len(out_shapes), len(tables)
    count = len(deps)
    fetches = len(pieces)
    extra_in = [weight] if fetches else []
    limit = max(limit, FETCHING) if fetches else limit

    def call(*refs):
        table_in, refs = refs[:many], refs[many:]
        own_in = refs[:inputs]
        position = inputs + len(extra_in) + count
        own_out = refs[position : position + outputs]
        fetched = refs[position + outputs : position + outputs + fetches]
        rest = list(refs[position + outputs + fetches :])
        copies, reads = [], []
        if fetches:
            source, sems = refs[inputs], rest.pop()
            for n, piece in enumerate(pieces):
                first = pl.multiple_of(piece_columns(piece, sizes), LANES)
                copies.append(
                    pltpu.make_async_copy(
                        source.at[:, pl.ds(first, sizes.quarter)], fetched[n], sems.at[n]
                    )
                )
        table_refs = []
        if many:
            sems = rest.pop()
            table_refs = rest[len(rest) - many :]
            rest = rest[: len(rest) - many]
            reads = [
                pltpu.make_async_copy(source, target, sems.at[n])
                for n, (source, target) in enumerate(zip(table_in, table_refs))
            ]

        def ready():
            for read in reads:
                read.wait()

        def launch():
            for copy in copies:
                copy.start()

        def each(step, action):
            if not grid:
                action()
            else:
                pl.when(pl.program_id(0) == step)(action)

        def begin():
            for read in reads:
                read.start()

        def end():
            for copy in copies:
                copy.wait()

        if reads:
            each(0, begin)
        kernel(ready, launch, *table_refs, *own_in, *own_out, *rest)
        if copies:
            each(grid[0] - 1 if grid else 0, end)

    result = pl.pallas_call(
        call,
        grid_spec=pltpu.PrefetchScalarGridSpec(
            num_scalar_prefetch=0,
            grid=grid,
            in_specs=[HBM] * many + list(in_specs) + [HBM] * len(extra_in) + [ANY] * count,
            out_specs=list(out_specs) + [ANY] * fetches,
            scratch_shapes=list(scratch)
            + [pltpu.SMEM(t.shape, t.dtype) for t in tables]
            + ([pltpu.SemaphoreType.DMA((many,))] if many else [])
            + ([pltpu.SemaphoreType.DMA((fetches,))] if fetches else []),
        ),
        out_shape=list(out_shapes)
        + [pltpu.VMEM((sizes.depth, sizes.quarter), jnp.bfloat16)] * fetches,
        input_output_aliases=aliases or {},
        compiler_params=pltpu.CompilerParams(vmem_limit_bytes=limit * MIB),
        cost_estimate=pl.CostEstimate(flops=0, bytes_accessed=1024, transcendentals=0),
        name=name,
    )(*tables, *operands, *extra_in, *deps)
    return result[:outputs], result[outputs:]


def pack_kernel(
    ready, launch, table_ref, dest_ref, pool_ref, query_ref, kv_ref, send_hbm, tail_q_ref,
    tail_kv_ref, pack_ref, sems, *, sizes
):
    inst = lax.axis_index("inst")
    ready()
    copies = []
    for m in range(sizes.mig_per):
        dest = dest_ref[inst * sizes.mig_per + m]

        def copy_block(b, carry, m=m):
            block = table_ref[0, m, b]
            for s in range(sizes.slots):
                pack_ref[m, s, b] = pool_ref[0, s, block]
            return carry

        lax.fori_loop(0, sizes.mig_blocks, copy_block, 0, unroll=8)
        copies.append(pltpu.make_async_copy(pack_ref.at[m], send_hbm.at[dest], sems.at[m]))
        copies[-1].start()
    tail_q_ref[...] = query_ref[...]
    tail_kv_ref[...] = kv_ref[...].reshape(sizes.tail_kv, 2 * sizes.width)
    for copy in copies:
        copy.wait()


def pack(src_table, mig_dest, out_pool, query_rows, new_kv, sizes):
    z = sizes
    last_q = query_rows.shape[0] // z.tail_q - 1
    last_kv = z.batch // z.insts - 1
    request = (z.slots, z.mig_blocks, z.block, 2 * z.width)
    result, _ = run(
        functools.partial(pack_kernel, sizes=z),
        [src_table, mig_dest], [out_pool, query_rows, new_kv],
        [
            VMEM,
            pl.BlockSpec((z.tail_q, z.width), lambda i: (last_q, 0)),
            pl.BlockSpec((z.insts,) + new_kv.shape[1:], lambda i: (last_kv, 0, 0, 0)),
        ],
        [],
        [
            pltpu.HBM((z.insts,) + request, out_pool.dtype),
            pltpu.HBM((z.tail_q, z.width), out_pool.dtype),
            pltpu.HBM((z.tail_kv, 2 * z.width), out_pool.dtype),
        ],
        [ANY, VMEM, VMEM], "pack", z, limit=60, grid=(1,),
        scratch=[
            pltpu.VMEM((z.mig_per,) + request, out_pool.dtype),
            pltpu.SemaphoreType.DMA((z.mig_per,)),
        ],
    )
    return result


def fresh_code(rows, keys, sizes):
    index = lax.broadcasted_iota(jnp.int32, (rows, keys), 0)
    key = lax.broadcasted_iota(jnp.int32, (rows, keys), 1)
    step = index // sizes.heads
    slot = lax.rem(index, sizes.heads) // (sizes.heads // sizes.slots)
    in_row = lax.rem(key, sizes.per_kv)
    seen = (in_row // sizes.slots <= step) & (lax.rem(in_row, sizes.slots) == slot)
    return jnp.where(seen, key // sizes.per_kv, -1)


def slot_index(extent, sizes):
    index = lax.broadcasted_iota(jnp.int32, (sizes.per, extent), 0)
    return lax.rem(index, sizes.heads) // (sizes.heads // sizes.slots)


def own_scores(scores, slot_of, slots):
    extent = scores.shape[1] // slots
    own = scores[:, :extent]
    for s in range(1, slots):
        own = jnp.where(slot_of == s, scores[:, s * extent : (s + 1) * extent], own)
    return own


def weigh(own, length, fresh, fresh_seen, scale):
    place = lax.broadcasted_iota(jnp.int32, own.shape, 1)
    own = jnp.where(place < length, own, LOW)
    fresh = jnp.where(fresh_seen, fresh, LOW)
    if own.shape == fresh.shape:
        largest = jnp.max(jnp.maximum(own, fresh), axis=1, keepdims=True)
    else:
        largest = jnp.maximum(
            jnp.max(own, axis=1, keepdims=True), jnp.max(fresh, axis=1, keepdims=True)
        )
    return jnp.exp2((own - largest) * scale), jnp.exp2((fresh - largest) * scale)


def spread(own, slot_of, slots):
    if slots == 1:
        return own.astype(jnp.bfloat16)
    parts = [jnp.where(slot_of == s, own, 0.0) for s in range(slots)]
    return jnp.concatenate(parts, axis=1).astype(jnp.bfloat16)


def gather_blocks(pool_ref, slots, ids):
    tiles = [pool_ref[0, s, block] for s in range(slots) for block in ids]
    return jnp.concatenate(tiles, axis=0)


def with_ones(values):
    return jnp.concatenate([values, jnp.ones_like(values)], axis=1)


def dot(left, right):
    return jnp.dot(left, right, preferred_element_type=jnp.float32)


def attend_kernel(
    ready, launch, table_ref, len_ref, query_hbm, kv_hbm, pool_ref, *refs, first_row,
    steps_in_all, sizes,
):
    z = sizes
    out_ref, query_all, kv_all, fresh_ref, pf_ref, blend_ref, done_ref, sems = refs
    width, per = z.width, z.per
    rows = GROUP
    step = pl.program_id(0)
    extent = z.blocks * z.block
    start = first_row + step * rows
    scale = math.log2(math.e) / math.sqrt(width)

    def copies(n):
        begin = first_row + n * rows
        return (
            pltpu.make_async_copy(
                query_hbm.at[pl.ds(pl.multiple_of(begin * per, rows * per), rows * per)],
                query_all.at[n], sems.at[0, n],
            ),
            pltpu.make_async_copy(kv_hbm.at[pl.ds(begin, rows)], kv_all.at[n], sems.at[1, n]),
        )

    @pl.when(step == 0)
    def _():
        for n in range(steps_in_all):
            for copy in copies(n):
                copy.start()
        launch()
        ready()

    for copy in copies(step):
        copy.wait()

    query_ref = query_all.at[step]
    new_kv = kv_all[step].reshape(rows * z.per_kv, 2 * width)
    fresh_ref[...] = dot_t(query_ref[...], new_kv[:, :width])
    code = fresh_code(per, rows * z.per_kv, z)
    slot_of = slot_index(extent, z)
    together = min(TOGETHER, rows)
    for begin in range(0, rows, together):
        group = range(begin, begin + together)
        at = [slice(r * per, (r + 1) * per) for r in group]
        known = [jnp.minimum(start + r, z.resident - 1) for r in group]
        length = [
            jnp.where(start + r < z.resident, len_ref[0, k], 0) for r, k in zip(group, known)
        ]
        both = [
            gather_blocks(pool_ref, z.slots, [table_ref[j, k] for j in range(z.blocks)])
            for k in known
        ]
        fresh = [fresh_ref[a, :] for a in at]
        scores = [dot_t(query_ref[a, :], b[:, :width]) for a, b in zip(at, both)]
        weights = [
            weigh(own_scores(s, slot_of, z.slots), n, f, code == r, scale)
            for s, n, f, r in zip(scores, length, fresh, group)
        ]
        context = [
            dot(spread(w[0], slot_of, z.slots), with_ones(b[:, width:]))
            for w, b in zip(weights, both)
        ]
        for a, c, w in zip(at, context, weights):
            blend_ref[a, :] = c
            pf_ref[a, :] = w[1].astype(jnp.bfloat16)

    done = blend_ref[...] + dot(pf_ref[...], with_ones(new_kv[:, width:]))
    done_ref[...] = done[:, :width] / done[:, width:]
    for h in range(z.heads):
        column = done_ref[pl.ds(h, rows * z.steps, stride=z.heads), :]
        out_ref[:, h * width : (h + 1) * width] = column.astype(jnp.bfloat16)


def attend(table, lengths, queries, new_kv, pool, into, first_row, rows, sizes, deps, limit=12,
           **fetch):
    z = sizes
    groups = rows // GROUP
    first = first_row // GROUP
    tokens = z.batch * z.steps
    aliases = {}
    if into is not None:
        deps = [into] + deps
        aliases = {5 + (1 if fetch else 0): 0}
    result, pieces = run(
        functools.partial(
            attend_kernel, first_row=first_row, steps_in_all=groups, sizes=z
        ),
        [table, lengths],
        [queries, new_kv, pool],
        [HBM, HBM, VMEM],
        deps,
        [jax.ShapeDtypeStruct((tokens, z.heads * z.width), jnp.bfloat16)],
        [pl.BlockSpec((GROUP * z.steps, z.heads * z.width), lambda i: (first + i, 0))],
        "attend", z, limit=limit,
        grid=(groups,),
        scratch=[
            pltpu.VMEM((groups, GROUP * z.per, z.width), jnp.bfloat16),
            pltpu.VMEM((groups, GROUP) + new_kv.shape[1:], jnp.bfloat16),
            pltpu.VMEM((GROUP * z.per, GROUP * z.per_kv), jnp.float32),
            pltpu.VMEM((GROUP * z.per, GROUP * z.per_kv), jnp.bfloat16),
            pltpu.VMEM((GROUP * z.per, 2 * z.width), jnp.float32),
            pltpu.VMEM((GROUP * z.per, z.width), jnp.float32),
            pltpu.SemaphoreType.DMA((2, groups)),
        ],
        aliases=aliases, **fetch,
    )
    return result[0], pieces


def settle_kernel(
    ready, launch, dest_ref, len_ref, got_hbm, query_ref, kv_ref, old_ref, out_ref, last_ref,
    arrived_hbm, rows_ref, got_ref, keep_ref, sems, *, sizes
):
    z = sizes
    ready()
    inst = lax.axis_index("inst")
    requests = row_plan(dest_ref, inst, z.cap)
    known = [jnp.maximum(request, 0) for request in requests]
    extent = z.mig_blocks * z.block
    reads = [
        pltpu.make_async_copy(got_hbm.at[known[a] // z.mig_per], got_ref.at[a], sems.at[0, a])
        for a in range(z.cap)
    ]
    writes = [
        pltpu.make_async_copy(keep_ref.at[a], arrived_hbm.at[0, a], sems.at[1, a])
        for a in range(z.cap)
    ]
    for read in reads:
        read.start()
    launch()
    new_kv = kv_ref[...]
    code = fresh_code(z.per, z.tail_kv, z)
    slot_of = slot_index(extent, z)
    scale = math.log2(math.e) / math.sqrt(z.width)
    tokens = z.insts * z.steps
    row = lax.broadcasted_iota(jnp.int32, (tokens, z.width), 0) // z.steps
    place = lax.broadcasted_iota(jnp.int32, (z.block, 2 * z.width), 0)
    filled = row < 0
    rows_ref[: z.per, :] = jnp.zeros((z.per, z.width), jnp.float32)
    for a in range(z.cap):
        length = jnp.where(requests[a] >= 0, len_ref[known[a]], 0)
        reads[a].wait()

        def one(b, carry, a=a, length=length):
            inside = place + b * z.block < length
            at = pl.ds(pl.multiple_of(b * z.block, z.block), z.block)
            for s in range(z.slots):
                value = got_ref[a, s, b].astype(jnp.float32)
                keep_ref[a, s, at, :] = jnp.where(inside, value, 0.0).astype(jnp.bfloat16)
            return carry

        lax.fori_loop(0, z.mig_blocks, one, 0, unroll=8)
        writes[a].start()
        at = slice((a + 1) * z.per, (a + 2) * z.per)
        both = jnp.concatenate([keep_ref[a, s] for s in range(z.slots)], axis=0)
        own = own_scores(dot_t(query_ref[at, :], both[:, : z.width]), slot_of, z.slots)
        fresh = dot_t(query_ref[at, :], new_kv[:, : z.width])
        own, fresh = weigh(own, length, fresh, code == a + 1, scale)
        done = dot(spread(own, slot_of, z.slots), with_ones(both[:, z.width :]))
        done = done + dot(fresh.astype(jnp.bfloat16), with_ones(new_kv[:, z.width :]))
        rows_ref[at, :] = done[:, : z.width] / done[:, z.width :]
        filled = filled | ((row == a + 1) & (requests[a] >= 0))
    for h in range(z.heads):
        at = slice(h * z.width, (h + 1) * z.width)
        column = rows_ref[pl.ds(h, tokens, stride=z.heads), :]
        old = old_ref[:, at].astype(jnp.float32)
        value = jnp.where(filled, column, old).astype(jnp.bfloat16)
        out_ref[:, at] = value
        last_ref[:, at] = value
    for write in writes:
        write.wait()


def settle(mig_dest, mig_len, got, tail_q, tail_kv, attention, sizes, deps, **fetch):
    z = sizes
    tokens = z.insts * z.steps
    last = attention.shape[0] // tokens - 1
    spec = pl.BlockSpec((tokens, attention.shape[1]), lambda i: (last, 0))
    cache = (z.slots, z.mig_blocks * z.block, 2 * z.width)
    return run(
        functools.partial(settle_kernel, sizes=z),
        [mig_dest, mig_len], [got, tail_q, tail_kv, attention],
        [HBM, VMEM, VMEM, spec],
        deps,
        [
            jax.ShapeDtypeStruct(attention.shape, jnp.bfloat16),
            jax.ShapeDtypeStruct((tokens, attention.shape[1]), jnp.bfloat16),
            jax.ShapeDtypeStruct((1, z.cap) + cache, jnp.bfloat16),
        ],
        [spec, VMEM, ANY], "settle", z, grid=(1,),
        scratch=[
            pltpu.VMEM((z.insts * z.per, z.width), jnp.float32),
            pltpu.VMEM((z.cap,) + got.shape[1:], jnp.bfloat16),
            pltpu.VMEM((z.cap,) + cache, jnp.bfloat16),
            pltpu.SemaphoreType.DMA((2, z.cap)),
        ],
        aliases={5: 0}, **fetch,
    )


def project_kernel(ready, launch, attention, *refs, first, tokens, count, added, joined, sizes):
    launch()
    weights, extra, out_refs = refs[:count], refs[count : count + added], refs[count + added :]
    width = sizes.quarter
    tile = min(width, 256)
    for n, weight in enumerate(weights):

        def one(j, carry, n=n, weight=weight):
            at = pl.ds(pl.multiple_of(j * tile, tile), tile)
            to = pl.ds(pl.multiple_of(n * width + j * tile, tile), tile)
            result = dot(attention[first : first + tokens, :], weight[:, at])
            if added == 1:
                result = result + extra[0][:, to].astype(jnp.float32)
            elif added:
                result = result + extra[n][:, at].astype(jnp.float32)
            if joined:
                out_refs[0][:, to] = result.astype(out_refs[0].dtype)
            else:
                out_refs[n][:, at] = result.astype(out_refs[n].dtype)
            return carry

        lax.fori_loop(0, width // tile, one, 0)


def project(attention, weights, mates, joined, dtype, sizes, name, deps, place=None, **fetch):
    attention, first, tokens = attention
    count = len(weights)
    if place is not None:
        shapes = [place((tokens, count * sizes.quarter), dtype)]
    elif joined:
        shapes = [jax.ShapeDtypeStruct((tokens, count * sizes.quarter), dtype)]
    else:
        shapes = [jax.ShapeDtypeStruct((tokens, sizes.quarter), dtype)] * count
    operands = [attention] + weights + mates
    return run(
        functools.partial(
            project_kernel, first=first, tokens=tokens, count=count, added=len(mates),
            joined=joined, sizes=sizes,
        ),
        [], operands, [VMEM] * len(operands), deps, shapes, [VMEM] * len(shapes), name, sizes,
        **fetch,
    )


def finish_kernel(ready, launch, own_low, own_high, *refs, fars, sizes):
    z = sizes
    refs = list(refs)

    def take(n):
        taken = refs[:n]
        del refs[:n]
        return taken

    low, high, second, late = take(fars), take(fars), take(fars), take(fars)
    out_hbm, block_ref, sems = refs
    tile = min(z.quarter, 256)
    writes = []
    for n in range(4):

        def one(j, carry, n=n):
            start = pl.multiple_of(j * tile, tile)
            at = pl.ds(n * z.quarter + start, tile)
            half = pl.ds((n % 2) * z.quarter + start, tile)
            sums = (own_low if n < 2 else own_high)[:, half]
            for k in range(fars):
                rows = late[k].shape[0]
                arrived = jnp.concatenate(
                    [
                        (low if n < 2 else high)[k][:, half],
                        second[k][:-rows, at],
                        late[k][:, at],
                    ],
                    axis=0,
                )
                sums = sums + arrived.astype(jnp.float32)
            block_ref[n, pl.ds(start, tile), :] = sums.T.astype(jnp.bfloat16)
            return carry

        lax.fori_loop(0, z.quarter // tile, one, 0)
        write = pltpu.make_async_copy(
            block_ref.at[n], out_hbm.at[pl.ds(n * z.quarter, z.quarter)], sems.at[n]
        )
        write.start()
        writes.append(write)
    for write in writes:
        write.wait()


def finish(own, low, high, second, late, sizes, deps):
    z = sizes
    tokens = own[0].shape[0]
    operands = own + low + high + second + late
    result, _ = run(
        functools.partial(finish_kernel, fars=len(low), sizes=z),
        [], operands, [VMEM] * len(operands), deps,
        [jax.ShapeDtypeStruct((z.features, tokens), jnp.bfloat16)], [ANY], "finish", z,
        scratch=[
            pltpu.VMEM((4, z.quarter, tokens), jnp.bfloat16), pltpu.SemaphoreType.DMA((4,))
        ],
    )
    return result[0]


def shards(
    res_pool,
    res_table,
    res_len,
    out_pool,
    src_table,
    mig_len,
    mig_dest,
    queries,
    new_kv,
    out_weight,
):
    z = Sizes(queries, res_pool, res_table, src_table, mig_dest, out_weight)
    tps, chips = z.tps, z.chips
    table = res_table[0].T
    out_weight, res_pool, out_pool, new_kv, query_rows, table, res_len, src_table, mig_dest, mig_len = (
        pltpu.with_memory_space_constraint(x, pltpu.HBM)
        for x in (
            out_weight, res_pool, out_pool, new_kv, queries.reshape(z.batch * z.per, z.width),
            table, res_len, src_table, mig_dest, mig_len,
        )
    )
    to_mate = [(i, i + 1 - 2 * (i % CORES)) for i in range(tps)]
    far = range(1, chips)
    held = {}

    def mate_of(x):
        return lax.ppermute(x, "tp", to_mate)

    def across(x, ahead):
        shift = ahead * CORES
        return lax.ppermute(x, "tp", [(i, (i + shift) % tps) for i in range(tps)])

    def bringing(pieces):
        return dict(pieces=pieces, weight=out_weight)

    def gives(ks, parts):
        return [(k, False, part) for k in ks for part in parts]

    def keeps(ks, parts):
        return [(k, True, part) for k in ks for part in parts]

    def hold(pieces, arrays):
        held.update(zip(pieces, arrays))

    def give(attention, ks, parts, name, deps, pieces=(), joined=False):
        weights = [held[piece] for piece in gives(ks, parts)]
        results, new = project(
            attention, weights, [], joined, jnp.bfloat16, z, name, deps, **bringing(pieces)
        )
        hold(pieces, new)
        return results[0], [mate_of(result) for result in results]

    def keep(attention, ks, parts, mates, name, deps, pieces=(), dtype=jnp.bfloat16, place=None):
        results = []
        for n, k in enumerate(ks):
            weights = [held[piece] for piece in keeps([k], parts)]
            if len(mates) == 1:
                width = mates[0].shape[1] // len(ks)
                now = [mates[0][:, n * width : (n + 1) * width] if len(ks) > 1 else mates[0]]
            else:
                now = mates[n * len(parts) : (n + 1) * len(parts)]
            bring = pieces if n == 0 else ()
            result, new = project(
                attention, weights, now, True, dtype, z, name, deps, place, **bringing(bring)
            )
            hold(bring, new)
            deps = [result[0]]
            results.append(result[0])
        return results

    def sent(results):
        return [across(result, k) for k, result in zip(far, results)]

    half = z.batch // 2
    low, high, every = (0, 1), (2, 3), (0, 1, 2, 3)

    sends, tail_q, tail_kv = pack(src_table, mig_dest, out_pool, query_rows, new_kv, z)
    arriving = lax.all_to_all(sends, "inst", split_axis=0, concat_axis=0, tiled=True)

    tokens = half * z.steps
    pieces = gives(far, low) + keeps(far, low) + gives(far, high)
    rows, new = attend(
        table, res_len, query_rows, new_kv, res_pool, None, 0, half, z, [sends],
        **bringing(pieces),
    )
    hold(pieces, new)
    a = (rows, 0, tokens)
    given, mates_low = give(a, far, low, "give", [], keeps(far, high))
    given, mates_high = give(a, far, high, "give", [given])
    kept = keep(a, far, low, mates_low, "keep", [given])
    got_low = sent(kept)
    kept = keep(a, far, high, mates_high, "keep", kept[-1:])
    got_high = sent(kept)
    rows, _ = attend(
        table, res_len, query_rows, new_kv, res_pool, rows, half, half, z, kept[-1:],
    )
    b = (rows, tokens, tokens)
    given, mates = give(b, far, every, "give", got_low)
    kept = keep(b, far, every, mates, "keep", [given] + got_high)
    got_second = sent(kept)

    tail_q, tail_kv = (
        pltpu.with_memory_space_constraint(x, pltpu.HBM) for x in (tail_q, tail_kv)
    )
    pieces = gives([0], low) + gives(far, (0,))
    (rows, last, arrived), new = settle(
        mig_dest, mig_len, arriving, tail_q, tail_kv, rows, z, kept[-1:],
        **bringing(pieces),
    )
    hold(pieces, new)
    late, whole = (last, 0, last.shape[0]), (rows, 0, 2 * tokens)
    given, mates_low = give(whole, [0], low, "give_own", [], gives(far, (1, 2, 3)))
    given, mates = give(late, far, every, "give_last", [given], gives([0], high), joined=True)
    given, mates_high = give(whole, [0], high, "give_own", [given], keeps(far, every))
    kept = keep(late, far, every, mates, "keep_last", [given], keeps([0], low))
    got_late = sent(kept)
    own = keep(
        whole, [0], low, mates_low, "keep_own", kept[-1:], keeps([0], high), jnp.float32
    )
    own += keep(whole, [0], high, mates_high, "keep_own", own, (), jnp.float32)
    hidden = finish(own, got_low, got_high, got_second, got_late, z, [])
    return (arrived, hidden)


def solution(mesh):
    placed = (
        P(("groups", "inst"), "tp", None, None, None),
        P(("groups", "inst"), None, None),
        P(("groups", "inst"), None),
        P(("groups", "inst"), "tp", None, None, None),
        P(("groups", "inst"), None, None),
        P("groups"),
        P("groups"),
        P(("groups", "inst"), None, "tp", None),
        P(("groups", "inst"), None, "tp", None),
        P("tp", None),
    )
    return jax.shard_map(
        shards,
        mesh=mesh,
        in_specs=placed,
        out_specs=(P(("groups", "inst"), None, "tp", None, None), P("tp", ("groups", "inst"))),
        check_vma=False,
    )
```

```python
import functools
import math

import jax
import jax.numpy as jnp
from jax import lax
from jax.experimental import pallas as pl
from jax.experimental.pallas import tpu as pltpu
from jax.sharding import PartitionSpec as P

CORES = 2
LOW = -1e30
MIB = 1 << 20
LANES = 128
GROUP = 16
TOGETHER = 8
LARGE_FIRST = 12
FETCHING = 16


def dot_t(left, right):
    return lax.dot_general(
        left, right, (((1,), (1,)), ((), ())), preferred_element_type=jnp.float32
    )


def row_plan(dest_ref, inst, cap):
    requests = [jnp.int32(-1)] * cap
    seen = jnp.int32(0)
    for g in range(dest_ref.shape[0]):
        here = dest_ref[g] == inst
        requests = [jnp.where(here & (seen == a), g, requests[a]) for a in range(cap)]
        seen = seen + here.astype(jnp.int32)
    return requests


VMEM = pl.BlockSpec(memory_space=pltpu.VMEM)
ANY = pl.BlockSpec(memory_space=pl.ANY)
HBM = pl.BlockSpec(memory_space=pltpu.HBM)


class Sizes:
    def __init__(self, queries, res_pool, res_table, src_table, mig_dest, out_weight):
        self.batch, self.steps, self.heads, self.width = queries.shape
        self.slots = res_pool.shape[1]
        self.block = res_pool.shape[3]
        self.resident, self.blocks = res_table.shape[1:]
        self.mig_per, self.mig_blocks = src_table.shape[1:]
        self.requests = mig_dest.shape[0]
        self.insts = lax.axis_size("inst")
        self.tps = lax.axis_size("tp")
        self.chips = self.tps // CORES
        self.cap = self.insts - 1
        self.per = self.steps * self.heads
        self.per_kv = self.steps * self.slots
        self.depth = out_weight.shape[0]
        self.features = out_weight.shape[1] // self.tps
        self.quarter = self.features // 4
        self.tail_q = self.insts * self.per
        self.tail_kv = self.insts * self.per_kv


def piece_columns(piece, sizes):
    ahead, mine, part = piece
    tp = lax.axis_index("tp")
    core = lax.rem(tp, CORES)
    chip = lax.rem(tp // CORES + ahead, sizes.chips)
    owner = chip * CORES + (core if mine else 1 - core)
    return owner * sizes.features + part * sizes.quarter


def run(kernel, tables, operands, in_specs, deps, out_shapes, out_specs, name, sizes,
        pieces=(), weight=None, limit=16, grid=(), scratch=(), aliases=None):
    inputs, outputs, many = len(operands), len(out_shapes), len(tables)
    count = len(deps)
    fetches = len(pieces)
    extra_in = [weight] if fetches else []
    limit = max(limit, FETCHING) if fetches else limit

    def call(*refs):
        table_in, refs = refs[:many], refs[many:]
        own_in = refs[:inputs]
        position = inputs + len(extra_in) + count
        own_out = refs[position : position + outputs]
        fetched = refs[position + outputs : position + outputs + fetches]
        rest = list(refs[position + outputs + fetches :])
        copies, reads = [], []
        if fetches:
            source, sems = refs[inputs], rest.pop()
            for n, piece in enumerate(pieces):
                first = pl.multiple_of(piece_columns(piece, sizes), LANES)
                copies.append(
                    pltpu.make_async_copy(
                        source.at[:, pl.ds(first, sizes.quarter)], fetched[n], sems.at[n]
                    )
                )
        table_refs = []
        if many:
            sems = rest.pop()
            table_refs = rest[len(rest) - many :]
            rest = rest[: len(rest) - many]
            reads = [
                pltpu.make_async_copy(source, target, sems.at[n])
                for n, (source, target) in enumerate(zip(table_in, table_refs))
            ]

        def ready():
            for read in reads:
                read.wait()

        def launch():
            for copy in copies:
                copy.start()

        def each(step, action):
            if not grid:
                action()
            else:
                pl.when(pl.program_id(0) == step)(action)

        def begin():
            for read in reads:
                read.start()

        def end():
            for copy in copies:
                copy.wait()

        if reads:
            each(0, begin)
        kernel(ready, launch, *table_refs, *own_in, *own_out, *rest)
        if copies:
            each(grid[0] - 1 if grid else 0, end)

    result = pl.pallas_call(
        call,
        grid_spec=pltpu.PrefetchScalarGridSpec(
            num_scalar_prefetch=0,
            grid=grid,
            in_specs=[HBM] * many + list(in_specs) + [HBM] * len(extra_in) + [ANY] * count,
            out_specs=list(out_specs) + [ANY] * fetches,
            scratch_shapes=list(scratch)
            + [pltpu.SMEM(t.shape, t.dtype) for t in tables]
            + ([pltpu.SemaphoreType.DMA((many,))] if many else [])
            + ([pltpu.SemaphoreType.DMA((fetches,))] if fetches else []),
        ),
        out_shape=list(out_shapes)
        + [pltpu.VMEM((sizes.depth, sizes.quarter), jnp.bfloat16)] * fetches,
        input_output_aliases=aliases or {},
        compiler_params=pltpu.CompilerParams(vmem_limit_bytes=limit * MIB),
        cost_estimate=pl.CostEstimate(flops=0, bytes_accessed=1024, transcendentals=0),
        name=name,
    )(*tables, *operands, *extra_in, *deps)
    return result[:outputs], result[outputs:]


def pack_kernel(
    ready, launch, table_ref, dest_ref, pool_hbm, send_hbm, pool_ref, pack_ref, sems, *, sizes
):
    inst = lax.axis_index("inst")
    pool_copy = pltpu.make_async_copy(pool_hbm, pool_ref, sems.at[sizes.mig_per])
    pool_copy.start()
    ready()
    pool_copy.wait()
    copies = []
    for m in range(sizes.mig_per):
        dest = dest_ref[inst * sizes.mig_per + m]

        def copy_block(b, carry, m=m):
            block = table_ref[0, m, b]
            for s in range(sizes.slots):
                pack_ref[m, s, b] = pool_ref[0, s, block]
            return carry

        lax.fori_loop(0, sizes.mig_blocks, copy_block, 0, unroll=8)
        copies.append(pltpu.make_async_copy(pack_ref.at[m], send_hbm.at[dest], sems.at[m]))
        copies[-1].start()
    for copy in copies:
        copy.wait()


def pack(src_table, mig_dest, out_pool, sizes):
    z = sizes
    request = (z.slots, z.mig_blocks, z.block, 2 * z.width)
    result, _ = run(
        functools.partial(pack_kernel, sizes=z),
        [src_table, mig_dest], [out_pool], [HBM], [],
        [pltpu.HBM((z.insts,) + request, out_pool.dtype)], [ANY], "pack", z, limit=60,
        scratch=[
            pltpu.VMEM(out_pool.shape, out_pool.dtype),
            pltpu.VMEM((z.mig_per,) + request, out_pool.dtype),
            pltpu.SemaphoreType.DMA((z.mig_per + 1,)),
        ],
    )
    return result[0]


def fresh_code(rows, keys, sizes):
    index = lax.broadcasted_iota(jnp.int32, (rows, keys), 0)
    key = lax.broadcasted_iota(jnp.int32, (rows, keys), 1)
    step = index // sizes.heads
    slot = lax.rem(index, sizes.heads) // (sizes.heads // sizes.slots)
    in_row = lax.rem(key, sizes.per_kv)
    seen = (in_row // sizes.slots <= step) & (lax.rem(in_row, sizes.slots) == slot)
    return jnp.where(seen, key // sizes.per_kv, -1)


def slot_index(extent, sizes):
    index = lax.broadcasted_iota(jnp.int32, (sizes.per, extent), 0)
    return lax.rem(index, sizes.heads) // (sizes.heads // sizes.slots)


def own_scores(scores, slot_of, slots):
    extent = scores.shape[1] // slots
    own = scores[:, :extent]
    for s in range(1, slots):
        own = jnp.where(slot_of == s, scores[:, s * extent : (s + 1) * extent], own)
    return own


def weigh(own, length, fresh, fresh_seen, scale):
    place = lax.broadcasted_iota(jnp.int32, own.shape, 1)
    own = jnp.where(place < length, own, LOW)
    fresh = jnp.where(fresh_seen, fresh, LOW)
    if own.shape == fresh.shape:
        largest = jnp.max(jnp.maximum(own, fresh), axis=1, keepdims=True)
    else:
        largest = jnp.maximum(
            jnp.max(own, axis=1, keepdims=True), jnp.max(fresh, axis=1, keepdims=True)
        )
    return jnp.exp2((own - largest) * scale), jnp.exp2((fresh - largest) * scale)


def spread(own, slot_of, slots):
    if slots == 1:
        return own.astype(jnp.bfloat16)
    parts = [jnp.where(slot_of == s, own, 0.0) for s in range(slots)]
    return jnp.concatenate(parts, axis=1).astype(jnp.bfloat16)


def gather_blocks(pool_ref, slots, ids):
    tiles = [pool_ref[0, s, block] for s in range(slots) for block in ids]
    return jnp.concatenate(tiles, axis=0)


def with_ones(values):
    return jnp.concatenate([values, jnp.ones_like(values)], axis=1)


def dot(left, right):
    return jnp.dot(left, right, preferred_element_type=jnp.float32)


def attend_kernel(
    ready, launch, table_ref, len_ref, query_hbm, kv_hbm, pool_ref, *refs, first_row,
    steps_in_all, sizes,
):
    z = sizes
    out_ref, query_all, kv_all, fresh_ref, pf_ref, blend_ref, done_ref, sems = refs
    width, per = z.width, z.per
    rows = GROUP
    step = pl.program_id(0)
    extent = z.blocks * z.block
    start = first_row + step * rows
    scale = math.log2(math.e) / math.sqrt(width)

    def copies(n):
        begin = first_row + n * rows
        return (
            pltpu.make_async_copy(
                query_hbm.at[pl.ds(pl.multiple_of(begin * per, rows * per), rows * per)],
                query_all.at[n], sems.at[0, n],
            ),
            pltpu.make_async_copy(kv_hbm.at[pl.ds(begin, rows)], kv_all.at[n], sems.at[1, n]),
        )

    @pl.when(step == 0)
    def _():
        for n in range(steps_in_all):
            for copy in copies(n):
                copy.start()
        launch()
        ready()

    for copy in copies(step):
        copy.wait()

    query_ref = query_all.at[step]
    new_kv = kv_all[step].reshape(rows * z.per_kv, 2 * width)
    fresh_ref[...] = dot_t(query_ref[...], new_kv[:, :width])
    code = fresh_code(per, rows * z.per_kv, z)
    slot_of = slot_index(extent, z)
    together = min(TOGETHER, rows)
    for begin in range(0, rows, together):
        group = range(begin, begin + together)
        at = [slice(r * per, (r + 1) * per) for r in group]
        known = [jnp.minimum(start + r, z.resident - 1) for r in group]
        length = [
            jnp.where(start + r < z.resident, len_ref[0, k], 0) for r, k in zip(group, known)
        ]
        both = [
            gather_blocks(pool_ref, z.slots, [table_ref[j, k] for j in range(z.blocks)])
            for k in known
        ]
        fresh = [fresh_ref[a, :] for a in at]
        scores = [dot_t(query_ref[a, :], b[:, :width]) for a, b in zip(at, both)]
        weights = [
            weigh(own_scores(s, slot_of, z.slots), n, f, code == r, scale)
            for s, n, f, r in zip(scores, length, fresh, group)
        ]
        context = [
            dot(spread(w[0], slot_of, z.slots), with_ones(b[:, width:]))
            for w, b in zip(weights, both)
        ]
        for a, c, w in zip(at, context, weights):
            blend_ref[a, :] = c
            pf_ref[a, :] = w[1].astype(jnp.bfloat16)

    done = blend_ref[...] + dot(pf_ref[...], with_ones(new_kv[:, width:]))
    done_ref[...] = done[:, :width] / done[:, width:]
    for h in range(z.heads):
        column = done_ref[pl.ds(h, rows * z.steps, stride=z.heads), :]
        out_ref[:, h * width : (h + 1) * width] = column.astype(jnp.bfloat16)


def attend(table, lengths, queries, new_kv, pool, into, first_row, rows, sizes, deps, limit=12,
           **fetch):
    z = sizes
    groups = rows // GROUP
    first = first_row // GROUP
    tokens = z.batch * z.steps
    aliases = {}
    if into is not None:
        deps = [into] + deps
        aliases = {5 + (1 if fetch else 0): 0}
    result, pieces = run(
        functools.partial(
            attend_kernel, first_row=first_row, steps_in_all=groups, sizes=z
        ),
        [table, lengths],
        [queries, new_kv, pool],
        [HBM, HBM, VMEM],
        deps,
        [jax.ShapeDtypeStruct((tokens, z.heads * z.width), jnp.bfloat16)],
        [pl.BlockSpec((GROUP * z.steps, z.heads * z.width), lambda i: (first + i, 0))],
        "attend", z, limit=limit,
        grid=(groups,),
        scratch=[
            pltpu.VMEM((groups, GROUP * z.per, z.width), jnp.bfloat16),
            pltpu.VMEM((groups, GROUP) + new_kv.shape[1:], jnp.bfloat16),
            pltpu.VMEM((GROUP * z.per, GROUP * z.per_kv), jnp.float32),
            pltpu.VMEM((GROUP * z.per, GROUP * z.per_kv), jnp.bfloat16),
            pltpu.VMEM((GROUP * z.per, 2 * z.width), jnp.float32),
            pltpu.VMEM((GROUP * z.per, z.width), jnp.float32),
            pltpu.SemaphoreType.DMA((2, groups)),
        ],
        aliases=aliases, **fetch,
    )
    return result[0], pieces


def settle_kernel(
    ready, launch, dest_ref, len_ref, got_hbm, query_ref, kv_ref, old_ref, out_ref, last_ref,
    arrived_hbm, rows_ref, got_ref, keep_ref, sems, *, sizes
):
    z = sizes
    ready()
    inst = lax.axis_index("inst")
    requests = row_plan(dest_ref, inst, z.cap)
    known = [jnp.maximum(request, 0) for request in requests]
    extent = z.mig_blocks * z.block
    reads = [
        pltpu.make_async_copy(got_hbm.at[known[a] // z.mig_per], got_ref.at[a], sems.at[0, a])
        for a in range(z.cap)
    ]
    writes = [
        pltpu.make_async_copy(keep_ref.at[a], arrived_hbm.at[0, a], sems.at[1, a])
        for a in range(z.cap)
    ]
    for read in reads:
        read.start()
    launch()
    new_kv = kv_ref[...].reshape(z.tail_kv, 2 * z.width)
    code = fresh_code(z.per, z.tail_kv, z)
    slot_of = slot_index(extent, z)
    scale = math.log2(math.e) / math.sqrt(z.width)
    tokens = z.insts * z.steps
    row = lax.broadcasted_iota(jnp.int32, (tokens, z.width), 0) // z.steps
    place = lax.broadcasted_iota(jnp.int32, (z.block, 2 * z.width), 0)
    filled = row < 0
    rows_ref[: z.per, :] = jnp.zeros((z.per, z.width), jnp.float32)
    for a in range(z.cap):
        length = jnp.where(requests[a] >= 0, len_ref[known[a]], 0)
        reads[a].wait()

        def one(b, carry, a=a, length=length):
            inside = place + b * z.block < length
            at = pl.ds(pl.multiple_of(b * z.block, z.block), z.block)
            for s in range(z.slots):
                value = got_ref[a, s, b].astype(jnp.float32)
                keep_ref[a, s, at, :] = jnp.where(inside, value, 0.0).astype(jnp.bfloat16)
            return carry

        lax.fori_loop(0, z.mig_blocks, one, 0, unroll=8)
        writes[a].start()
        at = slice((a + 1) * z.per, (a + 2) * z.per)
        both = jnp.concatenate([keep_ref[a, s] for s in range(z.slots)], axis=0)
        own = own_scores(dot_t(query_ref[at, :], both[:, : z.width]), slot_of, z.slots)
        fresh = dot_t(query_ref[at, :], new_kv[:, : z.width])
        own, fresh = weigh(own, length, fresh, code == a + 1, scale)
        done = dot(spread(own, slot_of, z.slots), with_ones(both[:, z.width :]))
        done = done + dot(fresh.astype(jnp.bfloat16), with_ones(new_kv[:, z.width :]))
        rows_ref[at, :] = done[:, : z.width] / done[:, z.width :]
        filled = filled | ((row == a + 1) & (requests[a] >= 0))
    for h in range(z.heads):
        at = slice(h * z.width, (h + 1) * z.width)
        column = rows_ref[pl.ds(h, tokens, stride=z.heads), :]
        old = old_ref[:, at].astype(jnp.float32)
        value = jnp.where(filled, column, old).astype(jnp.bfloat16)
        out_ref[:, at] = value
        last_ref[:, at] = value
    for write in writes:
        write.wait()


def settle(mig_dest, mig_len, got, query_rows, new_kv, attention, sizes, deps, **fetch):
    z = sizes
    tokens = z.insts * z.steps
    last = attention.shape[0] // tokens - 1
    last_q = query_rows.shape[0] // z.tail_q - 1
    last_kv = z.batch // z.insts - 1
    spec = pl.BlockSpec((tokens, attention.shape[1]), lambda i: (last, 0))
    cache = (z.slots, z.mig_blocks * z.block, 2 * z.width)
    return run(
        functools.partial(settle_kernel, sizes=z),
        [mig_dest, mig_len], [got, query_rows, new_kv, attention],
        [
            HBM,
            pl.BlockSpec((z.tail_q, z.width), lambda i: (last_q, 0)),
            pl.BlockSpec((z.insts,) + new_kv.shape[1:], lambda i: (last_kv, 0, 0, 0)),
            spec,
        ],
        deps,
        [
            jax.ShapeDtypeStruct(attention.shape, jnp.bfloat16),
            jax.ShapeDtypeStruct((tokens, attention.shape[1]), jnp.bfloat16),
            jax.ShapeDtypeStruct((1, z.cap) + cache, jnp.bfloat16),
        ],
        [spec, VMEM, ANY], "settle", z, grid=(1,),
        scratch=[
            pltpu.VMEM((z.insts * z.per, z.width), jnp.float32),
            pltpu.VMEM((z.cap,) + got.shape[1:], jnp.bfloat16),
            pltpu.VMEM((z.cap,) + cache, jnp.bfloat16),
            pltpu.SemaphoreType.DMA((2, z.cap)),
        ],
        aliases={5: 0}, **fetch,
    )


def project_kernel(ready, launch, attention, *refs, first, tokens, count, added, joined, sizes):
    launch()
    weights, extra, out_refs = refs[:count], refs[count : count + added], refs[count + added :]
    width = sizes.quarter
    tile = min(width, 256)
    for n, weight in enumerate(weights):

        def one(j, carry, n=n, weight=weight):
            at = pl.ds(pl.multiple_of(j * tile, tile), tile)
            to = pl.ds(pl.multiple_of(n * width + j * tile, tile), tile)
            result = dot(attention[first : first + tokens, :], weight[:, at])
            if added == 1:
                result = result + extra[0][:, to].astype(jnp.float32)
            elif added:
                result = result + extra[n][:, at].astype(jnp.float32)
            if joined:
                out_refs[0][:, to] = result.astype(out_refs[0].dtype)
            else:
                out_refs[n][:, at] = result.astype(out_refs[n].dtype)
            return carry

        lax.fori_loop(0, width // tile, one, 0)


def project(attention, weights, mates, joined, dtype, sizes, name, deps, place=None, **fetch):
    attention, first, tokens = attention
    count = len(weights)
    if place is not None:
        shapes = [place((tokens, count * sizes.quarter), dtype)]
    elif joined:
        shapes = [jax.ShapeDtypeStruct((tokens, count * sizes.quarter), dtype)]
    else:
        shapes = [jax.ShapeDtypeStruct((tokens, sizes.quarter), dtype)] * count
    operands = [attention] + weights + mates
    return run(
        functools.partial(
            project_kernel, first=first, tokens=tokens, count=count, added=len(mates),
            joined=joined, sizes=sizes,
        ),
        [], operands, [VMEM] * len(operands), deps, shapes, [VMEM] * len(shapes), name, sizes,
        **fetch,
    )


def finish_kernel(ready, launch, own_low, own_high, *refs, fars, sizes):
    z = sizes
    refs = list(refs)

    def take(n):
        taken = refs[:n]
        del refs[:n]
        return taken

    low, high, second, late = take(fars), take(fars), take(fars), take(fars)
    out_hbm, block_ref, sems = refs
    tile = min(z.quarter, 256)
    writes = []
    for n in range(4):

        def one(j, carry, n=n):
            start = pl.multiple_of(j * tile, tile)
            at = pl.ds(n * z.quarter + start, tile)
            half = pl.ds((n % 2) * z.quarter + start, tile)
            sums = (own_low if n < 2 else own_high)[:, half]
            for k in range(fars):
                rows = late[k].shape[0]
                arrived = jnp.concatenate(
                    [
                        (low if n < 2 else high)[k][:, half],
                        second[k][:-rows, at],
                        late[k][:, at],
                    ],
                    axis=0,
                )
                sums = sums + arrived.astype(jnp.float32)
            block_ref[n, pl.ds(start, tile), :] = sums.T.astype(jnp.bfloat16)
            return carry

        lax.fori_loop(0, z.quarter // tile, one, 0)
        write = pltpu.make_async_copy(
            block_ref.at[n], out_hbm.at[pl.ds(n * z.quarter, z.quarter)], sems.at[n]
        )
        write.start()
        writes.append(write)
    for write in writes:
        write.wait()


def finish(own, low, high, second, late, sizes, deps):
    z = sizes
    tokens = own[0].shape[0]
    operands = own + low + high + second + late
    result, _ = run(
        functools.partial(finish_kernel, fars=len(low), sizes=z),
        [], operands, [VMEM] * len(operands), deps,
        [jax.ShapeDtypeStruct((z.features, tokens), jnp.bfloat16)], [ANY], "finish", z,
        scratch=[
            pltpu.VMEM((4, z.quarter, tokens), jnp.bfloat16), pltpu.SemaphoreType.DMA((4,))
        ],
    )
    return result[0]


def shards(
    res_pool,
    res_table,
    res_len,
    out_pool,
    src_table,
    mig_len,
    mig_dest,
    queries,
    new_kv,
    out_weight,
):
    z = Sizes(queries, res_pool, res_table, src_table, mig_dest, out_weight)
    tps, chips = z.tps, z.chips
    table = res_table[0].T
    out_weight, res_pool, out_pool, new_kv, query_rows, table, res_len, src_table, mig_dest, mig_len = (
        pltpu.with_memory_space_constraint(x, pltpu.HBM)
        for x in (
            out_weight, res_pool, out_pool, new_kv, queries.reshape(z.batch * z.per, z.width),
            table, res_len, src_table, mig_dest, mig_len,
        )
    )
    to_mate = [(i, i + 1 - 2 * (i % CORES)) for i in range(tps)]
    far = range(1, chips)
    held = {}

    def mate_of(x):
        return lax.ppermute(x, "tp", to_mate)

    def across(x, ahead):
        shift = ahead * CORES
        return lax.ppermute(x, "tp", [(i, (i + shift) % tps) for i in range(tps)])

    def bringing(pieces):
        return dict(pieces=pieces, weight=out_weight)

    def gives(ks, parts):
        return [(k, False, part) for k in ks for part in parts]

    def keeps(ks, parts):
        return [(k, True, part) for k in ks for part in parts]

    def hold(pieces, arrays):
        held.update(zip(pieces, arrays))

    def give(attention, ks, parts, name, deps, pieces=(), joined=False):
        weights = [held[piece] for piece in gives(ks, parts)]
        results, new = project(
            attention, weights, [], joined, jnp.bfloat16, z, name, deps, **bringing(pieces)
        )
        hold(pieces, new)
        return results[0], [mate_of(result) for result in results]

    def keep(attention, ks, parts, mates, name, deps, pieces=(), dtype=jnp.bfloat16, place=None):
        results = []
        for n, k in enumerate(ks):
            weights = [held[piece] for piece in keeps([k], parts)]
            if len(mates) == 1:
                width = mates[0].shape[1] // len(ks)
                now = [mates[0][:, n * width : (n + 1) * width] if len(ks) > 1 else mates[0]]
            else:
                now = mates[n * len(parts) : (n + 1) * len(parts)]
            bring = pieces if n == 0 else ()
            result, new = project(
                attention, weights, now, True, dtype, z, name, deps, place, **bringing(bring)
            )
            hold(bring, new)
            deps = [result[0]]
            results.append(result[0])
        return results

    def sent(results):
        return [across(result, k) for k, result in zip(far, results)]

    half = z.batch // 2
    low, high, every = (0, 1), (2, 3), (0, 1, 2, 3)

    sends = pack(src_table, mig_dest, out_pool, z)
    arriving = lax.all_to_all(sends, "inst", split_axis=0, concat_axis=0, tiled=True)

    tokens = half * z.steps
    pieces = gives(far, low) + keeps(far, low) + gives(far, high)
    rows, new = attend(
        table, res_len, query_rows, new_kv, res_pool, None, 0, half, z, [sends],
        **bringing(pieces),
    )
    hold(pieces, new)
    a = (rows, 0, tokens)
    given, mates_low = give(a, far, low, "give", [], keeps(far, high))
    given, mates_high = give(a, far, high, "give", [given])
    kept = keep(a, far, low, mates_low, "keep", [given])
    got_low = sent(kept)
    kept = keep(a, far, high, mates_high, "keep", kept[-1:])
    got_high = sent(kept)
    rows, _ = attend(
        table, res_len, query_rows, new_kv, res_pool, rows, half, half, z, kept[-1:],
    )
    b = (rows, tokens, tokens)
    given, mates = give(b, far, every, "give", got_low)
    kept = keep(b, far, every, mates, "keep", [given] + got_high)
    got_second = sent(kept)

    pieces = gives([0], low) + gives(far, (0,))
    (rows, last, arrived), new = settle(
        mig_dest, mig_len, arriving, query_rows, new_kv, rows, z, kept[-1:],
        **bringing(pieces),
    )
    hold(pieces, new)
    late, whole = (last, 0, last.shape[0]), (rows, 0, 2 * tokens)
    given, mates_low = give(whole, [0], low, "give_own", [], gives(far, (1, 2, 3)))
    given, mates = give(late, far, every, "give_last", [given], gives([0], high), joined=True)
    given, mates_high = give(whole, [0], high, "give_own", [given], keeps(far, every))
    kept = keep(late, far, every, mates, "keep_last", [given], keeps([0], low))
    got_late = sent(kept)
    own = keep(
        whole, [0], low, mates_low, "keep_own", kept[-1:], keeps([0], high), jnp.float32
    )
    own += keep(whole, [0], high, mates_high, "keep_own", own, (), jnp.float32)
    hidden = finish(own, got_low, got_high, got_second, got_late, z, [])
    return (arrived, hidden)


def solution(mesh):
    placed = (
        P(("groups", "inst"), "tp", None, None, None),
        P(("groups", "inst"), None, None),
        P(("groups", "inst"), None),
        P(("groups", "inst"), "tp", None, None, None),
        P(("groups", "inst"), None, None),
        P("groups"),
        P("groups"),
        P(("groups", "inst"), None, "tp", None),
        P(("groups", "inst"), None, "tp", None),
        P("tp", None),
    )
    return jax.shard_map(
        shards,
        mesh=mesh,
        in_specs=placed,
        out_specs=(P(("groups", "inst"), None, "tp", None, None), P("tp", ("groups", "inst"))),
        check_vma=False,
    )
```

```python
import functools
import math

import jax
import jax.numpy as jnp
from jax import lax
from jax.experimental import pallas as pl
from jax.experimental.pallas import tpu as pltpu
from jax.sharding import PartitionSpec as P

CORES = 2
LOW = -1e30
MIB = 1 << 20
LANES = 128
GROUP = 16
TOGETHER = 8
LARGE_FIRST = 12
FETCHING = 16


def dot_t(left, right):
    return lax.dot_general(
        left, right, (((1,), (1,)), ((), ())), preferred_element_type=jnp.float32
    )


def row_plan(dest_ref, inst, cap):
    requests = [jnp.int32(-1)] * cap
    seen = jnp.int32(0)
    for g in range(dest_ref.shape[0]):
        here = dest_ref[g] == inst
        requests = [jnp.where(here & (seen == a), g, requests[a]) for a in range(cap)]
        seen = seen + here.astype(jnp.int32)
    return requests


VMEM = pl.BlockSpec(memory_space=pltpu.VMEM)
ANY = pl.BlockSpec(memory_space=pl.ANY)
HBM = pl.BlockSpec(memory_space=pltpu.HBM)


class Sizes:
    def __init__(self, queries, res_pool, res_table, src_table, mig_dest, out_weight):
        self.batch, self.steps, self.heads, self.width = queries.shape
        self.slots = res_pool.shape[1]
        self.block = res_pool.shape[3]
        self.resident, self.blocks = res_table.shape[1:]
        self.mig_per, self.mig_blocks = src_table.shape[1:]
        self.requests = mig_dest.shape[0]
        self.insts = lax.axis_size("inst")
        self.tps = lax.axis_size("tp")
        self.chips = self.tps // CORES
        self.cap = self.insts - 1
        self.per = self.steps * self.heads
        self.per_kv = self.steps * self.slots
        self.depth = out_weight.shape[0]
        self.features = out_weight.shape[1] // self.tps
        self.quarter = self.features // 4
        self.tail_q = self.insts * self.per
        self.tail_kv = self.insts * self.per_kv


def piece_columns(piece, sizes):
    ahead, mine, part = piece
    tp = lax.axis_index("tp")
    core = lax.rem(tp, CORES)
    chip = lax.rem(tp // CORES + ahead, sizes.chips)
    owner = chip * CORES + (core if mine else 1 - core)
    return owner * sizes.features + part * sizes.quarter


def run(kernel, tables, operands, in_specs, deps, out_shapes, out_specs, name, sizes,
        pieces=(), weight=None, limit=16, grid=(), scratch=(), aliases=None):
    inputs, outputs, many = len(operands), len(out_shapes), len(tables)
    count = len(deps)
    fetches = len(pieces)
    extra_in = [weight] if fetches else []
    limit = max(limit, FETCHING) if fetches else limit

    def call(*refs):
        table_in, refs = refs[:many], refs[many:]
        own_in = refs[:inputs]
        position = inputs + len(extra_in) + count
        own_out = refs[position : position + outputs]
        fetched = refs[position + outputs : position + outputs + fetches]
        rest = list(refs[position + outputs + fetches :])
        copies, reads = [], []
        if fetches:
            source, sems = refs[inputs], rest.pop()
            for n, piece in enumerate(pieces):
                first = pl.multiple_of(piece_columns(piece, sizes), LANES)
                copies.append(
                    pltpu.make_async_copy(
                        source.at[:, pl.ds(first, sizes.quarter)], fetched[n], sems.at[n]
                    )
                )
        table_refs = []
        if many:
            sems = rest.pop()
            table_refs = rest[len(rest) - many :]
            rest = rest[: len(rest) - many]
            reads = [
                pltpu.make_async_copy(source, target, sems.at[n])
                for n, (source, target) in enumerate(zip(table_in, table_refs))
            ]

        def ready():
            for read in reads:
                read.wait()

        def launch():
            for copy in copies:
                copy.start()

        def each(step, action):
            if not grid:
                action()
            else:
                pl.when(pl.program_id(0) == step)(action)

        def begin():
            for read in reads:
                read.start()

        def end():
            for copy in copies:
                copy.wait()

        if reads:
            each(0, begin)
        kernel(ready, launch, *table_refs, *own_in, *own_out, *rest)
        if copies:
            each(grid[0] - 1 if grid else 0, end)

    result = pl.pallas_call(
        call,
        grid_spec=pltpu.PrefetchScalarGridSpec(
            num_scalar_prefetch=0,
            grid=grid,
            in_specs=[HBM] * many + list(in_specs) + [HBM] * len(extra_in) + [ANY] * count,
            out_specs=list(out_specs) + [ANY] * fetches,
            scratch_shapes=list(scratch)
            + [pltpu.SMEM(t.shape, t.dtype) for t in tables]
            + ([pltpu.SemaphoreType.DMA((many,))] if many else [])
            + ([pltpu.SemaphoreType.DMA((fetches,))] if fetches else []),
        ),
        out_shape=list(out_shapes)
        + [pltpu.VMEM((sizes.depth, sizes.quarter), jnp.bfloat16)] * fetches,
        input_output_aliases=aliases or {},
        compiler_params=pltpu.CompilerParams(vmem_limit_bytes=limit * MIB),
        cost_estimate=pl.CostEstimate(flops=0, bytes_accessed=1024, transcendentals=0),
        name=name,
    )(*tables, *operands, *extra_in, *deps)
    return result[:outputs], result[outputs:]


def pack_kernel(
    ready, launch, table_ref, dest_ref, pool_hbm, send_hbm, pool_ref, pack_ref, sems, *, sizes
):
    inst = lax.axis_index("inst")
    pool_copy = pltpu.make_async_copy(pool_hbm, pool_ref, sems.at[sizes.mig_per])
    pool_copy.start()
    ready()
    pool_copy.wait()
    copies = []
    for m in range(sizes.mig_per):
        dest = dest_ref[inst * sizes.mig_per + m]

        def copy_block(b, carry, m=m):
            block = table_ref[0, m, b]
            for s in range(sizes.slots):
                pack_ref[m, s, b] = pool_ref[0, s, block]
            return carry

        lax.fori_loop(0, sizes.mig_blocks, copy_block, 0, unroll=8)
        copies.append(pltpu.make_async_copy(pack_ref.at[m], send_hbm.at[dest], sems.at[m]))
        copies[-1].start()
    for copy in copies:
        copy.wait()


def pack(src_table, mig_dest, out_pool, sizes):
    z = sizes
    request = (z.slots, z.mig_blocks, z.block, 2 * z.width)
    result, _ = run(
        functools.partial(pack_kernel, sizes=z),
        [src_table, mig_dest], [out_pool], [HBM], [],
        [pltpu.HBM((z.insts,) + request, out_pool.dtype)], [ANY], "pack", z, limit=60,
        scratch=[
            pltpu.VMEM(out_pool.shape, out_pool.dtype),
            pltpu.VMEM((z.mig_per,) + request, out_pool.dtype),
            pltpu.SemaphoreType.DMA((z.mig_per + 1,)),
        ],
    )
    return result[0]


def fresh_code(rows, keys, sizes):
    index = lax.broadcasted_iota(jnp.int32, (rows, keys), 0)
    key = lax.broadcasted_iota(jnp.int32, (rows, keys), 1)
    step = index // sizes.heads
    slot = lax.rem(index, sizes.heads) // (sizes.heads // sizes.slots)
    in_row = lax.rem(key, sizes.per_kv)
    seen = (in_row // sizes.slots <= step) & (lax.rem(in_row, sizes.slots) == slot)
    return jnp.where(seen, key // sizes.per_kv, -1)


def slot_index(extent, sizes):
    index = lax.broadcasted_iota(jnp.int32, (sizes.per, extent), 0)
    return lax.rem(index, sizes.heads) // (sizes.heads // sizes.slots)


def own_scores(scores, slot_of, slots):
    extent = scores.shape[1] // slots
    own = scores[:, :extent]
    for s in range(1, slots):
        own = jnp.where(slot_of == s, scores[:, s * extent : (s + 1) * extent], own)
    return own


def weigh(own, length, fresh, fresh_seen, scale):
    place = lax.broadcasted_iota(jnp.int32, own.shape, 1)
    own = jnp.where(place < length, own, LOW)
    fresh = jnp.where(fresh_seen, fresh, LOW)
    if own.shape == fresh.shape:
        largest = jnp.max(jnp.maximum(own, fresh), axis=1, keepdims=True)
    else:
        largest = jnp.maximum(
            jnp.max(own, axis=1, keepdims=True), jnp.max(fresh, axis=1, keepdims=True)
        )
    return jnp.exp2((own - largest) * scale), jnp.exp2((fresh - largest) * scale)


def spread(own, slot_of, slots):
    if slots == 1:
        return own.astype(jnp.bfloat16)
    parts = [jnp.where(slot_of == s, own, 0.0) for s in range(slots)]
    return jnp.concatenate(parts, axis=1).astype(jnp.bfloat16)


def gather_blocks(pool_ref, slots, ids):
    tiles = [pool_ref[0, s, block] for s in range(slots) for block in ids]
    return jnp.concatenate(tiles, axis=0)


def with_ones(values):
    return jnp.concatenate([values, jnp.ones_like(values)], axis=1)


def dot(left, right):
    return jnp.dot(left, right, preferred_element_type=jnp.float32)


def attend_kernel(
    ready, launch, table_ref, len_ref, query_hbm, kv_hbm, pool_ref, *refs, first_row,
    steps_in_all, sizes,
):
    z = sizes
    out_ref, query_all, kv_all, fresh_ref, pf_ref, blend_ref, done_ref, sems = refs
    width, per = z.width, z.per
    rows = GROUP
    step = pl.program_id(0)
    extent = z.blocks * z.block
    start = first_row + step * rows
    scale = math.log2(math.e) / math.sqrt(width)

    def copies(n):
        begin = first_row + n * rows
        return (
            pltpu.make_async_copy(
                query_hbm.at[pl.ds(pl.multiple_of(begin * per, rows * per), rows * per)],
                query_all.at[n], sems.at[0, n],
            ),
            pltpu.make_async_copy(kv_hbm.at[pl.ds(begin, rows)], kv_all.at[n], sems.at[1, n]),
        )

    @pl.when(step == 0)
    def _():
        for n in range(steps_in_all):
            for copy in copies(n):
                copy.start()
        launch()
        ready()

    for copy in copies(step):
        copy.wait()

    query_ref = query_all.at[step]
    new_kv = kv_all[step].reshape(rows * z.per_kv, 2 * width)
    fresh_ref[...] = dot_t(query_ref[...], new_kv[:, :width])
    code = fresh_code(per, rows * z.per_kv, z)
    slot_of = slot_index(extent, z)
    together = min(TOGETHER, rows)
    for begin in range(0, rows, together):
        group = range(begin, begin + together)
        at = [slice(r * per, (r + 1) * per) for r in group]
        known = [jnp.minimum(start + r, z.resident - 1) for r in group]
        length = [
            jnp.where(start + r < z.resident, len_ref[0, k], 0) for r, k in zip(group, known)
        ]
        both = [
            gather_blocks(pool_ref, z.slots, [table_ref[j, k] for j in range(z.blocks)])
            for k in known
        ]
        fresh = [fresh_ref[a, :] for a in at]
        scores = [dot_t(query_ref[a, :], b[:, :width]) for a, b in zip(at, both)]
        weights = [
            weigh(own_scores(s, slot_of, z.slots), n, f, code == r, scale)
            for s, n, f, r in zip(scores, length, fresh, group)
        ]
        context = [
            dot(spread(w[0], slot_of, z.slots), with_ones(b[:, width:]))
            for w, b in zip(weights, both)
        ]
        for a, c, w in zip(at, context, weights):
            blend_ref[a, :] = c
            pf_ref[a, :] = w[1].astype(jnp.bfloat16)

    done = blend_ref[...] + dot(pf_ref[...], with_ones(new_kv[:, width:]))
    done_ref[...] = done[:, :width] / done[:, width:]
    for h in range(z.heads):
        column = done_ref[pl.ds(h, rows * z.steps, stride=z.heads), :]
        out_ref[:, h * width : (h + 1) * width] = column.astype(jnp.bfloat16)


def attend(table, lengths, queries, new_kv, pool, into, first_row, rows, sizes, deps, limit=12,
           **fetch):
    z = sizes
    groups = rows // GROUP
    first = first_row // GROUP
    tokens = z.batch * z.steps
    aliases = {}
    if into is not None:
        deps = [into] + deps
        aliases = {5 + (1 if fetch else 0): 0}
    result, pieces = run(
        functools.partial(
            attend_kernel, first_row=first_row, steps_in_all=groups, sizes=z
        ),
        [table, lengths],
        [queries, new_kv, pool],
        [HBM, HBM, VMEM],
        deps,
        [jax.ShapeDtypeStruct((tokens, z.heads * z.width), jnp.bfloat16)],
        [pl.BlockSpec((GROUP * z.steps, z.heads * z.width), lambda i: (first + i, 0))],
        "attend", z, limit=limit,
        grid=(groups,),
        scratch=[
            pltpu.VMEM((groups, GROUP * z.per, z.width), jnp.bfloat16),
            pltpu.VMEM((groups, GROUP) + new_kv.shape[1:], jnp.bfloat16),
            pltpu.VMEM((GROUP * z.per, GROUP * z.per_kv), jnp.float32),
            pltpu.VMEM((GROUP * z.per, GROUP * z.per_kv), jnp.bfloat16),
            pltpu.VMEM((GROUP * z.per, 2 * z.width), jnp.float32),
            pltpu.VMEM((GROUP * z.per, z.width), jnp.float32),
            pltpu.SemaphoreType.DMA((2, groups)),
        ],
        aliases=aliases, **fetch,
    )
    return result[0], pieces


def settle_kernel(
    ready, launch, dest_ref, len_ref, got_hbm, query_ref, kv_ref, old_ref, out_ref, last_ref,
    arrived_hbm, rows_ref, got_ref, keep_ref, sems, *, sizes
):
    z = sizes
    inst = lax.axis_index("inst")
    extent = z.mig_blocks * z.block
    reads = [
        pltpu.make_async_copy(
            got_hbm.at[lax.rem(inst + k, z.insts)], got_ref.at[k - 1], sems.at[0, k - 1]
        )
        for k in range(1, z.insts)
    ]
    writes = [
        pltpu.make_async_copy(keep_ref.at[a], arrived_hbm.at[0, a], sems.at[1, a])
        for a in range(z.cap)
    ]
    for read in reads:
        read.start()
    ready()
    requests = row_plan(dest_ref, inst, z.cap)
    known = [jnp.maximum(request, 0) for request in requests]
    for read in reads:
        read.wait()
    launch()
    new_kv = kv_ref[...].reshape(z.tail_kv, 2 * z.width)
    code = fresh_code(z.per, z.tail_kv, z)
    slot_of = slot_index(extent, z)
    scale = math.log2(math.e) / math.sqrt(z.width)
    tokens = z.insts * z.steps
    row = lax.broadcasted_iota(jnp.int32, (tokens, z.width), 0) // z.steps
    place = lax.broadcasted_iota(jnp.int32, (z.block, 2 * z.width), 0)
    filled = row < 0
    rows_ref[: z.per, :] = jnp.zeros((z.per, z.width), jnp.float32)
    for a in range(z.cap):
        length = jnp.where(requests[a] >= 0, len_ref[known[a]], 0)
        ahead = lax.rem(known[a] // z.mig_per - inst + z.insts, z.insts)
        at_hand = jnp.maximum(ahead - 1, 0)

        def one(b, carry, a=a, length=length, at_hand=at_hand):
            inside = place + b * z.block < length
            at = pl.ds(pl.multiple_of(b * z.block, z.block), z.block)
            for s in range(z.slots):
                value = got_ref[at_hand, s, b].astype(jnp.float32)
                keep_ref[a, s, at, :] = jnp.where(inside, value, 0.0).astype(jnp.bfloat16)
            return carry

        lax.fori_loop(0, z.mig_blocks, one, 0, unroll=8)
        writes[a].start()
        at = slice((a + 1) * z.per, (a + 2) * z.per)
        both = jnp.concatenate([keep_ref[a, s] for s in range(z.slots)], axis=0)
        own = own_scores(dot_t(query_ref[at, :], both[:, : z.width]), slot_of, z.slots)
        fresh = dot_t(query_ref[at, :], new_kv[:, : z.width])
        own, fresh = weigh(own, length, fresh, code == a + 1, scale)
        done = dot(spread(own, slot_of, z.slots), with_ones(both[:, z.width :]))
        done = done + dot(fresh.astype(jnp.bfloat16), with_ones(new_kv[:, z.width :]))
        rows_ref[at, :] = done[:, : z.width] / done[:, z.width :]
        filled = filled | ((row == a + 1) & (requests[a] >= 0))
    for h in range(z.heads):
        at = slice(h * z.width, (h + 1) * z.width)
        column = rows_ref[pl.ds(h, tokens, stride=z.heads), :]
        old = old_ref[:, at].astype(jnp.float32)
        value = jnp.where(filled, column, old).astype(jnp.bfloat16)
        out_ref[:, at] = value
        last_ref[:, at] = value
    for write in writes:
        write.wait()


def settle(mig_dest, mig_len, got, query_rows, new_kv, attention, sizes, deps, **fetch):
    z = sizes
    tokens = z.insts * z.steps
    last = attention.shape[0] // tokens - 1
    last_q = query_rows.shape[0] // z.tail_q - 1
    last_kv = z.batch // z.insts - 1
    spec = pl.BlockSpec((tokens, attention.shape[1]), lambda i: (last, 0))
    cache = (z.slots, z.mig_blocks * z.block, 2 * z.width)
    return run(
        functools.partial(settle_kernel, sizes=z),
        [mig_dest, mig_len], [got, query_rows, new_kv, attention],
        [
            HBM,
            pl.BlockSpec((z.tail_q, z.width), lambda i: (last_q, 0)),
            pl.BlockSpec((z.insts,) + new_kv.shape[1:], lambda i: (last_kv, 0, 0, 0)),
            spec,
        ],
        deps,
        [
            jax.ShapeDtypeStruct(attention.shape, jnp.bfloat16),
            jax.ShapeDtypeStruct((tokens, attention.shape[1]), jnp.bfloat16),
            jax.ShapeDtypeStruct((1, z.cap) + cache, jnp.bfloat16),
        ],
        [spec, VMEM, ANY], "settle", z, grid=(1,),
        scratch=[
            pltpu.VMEM((z.insts * z.per, z.width), jnp.float32),
            pltpu.VMEM((z.cap,) + got.shape[1:], jnp.bfloat16),
            pltpu.VMEM((z.cap,) + cache, jnp.bfloat16),
            pltpu.SemaphoreType.DMA((2, z.cap)),
        ],
        aliases={5: 0}, **fetch,
    )


def project_kernel(ready, launch, attention, *refs, first, tokens, count, added, joined, sizes):
    launch()
    weights, extra, out_refs = refs[:count], refs[count : count + added], refs[count + added :]
    width = sizes.quarter
    tile = min(width, 256)
    for n, weight in enumerate(weights):

        def one(j, carry, n=n, weight=weight):
            at = pl.ds(pl.multiple_of(j * tile, tile), tile)
            to = pl.ds(pl.multiple_of(n * width + j * tile, tile), tile)
            result = dot(attention[first : first + tokens, :], weight[:, at])
            if added == 1:
                result = result + extra[0][:, to].astype(jnp.float32)
            elif added:
                result = result + extra[n][:, at].astype(jnp.float32)
            if joined:
                out_refs[0][:, to] = result.astype(out_refs[0].dtype)
            else:
                out_refs[n][:, at] = result.astype(out_refs[n].dtype)
            return carry

        lax.fori_loop(0, width // tile, one, 0)


def project(attention, weights, mates, joined, dtype, sizes, name, deps, place=None, **fetch):
    attention, first, tokens = attention
    count = len(weights)
    if place is not None:
        shapes = [place((tokens, count * sizes.quarter), dtype)]
    elif joined:
        shapes = [jax.ShapeDtypeStruct((tokens, count * sizes.quarter), dtype)]
    else:
        shapes = [jax.ShapeDtypeStruct((tokens, sizes.quarter), dtype)] * count
    operands = [attention] + weights + mates
    return run(
        functools.partial(
            project_kernel, first=first, tokens=tokens, count=count, added=len(mates),
            joined=joined, sizes=sizes,
        ),
        [], operands, [VMEM] * len(operands), deps, shapes, [VMEM] * len(shapes), name, sizes,
        **fetch,
    )


def finish_kernel(ready, launch, own_low, own_high, *refs, fars, sizes):
    z = sizes
    refs = list(refs)

    def take(n):
        taken = refs[:n]
        del refs[:n]
        return taken

    low, high, second, late = take(fars), take(fars), take(fars), take(fars)
    out_hbm, block_ref, sems = refs
    tile = min(z.quarter, 256)
    writes = []
    for n in range(4):

        def one(j, carry, n=n):
            start = pl.multiple_of(j * tile, tile)
            at = pl.ds(n * z.quarter + start, tile)
            half = pl.ds((n % 2) * z.quarter + start, tile)
            sums = (own_low if n < 2 else own_high)[:, half]
            for k in range(fars):
                rows = late[k].shape[0]
                arrived = jnp.concatenate(
                    [
                        (low if n < 2 else high)[k][:, half],
                        second[k][:-rows, at],
                        late[k][:, at],
                    ],
                    axis=0,
                )
                sums = sums + arrived.astype(jnp.float32)
            block_ref[n, pl.ds(start, tile), :] = sums.T.astype(jnp.bfloat16)
            return carry

        lax.fori_loop(0, z.quarter // tile, one, 0)
        write = pltpu.make_async_copy(
            block_ref.at[n], out_hbm.at[pl.ds(n * z.quarter, z.quarter)], sems.at[n]
        )
        write.start()
        writes.append(write)
    for write in writes:
        write.wait()


def finish(own, low, high, second, late, sizes, deps):
    z = sizes
    tokens = own[0].shape[0]
    operands = own + low + high + second + late
    result, _ = run(
        functools.partial(finish_kernel, fars=len(low), sizes=z),
        [], operands, [VMEM] * len(operands), deps,
        [jax.ShapeDtypeStruct((z.features, tokens), jnp.bfloat16)], [ANY], "finish", z,
        scratch=[
            pltpu.VMEM((4, z.quarter, tokens), jnp.bfloat16), pltpu.SemaphoreType.DMA((4,))
        ],
    )
    return result[0]


def shards(
    res_pool,
    res_table,
    res_len,
    out_pool,
    src_table,
    mig_len,
    mig_dest,
    queries,
    new_kv,
    out_weight,
):
    z = Sizes(queries, res_pool, res_table, src_table, mig_dest, out_weight)
    tps, chips = z.tps, z.chips
    table = res_table[0].T
    out_weight, res_pool, out_pool, new_kv, query_rows, table, res_len, src_table, mig_dest, mig_len = (
        pltpu.with_memory_space_constraint(x, pltpu.HBM)
        for x in (
            out_weight, res_pool, out_pool, new_kv, queries.reshape(z.batch * z.per, z.width),
            table, res_len, src_table, mig_dest, mig_len,
        )
    )
    to_mate = [(i, i + 1 - 2 * (i % CORES)) for i in range(tps)]
    far = range(1, chips)
    held = {}

    def mate_of(x):
        return lax.ppermute(x, "tp", to_mate)

    def across(x, ahead):
        shift = ahead * CORES
        return lax.ppermute(x, "tp", [(i, (i + shift) % tps) for i in range(tps)])

    def bringing(pieces):
        return dict(pieces=pieces, weight=out_weight)

    def gives(ks, parts):
        return [(k, False, part) for k in ks for part in parts]

    def keeps(ks, parts):
        return [(k, True, part) for k in ks for part in parts]

    def hold(pieces, arrays):
        held.update(zip(pieces, arrays))

    def give(attention, ks, parts, name, deps, pieces=(), joined=False):
        weights = [held[piece] for piece in gives(ks, parts)]
        results, new = project(
            attention, weights, [], joined, jnp.bfloat16, z, name, deps, **bringing(pieces)
        )
        hold(pieces, new)
        return results[0], [mate_of(result) for result in results]

    def keep(attention, ks, parts, mates, name, deps, pieces=(), dtype=jnp.bfloat16, place=None):
        results = []
        for n, k in enumerate(ks):
            weights = [held[piece] for piece in keeps([k], parts)]
            if len(mates) == 1:
                width = mates[0].shape[1] // len(ks)
                now = [mates[0][:, n * width : (n + 1) * width] if len(ks) > 1 else mates[0]]
            else:
                now = mates[n * len(parts) : (n + 1) * len(parts)]
            bring = pieces if n == 0 else ()
            result, new = project(
                attention, weights, now, True, dtype, z, name, deps, place, **bringing(bring)
            )
            hold(bring, new)
            deps = [result[0]]
            results.append(result[0])
        return results

    def sent(results):
        return [across(result, k) for k, result in zip(far, results)]

    half = z.batch // 2
    low, high, every = (0, 1), (2, 3), (0, 1, 2, 3)

    sends = pack(src_table, mig_dest, out_pool, z)
    arriving = lax.all_to_all(sends, "inst", split_axis=0, concat_axis=0, tiled=True)

    tokens = half * z.steps
    pieces = gives(far, low) + keeps(far, low) + gives(far, high)
    rows, new = attend(
        table, res_len, query_rows, new_kv, res_pool, None, 0, half, z, [sends],
        **bringing(pieces),
    )
    hold(pieces, new)
    a = (rows, 0, tokens)
    given, mates_low = give(a, far, low, "give", [], keeps(far, high))
    given, mates_high = give(a, far, high, "give", [given])
    kept = keep(a, far, low, mates_low, "keep", [given])
    got_low = sent(kept)
    kept = keep(a, far, high, mates_high, "keep", kept[-1:])
    got_high = sent(kept)
    rows, _ = attend(
        table, res_len, query_rows, new_kv, res_pool, rows, half, half, z, kept[-1:],
    )
    b = (rows, tokens, tokens)
    given, mates = give(b, far, every, "give", got_low)
    kept = keep(b, far, every, mates, "keep", [given] + got_high)
    got_second = sent(kept)

    pieces = gives([0], low) + gives(far, (0,))
    (rows, last, arrived), new = settle(
        mig_dest, mig_len, arriving, query_rows, new_kv, rows, z, kept[-1:],
        **bringing(pieces),
    )
    hold(pieces, new)
    late, whole = (last, 0, last.shape[0]), (rows, 0, 2 * tokens)
    given, mates_low = give(whole, [0], low, "give_own", [], gives(far, (1, 2, 3)))
    given, mates = give(late, far, every, "give_last", [given], gives([0], high), joined=True)
    given, mates_high = give(whole, [0], high, "give_own", [given], keeps(far, every))
    kept = keep(late, far, every, mates, "keep_last", [given], keeps([0], low))
    got_late = sent(kept)
    own = keep(
        whole, [0], low, mates_low, "keep_own", kept[-1:], keeps([0], high), jnp.float32
    )
    own += keep(whole, [0], high, mates_high, "keep_own", own, (), jnp.float32)
    hidden = finish(own, got_low, got_high, got_second, got_late, z, [])
    return (arrived, hidden)


def solution(mesh):
    placed = (
        P(("groups", "inst"), "tp", None, None, None),
        P(("groups", "inst"), None, None),
        P(("groups", "inst"), None),
        P(("groups", "inst"), "tp", None, None, None),
        P(("groups", "inst"), None, None),
        P("groups"),
        P("groups"),
        P(("groups", "inst"), None, "tp", None),
        P(("groups", "inst"), None, "tp", None),
        P("tp", None),
    )
    return jax.shard_map(
        shards,
        mesh=mesh,
        in_specs=placed,
        out_specs=(P(("groups", "inst"), None, "tp", None, None), P("tp", ("groups", "inst"))),
        check_vma=False,
    )
```
